32 devices in a mesh: grp: 2 (over y), ep: 16 (over z, x, core).
Axes of the slice: x: 2, y: 2, z: 4, core: 2. Of those that a mesh axis runs over, the one named last changes fastest.
Arguments:
- tokens: bfloat16 [4096, 2048], P(('grp', 'ep')), may hold values from -18 to 18
- w_query: bfloat16 [2048, 2048], P(('grp', 'ep')), may hold values from -0.125 to 0.125
- w_key: bfloat16 [2048, 2048], P(('grp', 'ep')), may hold values from -0.125 to 0.125
- w_value: bfloat16 [2048, 2048], P(('grp', 'ep')), may hold values from -0.125 to 0.125
- w_output: bfloat16 [2048, 2048], P(('grp', 'ep')), may hold values from -2 to 2
- w_router: bfloat16 [2048, 64], P(('grp', 'ep')), may hold values from -0.0625 to 0.0625
- attn_gain: bfloat16 [2048], P(('grp', 'ep')), may hold values from 0.099609375 to 1.8984375
- query_gain: bfloat16 [2048], P(('grp', 'ep')), may hold values from 0.099609375 to 1.8984375
- key_gain: bfloat16 [2048], P(('grp', 'ep')), may hold values from 0.099609375 to 1.8984375
- moe_gain: bfloat16 [2048], P(('grp', 'ep')), may hold values from 0.099609375 to 1.8984375
- w_gate: bfloat16 [64, 2048, 1024], P('ep'), may hold values from -0.125 to 0.125
- w_up: bfloat16 [64, 2048, 1024], P('ep'), may hold values from -0.125 to 0.125
- w_down: bfloat16 [64, 1024, 2048], P('ep'), may hold values from -6 to 6
- routes: int32 [4096, 8], P(('grp', 'ep')), may hold values from 0 to 63, all different within a row; in each aligned block of 128 rows (0 to 127, 128 to 255, ...) at most 24 rows name the same one
- cotangent: bfloat16 [4096, 2048], P(('grp', 'ep')), may hold values from -6 to 6
Outputs:
- output: bfloat16 [4096, 2048], P(('grp', 'ep'))
- tokens_grad: bfloat16 [4096, 2048], P(('grp', 'ep'))
- query_grad: float32 [2048, 2048], P(('grp', 'ep'))
- key_grad: float32 [2048, 2048], P(('grp', 'ep'))
- value_grad: float32 [2048, 2048], P(('grp', 'ep'))
- output_grad: float32 [2048, 2048], P(('grp', 'ep'))
- router_grad: float32 [2048, 64], P(('grp', 'ep'))
- attn_gain_grad: float32 [2048], P(('grp', 'ep'))
- query_gain_grad: float32 [2048], P(('grp', 'ep'))
- key_gain_grad: float32 [2048], P(('grp', 'ep'))
- moe_gain_grad: float32 [2048], P(('grp', 'ep'))
- gate_grad: float32 [64, 2048, 1024], P('ep', 'grp')
- up_grad: float32 [64, 2048, 1024], P('ep', 'grp')
- down_grad: float32 [64, 1024, 2048], P('ep', 'grp')
- rms_stats: float32 [2, 3], P('grp')
The draws below stay inside these ranges and needn't reach their ends.
Inputs may be any that keep to these rules, and one draw needn't show every extreme that they name: `routes`: each row names 8 different experts. Within the rows of one device no expert is named by more than 24 rows, and in every draw some expert is named by exactly 24 rows of some device.
All inputs are finite; a program needn't handle non-finite values.
Results may differ from the reference program's by a relative error of at most 0.024.
Values may be sent and summed in bfloat16 or wider, within the bound.
No kernel may reach another device: no remote copies, remote signals or barrier semaphores. Data moves between devices by JAX's collectives and lax.ppermute only.
A program may use at most 448 MiB of HBM per device.

```python
import math
import jax
import jax.numpy as jnp
import numpy as np
from jax import lax

D = 2048
HEADS = 16
HD = 128
FF = 1024
EXPERTS = 64
TOPK = 8
TOK_DEV = 128
BLOCK = 256
CAP = 24
GROUP = 2048
TOKENS = 4096
N_GRP = 2
DEVICES = 32


def draw_tokens(key, part):
    key = jax.random.fold_in(key, 11)
    row_pos = jnp.arange(TOKENS, dtype=jnp.int32) % GROUP
    ramp_up = 1.0 + 2.0 * row_pos.astype(jnp.float32) / GROUP
    sample = jnp.clip(jax.random.normal(key, (TOKENS, D), jnp.float32), -6.0, 6.0)
    return (sample * ramp_up[:, None]).astype(jnp.bfloat16)


def block_levels(key, extent, cuts, smallest, largest):
    gain = 1.0
    for axis_at, shards_of in cuts:
        draws = jax.random.uniform(jax.random.fold_in(jax.random.fold_in(key, 6), axis_at), (shards_of,), jnp.float32, smallest / len(cuts), largest / len(cuts))
        gain = gain * jnp.repeat(jnp.exp(draws), extent[axis_at] // shards_of).reshape((-1,) + (1,) * (len(extent) - 1 - axis_at))
    return gain


def shared_out(key, own, number, rows, count, top, limit, lean):
    ranking = jax.random.permutation(key, count)
    crowded, common = shares(count, rows * top, limit, lean, True), shares(count, rows * top, limit, lean, False)
    places = jnp.arange(count)

    def named(sizes, offset_by):
        used = int((sizes > 0).sum())
        fixed = max(1, used // 4)
        moved = fixed + (places - fixed + offset_by * (used - fixed)) % max(1, count - fixed)
        return jnp.zeros((count,), jnp.int32).at[ranking[jnp.where(places < fixed, places, moved)]].set(jnp.asarray(sizes, jnp.int32))

    sizes = jnp.where(number % 4 == 0, named(crowded, number // 4), named(common, number - number // 4 - 1))
    mixed = jax.random.permutation(jax.random.fold_in(own, 3), count)
    source_of, sink = mixed[0:count // 2 * 2:2], mixed[1:count // 2 * 2:2]
    margin = jnp.minimum(sizes[source_of] - 1, limit - sizes[sink]) // 2
    margin = jnp.where((source_of == ranking[0]) | (sink == ranking[0]) | (sizes[sink] == 0), 0, jnp.maximum(margin, 0))
    moved = jax.random.randint(jax.random.fold_in(own, 4), (count // 2,), 0, 1 << 20) % (margin + 1)
    sizes = sizes.at[source_of].add(-moved).at[sink].add(moved)
    labels = jnp.searchsorted(jnp.cumsum(sizes), jnp.arange(rows * top), side="right").astype(jnp.int32)
    listing = labels.reshape(top, rows).T
    listing = listing[jax.random.permutation(jax.random.fold_in(own, 1), rows)]
    offset_by = jax.random.randint(jax.random.fold_in(own, 2), (rows, 1), 0, top)
    return jnp.take_along_axis(listing, (jnp.arange(top)[None, :] + offset_by) % top, axis=1)


def shares(number_of, total, limit, skew, full):
    portions = [(1 << 20) // math.isqrt(standing ** skew) + 1 for standing in range(1, number_of + 1)]
    largest = limit if full else min(limit, max(-(-total // number_of), total * portions[0] // sum(portions)))
    least = 1 if total - largest >= number_of - 1 else 0
    given, rest = [largest] + [least] * (number_of - 1), total - largest - least * (number_of - 1)
    while rest > 0:
        free = [i for i in range(1, number_of) if given[i] < largest] or [i for i in range(1, number_of) if given[i] < limit]
        whole, left = sum([portions[i] for i in free]), rest
        for i in free:
            addition = min(limit - given[i], max(1, left * portions[i] // whole), rest)
            given[i] = given[i] + addition
            rest = rest - addition
    return np.array(given)


def scatter_about(own_key, dims, deviation, limit, cuts=(), kind=jnp.bfloat16):
    level = block_levels(own_key, dims, cuts, -0.22, 0.18) if cuts else 1.0
    entries = jax.random.normal(own_key, dims, jnp.float32) * deviation * level
    return jnp.minimum(jnp.maximum(entries, -limit), limit).astype(kind)


def setup_inputs(seed: int = 0) -> dict:
    seeds = jax.random.split(jax.random.key(seed), 16)
    tokens = draw_tokens(jax.random.fold_in(seeds[15], 71), 0)
    w_query = scatter_about(seeds[1], (D, D), D ** -0.5, 0.125, ((0, 32),))
    w_key = scatter_about(seeds[2], (D, D), D ** -0.5, 0.125, ((0, 32),))
    w_value = scatter_about(seeds[3], (D, D), D ** -0.5, 0.125, ((0, 32),))
    w_output = scatter_about(seeds[4], (D, D), (max(D // 256, 1)) ** -0.5, 2.0, ((0, 32),))
    w_router = scatter_about(seeds[5], (D, EXPERTS), (4 * D) ** -0.5, 0.0625, ((0, 32),))
    attn_gain = jnp.clip(1.0 + 0.18 * jax.random.normal(seeds[6], (D,), jnp.float32), 0.099609375, 1.8984375).astype(jnp.bfloat16)
    query_gain = jnp.clip(1.0 + 0.18 * jax.random.normal(seeds[7], (D,), jnp.float32), 0.099609375, 1.8984375).astype(jnp.bfloat16)
    key_gain = jnp.clip(1.0 + 0.18 * jax.random.normal(seeds[8], (D,), jnp.float32), 0.099609375, 1.8984375).astype(jnp.bfloat16)
    moe_gain = jnp.clip(1.0 + 0.18 * jax.random.normal(seeds[9], (D,), jnp.float32), 0.099609375, 1.8984375).astype(jnp.bfloat16)
    w_gate = scatter_about(seeds[10], (EXPERTS, D, FF), D ** -0.5, 0.125, ((0, 16),))
    w_up = scatter_about(seeds[11], (EXPERTS, D, FF), D ** -0.5, 0.125, ((0, 16),))
    w_down = scatter_about(seeds[12], (EXPERTS, FF, D), (max(FF // 1024, 1)) ** -0.5, 6.0, ((0, 16),))
    routes_keys = jax.random.split(jax.random.fold_in(seeds[13], 1), TOKENS // TOK_DEV)
    routes_turns = jax.random.permutation(jax.random.fold_in(seeds[13], 3), TOKENS // TOK_DEV)
    routes = jax.vmap(lambda own, number: shared_out(jax.random.fold_in(seeds[13], 2), own, number, TOK_DEV, EXPERTS, TOPK, CAP, 2))(routes_keys, routes_turns).reshape((TOKENS, TOPK))
    cotangent = scatter_about(seeds[14], (TOKENS, D), 1.0, 6.0, ((0, 32),))
    return dict(tokens=tokens, w_query=w_query, w_key=w_key, w_value=w_value, w_output=w_output, w_router=w_router, attn_gain=attn_gain, query_gain=query_gain, key_gain=key_gain, moe_gain=moe_gain, w_gate=w_gate, w_up=w_up, w_down=w_down, routes=routes, cotangent=cotangent)


EPSILON = 1e-05

@jax.custom_vjp
def low(v):
    return lax.optimization_barrier(v.astype(jnp.bfloat16)).astype(jnp.float32)

@jax.custom_vjp
def low_back(v):
    return v

def low_keep(v):
    return (low(v), None)

def low_pass(kept, grad):
    return (grad,)

def back_keep(v):
    return (v, None)

def back_low(kept, grad):
    return (low(grad),)
low.defvjp(low_keep, low_pass)
low_back.defvjp(back_keep, back_low)

def high_dot(first_arr, second_arr):
    return jnp.dot(first_arr, second_arr, precision=lax.Precision.HIGHEST, preferred_element_type=jnp.float32)

def rms_norm(values, gain_vec):
    return values * lax.rsqrt(lax.optimization_barrier(jnp.mean(values * values, -1, keepdims=True)) + EPSILON) * gain_vec

def rotary(values, positions):
    half_dim = HD // 2
    frequency = jnp.exp(-(2.0 * jnp.arange(half_dim, dtype=jnp.float32) / HD) * math.log(10000.0))
    angles = positions.astype(jnp.float32)[:, None] * frequency[None, :]
    cosine = jnp.cos(angles)[:, None, :]
    sine_tab = jnp.sin(angles)[:, None, :]
    first_half = values[..., :half_dim]
    second_half = values[..., half_dim:]
    return jnp.concatenate([first_half * cosine - second_half * sine_tab, second_half * cosine + first_half * sine_tab], -1)

def attend_block(query_blk, query_pos, keys_all, values_all):
    key_pos = jnp.arange(GROUP, dtype=jnp.int32)
    scores = low_back(jnp.einsum('qhd,khd->hqk', query_blk, keys_all, precision=lax.Precision.HIGHEST) * HD ** (-0.5))
    allowed = (key_pos // BLOCK)[None, None, :] <= (query_pos // BLOCK)[None, :, None]
    scores = jnp.where(allowed, scores, -1e+30)
    top_val = lax.optimization_barrier(jnp.max(scores, -1, keepdims=True))
    exp_scores = jnp.exp(scores - top_val)
    prob_vals = exp_scores / lax.optimization_barrier(jnp.sum(exp_scores, -1, keepdims=True))
    return jnp.einsum('hqk,khd->qhd', low(prob_vals), values_all, precision=lax.Precision.HIGHEST)

def sequence_attention(seq_items):
    queries, keys_all, values_all = seq_items
    q_rows = min(512, GROUP)
    positions = jnp.arange(GROUP, dtype=jnp.int32)
    query_blocks = queries.reshape(GROUP // q_rows, q_rows, HEADS, HD)
    pos_blocks = positions.reshape(GROUP // q_rows, q_rows)

    def one_block(block_items):
        return attend_block(block_items[0], block_items[1], keys_all, values_all)
    outcome = lax.map(jax.checkpoint(one_block), (query_blocks, pos_blocks))
    return outcome.reshape(GROUP, HEADS, HD)

def layer_forward(tokens, w_query, w_key, w_value, w_output, w_router, attn_gain, query_gain, key_gain, moe_gain, w_gate, w_up, w_down, routes):
    positions = jnp.arange(TOKENS, dtype=jnp.int32) % GROUP
    normed = low(rms_norm(tokens, attn_gain))
    query_raw = low_back(high_dot(normed, w_query))
    key_raw = low_back(high_dot(normed, w_key))
    values = low(low_back(high_dot(normed, w_value)))
    queries = low(low_back(rotary(rms_norm(query_raw, query_gain).reshape(TOKENS, HEADS, HD), positions)))
    keys = low(low_back(rotary(rms_norm(key_raw, key_gain).reshape(TOKENS, HEADS, HD), positions)))
    attended = lax.map(sequence_attention, (queries.reshape(N_GRP, GROUP, HEADS, HD), keys.reshape(N_GRP, GROUP, HEADS, HD), values.reshape(N_GRP, GROUP, HEADS, HD)))
    attended = low(low_back(attended.reshape(TOKENS, D)))
    branch_attn = low_back(high_dot(attended, w_output))
    hidden = tokens + branch_attn
    mixed_in = low(rms_norm(hidden, moe_gain))
    logits = low_back(high_dot(mixed_in, w_router))
    route_probs = jax.nn.softmax(logits, -1)
    gate_vals = jnp.take_along_axis(route_probs, routes, 1)
    pair_count = TOKENS * TOPK
    rows_cap = DEVICES * CAP
    flat_expert = routes.reshape(-1).astype(jnp.int32)
    sorted_pairs = jnp.argsort(flat_expert, stable=True).astype(jnp.int32)
    counts = lax.optimization_barrier(jnp.sum((flat_expert[:, None] == jnp.arange(EXPERTS, dtype=jnp.int32)[None, :]).astype(jnp.int32), 0))
    offsets = jnp.cumsum(counts) - counts
    slot_ids = jnp.arange(rows_cap, dtype=jnp.int32)
    lookup = jnp.minimum(offsets[:, None] + slot_ids[None, :], pair_count - 1).astype(jnp.int32)
    slot_table = jnp.where(slot_ids[None, :] < counts[:, None], sorted_pairs[lookup], pair_count).astype(jnp.int32)
    token_of = jnp.concatenate([jnp.arange(pair_count, dtype=jnp.int32) // TOPK, jnp.zeros((1,), jnp.int32)])
    gate_of = jnp.concatenate([gate_vals.reshape(-1), jnp.zeros((1,), gate_vals.dtype)])

    def expert_rows(unused, expert_items):
        gate_w, up_w, down_w, slot_rows = expert_items
        token_rows = token_of[slot_rows]
        pair_in = low_back(mixed_in[token_rows])
        gate_pre = low_back(high_dot(pair_in, gate_w))
        up_pre = low_back(high_dot(pair_in, up_w))
        activation = low(jax.nn.silu(gate_pre) * up_pre)
        expert_out = low(low_back(high_dot(activation, down_w)))
        return (unused, gate_of[slot_rows][:, None] * expert_out)
    unused_carry, weighted = lax.scan(jax.checkpoint(expert_rows), jnp.zeros((), jnp.float32), (w_gate, w_up, w_down, slot_table))
    branch_moe = jnp.zeros((TOKENS, D), jnp.float32).at[token_of[slot_table].reshape(-1)].add(weighted.reshape(-1, D))
    result = low(hidden + branch_moe)

    def seq_rms(values_in):
        grouped = values_in.reshape(N_GRP, GROUP * D)
        return jnp.sqrt(lax.optimization_barrier(jnp.mean(grouped * grouped, 1)))
    stats = jnp.stack([seq_rms(tokens), seq_rms(branch_attn), seq_rms(branch_moe)], 1)
    return (result, stats)

def reference(tokens, w_query, w_key, w_value, w_output, w_router, attn_gain, query_gain, key_gain, moe_gain, w_gate, w_up, w_down, routes, cotangent):

    def wrapped(tok_f, query_f, key_f, value_f, output_f, router_f, again_f, qgain_f, kgain_f, mgain_f, gate_f, up_f, down_f):
        return layer_forward(tok_f, query_f, key_f, value_f, output_f, router_f, again_f, qgain_f, kgain_f, mgain_f, gate_f, up_f, down_f, routes)
    output, pullback, stats = jax.vjp(wrapped, tokens.astype(jnp.float32), w_query.astype(jnp.float32), w_key.astype(jnp.float32), w_value.astype(jnp.float32), w_output.astype(jnp.float32), w_router.astype(jnp.float32), attn_gain.astype(jnp.float32), query_gain.astype(jnp.float32), key_gain.astype(jnp.float32), moe_gain.astype(jnp.float32), w_gate.astype(jnp.float32), w_up.astype(jnp.float32), w_down.astype(jnp.float32), has_aux=True)
    gradients = pullback(cotangent.astype(jnp.float32))
    return (output.astype(jnp.bfloat16), gradients[0].astype(jnp.bfloat16), gradients[1], gradients[2], gradients[3], gradients[4], gradients[5], gradients[6], gradients[7], gradients[8], gradients[9], gradients[10], gradients[11], gradients[12], stats)
```

```python
import functools
import math

import jax
import jax.numpy as jnp
from jax import lax
from jax.experimental import pallas as pl
from jax.experimental.pallas import tpu as pltpu
from jax.sharding import PartitionSpec as P

D = 2048
HEADS = 16
HD = 128
EXPERTS = 64
TOPK = 8
TOK_DEV = 128
BLOCK = 256
CAP = 24


EPSILON = 1e-05
NEG_FILL = -1e30


def inv_rms(values):
    return lax.rsqrt(jnp.mean(values * values, -1, keepdims=True) + EPSILON)


def norm_back(grad_out, values, inverse, gain_vec):
    scaled = grad_out * gain_vec
    grad_in = inverse * (
        scaled - values * inverse * inverse * jnp.mean(scaled * values, -1, keepdims=True)
    )
    return (grad_in, jnp.sum(grad_out * values * inverse, 0))


def rope_tables(positions):
    half_dim = HD // 2
    frequency = jnp.exp(-(2.0 * jnp.arange(half_dim, dtype=jnp.float32) / HD) * math.log(10000.0))
    angles = positions.astype(jnp.float32)[:, None] * frequency[None, :]
    return (jnp.cos(angles)[:, None, :], jnp.sin(angles)[:, None, :])


def rotate(values, cosine, sine_tab):
    half_dim = HD // 2
    first_half = values[..., :half_dim]
    second_half = values[..., half_dim:]
    return jnp.concatenate(
        [
            first_half * cosine - second_half * sine_tab,
            second_half * cosine + first_half * sine_tab,
        ],
        -1,
    )


def rotate_back(grad_in, cosine, sine_tab):
    half_dim = HD // 2
    first_half = grad_in[..., :half_dim]
    second_half = grad_in[..., half_dim:]
    return jnp.concatenate(
        [
            first_half * cosine + second_half * sine_tab,
            second_half * cosine - first_half * sine_tab,
        ],
        -1,
    )


def fold_keys(state_now, key_piece, queries, query_pos):
    keys_in, values_in = key_piece
    piece_rows = keys_in.shape[0]
    blk_rows = math.gcd(piece_rows, 1024)
    key_blocks = keys_in.reshape(piece_rows // blk_rows, blk_rows, HEADS, HD)
    value_blocks = values_in.reshape(piece_rows // blk_rows, blk_rows, HEADS, HD)
    last_block = query_pos[-1] // BLOCK

    def block_step(state_in, block_items):
        key_blk, value_blk, block_num = block_items
        key_start = block_num * blk_rows

        def block_compute(state_cur):
            top_now, total_now, acc_now = state_cur
            key_pos = key_start + jnp.arange(blk_rows, dtype=jnp.int32)
            scores = jnp.einsum(
                "qhd,khd->hqk", queries, key_blk, preferred_element_type=jnp.float32
            ) * HD ** (-0.5)
            allowed = (key_pos // BLOCK)[None, None, :] <= (query_pos // BLOCK)[None, :, None]
            scores = jnp.where(allowed, scores, NEG_FILL)
            top_new = jnp.maximum(top_now, jnp.max(scores, -1, keepdims=True))
            weights = jnp.where(allowed, jnp.exp(scores - top_new), 0.0)
            rescale = jnp.exp(top_now - top_new)
            total_new = total_now * rescale + jnp.sum(weights, -1, keepdims=True)
            acc_new = acc_now * jnp.transpose(rescale, (1, 0, 2)) + jnp.einsum(
                "hqk,khd->qhd",
                weights.astype(jnp.bfloat16),
                value_blk,
                preferred_element_type=jnp.float32,
            )
            return (top_new, total_new, acc_new)

        def block_passing(state_cur):
            return state_cur

        return (
            lax.cond(key_start // BLOCK <= last_block, block_compute, block_passing, state_in),
            None,
        )

    state_out, unused = lax.scan(
        block_step,
        state_now,
        (key_blocks, value_blocks, jnp.arange(piece_rows // blk_rows, dtype=jnp.int32)),
    )
    return state_out


def score_grads(queries, grad_attended, row_delta, log_sum, query_pos, key_blk, value_blk, key_pos):
    scores = jnp.einsum(
        "qhd,khd->hqk", queries, key_blk, preferred_element_type=jnp.float32
    ) * HD ** (-0.5)
    allowed = (key_pos // BLOCK)[None, None, :] <= (query_pos // BLOCK)[None, :, None]
    prob_vals = jnp.where(allowed, jnp.exp(scores - log_sum), 0.0)
    grad_probs = jnp.einsum(
        "qhd,khd->hqk", grad_attended, value_blk, preferred_element_type=jnp.float32
    )
    grad_scores = (prob_vals * (grad_probs - row_delta)).astype(jnp.bfloat16)
    return (prob_vals, grad_scores)


def shards(
    tokens,
    w_query,
    w_key,
    w_value,
    w_output,
    w_router,
    attn_gain,
    query_gain,
    key_gain,
    moe_gain,
    w_gate,
    w_up,
    w_down,
    routes,
    cotangent,
):
    gathered = (
        lax.all_gather(w_query, ("grp", "ep"), axis=0, tiled=True),
        lax.all_gather(w_key, ("grp", "ep"), axis=0, tiled=True),
        lax.all_gather(w_value, ("grp", "ep"), axis=0, tiled=True),
        lax.all_gather(w_output, ("grp", "ep"), axis=0, tiled=True),
        lax.all_gather(w_router, ("grp", "ep"), axis=0, tiled=True),
        lax.all_gather(attn_gain, ("grp", "ep"), axis=0, tiled=True),
        lax.all_gather(query_gain, ("grp", "ep"), axis=0, tiled=True),
        lax.all_gather(key_gain, ("grp", "ep"), axis=0, tiled=True),
        lax.all_gather(moe_gain, ("grp", "ep"), axis=0, tiled=True),
    )
    query_full, key_full, value_full, output_full, router_full = (
        gathered[0],
        gathered[1],
        gathered[2],
        gathered[3],
        gathered[4],
    )
    attn_scale = gathered[5].astype(jnp.float32)
    query_scale = gathered[6].astype(jnp.float32)
    key_scale = gathered[7].astype(jnp.float32)
    moe_scale = gathered[8].astype(jnp.float32)
    ep_count = lax.axis_size("ep")
    exp_local = EXPERTS // ep_count
    score_scale = HD ** (-0.5)
    inputs = tokens.astype(jnp.float32)
    positions = lax.axis_index("ep") * TOK_DEV + jnp.arange(TOK_DEV, dtype=jnp.int32)
    cosine, sine_tab = rope_tables(positions)
    attn_inv = inv_rms(inputs)
    normed = (inputs * attn_inv * attn_scale).astype(jnp.bfloat16)
    query_raw = jnp.dot(normed, query_full, preferred_element_type=jnp.float32)
    key_raw = jnp.dot(normed, key_full, preferred_element_type=jnp.float32)
    values16 = jnp.dot(normed, value_full, preferred_element_type=jnp.float32).astype(jnp.bfloat16)
    query_inv = inv_rms(query_raw)
    queries16 = rotate(
        (query_raw * query_inv * query_scale).reshape(TOK_DEV, HEADS, HD), cosine, sine_tab
    ).astype(jnp.bfloat16)
    key_inv = inv_rms(key_raw)
    keys16 = (
        rotate((key_raw * key_inv * key_scale).reshape(TOK_DEV, HEADS, HD), cosine, sine_tab)
        .astype(jnp.bfloat16)
        .reshape(TOK_DEV, D)
    )
    start_state = (
        jnp.full((HEADS, TOK_DEV, 1), NEG_FILL, jnp.float32),
        jnp.zeros((HEADS, TOK_DEV, 1), jnp.float32),
        jnp.zeros((TOK_DEV, HEADS, HD), jnp.float32),
    )
    folded = fold_keys(
        start_state,
        (
            lax.all_gather(keys16, "ep", axis=0, tiled=True),
            lax.all_gather(values16, "ep", axis=0, tiled=True),
        ),
        queries16,
        positions,
    )
    top_score, total_weight, acc_sum = folded
    log_sum = top_score + jnp.log(total_weight)
    attn_float = acc_sum / jnp.transpose(total_weight, (1, 0, 2))
    attended16 = attn_float.reshape(TOK_DEV, D).astype(jnp.bfloat16)
    branch_attn = jnp.dot(attended16, output_full, preferred_element_type=jnp.float32)
    hidden = inputs + branch_attn
    moe_inv = inv_rms(hidden)
    mixed_in = (hidden * moe_inv * moe_scale).astype(jnp.bfloat16)
    logits = jnp.dot(mixed_in, router_full, preferred_element_type=jnp.float32)
    route_probs = jax.nn.softmax(logits, -1)
    chosen = (routes[:, :, None] == jnp.arange(EXPERTS, dtype=jnp.int32)[None, None, :]).astype(
        jnp.float32
    )
    gate_vals = jnp.sum(chosen * route_probs[:, None, :], -1)
    pair_expert = routes.reshape(-1)
    one_hot = (pair_expert[:, None] == jnp.arange(EXPERTS, dtype=jnp.int32)[None, :]).astype(
        jnp.int32
    )
    pair_rank = jnp.sum(jnp.cumsum(one_hot, 0) * one_hot, 1) - 1
    slot_index = pair_expert * CAP + pair_rank
    pair_token = jnp.arange(TOK_DEV * TOPK, dtype=jnp.int32) // TOPK
    send_rows = jnp.zeros((EXPERTS * CAP, D), jnp.bfloat16).at[slot_index].set(mixed_in[pair_token])
    send_rows = send_rows.reshape(ep_count, exp_local, CAP, D)
    received = lax.all_to_all(send_rows, "ep", split_axis=0, concat_axis=0, tiled=True)
    gate_pre = jnp.einsum("secd,edf->secf", received, w_gate, preferred_element_type=jnp.float32)
    up_pre = jnp.einsum("secd,edf->secf", received, w_up, preferred_element_type=jnp.float32)
    activation = (jax.nn.silu(gate_pre) * up_pre).astype(jnp.bfloat16)
    expert_out = jnp.einsum(
        "secf,efd->secd", activation, w_down, preferred_element_type=jnp.float32
    ).astype(jnp.bfloat16)
    expert_out, gate_pre, up_pre, activation, received = (
        expert_out,
        gate_pre,
        up_pre,
        activation,
        received,
    )
    returned = lax.all_to_all(expert_out, "ep", split_axis=0, concat_axis=0, tiled=True).reshape(
        EXPERTS * CAP, D
    )
    pair_out = returned[slot_index].astype(jnp.float32).reshape(TOK_DEV, TOPK, D)
    branch_moe = jnp.sum(gate_vals[:, :, None] * pair_out, 1)
    output = (hidden + branch_moe).astype(jnp.bfloat16)
    local_sums = jnp.stack(
        [
            jnp.sum(inputs * inputs),
            jnp.sum(branch_attn * branch_attn),
            jnp.sum(branch_moe * branch_moe),
        ]
    )
    seq_sums = lax.psum(local_sums, "ep")
    rms_stats = jnp.sqrt(seq_sums / (TOK_DEV * ep_count * D)).reshape(1, 3)
    grad_out = cotangent.astype(jnp.float32)
    grad_gates = jnp.sum(pair_out * grad_out[:, None, :], -1)
    grad_pairs = (
        (gate_vals[:, :, None] * grad_out[:, None, :])
        .astype(jnp.bfloat16)
        .reshape(TOK_DEV * TOPK, D)
    )
    send_grads = jnp.zeros((EXPERTS * CAP, D), jnp.bfloat16).at[slot_index].set(grad_pairs)
    send_grads = send_grads.reshape(ep_count, exp_local, CAP, D)
    grad_received = lax.all_to_all(send_grads, "ep", split_axis=0, concat_axis=0, tiled=True)
    grad_activation = jnp.einsum(
        "secd,efd->secf", grad_received, w_down, preferred_element_type=jnp.float32
    )
    grad_down = jnp.einsum(
        "secf,secd->efd", activation, grad_received, preferred_element_type=jnp.float32
    )
    sig_gate = jax.nn.sigmoid(gate_pre)
    grad_gate_pre = (
        grad_activation * up_pre * sig_gate * (1.0 + gate_pre * (1.0 - sig_gate))
    ).astype(jnp.bfloat16)
    grad_up_pre = (grad_activation * gate_pre * sig_gate).astype(jnp.bfloat16)
    grad_gate_w = jnp.einsum(
        "secd,secf->edf", received, grad_gate_pre, preferred_element_type=jnp.float32
    )
    grad_up_w = jnp.einsum(
        "secd,secf->edf", received, grad_up_pre, preferred_element_type=jnp.float32
    )
    grad_inputs = (
        jnp.einsum("secf,edf->secd", grad_gate_pre, w_gate, preferred_element_type=jnp.float32)
        + jnp.einsum("secf,edf->secd", grad_up_pre, w_up, preferred_element_type=jnp.float32)
    ).astype(jnp.bfloat16)
    grad_back = lax.all_to_all(grad_inputs, "ep", split_axis=0, concat_axis=0, tiled=True).reshape(
        EXPERTS * CAP, D
    )
    grad_mixed = jnp.sum(grad_back[slot_index].astype(jnp.float32).reshape(TOK_DEV, TOPK, D), 1)
    spread = jnp.sum(chosen * grad_gates[:, :, None], 1)
    grad_logits = (
        route_probs * (spread - jnp.sum(route_probs * spread, -1, keepdims=True))
    ).astype(jnp.bfloat16)
    router_grad = jnp.einsum("td,te->de", mixed_in, grad_logits, preferred_element_type=jnp.float32)
    grad_mixed = grad_mixed + jnp.einsum(
        "te,de->td", grad_logits, router_full, preferred_element_type=jnp.float32
    )
    grad_hid_norm, moe_gain_grad = norm_back(grad_mixed, hidden, moe_inv, moe_scale)
    grad_hidden = grad_out + grad_hid_norm
    grad_branch = grad_hidden.astype(jnp.bfloat16)
    output_grad = jnp.einsum(
        "td,tf->df", attended16, grad_branch, preferred_element_type=jnp.float32
    )
    grad_attended = jnp.einsum(
        "tf,df->td", grad_branch, output_full, preferred_element_type=jnp.float32
    ).astype(jnp.bfloat16)
    grad_attended = grad_attended.reshape(TOK_DEV, HEADS, HD)
    row_delta = jnp.transpose(jnp.sum(grad_attended.astype(jnp.float32) * attn_float, -1), (1, 0))[
        :, :, None
    ]
    gathered_keys, gathered_values = (
        lax.all_gather(keys16, "ep", axis=0, tiled=True),
        lax.all_gather(values16, "ep", axis=0, tiled=True),
    )
    total_rows = gathered_keys.shape[0]
    blk_rows = math.gcd(total_rows, 1024)
    last_query_block = positions[-1] // BLOCK

    def query_step(grad_now, block_num):
        begin_row = block_num * blk_rows

        def query_compute(grad_cur):
            key_blk = lax.dynamic_slice_in_dim(gathered_keys, begin_row, blk_rows, 0).reshape(
                blk_rows, HEADS, HD
            )
            value_blk = lax.dynamic_slice_in_dim(gathered_values, begin_row, blk_rows, 0).reshape(
                blk_rows, HEADS, HD
            )
            key_pos = begin_row + jnp.arange(blk_rows, dtype=jnp.int32)
            prob_vals, grad_scores = score_grads(
                queries16, grad_attended, row_delta, log_sum, positions, key_blk, value_blk, key_pos
            )
            return (
                grad_cur
                + jnp.einsum(
                    "hqk,khd->qhd", grad_scores, key_blk, preferred_element_type=jnp.float32
                )
                * score_scale
            )

        def query_passing(grad_cur):
            return grad_cur

        return (
            lax.cond(
                begin_row // BLOCK <= last_query_block, query_compute, query_passing, grad_now
            ),
            None,
        )

    grad_queries, unused = lax.scan(
        query_step,
        jnp.zeros((TOK_DEV, HEADS, HD), jnp.float32),
        jnp.arange(total_rows // blk_rows, dtype=jnp.int32),
    )
    all_queries, all_grad_att = (
        lax.all_gather(queries16, "ep", axis=0, tiled=True),
        lax.all_gather(grad_attended, "ep", axis=0, tiled=True),
    )
    all_delta, all_log_sum = (
        lax.all_gather(row_delta, "ep", axis=1, tiled=True),
        lax.all_gather(log_sum, "ep", axis=1, tiled=True),
    )
    query_rows = all_queries.shape[0]
    query_blk_rows = math.gcd(query_rows, 1024)
    own_keys = keys16.reshape(TOK_DEV, HEADS, HD)
    own_values = values16.reshape(TOK_DEV, HEADS, HD)
    first_key_block = positions[0] // BLOCK

    def key_step(grads_now, block_num):
        begin_row = block_num * query_blk_rows

        def key_compute(grads_cur):
            query_blk = lax.dynamic_slice_in_dim(all_queries, begin_row, query_blk_rows, 0)
            grad_att_blk = lax.dynamic_slice_in_dim(all_grad_att, begin_row, query_blk_rows, 0)
            delta_blk = lax.dynamic_slice_in_dim(all_delta, begin_row, query_blk_rows, 1)
            log_blk = lax.dynamic_slice_in_dim(all_log_sum, begin_row, query_blk_rows, 1)
            query_pos = begin_row + jnp.arange(query_blk_rows, dtype=jnp.int32)
            prob_vals, grad_scores = score_grads(
                query_blk,
                grad_att_blk,
                delta_blk,
                log_blk,
                query_pos,
                own_keys,
                own_values,
                positions,
            )
            key_part = (
                jnp.einsum(
                    "hqk,qhd->khd", grad_scores, query_blk, preferred_element_type=jnp.float32
                )
                * score_scale
            )
            value_part = jnp.einsum(
                "hqk,qhd->khd",
                prob_vals.astype(jnp.bfloat16),
                grad_att_blk,
                preferred_element_type=jnp.float32,
            )
            return (grads_cur[0] + key_part, grads_cur[1] + value_part)

        def key_passing(grads_cur):
            return grads_cur

        return (
            lax.cond(
                (begin_row + query_blk_rows - 1) // BLOCK >= first_key_block,
                key_compute,
                key_passing,
                grads_now,
            ),
            None,
        )

    key_start = (
        jnp.zeros((TOK_DEV, HEADS, HD), jnp.float32),
        jnp.zeros((TOK_DEV, HEADS, HD), jnp.float32),
    )
    key_value_grads, unused = lax.scan(
        key_step, key_start, jnp.arange(query_rows // query_blk_rows, dtype=jnp.int32)
    )
    grad_keys16 = key_value_grads[0].astype(jnp.bfloat16)
    grad_values16 = key_value_grads[1].reshape(TOK_DEV, D).astype(jnp.bfloat16)
    grad_keys = lax.optimization_barrier(grad_keys16).astype(jnp.float32)
    grad_queries = lax.optimization_barrier(grad_queries.astype(jnp.bfloat16)).astype(jnp.float32)
    grad_query_rot = rotate_back(grad_queries, cosine, sine_tab).reshape(TOK_DEV, D)
    grad_query_raw, query_gain_grad = norm_back(grad_query_rot, query_raw, query_inv, query_scale)
    grad_query16 = grad_query_raw.astype(jnp.bfloat16)
    grad_key_rot = rotate_back(grad_keys, cosine, sine_tab).reshape(TOK_DEV, D)
    grad_key_raw, key_gain_grad = norm_back(grad_key_rot, key_raw, key_inv, key_scale)
    grad_key16 = grad_key_raw.astype(jnp.bfloat16)
    query_grad = jnp.einsum("td,tf->df", normed, grad_query16, preferred_element_type=jnp.float32)
    key_grad = jnp.einsum("td,tf->df", normed, grad_key16, preferred_element_type=jnp.float32)
    value_grad = jnp.einsum("td,tf->df", normed, grad_values16, preferred_element_type=jnp.float32)
    grad_normed = (
        jnp.einsum("tf,df->td", grad_query16, query_full, preferred_element_type=jnp.float32)
        + jnp.einsum("tf,df->td", grad_key16, key_full, preferred_element_type=jnp.float32)
        + jnp.einsum("tf,df->td", grad_values16, value_full, preferred_element_type=jnp.float32)
    )
    grad_tok_norm, attn_gain_grad = norm_back(grad_normed, inputs, attn_inv, attn_scale)
    tokens_grad = (grad_hidden + grad_tok_norm).astype(jnp.bfloat16)
    dense_sums = (
        lax.psum_scatter(query_grad, ("grp", "ep"), scatter_dimension=0, tiled=True),
        lax.psum_scatter(key_grad, ("grp", "ep"), scatter_dimension=0, tiled=True),
        lax.psum_scatter(value_grad, ("grp", "ep"), scatter_dimension=0, tiled=True),
        lax.psum_scatter(output_grad, ("grp", "ep"), scatter_dimension=0, tiled=True),
        lax.psum_scatter(router_grad, ("grp", "ep"), scatter_dimension=0, tiled=True),
        lax.psum_scatter(attn_gain_grad, ("grp", "ep"), scatter_dimension=0, tiled=True),
        lax.psum_scatter(query_gain_grad, ("grp", "ep"), scatter_dimension=0, tiled=True),
        lax.psum_scatter(key_gain_grad, ("grp", "ep"), scatter_dimension=0, tiled=True),
        lax.psum_scatter(moe_gain_grad, ("grp", "ep"), scatter_dimension=0, tiled=True),
    )
    expert_sums = (
        lax.psum_scatter(
            grad_gate_w.astype(jnp.bfloat16), "grp", scatter_dimension=1, tiled=True
        ).astype(jnp.float32),
        lax.psum_scatter(
            grad_up_w.astype(jnp.bfloat16), "grp", scatter_dimension=1, tiled=True
        ).astype(jnp.float32),
        lax.psum_scatter(
            grad_down.astype(jnp.bfloat16), "grp", scatter_dimension=1, tiled=True
        ).astype(jnp.float32),
    )
    return (
        output,
        tokens_grad,
        dense_sums[0],
        dense_sums[1],
        dense_sums[2],
        dense_sums[3],
        dense_sums[4],
        dense_sums[5],
        dense_sums[6],
        dense_sums[7],
        dense_sums[8],
        expert_sums[0],
        expert_sums[1],
        expert_sums[2],
        rms_stats,
    )


F32 = jnp.float32
BF16 = jnp.bfloat16
EP = ("z", "x", "core")
ALL = ("grp", "z", "x", "core")
PAIR = 2 * TOK_DEV
SLOTS = 2 * CAP
SIDES = {16: (4, 2, 2)}


def nt(left, right):
    return lax.dot_general(left, right, (((1,), (1,)), ((), ())), preferred_element_type=F32)


def nn(left, right):
    return lax.dot_general(left, right, (((1,), (0,)), ((), ())), preferred_element_type=F32)


def tn(left, right):
    return lax.dot_general(left, right, (((0,), (0,)), ((), ())), preferred_element_type=F32)


def as_row(column):
    return jnp.broadcast_to(column, (column.shape[0], 128)).T[0:1]


def as_column(row):
    return jnp.broadcast_to(row, (128, row.shape[1])).T


def inv_of(sum_row):
    return as_column(lax.rsqrt(sum_row / D + EPSILON))


def params(mebibytes):
    return pltpu.CompilerParams(vmem_limit_bytes=mebibytes * 1024 * 1024)


def cost(flops, moved):
    return pl.CostEstimate(flops=int(flops), bytes_accessed=int(moved), transcendentals=0)


def whole(*dims):
    return pl.BlockSpec(dims, lambda *_: (0,) * len(dims))


def project_kernel(tok_ref, w_ref, gain_ref, qkv_ref, stat_ref):
    rows = tok_ref[...].astype(F32)
    inverse = lax.rsqrt(jnp.mean(rows * rows, -1, keepdims=True) + EPSILON)
    normed = (rows * inverse * gain_ref[...]).astype(BF16)
    out = nn(normed, w_ref[...])
    qkv_ref[...] = out
    stat_ref[0:1, :] = as_row(jnp.sum(out[:, :HD] * out[:, :HD], -1, keepdims=True))
    stat_ref[1:2, :] = as_row(jnp.sum(out[:, HD : 2 * HD] * out[:, HD : 2 * HD], -1, keepdims=True))


def project(tok_all, w_head, gain_row):
    rows = tok_all.shape[0]
    return pl.pallas_call(
        project_kernel,
        grid=(rows // PAIR,),
        in_specs=[
            pl.BlockSpec((PAIR, D), lambda i: (i, 0)),
            whole(D, 3 * HD),
            whole(1, D),
        ],
        out_specs=[
            pl.BlockSpec((PAIR, 3 * HD), lambda i: (i, 0)),
            pl.BlockSpec((2, PAIR), lambda i: (0, i)),
        ],
        out_shape=[
            jax.ShapeDtypeStruct((rows, 3 * HD), F32),
            jax.ShapeDtypeStruct((2, rows), F32),
        ],
        compiler_params=params(32),
        cost_estimate=cost(2 * rows * D * 3 * HD, 2 * rows * D + 4 * rows * 384),
        name="project",
    )(tok_all, w_head, gain_row)


def attend_kernel(
    qkv_ref, stat_ref, gq_ref, gk_ref, cos_ref, sin_ref,
    q_ref, k_ref, v_ref, of_ref, att_ref, lse_ref, vt_ref,
):
    blocks = q_ref.shape[0] // BLOCK
    for i in range(blocks):
        rows = slice(i * BLOCK, (i + 1) * BLOCK)
        cosine, sine = cos_ref[rows, :], sin_ref[rows, :]
        for part, gain_ref, out_ref in ((0, gq_ref, q_ref), (1, gk_ref, k_ref)):
            raw = qkv_ref[rows, part * HD : (part + 1) * HD]
            scaled = raw * inv_of(stat_ref[part : part + 1, rows]) * gain_ref[...]
            turned = scaled * cosine + pltpu.roll(scaled, HD // 2, 1) * sine
            out_ref[rows, :] = turned.astype(BF16)
        value = qkv_ref[rows, 2 * HD :]
        v_ref[rows, :] = value.astype(BF16)
        vt_ref[:, rows] = value.T.astype(BF16)
    for i in range(blocks):
        rows = slice(i * BLOCK, (i + 1) * BLOCK)
        reach = (i + 1) * BLOCK
        scores = nt(k_ref[0:reach, :], q_ref[rows, :]) * HD ** (-0.5)
        top = jnp.max(scores, 0, keepdims=True)
        weights = jnp.exp(scores - top)
        total = jnp.sum(weights, 0, keepdims=True)
        probs = (weights * (1.0 / total)).astype(BF16)
        out = nn(vt_ref[:, 0:reach], probs).T
        of_ref[rows, :] = out
        att_ref[rows, :] = out.astype(BF16)
        lse_ref[:, rows] = top + jnp.log(total)


def attend(qkv, stat, gain_q, gain_k, cosine, sine):
    rows = qkv.shape[0]
    shape = lambda kind: jax.ShapeDtypeStruct((rows, HD), kind)
    return pl.pallas_call(
        attend_kernel,
        out_shape=[shape(BF16), shape(BF16), shape(BF16), shape(F32), shape(BF16),
                   jax.ShapeDtypeStruct((1, rows), F32)],
        scratch_shapes=[pltpu.VMEM((HD, rows), BF16)],
        compiler_params=params(48),
        cost_estimate=cost(8 * rows * rows * HD, 10 * rows * 384),
        name="attend",
    )(qkv, stat, gain_q, gain_k, cosine, sine)


def attend_back_kernel(
    q_ref, k_ref, v_ref, do_ref, of_ref, lse_ref, qkv_ref, stat_ref, gq_ref, gk_ref,
    cos_ref, sin_ref, dnq_ref, dnk_ref, dv_ref, means_ref, gains_ref, dk_acc, dv_acc,
):
    blocks = q_ref.shape[0] // BLOCK
    scale = HD ** (-0.5)
    dk_acc[...] = jnp.zeros_like(dk_acc)
    dv_acc[...] = jnp.zeros_like(dv_acc)

    def turn_back(grad, rows, part, gain_ref, out_ref):
        grad = grad.astype(BF16).astype(F32)
        grad = grad * cos_ref[rows, :] - pltpu.roll(grad, HD // 2, 1) * sin_ref[rows, :]
        raw = qkv_ref[rows, part * HD : (part + 1) * HD]
        out_ref[rows, :] = grad
        means_ref[part : part + 1, rows] = jnp.sum((grad * gain_ref[...] * raw).T, 0, keepdims=True)
        inverse = inv_of(stat_ref[part : part + 1, rows])
        return jnp.sum(grad * raw * inverse, 0, keepdims=True)

    gain_q = jnp.zeros((1, HD), F32)
    gain_k = jnp.zeros((1, HD), F32)
    for i in range(blocks):
        rows = slice(i * BLOCK, (i + 1) * BLOCK)
        reach = (i + 1) * BLOCK
        queries, grads = q_ref[rows, :], do_ref[rows, :]
        delta = jnp.sum((grads.astype(F32) * of_ref[rows, :]).T, 0, keepdims=True)
        scores = nt(k_ref[0:reach, :], queries) * scale
        probs = jnp.exp(scores - lse_ref[:, rows])
        slopes = nt(v_ref[0:reach, :], grads)
        grad_scores = (probs * (slopes - delta)).astype(BF16)
        dv_acc[0:reach, :] += nn(probs.astype(BF16), grads)
        dk_acc[0:reach, :] += nn(grad_scores, queries)
        gain_q += turn_back(tn(grad_scores, k_ref[0:reach, :]) * scale, rows, 0, gq_ref, dnq_ref)
    for i in range(blocks):
        rows = slice(i * BLOCK, (i + 1) * BLOCK)
        dv_ref[rows, :] = dv_acc[rows, :].astype(BF16)
        gain_k += turn_back(dk_acc[rows, :] * scale, rows, 1, gk_ref, dnk_ref)
    gains_ref[0:1, :] = gain_q
    gains_ref[1:2, :] = gain_k


def attend_back(q, k, v, grad, out, lse, qkv, stat, gain_q, gain_k, cosine, sine):
    rows = q.shape[0]
    shape = lambda kind: jax.ShapeDtypeStruct((rows, HD), kind)
    return pl.pallas_call(
        attend_back_kernel,
        out_shape=[shape(F32), shape(F32), shape(BF16),
                   jax.ShapeDtypeStruct((2, rows), F32), jax.ShapeDtypeStruct((2, HD), F32)],
        scratch_shapes=[pltpu.VMEM((rows, HD), F32), pltpu.VMEM((rows, HD), F32)],
        compiler_params=params(48),
        cost_estimate=cost(20 * rows * rows * HD, 20 * rows * 384),
        name="attend_back",
    )(q, k, v, grad, out, lse, qkv, stat, gain_q, gain_k, cosine, sine)


def project_back_kernel(
    dnq_ref, dnk_ref, dv_ref, qkv_ref, stat_ref, means_ref, gq_ref, gk_ref, tok_ref, gain_ref,
    w_ref, part_ref, dw_ref,
):
    grads = []
    for part, dn_ref, g_ref in ((0, dnq_ref, gq_ref), (1, dnk_ref, gk_ref)):
        raw = qkv_ref[:, part * HD : (part + 1) * HD]
        inverse = inv_of(stat_ref[part : part + 1, :])
        mean = as_column(means_ref[part : part + 1, :] / D)
        grad = inverse * (dn_ref[...] * g_ref[...] - raw * inverse * inverse * mean)
        grads.append(grad.astype(BF16))
    grad = jnp.concatenate(grads + [dv_ref[...]], 1)
    part_ref[...] = nt(grad, w_ref[...]).astype(BF16)
    rows = tok_ref[...].astype(F32)
    inverse = lax.rsqrt(jnp.mean(rows * rows, -1, keepdims=True) + EPSILON)
    normed = (rows * inverse * gain_ref[...]).astype(BF16)

    @pl.when(pl.program_id(0) == 0)
    def _():
        dw_ref[...] = jnp.zeros_like(dw_ref)

    dw_ref[...] += tn(normed, grad)


def project_back(dnq, dnk, dv, qkv, stat, means, gain_q, gain_k, tok_all, gain_row, w_head):
    rows = tok_all.shape[0]
    head = pl.BlockSpec((PAIR, HD), lambda i: (i, 0))
    line = pl.BlockSpec((2, PAIR), lambda i: (0, i))
    return pl.pallas_call(
        project_back_kernel,
        grid=(rows // PAIR,),
        in_specs=[
            head, head, head, pl.BlockSpec((PAIR, 3 * HD), lambda i: (i, 0)), line, line,
            whole(1, HD), whole(1, HD), pl.BlockSpec((PAIR, D), lambda i: (i, 0)),
            whole(1, D), whole(D, 3 * HD),
        ],
        out_specs=[pl.BlockSpec((PAIR, D), lambda i: (i, 0)), whole(D, 3 * HD)],
        out_shape=[
            jax.ShapeDtypeStruct((rows, D), BF16),
            jax.ShapeDtypeStruct((D, 3 * HD), F32),
        ],
        compiler_params=params(40),
        cost_estimate=cost(4 * rows * D * 3 * HD, 4 * rows * D + 8 * rows * 384),
        name="project_back",
    )(dnq, dnk, dv, qkv, stat, means, gain_q, gain_k, tok_all, gain_row, w_head)


def picks(slot_ref, dtype):
    shape = (SLOTS, PAIR)
    numbers = lax.broadcasted_iota(jnp.int32, shape, 0)
    return [
        (numbers == slot_ref[j : j + 1, :]).astype(dtype) for j in range(slot_ref.shape[0])
    ]


def dispatch_kernel(row_ref, slot_ref, out_ref):
    pick = jnp.concatenate(picks(slot_ref, F32), 0).astype(BF16)
    out = nn(pick, row_ref[...]).astype(BF16)
    for j in range(slot_ref.shape[0]):
        out_ref[j] = out[j * SLOTS : (j + 1) * SLOTS]


def dispatch(rows_all, slots):
    rows, local = rows_all.shape[0], slots.shape[0]
    pairs = rows // PAIR
    return pl.pallas_call(
        dispatch_kernel,
        grid=(pairs,),
        in_specs=[
            pl.BlockSpec((PAIR, D), lambda i: (i, 0)),
            pl.BlockSpec((local, PAIR), lambda i: (0, i)),
        ],
        out_specs=pl.BlockSpec((local, SLOTS, D), lambda i: (0, i, 0)),
        out_shape=jax.ShapeDtypeStruct((local, pairs * SLOTS, D), BF16),
        compiler_params=params(24),
        cost_estimate=cost(2 * rows * D * local * SLOTS, 4 * rows * D),
        name="dispatch",
    )(rows_all, slots)


def combine_kernel(row_ref, slot_ref, out_ref):
    local = slot_ref.shape[0]
    pick = jnp.concatenate(picks(slot_ref, F32), 0).astype(BF16)
    rows = jnp.concatenate([row_ref[j] for j in range(local)], 0)
    out_ref[...] = tn(pick, rows).astype(BF16)


def combine(slot_rows, slots):
    local, rows = slots.shape
    pairs = rows // PAIR
    return pl.pallas_call(
        combine_kernel,
        grid=(pairs,),
        in_specs=[
            pl.BlockSpec((local, SLOTS, D), lambda i: (0, i, 0)),
            pl.BlockSpec((local, PAIR), lambda i: (0, i)),
        ],
        out_specs=pl.BlockSpec((PAIR, D), lambda i: (i, 0)),
        out_shape=jax.ShapeDtypeStruct((rows, D), BF16),
        compiler_params=params(24),
        cost_estimate=cost(2 * rows * D * local * SLOTS, 4 * rows * D),
        name="combine",
    )(slot_rows, slots)


def spread_kernel(dp_ref, slot_ref, out_ref):
    for j, pick in enumerate(picks(slot_ref, F32)):
        column = jnp.concatenate([dp_ref[j]] * (PAIR // HD), 1)
        out_ref[j : j + 1, :] = jnp.sum(pick * column, 0, keepdims=True)


def spread_back(dp_slots, slots):
    local, rows = slots.shape
    return pl.pallas_call(
        spread_kernel,
        grid=(rows // PAIR,),
        in_specs=[
            pl.BlockSpec((local, SLOTS, HD), lambda i: (0, i, 0)),
            pl.BlockSpec((local, PAIR), lambda i: (0, i)),
        ],
        out_specs=pl.BlockSpec((local, PAIR), lambda i: (0, i)),
        out_shape=jax.ShapeDtypeStruct((local, rows), F32),
        compiler_params=params(24),
        name="spread_back",
    )(dp_slots, slots)


def expert_kernel(
    first_ref, x_ref, g_ref, wg_ref, wu_ref, wd_ref, wr_ref, *rest, full
):
    if full:
        (act_ref, dg_ref, du_ref, ge_ref, y_ref, z_ref, dp_ref, gate_s, y_s, z_s, dp_s) = rest
    else:
        (act_ref, dg_ref, du_ref, ge_ref, gate_s) = rest
    step, steps = pl.program_id(1), pl.num_programs(1)
    rows, grads = x_ref[0], g_ref[0]

    @pl.when(step == 0)
    def _():
        logits = nn(rows, wr_ref[...])
        lane = lax.broadcasted_iota(jnp.int32, logits.shape, 1)
        logits = jnp.where(lane < EXPERTS, logits, NEG_FILL)
        powers = jnp.exp(logits - jnp.max(logits, -1, keepdims=True))
        mine = jnp.where(lane == first_ref[0] + pl.program_id(0), powers, 0.0)
        gate = jnp.sum(mine, -1, keepdims=True) / jnp.sum(powers, -1, keepdims=True)
        gate_s[...] = jnp.broadcast_to(gate, gate_s.shape)
        ge_ref[0] = (grads.astype(F32) * gate).astype(BF16)
        if full:
            y_s[...] = jnp.zeros_like(y_s)
            z_s[...] = jnp.zeros_like(z_s)
            dp_s[...] = jnp.zeros_like(dp_s)

    gate = gate_s[:, 0:1]
    gate_pre = nn(rows, wg_ref[0])
    up_pre = nn(rows, wu_ref[0])
    slope = nt(grads, wd_ref[0])
    sig = jax.nn.sigmoid(gate_pre)
    silu = gate_pre * sig
    act = (silu * up_pre).astype(BF16)
    grad_act = slope * gate
    grad_gate = (grad_act * up_pre * sig * (1.0 + gate_pre * (1.0 - sig))).astype(BF16)
    grad_up = (grad_act * silu).astype(BF16)
    act_ref[0] = act
    dg_ref[0] = grad_gate
    du_ref[0] = grad_up
    if full:
        dp_s[...] += jnp.broadcast_to(
            jnp.sum(act.astype(F32) * slope, -1, keepdims=True), dp_s.shape
        )
        y_s[...] += nn(act, wd_ref[0])
        z_s[...] += nt(grad_gate, wg_ref[0]) + nt(grad_up, wu_ref[0])

        @pl.when(step == steps - 1)
        def _():
            y_ref[0] = (y_s[...] * gate).astype(BF16)
            z_ref[0] = z_s[...].astype(BF16)
            dp_ref[0] = dp_s[...]


def experts(first, rows, grads, w_gate, w_up, w_down, router, full):
    local, count, _ = rows.shape
    hidden = w_gate.shape[2]
    chunk = hidden // 2
    row_spec = pl.BlockSpec((1, count, D), lambda j, f, s: (j, 0, 0))
    mid_spec = pl.BlockSpec((1, count, chunk), lambda j, f, s: (j, 0, f))
    in_w = pl.BlockSpec((1, D, chunk), lambda j, f, s: (j, 0, f))
    mid_shape = jax.ShapeDtypeStruct((local, count, hidden), BF16)
    row_shape = jax.ShapeDtypeStruct((local, count, D), BF16)
    out_specs = [mid_spec, mid_spec, mid_spec, row_spec]
    out_shape = [mid_shape, mid_shape, mid_shape, row_shape]
    scratch = [pltpu.VMEM((count, HD), F32)]
    if full:
        out_specs += [row_spec, row_spec, pl.BlockSpec((1, count, HD), lambda j, f, s: (j, 0, 0))]
        out_shape += [row_shape, row_shape, jax.ShapeDtypeStruct((local, count, HD), F32)]
        scratch += [
            pltpu.VMEM((count, D), F32),
            pltpu.VMEM((count, D), F32),
            pltpu.VMEM((count, HD), F32),
        ]
    unit = 2 * local * count * hidden * D
    return pl.pallas_call(
        functools.partial(expert_kernel, full=full),
        grid_spec=pltpu.PrefetchScalarGridSpec(
            num_scalar_prefetch=1,
            grid=(local, 2),
            in_specs=[
                row_spec, row_spec, in_w, in_w,
                pl.BlockSpec((1, chunk, D), lambda j, f, s: (j, f, 0)),
                pl.BlockSpec((D, HD), lambda j, f, s: (0, 0)),
            ],
            out_specs=out_specs,
            scratch_shapes=scratch,
        ),
        out_shape=out_shape,
        compiler_params=params(60),
        cost_estimate=cost((6 if full else 3) * unit, 6 * local * hidden * D + 8 * local * count * D),
        name="experts_full" if full else "experts_half",
    )(first, rows, grads, w_gate, w_up, w_down, router)


def weights_kernel(
    half_ref, xa, xb, dga, dgb, dua, dub, aa, ab, gea, geb, gate_ref, up_ref, down_ref
):
    gate_ref[0] = tn(xa[0], dga[0]) + tn(xb[0], dgb[0])
    up_ref[0] = tn(xa[0], dua[0]) + tn(xb[0], dub[0])
    down_ref[0] = tn(aa[0], gea[0]) + tn(ab[0], geb[0])


def weight_grads(half, x_pair, dg_pair, du_pair, act_pair, ge_pair):
    local, count, _ = x_pair[0].shape
    hidden = dg_pair[0].shape[2]
    x_spec = pl.BlockSpec((1, count, D // 2), lambda j, f, s: (j, 0, s[0]))
    d_spec = pl.BlockSpec((1, count, hidden // 2), lambda j, f, s: (j, 0, f))
    a_spec = pl.BlockSpec((1, count, hidden // 2), lambda j, f, s: (j, 0, s[0]))
    g_spec = pl.BlockSpec((1, count, D // 2), lambda j, f, s: (j, 0, f))
    unit = 2 * local * count * hidden * D
    return pl.pallas_call(
        weights_kernel,
        grid_spec=pltpu.PrefetchScalarGridSpec(
            num_scalar_prefetch=1,
            grid=(local, 2),
            in_specs=[x_spec] * 2 + [d_spec] * 4 + [a_spec] * 2 + [g_spec] * 2,
            out_specs=[
                pl.BlockSpec((1, D // 2, hidden // 2), lambda j, f, s: (j, 0, f)),
                pl.BlockSpec((1, D // 2, hidden // 2), lambda j, f, s: (j, 0, f)),
                pl.BlockSpec((1, hidden // 2, D // 2), lambda j, f, s: (j, 0, f)),
            ],
        ),
        out_shape=[
            jax.ShapeDtypeStruct((local, D // 2, hidden), F32),
            jax.ShapeDtypeStruct((local, D // 2, hidden), F32),
            jax.ShapeDtypeStruct((local, hidden // 2, D), F32),
        ],
        compiler_params=params(60),
        cost_estimate=cost(3 * unit, 6 * local * hidden * D + 8 * local * count * D),
        name="weight_grads",
    )(half, *x_pair, *dg_pair, *du_pair, *act_pair, *ge_pair)


def swap(value, axis):
    return lax.ppermute(value, axis, [(0, 1), (1, 0)])


def total_over_ep(value):
    value = value + swap(value, "core")
    value = value + swap(value, "x")
    value = value + lax.ppermute(value, "z", [(0, 1), (1, 0), (2, 3), (3, 2)])
    return value + lax.ppermute(value, "z", [(0, 2), (2, 0), (1, 3), (3, 1)])


def gather_rows(value):
    return lax.all_gather(value, EP, axis=0, tiled=True)


def reduce_rows(value):
    return lax.psum_scatter(value, EP, scatter_dimension=0, tiled=True)


def expert_slots(routes_all, first, local):
    rows = routes_all.shape[0]
    ids = first + jnp.arange(local, dtype=jnp.int32)
    named = jnp.any(routes_all[None, :, :] == ids[:, None, None], -1).reshape(
        local, rows // TOK_DEV, TOK_DEV
    )
    places = jnp.arange(TOK_DEV, dtype=jnp.int32)
    upto = (places[:, None] <= places[None, :]).astype(BF16)
    rank = jnp.einsum(
        "ebt,ts->ebs", named.astype(BF16), upto, preferred_element_type=F32
    ).astype(jnp.int32)
    base = (jnp.arange(rows // TOK_DEV, dtype=jnp.int32) % 2) * CAP
    return jnp.where(named, rank - 1 + base[None, :, None], -1).reshape(local, rows)


def fast_shards(
    tokens, w_query, w_key, w_value, w_output, w_router, attn_gain, query_gain, key_gain,
    moe_gain, w_gate, w_up, w_down, routes, cotangent,
):
    group = lax.axis_index("grp")
    place = lax.axis_index(EP)
    members = lax.axis_size(EP)
    seq = TOK_DEV * members
    local = w_gate.shape[0]
    wide = w_query.shape[0]
    first = (place * local).reshape(1).astype(jnp.int32)

    small = jnp.concatenate(
        [
            w_router,
            routes.reshape(-1, EXPERTS).astype(BF16),
            jnp.stack([attn_gain, query_gain, key_gain, moe_gain]),
            jnp.zeros((12, EXPERTS), BF16),
        ],
        0,
    )
    small_all = lax.all_gather(small, ALL)
    route_rows = TOK_DEV * TOPK // EXPERTS
    router_full = small_all[:, :wide].reshape(D, EXPERTS)
    routes_all = (
        small_all[:, wide : wide + route_rows].reshape(2, seq, TOPK).astype(jnp.int32)
    )
    gains = jnp.transpose(
        small_all[:, wide + route_rows : wide + route_rows + 4], (1, 0, 2)
    ).reshape(4, D).astype(F32)
    router_wide = jnp.concatenate([router_full, jnp.zeros((D, HD - EXPERTS), BF16)], 1)
    head_gains = lax.dynamic_slice(gains, (0, place * HD), (4, HD))
    gain_q, gain_k = head_gains[1:2], head_gains[2:3]
    attn_row, moe_row = gains[0:1], gains[3:4]

    tok_all = gather_rows(tokens)
    columns = jnp.stack([w_query, w_key, w_value], 1).reshape(wide, 3, HEADS, HD)
    columns = jnp.transpose(columns, (2, 0, 1, 3)).reshape(HEADS, wide, 3 * HD)
    mine = lax.all_to_all(columns, EP, 0, 0, tiled=True).reshape(D // 2, 3 * HD)
    other = swap(mine, "grp")
    w_head = jnp.where(
        group == 0, jnp.concatenate([mine, other], 0), jnp.concatenate([other, mine], 0)
    )
    half_out = gather_rows(w_output)
    other_out = swap(half_out, "grp")
    output_full = jnp.where(
        group == 0,
        jnp.concatenate([half_out, other_out], 0),
        jnp.concatenate([other_out, half_out], 0),
    )
    cot_own = gather_rows(cotangent)
    cot_other = swap(cot_own, "grp")

    slots_own = expert_slots(lax.dynamic_index_in_dim(routes_all, group, 0, False), first, local)
    slots_other = expert_slots(
        lax.dynamic_index_in_dim(routes_all, 1 - group, 0, False), first, local
    )

    positions = jnp.arange(seq, dtype=jnp.int32)
    half_dim = HD // 2
    frequency = jnp.exp(-(2.0 * jnp.arange(half_dim, dtype=F32) / HD) * math.log(10000.0))
    angles = positions.astype(F32)[:, None] * frequency[None, :]
    cosine = jnp.concatenate([jnp.cos(angles)] * 2, 1)
    sine = jnp.concatenate([-jnp.sin(angles), jnp.sin(angles)], 1)

    qkv, stat = project(tok_all, w_head, attn_row)
    stat = total_over_ep(stat)
    q16, k16, v16, attn_float, att_head, lse = attend(qkv, stat, gain_q, gain_k, cosine, sine)
    attended = lax.all_to_all(att_head.reshape(members, TOK_DEV, HD), EP, 0, 0, tiled=True)
    attended = jnp.transpose(attended, (1, 0, 2)).reshape(TOK_DEV, D)

    inputs = tokens.astype(F32)
    branch_attn = nn(attended, output_full)
    hidden = inputs + branch_attn
    moe_inv = inv_rms(hidden)
    mixed = (hidden * moe_inv * moe_row).astype(BF16)
    mixed_own = gather_rows(mixed)
    mixed_other = swap(mixed_own, "grp")

    route_probs = jax.nn.softmax(nn(mixed, router_full), -1)
    g_own = dispatch(cot_own, slots_own)
    x_own = dispatch(mixed_own, slots_own)
    act_a, dg_a, du_a, ge_a, y_rows, z_rows, dp_slots = experts(
        first, x_own, g_own, w_gate, w_up, w_down, router_wide, True
    )
    mixed_part = combine(z_rows, slots_own)
    grad_mixed = reduce_rows(mixed_part).astype(F32)
    dp_part = spread_back(dp_slots, slots_own)
    dp_part = jnp.transpose(dp_part.reshape(local, members, TOK_DEV), (1, 0, 2))
    dp = lax.all_to_all(dp_part, EP, 0, 0, tiled=True).reshape(EXPERTS, TOK_DEV).T

    branch_moe = reduce_rows(combine(y_rows, slots_own)).astype(F32)
    output = (hidden + branch_moe).astype(BF16)

    grad_logits = (
        route_probs * (dp - jnp.sum(route_probs * dp, -1, keepdims=True))
    ).astype(BF16)
    router_part = tn(mixed, grad_logits)
    grad_mixed = grad_mixed + nt(grad_logits, router_full)
    grad_hid_norm, moe_gain_part = norm_back(grad_mixed, hidden, moe_inv, moe_row)
    grad_hidden = cotangent.astype(F32) + grad_hid_norm
    grad_branch = grad_hidden.astype(BF16)
    grad_attended = nt(grad_branch, output_full).astype(BF16)
    grad_att_head = lax.all_to_all(
        jnp.transpose(grad_attended.reshape(TOK_DEV, HEADS, HD), (1, 0, 2)), EP, 0, 0, tiled=True
    ).reshape(seq, HD)

    output_part = tn(attended, grad_branch).astype(BF16)
    output_keep = lax.dynamic_slice_in_dim(output_part, group * (D // 2), D // 2, 0)
    output_send = lax.dynamic_slice_in_dim(output_part, (1 - group) * (D // 2), D // 2, 0)
    output_grad = reduce_rows(
        (output_keep.astype(F32) + swap(output_send, "grp").astype(F32)).astype(BF16)
    ).astype(F32)

    dnq, dnk, dv16, means, gain_parts = attend_back(
        q16, k16, v16, grad_att_head, attn_float, lse, qkv, stat, gain_q, gain_k, cosine, sine
    )
    means = total_over_ep(means)
    normed_part, dw_head = project_back(
        dnq, dnk, dv16, qkv, stat, means, gain_q, gain_k, tok_all, attn_row, w_head
    )
    grad_normed = reduce_rows(normed_part).astype(F32)
    attn_inv = inv_rms(inputs)
    scaled = grad_normed * attn_row
    grad_tok = attn_inv * (
        scaled - inputs * attn_inv * attn_inv * jnp.mean(scaled * inputs, -1, keepdims=True)
    )
    tokens_grad = (grad_hidden + grad_tok).astype(BF16)

    dw_keep = lax.dynamic_slice_in_dim(dw_head, group * (D // 2), D // 2, 0)
    dw_send = lax.dynamic_slice_in_dim(dw_head, (1 - group) * (D // 2), D // 2, 0)
    dw_half = (dw_keep + swap(dw_send.astype(BF16), "grp").astype(F32)).astype(BF16)
    gain_parts = gain_parts + swap(gain_parts, "grp")
    sums = jnp.stack(
        [jnp.sum(inputs * inputs), jnp.sum(branch_attn * branch_attn), jnp.sum(branch_moe * branch_moe)]
    )
    extra = jnp.concatenate(
        [gain_parts.reshape(1, 2 * HD), sums[None, :], jnp.zeros((1, HD - 3), F32)], 1
    )
    high = extra.astype(BF16)
    low = (extra - high.astype(F32)).astype(BF16)
    extra = jnp.concatenate([high, low, jnp.zeros((14, 3 * HD), BF16)], 0)
    payload = jnp.concatenate(
        [
            dw_half.reshape(members, wide, 3 * HD),
            jnp.broadcast_to(extra[None], (members, 16, 3 * HD)),
        ],
        1,
    )
    arrived = lax.all_to_all(payload, EP, 0, 0, tiled=True).astype(F32)
    dense = jnp.transpose(
        arrived[:, :wide].reshape(HEADS, wide, 3, HD), (2, 1, 0, 3)
    ).reshape(3, wide, D)
    extras = arrived[:, wide] + arrived[:, wide + 1]
    rms_stats = jnp.sqrt(jnp.sum(extras[:, 2 * HD : 2 * HD + 3], 0) / (seq * D)).reshape(1, 3)
    flat = group * members + place
    head_row = lax.dynamic_slice(
        extras[:, : 2 * HD].reshape(HEADS, 2, HD // wide, wide),
        (flat // (HD // wide), 0, flat % (HD // wide), 0),
        (1, 2, 1, wide),
    ).reshape(2, wide)
    attn_gain_grad = (
        jnp.sum(
            w_query.astype(F32) * dense[0]
            + w_key.astype(F32) * dense[1]
            + w_value.astype(F32) * dense[2],
            -1,
        )
        / attn_gain.astype(F32)
    )

    rest_part = jnp.concatenate(
        [router_part, moe_gain_part[:, None], jnp.zeros((D, HD - EXPERTS - 1), F32)], 1
    )
    rest = lax.psum_scatter(rest_part, ALL, scatter_dimension=0, tiled=True)
    router_grad, moe_gain_grad = rest[:, :EXPERTS], rest[:, EXPERTS]

    g_other = dispatch(cot_other, slots_other)
    x_other = dispatch(mixed_other, slots_other)
    act_b, dg_b, du_b, ge_b = experts(
        first, x_other, g_other, w_gate, w_up, w_down, router_wide, False
    )
    half = group.reshape(1).astype(jnp.int32)
    gate_grad, up_grad, down_grad = weight_grads(
        half, (x_own, x_other), (dg_a, dg_b), (du_a, du_b), (act_a, act_b), (ge_a, ge_b)
    )
    return (
        output, tokens_grad, dense[0], dense[1], dense[2], output_grad, router_grad,
        attn_gain_grad, head_row[0], head_row[1], moe_gain_grad, gate_grad, up_grad, down_grad,
        rms_stats,
    )


def fast_solution(mesh, sides):
    inner = jax.sharding.Mesh(mesh.devices.reshape((2,) + sides), ALL)
    rows = P(ALL, None)
    expert = P(EP, None, None)
    return jax.shard_map(
        fast_shards,
        mesh=inner,
        in_specs=(rows,) * 6 + (P(ALL),) * 4 + (expert,) * 3 + (rows,) * 2,
        out_specs=(rows,) * 7 + (P(ALL),) * 4 + (P(EP, "grp", None),) * 3 + (P("grp", None),),
        check_vma=False,
    )


def solution(mesh):
    sides = SIDES.get(mesh.shape["ep"])
    if sides is not None and mesh.shape["grp"] == 2:
        return fast_solution(mesh, sides)
    return jax.shard_map(
        shards,
        mesh=mesh,
        in_specs=(
            P(("grp", "ep"), None),
            P(("grp", "ep"), None),
            P(("grp", "ep"), None),
            P(("grp", "ep"), None),
            P(("grp", "ep"), None),
            P(("grp", "ep"), None),
            P(("grp", "ep")),
            P(("grp", "ep")),
            P(("grp", "ep")),
            P(("grp", "ep")),
            P("ep", None, None),
            P("ep", None, None),
            P("ep", None, None),
            P(("grp", "ep"), None),
            P(("grp", "ep"), None),
        ),
        out_specs=(
            P(("grp", "ep"), None),
            P(("grp", "ep"), None),
            P(("grp", "ep"), None),
            P(("grp", "ep"), None),
            P(("grp", "ep"), None),
            P(("grp", "ep"), None),
            P(("grp", "ep"), None),
            P(("grp", "ep")),
            P(("grp", "ep")),
            P(("grp", "ep")),
            P(("grp", "ep")),
            P("ep", "grp", None),
            P("ep", "grp", None),
            P("ep", "grp", None),
            P("grp", None),
        ),
        check_vma=False,
    )
```

```python
import functools
import math

import jax
import jax.numpy as jnp
from jax import lax
from jax.experimental import pallas as pl
from jax.experimental.pallas import tpu as pltpu
from jax.sharding import PartitionSpec as P

D = 2048
HEADS = 16
HD = 128
EXPERTS = 64
TOPK = 8
TOK_DEV = 128
BLOCK = 256
CAP = 24


EPSILON = 1e-05
NEG_FILL = -1e30


def inv_rms(values):
    return lax.rsqrt(jnp.mean(values * values, -1, keepdims=True) + EPSILON)


def norm_back(grad_out, values, inverse, gain_vec):
    scaled = grad_out * gain_vec
    grad_in = inverse * (
        scaled - values * inverse * inverse * jnp.mean(scaled * values, -1, keepdims=True)
    )
    return (grad_in, jnp.sum(grad_out * values * inverse, 0))


def rope_tables(positions):
    half_dim = HD // 2
    frequency = jnp.exp(-(2.0 * jnp.arange(half_dim, dtype=jnp.float32) / HD) * math.log(10000.0))
    angles = positions.astype(jnp.float32)[:, None] * frequency[None, :]
    return (jnp.cos(angles)[:, None, :], jnp.sin(angles)[:, None, :])


def rotate(values, cosine, sine_tab):
    half_dim = HD // 2
    first_half = values[..., :half_dim]
    second_half = values[..., half_dim:]
    return jnp.concatenate(
        [
            first_half * cosine - second_half * sine_tab,
            second_half * cosine + first_half * sine_tab,
        ],
        -1,
    )


def rotate_back(grad_in, cosine, sine_tab):
    half_dim = HD // 2
    first_half = grad_in[..., :half_dim]
    second_half = grad_in[..., half_dim:]
    return jnp.concatenate(
        [
            first_half * cosine + second_half * sine_tab,
            second_half * cosine - first_half * sine_tab,
        ],
        -1,
    )


def fold_keys(state_now, key_piece, queries, query_pos):
    keys_in, values_in = key_piece
    piece_rows = keys_in.shape[0]
    blk_rows = math.gcd(piece_rows, 1024)
    key_blocks = keys_in.reshape(piece_rows // blk_rows, blk_rows, HEADS, HD)
    value_blocks = values_in.reshape(piece_rows // blk_rows, blk_rows, HEADS, HD)
    last_block = query_pos[-1] // BLOCK

    def block_step(state_in, block_items):
        key_blk, value_blk, block_num = block_items
        key_start = block_num * blk_rows

        def block_compute(state_cur):
            top_now, total_now, acc_now = state_cur
            key_pos = key_start + jnp.arange(blk_rows, dtype=jnp.int32)
            scores = jnp.einsum(
                "qhd,khd->hqk", queries, key_blk, preferred_element_type=jnp.float32
            ) * HD ** (-0.5)
            allowed = (key_pos // BLOCK)[None, None, :] <= (query_pos // BLOCK)[None, :, None]
            scores = jnp.where(allowed, scores, NEG_FILL)
            top_new = jnp.maximum(top_now, jnp.max(scores, -1, keepdims=True))
            weights = jnp.where(allowed, jnp.exp(scores - top_new), 0.0)
            rescale = jnp.exp(top_now - top_new)
            total_new = total_now * rescale + jnp.sum(weights, -1, keepdims=True)
            acc_new = acc_now * jnp.transpose(rescale, (1, 0, 2)) + jnp.einsum(
                "hqk,khd->qhd",
                weights.astype(jnp.bfloat16),
                value_blk,
                preferred_element_type=jnp.float32,
            )
            return (top_new, total_new, acc_new)

        def block_passing(state_cur):
            return state_cur

        return (
            lax.cond(key_start // BLOCK <= last_block, block_compute, block_passing, state_in),
            None,
        )

    state_out, unused = lax.scan(
        block_step,
        state_now,
        (key_blocks, value_blocks, jnp.arange(piece_rows // blk_rows, dtype=jnp.int32)),
    )
    return state_out


def score_grads(queries, grad_attended, row_delta, log_sum, query_pos, key_blk, value_blk, key_pos):
    scores = jnp.einsum(
        "qhd,khd->hqk", queries, key_blk, preferred_element_type=jnp.float32
    ) * HD ** (-0.5)
    allowed = (key_pos // BLOCK)[None, None, :] <= (query_pos // BLOCK)[None, :, None]
    prob_vals = jnp.where(allowed, jnp.exp(scores - log_sum), 0.0)
    grad_probs = jnp.einsum(
        "qhd,khd->hqk", grad_attended, value_blk, preferred_element_type=jnp.float32
    )
    grad_scores = (prob_vals * (grad_probs - row_delta)).astype(jnp.bfloat16)
    return (prob_vals, grad_scores)


def shards(
    tokens,
    w_query,
    w_key,
    w_value,
    w_output,
    w_router,
    attn_gain,
    query_gain,
    key_gain,
    moe_gain,
    w_gate,
    w_up,
    w_down,
    routes,
    cotangent,
):
    gathered = (
        lax.all_gather(w_query, ("grp", "ep"), axis=0, tiled=True),
        lax.all_gather(w_key, ("grp", "ep"), axis=0, tiled=True),
        lax.all_gather(w_value, ("grp", "ep"), axis=0, tiled=True),
        lax.all_gather(w_output, ("grp", "ep"), axis=0, tiled=True),
        lax.all_gather(w_router, ("grp", "ep"), axis=0, tiled=True),
        lax.all_gather(attn_gain, ("grp", "ep"), axis=0, tiled=True),
        lax.all_gather(query_gain, ("grp", "ep"), axis=0, tiled=True),
        lax.all_gather(key_gain, ("grp", "ep"), axis=0, tiled=True),
        lax.all_gather(moe_gain, ("grp", "ep"), axis=0, tiled=True),
    )
    query_full, key_full, value_full, output_full, router_full = (
        gathered[0],
        gathered[1],
        gathered[2],
        gathered[3],
        gathered[4],
    )
    attn_scale = gathered[5].astype(jnp.float32)
    query_scale = gathered[6].astype(jnp.float32)
    key_scale = gathered[7].astype(jnp.float32)
    moe_scale = gathered[8].astype(jnp.float32)
    ep_count = lax.axis_size("ep")
    exp_local = EXPERTS // ep_count
    score_scale = HD ** (-0.5)
    inputs = tokens.astype(jnp.float32)
    positions = lax.axis_index("ep") * TOK_DEV + jnp.arange(TOK_DEV, dtype=jnp.int32)
    cosine, sine_tab = rope_tables(positions)
    attn_inv = inv_rms(inputs)
    normed = (inputs * attn_inv * attn_scale).astype(jnp.bfloat16)
    query_raw = jnp.dot(normed, query_full, preferred_element_type=jnp.float32)
    key_raw = jnp.dot(normed, key_full, preferred_element_type=jnp.float32)
    values16 = jnp.dot(normed, value_full, preferred_element_type=jnp.float32).astype(jnp.bfloat16)
    query_inv = inv_rms(query_raw)
    queries16 = rotate(
        (query_raw * query_inv * query_scale).reshape(TOK_DEV, HEADS, HD), cosine, sine_tab
    ).astype(jnp.bfloat16)
    key_inv = inv_rms(key_raw)
    keys16 = (
        rotate((key_raw * key_inv * key_scale).reshape(TOK_DEV, HEADS, HD), cosine, sine_tab)
        .astype(jnp.bfloat16)
        .reshape(TOK_DEV, D)
    )
    start_state = (
        jnp.full((HEADS, TOK_DEV, 1), NEG_FILL, jnp.float32),
        jnp.zeros((HEADS, TOK_DEV, 1), jnp.float32),
        jnp.zeros((TOK_DEV, HEADS, HD), jnp.float32),
    )
    folded = fold_keys(
        start_state,
        (
            lax.all_gather(keys16, "ep", axis=0, tiled=True),
            lax.all_gather(values16, "ep", axis=0, tiled=True),
        ),
        queries16,
        positions,
    )
    top_score, total_weight, acc_sum = folded
    log_sum = top_score + jnp.log(total_weight)
    attn_float = acc_sum / jnp.transpose(total_weight, (1, 0, 2))
    attended16 = attn_float.reshape(TOK_DEV, D).astype(jnp.bfloat16)
    branch_attn = jnp.dot(attended16, output_full, preferred_element_type=jnp.float32)
    hidden = inputs + branch_attn
    moe_inv = inv_rms(hidden)
    mixed_in = (hidden * moe_inv * moe_scale).astype(jnp.bfloat16)
    logits = jnp.dot(mixed_in, router_full, preferred_element_type=jnp.float32)
    route_probs = jax.nn.softmax(logits, -1)
    chosen = (routes[:, :, None] == jnp.arange(EXPERTS, dtype=jnp.int32)[None, None, :]).astype(
        jnp.float32
    )
    gate_vals = jnp.sum(chosen * route_probs[:, None, :], -1)
    pair_expert = routes.reshape(-1)
    one_hot = (pair_expert[:, None] == jnp.arange(EXPERTS, dtype=jnp.int32)[None, :]).astype(
        jnp.int32
    )
    pair_rank = jnp.sum(jnp.cumsum(one_hot, 0) * one_hot, 1) - 1
    slot_index = pair_expert * CAP + pair_rank
    pair_token = jnp.arange(TOK_DEV * TOPK, dtype=jnp.int32) // TOPK
    send_rows = jnp.zeros((EXPERTS * CAP, D), jnp.bfloat16).at[slot_index].set(mixed_in[pair_token])
    send_rows = send_rows.reshape(ep_count, exp_local, CAP, D)
    received = lax.all_to_all(send_rows, "ep", split_axis=0, concat_axis=0, tiled=True)
    gate_pre = jnp.einsum("secd,edf->secf", received, w_gate, preferred_element_type=jnp.float32)
    up_pre = jnp.einsum("secd,edf->secf", received, w_up, preferred_element_type=jnp.float32)
    activation = (jax.nn.silu(gate_pre) * up_pre).astype(jnp.bfloat16)
    expert_out = jnp.einsum(
        "secf,efd->secd", activation, w_down, preferred_element_type=jnp.float32
    ).astype(jnp.bfloat16)
    expert_out, gate_pre, up_pre, activation, received = (
        expert_out,
        gate_pre,
        up_pre,
        activation,
        received,
    )
    returned = lax.all_to_all(expert_out, "ep", split_axis=0, concat_axis=0, tiled=True).reshape(
        EXPERTS * CAP, D
    )
    pair_out = returned[slot_index].astype(jnp.float32).reshape(TOK_DEV, TOPK, D)
    branch_moe = jnp.sum(gate_vals[:, :, None] * pair_out, 1)
    output = (hidden + branch_moe).astype(jnp.bfloat16)
    local_sums = jnp.stack(
        [
            jnp.sum(inputs * inputs),
            jnp.sum(branch_attn * branch_attn),
            jnp.sum(branch_moe * branch_moe),
        ]
    )
    seq_sums = lax.psum(local_sums, "ep")
    rms_stats = jnp.sqrt(seq_sums / (TOK_DEV * ep_count * D)).reshape(1, 3)
    grad_out = cotangent.astype(jnp.float32)
    grad_gates = jnp.sum(pair_out * grad_out[:, None, :], -1)
    grad_pairs = (
        (gate_vals[:, :, None] * grad_out[:, None, :])
        .astype(jnp.bfloat16)
        .reshape(TOK_DEV * TOPK, D)
    )
    send_grads = jnp.zeros((EXPERTS * CAP, D), jnp.bfloat16).at[slot_index].set(grad_pairs)
    send_grads = send_grads.reshape(ep_count, exp_local, CAP, D)
    grad_received = lax.all_to_all(send_grads, "ep", split_axis=0, concat_axis=0, tiled=True)
    grad_activation = jnp.einsum(
        "secd,efd->secf", grad_received, w_down, preferred_element_type=jnp.float32
    )
    grad_down = jnp.einsum(
        "secf,secd->efd", activation, grad_received, preferred_element_type=jnp.float32
    )
    sig_gate = jax.nn.sigmoid(gate_pre)
    grad_gate_pre = (
        grad_activation * up_pre * sig_gate * (1.0 + gate_pre * (1.0 - sig_gate))
    ).astype(jnp.bfloat16)
    grad_up_pre = (grad_activation * gate_pre * sig_gate).astype(jnp.bfloat16)
    grad_gate_w = jnp.einsum(
        "secd,secf->edf", received, grad_gate_pre, preferred_element_type=jnp.float32
    )
    grad_up_w = jnp.einsum(
        "secd,secf->edf", received, grad_up_pre, preferred_element_type=jnp.float32
    )
    grad_inputs = (
        jnp.einsum("secf,edf->secd", grad_gate_pre, w_gate, preferred_element_type=jnp.float32)
        + jnp.einsum("secf,edf->secd", grad_up_pre, w_up, preferred_element_type=jnp.float32)
    ).astype(jnp.bfloat16)
    grad_back = lax.all_to_all(grad_inputs, "ep", split_axis=0, concat_axis=0, tiled=True).reshape(
        EXPERTS * CAP, D
    )
    grad_mixed = jnp.sum(grad_back[slot_index].astype(jnp.float32).reshape(TOK_DEV, TOPK, D), 1)
    spread = jnp.sum(chosen * grad_gates[:, :, None], 1)
    grad_logits = (
        route_probs * (spread - jnp.sum(route_probs * spread, -1, keepdims=True))
    ).astype(jnp.bfloat16)
    router_grad = jnp.einsum("td,te->de", mixed_in, grad_logits, preferred_element_type=jnp.float32)
    grad_mixed = grad_mixed + jnp.einsum(
        "te,de->td", grad_logits, router_full, preferred_element_type=jnp.float32
    )
    grad_hid_norm, moe_gain_grad = norm_back(grad_mixed, hidden, moe_inv, moe_scale)
    grad_hidden = grad_out + grad_hid_norm
    grad_branch = grad_hidden.astype(jnp.bfloat16)
    output_grad = jnp.einsum(
        "td,tf->df", attended16, grad_branch, preferred_element_type=jnp.float32
    )
    grad_attended = jnp.einsum(
        "tf,df->td", grad_branch, output_full, preferred_element_type=jnp.float32
    ).astype(jnp.bfloat16)
    grad_attended = grad_attended.reshape(TOK_DEV, HEADS, HD)
    row_delta = jnp.transpose(jnp.sum(grad_attended.astype(jnp.float32) * attn_float, -1), (1, 0))[
        :, :, None
    ]
    gathered_keys, gathered_values = (
        lax.all_gather(keys16, "ep", axis=0, tiled=True),
        lax.all_gather(values16, "ep", axis=0, tiled=True),
    )
    total_rows = gathered_keys.shape[0]
    blk_rows = math.gcd(total_rows, 1024)
    last_query_block = positions[-1] // BLOCK

    def query_step(grad_now, block_num):
        begin_row = block_num * blk_rows

        def query_compute(grad_cur):
            key_blk = lax.dynamic_slice_in_dim(gathered_keys, begin_row, blk_rows, 0).reshape(
                blk_rows, HEADS, HD
            )
            value_blk = lax.dynamic_slice_in_dim(gathered_values, begin_row, blk_rows, 0).reshape(
                blk_rows, HEADS, HD
            )
            key_pos = begin_row + jnp.arange(blk_rows, dtype=jnp.int32)
            prob_vals, grad_scores = score_grads(
                queries16, grad_attended, row_delta, log_sum, positions, key_blk, value_blk, key_pos
            )
            return (
                grad_cur
                + jnp.einsum(
                    "hqk,khd->qhd", grad_scores, key_blk, preferred_element_type=jnp.float32
                )
                * score_scale
            )

        def query_passing(grad_cur):
            return grad_cur

        return (
            lax.cond(
                begin_row // BLOCK <= last_query_block, query_compute, query_passing, grad_now
            ),
            None,
        )

    grad_queries, unused = lax.scan(
        query_step,
        jnp.zeros((TOK_DEV, HEADS, HD), jnp.float32),
        jnp.arange(total_rows // blk_rows, dtype=jnp.int32),
    )
    all_queries, all_grad_att = (
        lax.all_gather(queries16, "ep", axis=0, tiled=True),
        lax.all_gather(grad_attended, "ep", axis=0, tiled=True),
    )
    all_delta, all_log_sum = (
        lax.all_gather(row_delta, "ep", axis=1, tiled=True),
        lax.all_gather(log_sum, "ep", axis=1, tiled=True),
    )
    query_rows = all_queries.shape[0]
    query_blk_rows = math.gcd(query_rows, 1024)
    own_keys = keys16.reshape(TOK_DEV, HEADS, HD)
    own_values = values16.reshape(TOK_DEV, HEADS, HD)
    first_key_block = positions[0] // BLOCK

    def key_step(grads_now, block_num):
        begin_row = block_num * query_blk_rows

        def key_compute(grads_cur):
            query_blk = lax.dynamic_slice_in_dim(all_queries, begin_row, query_blk_rows, 0)
            grad_att_blk = lax.dynamic_slice_in_dim(all_grad_att, begin_row, query_blk_rows, 0)
            delta_blk = lax.dynamic_slice_in_dim(all_delta, begin_row, query_blk_rows, 1)
            log_blk = lax.dynamic_slice_in_dim(all_log_sum, begin_row, query_blk_rows, 1)
            query_pos = begin_row + jnp.arange(query_blk_rows, dtype=jnp.int32)
            prob_vals, grad_scores = score_grads(
                query_blk,
                grad_att_blk,
                delta_blk,
                log_blk,
                query_pos,
                own_keys,
                own_values,
                positions,
            )
            key_part = (
                jnp.einsum(
                    "hqk,qhd->khd", grad_scores, query_blk, preferred_element_type=jnp.float32
                )
                * score_scale
            )
            value_part = jnp.einsum(
                "hqk,qhd->khd",
                prob_vals.astype(jnp.bfloat16),
                grad_att_blk,
                preferred_element_type=jnp.float32,
            )
            return (grads_cur[0] + key_part, grads_cur[1] + value_part)

        def key_passing(grads_cur):
            return grads_cur

        return (
            lax.cond(
                (begin_row + query_blk_rows - 1) // BLOCK >= first_key_block,
                key_compute,
                key_passing,
                grads_now,
            ),
            None,
        )

    key_start = (
        jnp.zeros((TOK_DEV, HEADS, HD), jnp.float32),
        jnp.zeros((TOK_DEV, HEADS, HD), jnp.float32),
    )
    key_value_grads, unused = lax.scan(
        key_step, key_start, jnp.arange(query_rows // query_blk_rows, dtype=jnp.int32)
    )
    grad_keys16 = key_value_grads[0].astype(jnp.bfloat16)
    grad_values16 = key_value_grads[1].reshape(TOK_DEV, D).astype(jnp.bfloat16)
    grad_keys = lax.optimization_barrier(grad_keys16).astype(jnp.float32)
    grad_queries = lax.optimization_barrier(grad_queries.astype(jnp.bfloat16)).astype(jnp.float32)
    grad_query_rot = rotate_back(grad_queries, cosine, sine_tab).reshape(TOK_DEV, D)
    grad_query_raw, query_gain_grad = norm_back(grad_query_rot, query_raw, query_inv, query_scale)
    grad_query16 = grad_query_raw.astype(jnp.bfloat16)
    grad_key_rot = rotate_back(grad_keys, cosine, sine_tab).reshape(TOK_DEV, D)
    grad_key_raw, key_gain_grad = norm_back(grad_key_rot, key_raw, key_inv, key_scale)
    grad_key16 = grad_key_raw.astype(jnp.bfloat16)
    query_grad = jnp.einsum("td,tf->df", normed, grad_query16, preferred_element_type=jnp.float32)
    key_grad = jnp.einsum("td,tf->df", normed, grad_key16, preferred_element_type=jnp.float32)
    value_grad = jnp.einsum("td,tf->df", normed, grad_values16, preferred_element_type=jnp.float32)
    grad_normed = (
        jnp.einsum("tf,df->td", grad_query16, query_full, preferred_element_type=jnp.float32)
        + jnp.einsum("tf,df->td", grad_key16, key_full, preferred_element_type=jnp.float32)
        + jnp.einsum("tf,df->td", grad_values16, value_full, preferred_element_type=jnp.float32)
    )
    grad_tok_norm, attn_gain_grad = norm_back(grad_normed, inputs, attn_inv, attn_scale)
    tokens_grad = (grad_hidden + grad_tok_norm).astype(jnp.bfloat16)
    dense_sums = (
        lax.psum_scatter(query_grad, ("grp", "ep"), scatter_dimension=0, tiled=True),
        lax.psum_scatter(key_grad, ("grp", "ep"), scatter_dimension=0, tiled=True),
        lax.psum_scatter(value_grad, ("grp", "ep"), scatter_dimension=0, tiled=True),
        lax.psum_scatter(output_grad, ("grp", "ep"), scatter_dimension=0, tiled=True),
        lax.psum_scatter(router_grad, ("grp", "ep"), scatter_dimension=0, tiled=True),
        lax.psum_scatter(attn_gain_grad, ("grp", "ep"), scatter_dimension=0, tiled=True),
        lax.psum_scatter(query_gain_grad, ("grp", "ep"), scatter_dimension=0, tiled=True),
        lax.psum_scatter(key_gain_grad, ("grp", "ep"), scatter_dimension=0, tiled=True),
        lax.psum_scatter(moe_gain_grad, ("grp", "ep"), scatter_dimension=0, tiled=True),
    )
    expert_sums = (
        lax.psum_scatter(
            grad_gate_w.astype(jnp.bfloat16), "grp", scatter_dimension=1, tiled=True
        ).astype(jnp.float32),
        lax.psum_scatter(
            grad_up_w.astype(jnp.bfloat16), "grp", scatter_dimension=1, tiled=True
        ).astype(jnp.float32),
        lax.psum_scatter(
            grad_down.astype(jnp.bfloat16), "grp", scatter_dimension=1, tiled=True
        ).astype(jnp.float32),
    )
    return (
        output,
        tokens_grad,
        dense_sums[0],
        dense_sums[1],
        dense_sums[2],
        dense_sums[3],
        dense_sums[4],
        dense_sums[5],
        dense_sums[6],
        dense_sums[7],
        dense_sums[8],
        expert_sums[0],
        expert_sums[1],
        expert_sums[2],
        rms_stats,
    )


F32 = jnp.float32
BF16 = jnp.bfloat16
EP = ("z", "x", "core")
ALL = ("grp", "z", "x", "core")
PAIR = 2 * TOK_DEV
SLOTS = 2 * CAP
COST = 0.01
SIDES = {16: (4, 2, 2)}


def nt(left, right):
    return lax.dot_general(left, right, (((1,), (1,)), ((), ())), preferred_element_type=F32)


def nn(left, right):
    return lax.dot_general(left, right, (((1,), (0,)), ((), ())), preferred_element_type=F32)


def tn(left, right):
    return lax.dot_general(left, right, (((0,), (0,)), ((), ())), preferred_element_type=F32)


def as_row(column):
    return jnp.broadcast_to(column, (column.shape[0], 128)).T[0:1]


def as_column(row):
    return jnp.broadcast_to(row, (128, row.shape[1])).T


def inv_of(sum_row):
    return as_column(lax.rsqrt(sum_row / D + EPSILON))


def params(mebibytes):
    return pltpu.CompilerParams(vmem_limit_bytes=mebibytes * 1024 * 1024)


def cost(flops, moved):
    return pl.CostEstimate(flops=int(flops * COST), bytes_accessed=int(moved * COST), transcendentals=0)


def whole(*dims):
    return pl.BlockSpec(dims, lambda *_: (0,) * len(dims))


def ordered(kernel, after, specs, **settings):
    after = [array for array in after if not any(array is other for other in specs.pop("kept", ()))]
    inputs = len(specs["in_specs"])
    prefetch = specs.pop("num_scalar_prefetch", 0)
    extra = len(after)

    def body(*refs):
        kept = refs[: prefetch + inputs] + refs[prefetch + inputs + extra :]
        kernel(*kept)

    specs["in_specs"] = list(specs["in_specs"]) + [pl.BlockSpec(memory_space=pl.ANY)] * extra
    call = pl.pallas_call(
        body,
        grid_spec=pltpu.PrefetchScalarGridSpec(num_scalar_prefetch=prefetch, **specs),
        **settings,
    )
    return lambda *args: call(*args, *after)


ANYWHERE = pl.BlockSpec(memory_space=pl.ANY)
BLOCK_SHAPE = (TOK_DEV, D)


def project_kernel(place_ref, own_ref, other_ref, w_ref, gain_ref, *refs):
    normed_ref, qkv_ref, stat_ref = refs[-3:]
    core = place_ref[1]
    for side, tok_ref in ((core, own_ref), (1 - core, other_ref)):
        here = pl.ds(pl.multiple_of(side * TOK_DEV, TOK_DEV), TOK_DEV)
        rows = tok_ref[...].astype(F32)
        inverse = lax.rsqrt(jnp.mean(rows * rows, -1, keepdims=True) + EPSILON)
        normed = (rows * inverse * gain_ref[...]).astype(BF16)
        normed_ref[here, :] = normed
        out = nn(normed, w_ref[...])
        qkv_ref[here, :] = out
        for part in range(2):
            piece = out[:, part * HD : (part + 1) * HD]
            stat_ref[part : part + 1, here] = as_row(jnp.sum(piece * piece, -1, keepdims=True))


def project(chip_core, own, other, w_head, gain_row, buffers, seq, after=()):
    kept = [] if buffers is None else list(buffers)
    return ordered(
        project_kernel,
        after,
        dict(
            num_scalar_prefetch=1,
            grid=(1,),
            in_specs=[whole(TOK_DEV, D), whole(TOK_DEV, D), whole(D, 3 * HD), whole(1, D)]
            + [ANYWHERE] * len(kept),
            kept=kept,
            out_specs=[
                pl.BlockSpec((PAIR, D), lambda i, s: (s[0], 0)),
                pl.BlockSpec((PAIR, 3 * HD), lambda i, s: (s[0], 0)),
                pl.BlockSpec((2, PAIR), lambda i, s: (0, s[0])),
            ],
        ),
        out_shape=[
            jax.ShapeDtypeStruct((seq, D), BF16),
            jax.ShapeDtypeStruct((seq, 3 * HD), F32),
            jax.ShapeDtypeStruct((2, seq), F32),
        ],
        input_output_aliases={5 + i: i for i in range(len(kept))},
        compiler_params=params(24),
        cost_estimate=cost(2 * PAIR * D * 3 * HD, 10 * PAIR * D),
        name="project",
    )(chip_core, own, other, w_head, gain_row, *kept)


def attend_kernel(
    qkv_ref, stat_ref, gq_ref, gk_ref, cos_ref, sin_ref,
    q_ref, k_ref, v_ref, of_ref, att_ref, lse_ref, vt_ref,
):
    blocks = q_ref.shape[0] // BLOCK
    for i in range(blocks):
        rows = slice(i * BLOCK, (i + 1) * BLOCK)
        cosine, sine = cos_ref[rows, :], sin_ref[rows, :]
        for part, gain_ref, out_ref in ((0, gq_ref, q_ref), (1, gk_ref, k_ref)):
            raw = qkv_ref[rows, part * HD : (part + 1) * HD]
            scaled = raw * inv_of(stat_ref[part : part + 1, rows]) * gain_ref[...]
            turned = scaled * cosine + pltpu.roll(scaled, HD // 2, 1) * sine
            out_ref[rows, :] = turned.astype(BF16)
        value = qkv_ref[rows, 2 * HD :]
        v_ref[rows, :] = value.astype(BF16)
        vt_ref[:, rows] = value.T.astype(BF16)
    for i in range(blocks):
        rows = slice(i * BLOCK, (i + 1) * BLOCK)
        reach = (i + 1) * BLOCK
        scores = nt(k_ref[0:reach, :], q_ref[rows, :]) * HD ** (-0.5)
        top = jnp.max(scores, 0, keepdims=True)
        weights = jnp.exp(scores - top)
        total = jnp.sum(weights, 0, keepdims=True)
        probs = (weights * (1.0 / total)).astype(BF16)
        out = nn(vt_ref[:, 0:reach], probs).T
        of_ref[rows, :] = out
        att_ref[rows, :] = out.astype(BF16)
        lse_ref[:, rows] = top + jnp.log(total)


def attend(qkv, stat, gain_q, gain_k, cosine, sine):
    rows = qkv.shape[0]
    shape = lambda kind: jax.ShapeDtypeStruct((rows, HD), kind)
    return pl.pallas_call(
        attend_kernel,
        out_shape=[shape(BF16), shape(BF16), shape(BF16), shape(F32), shape(BF16),
                   jax.ShapeDtypeStruct((1, rows), F32)],
        scratch_shapes=[pltpu.VMEM((HD, rows), BF16)],
        compiler_params=params(48),
        cost_estimate=cost(8 * rows * rows * HD, 10 * rows * 384),
        name="attend",
    )(qkv, stat, gain_q, gain_k, cosine, sine)


def attend_back_kernel(
    q_ref, k_ref, v_ref, do_ref, of_ref, lse_ref, qkv_ref, stat_ref, gq_ref, gk_ref,
    cos_ref, sin_ref, dnq_ref, dnk_ref, dv_ref, means_ref, gains_ref, dk_acc, dv_acc,
):
    blocks = q_ref.shape[0] // BLOCK
    scale = HD ** (-0.5)
    dk_acc[...] = jnp.zeros_like(dk_acc)
    dv_acc[...] = jnp.zeros_like(dv_acc)

    def turn_back(grad, rows, part, gain_ref, out_ref):
        grad = grad.astype(BF16).astype(F32)
        grad = grad * cos_ref[rows, :] - pltpu.roll(grad, HD // 2, 1) * sin_ref[rows, :]
        raw = qkv_ref[rows, part * HD : (part + 1) * HD]
        out_ref[rows, :] = grad
        means_ref[part : part + 1, rows] = jnp.sum((grad * gain_ref[...] * raw).T, 0, keepdims=True)
        inverse = inv_of(stat_ref[part : part + 1, rows])
        return jnp.sum(grad * raw * inverse, 0, keepdims=True)

    gain_q = jnp.zeros((1, HD), F32)
    gain_k = jnp.zeros((1, HD), F32)
    for i in range(blocks):
        rows = slice(i * BLOCK, (i + 1) * BLOCK)
        reach = (i + 1) * BLOCK
        queries, grads = q_ref[rows, :], do_ref[rows, :]
        delta = jnp.sum((grads.astype(F32) * of_ref[rows, :]).T, 0, keepdims=True)
        scores = nt(k_ref[0:reach, :], queries) * scale
        probs = jnp.exp(scores - lse_ref[:, rows])
        slopes = nt(v_ref[0:reach, :], grads)
        grad_scores = (probs * (slopes - delta)).astype(BF16)
        dv_acc[0:reach, :] += nn(probs.astype(BF16), grads)
        dk_acc[0:reach, :] += nn(grad_scores, queries)
        gain_q += turn_back(tn(grad_scores, k_ref[0:reach, :]) * scale, rows, 0, gq_ref, dnq_ref)
    for i in range(blocks):
        rows = slice(i * BLOCK, (i + 1) * BLOCK)
        dv_ref[rows, :] = dv_acc[rows, :].astype(BF16)
        gain_k += turn_back(dk_acc[rows, :] * scale, rows, 1, gk_ref, dnk_ref)
    gains_ref[0:1, :] = gain_q
    gains_ref[1:2, :] = gain_k


def attend_back(q, k, v, grad, out, lse, qkv, stat, gain_q, gain_k, cosine, sine):
    rows = q.shape[0]
    shape = lambda kind: jax.ShapeDtypeStruct((rows, HD), kind)
    return pl.pallas_call(
        attend_back_kernel,
        out_shape=[shape(F32), shape(F32), shape(BF16),
                   jax.ShapeDtypeStruct((2, rows), F32), jax.ShapeDtypeStruct((2, HD), F32)],
        scratch_shapes=[pltpu.VMEM((rows, HD), F32), pltpu.VMEM((rows, HD), F32)],
        compiler_params=params(48),
        cost_estimate=cost(20 * rows * rows * HD, 20 * rows * 384),
        name="attend_back",
    )(q, k, v, grad, out, lse, qkv, stat, gain_q, gain_k, cosine, sine)


def finish_kernel(
    dnq_ref, dnk_ref, dv_ref, qkv_ref, stat_ref, means_ref, gq_ref, gk_ref, out_ref
):
    for part, dn_ref, g_ref in ((0, dnq_ref, gq_ref), (1, dnk_ref, gk_ref)):
        raw = qkv_ref[:, part * HD : (part + 1) * HD]
        inverse = inv_of(stat_ref[part : part + 1, :])
        mean = as_column(means_ref[part : part + 1, :] / D)
        grad = inverse * (dn_ref[...] * g_ref[...] - raw * inverse * inverse * mean)
        out_ref[:, part * HD : (part + 1) * HD] = grad.astype(BF16)
    out_ref[:, 2 * HD :] = dv_ref[...]


def finish(dnq, dnk, dv, qkv, stat, means, gain_q, gain_k):
    rows = dnq.shape[0]
    head = pl.BlockSpec((PAIR, HD), lambda i: (i, 0))
    line = pl.BlockSpec((2, PAIR), lambda i: (0, i))
    full = pl.BlockSpec((PAIR, 3 * HD), lambda i: (i, 0))
    return pl.pallas_call(
        finish_kernel,
        grid=(rows // PAIR,),
        in_specs=[head, head, head, full, line, line, whole(1, HD), whole(1, HD)],
        out_specs=full,
        out_shape=jax.ShapeDtypeStruct((rows, 3 * HD), BF16),
        compiler_params=params(24),
        cost_estimate=cost(20 * rows * 3 * HD, 12 * rows * 3 * HD),
        name="finish",
    )(dnq, dnk, dv, qkv, stat, means, gain_q, gain_k)


def sort_cores(core, first, second, own_ref, other_ref, at):
    @pl.when(core == 0)
    def _():
        own_ref[at] = first
        other_ref[at] = second

    @pl.when(core == 1)
    def _():
        own_ref[at] = second
        other_ref[at] = first


def normed_part_kernel(place_ref, a_ref, b_ref, w_ref, own_ref, other_ref):
    for at, g_ref in enumerate((a_ref, b_ref)):
        out = nt(g_ref[...], w_ref[...]).astype(BF16)
        sort_cores(place_ref[2], out[:TOK_DEV], out[TOK_DEV:], own_ref, other_ref, at)


def normed_part(place, grads, w_head, after=()):
    blocks = jax.ShapeDtypeStruct((2, TOK_DEV, D), BF16)
    return ordered(
        normed_part_kernel,
        after,
        dict(
            num_scalar_prefetch=1,
            grid=(1,),
            in_specs=[
                pl.BlockSpec((PAIR, 3 * HD), lambda i, s: (s[0], 0)),
                pl.BlockSpec((PAIR, 3 * HD), lambda i, s: (s[1], 0)),
                whole(D, 3 * HD),
            ],
            out_specs=[whole(2, TOK_DEV, D)] * 2,
        ),
        out_shape=[blocks, blocks],
        compiler_params=params(24),
        cost_estimate=cost(4 * PAIR * D * 3 * HD, 8 * PAIR * D),
        name="normed_part",
    )(place, grads, grads, w_head)


def dw_kernel(normed_ref, grad_ref, out_ref):
    @pl.when(pl.program_id(0) == 0)
    def _():
        out_ref[...] = jnp.zeros_like(out_ref)

    out_ref[...] += tn(normed_ref[...], grad_ref[...])


def dw_product(normed, grads, after=()):
    rows = normed.shape[0]
    return ordered(
        dw_kernel,
        after,
        dict(
            grid=(rows // 512,),
            in_specs=[
                pl.BlockSpec((512, D), lambda i: (i, 0)),
                pl.BlockSpec((512, 3 * HD), lambda i: (i, 0)),
            ],
            out_specs=whole(D, 3 * HD),
        ),
        out_shape=jax.ShapeDtypeStruct((D, 3 * HD), F32),
        compiler_params=params(32),
        cost_estimate=cost(2 * rows * D * 3 * HD, 3 * rows * D),
        name="dw_product",
    )(normed, grads)


def picks(slots, dtype):
    shape = (SLOTS, slots.shape[1])
    numbers = lax.broadcasted_iota(jnp.int32, shape, 0)
    return [(numbers == slots[j : j + 1, :]).astype(dtype) for j in range(slots.shape[0])]


def pick_matrix(slots):
    return jnp.concatenate(picks(slots, F32), 0).astype(BF16)


def dispatch_kernel(place_ref, own_ref, other_ref, own_slot, other_slot, *refs):
    out_ref, column_ref = refs[-2:]
    core = place_ref[1]
    lanes = pl.ds(pl.multiple_of(place_ref[2] * HD, HD), HD)
    out = nn(pick_matrix(own_slot[0]), own_ref[...])
    out = (out + nn(pick_matrix(other_slot[0]), other_ref[...])).astype(BF16)
    for j in range(out_ref.shape[0]):
        out_ref[j] = out[j * SLOTS : (j + 1) * SLOTS]
    for side, row_ref in ((core, own_ref), (1 - core, other_ref)):
        column_ref[pl.ds(pl.multiple_of(side * TOK_DEV, TOK_DEV), TOK_DEV), :] = row_ref[:, lanes]


def dispatch(place, own, other, slots, buffers, after=()):
    blocks, local, _ = slots.shape
    kept = [] if buffers is None else list(buffers)
    return ordered(
        dispatch_kernel,
        after,
        dict(
            num_scalar_prefetch=1,
            grid=(1,),
            in_specs=[
                whole(*BLOCK_SHAPE),
                whole(*BLOCK_SHAPE),
                pl.BlockSpec((1, local, TOK_DEV), lambda i, s: (2 * s[0] + s[1], 0, 0)),
                pl.BlockSpec((1, local, TOK_DEV), lambda i, s: (2 * s[0] + 1 - s[1], 0, 0)),
            ]
            + [ANYWHERE] * len(kept),
            kept=kept,
            out_specs=[
                pl.BlockSpec((local, SLOTS, D), lambda i, s: (0, s[0], 0)),
                pl.BlockSpec((PAIR, HD), lambda i, s: (s[0], 0)),
            ],
        ),
        out_shape=[
            jax.ShapeDtypeStruct((local, blocks // 2 * SLOTS, D), BF16),
            jax.ShapeDtypeStruct((blocks * TOK_DEV, HD), BF16),
        ],
        input_output_aliases={5 + i: i for i in range(len(kept))},
        compiler_params=params(24),
        cost_estimate=cost(2 * PAIR * D * local * SLOTS, 4 * PAIR * D),
        name="dispatch",
    )(place, own, other, slots, slots, *kept)


def plain_dispatch_kernel(row_ref, slot_ref, out_ref):
    out = sum(nn(pick_matrix(slot_ref[i]), row_ref[i]) for i in range(2)).astype(BF16)
    for j in range(out_ref.shape[0]):
        out_ref[j] = out[j * SLOTS : (j + 1) * SLOTS]


def plain_dispatch(rows, slots, after=()):
    blocks, local, _ = slots.shape
    rows = rows.reshape(blocks, TOK_DEV, D)
    return ordered(
        plain_dispatch_kernel,
        after,
        dict(
            grid=(blocks // 2,),
            in_specs=[
                pl.BlockSpec((2, TOK_DEV, D), lambda i: (i, 0, 0)),
                pl.BlockSpec((2, local, TOK_DEV), lambda i: (i, 0, 0)),
            ],
            out_specs=pl.BlockSpec((local, SLOTS, D), lambda i: (0, i, 0)),
        ),
        out_shape=jax.ShapeDtypeStruct((local, blocks // 2 * SLOTS, D), BF16),
        compiler_params=params(24),
        cost_estimate=cost(2 * blocks * TOK_DEV * D * local * SLOTS, 4 * blocks * TOK_DEV * D),
        name="plain_dispatch",
    )(rows, slots)


def combine_chip(row_ref, slot_ref):
    rows = jnp.concatenate([row_ref[j] for j in range(row_ref.shape[0])], 0)
    return [tn(pick_matrix(slot_ref[i]), rows).astype(BF16) for i in range(2)]


def combine_kernel(row_ref, slot_ref, out_ref):
    first, second = combine_chip(row_ref, slot_ref)
    out_ref[:TOK_DEV] = first
    out_ref[TOK_DEV:] = second


def combine(slot_rows, slots, after=()):
    blocks, local, _ = slots.shape
    rows = blocks * TOK_DEV
    return ordered(
        combine_kernel,
        after,
        dict(
            grid=(blocks // 2,),
            in_specs=[
                pl.BlockSpec((local, SLOTS, D), lambda i: (0, i, 0)),
                pl.BlockSpec((2, local, TOK_DEV), lambda i: (i, 0, 0)),
            ],
            out_specs=pl.BlockSpec((PAIR, D), lambda i: (i, 0)),
        ),
        out_shape=jax.ShapeDtypeStruct((rows, D), BF16),
        compiler_params=params(24),
        cost_estimate=cost(2 * rows * D * local * SLOTS, 4 * rows * D),
        name="combine",
    )(slot_rows, slots)


def combine_part_kernel(place_ref, a_ref, b_ref, a_slot, b_slot, own_ref, other_ref):
    for at, (row_ref, slot_ref) in enumerate(((a_ref, a_slot), (b_ref, b_slot))):
        first, second = combine_chip(row_ref, slot_ref)
        sort_cores(place_ref[2], first, second, own_ref, other_ref, at)


def combine_part(place, slot_rows, slots, after=()):
    local = slots.shape[1]
    shape = jax.ShapeDtypeStruct((2, TOK_DEV, D), BF16)
    rows = lambda n: pl.BlockSpec((local, SLOTS, D), lambda i, s: (0, s[n], 0))
    spots = lambda n: pl.BlockSpec((2, local, TOK_DEV), lambda i, s: (s[n], 0, 0))
    return ordered(
        combine_part_kernel,
        after,
        dict(
            num_scalar_prefetch=1,
            grid=(1,),
            in_specs=[rows(0), rows(1), spots(0), spots(1)],
            out_specs=[whole(2, TOK_DEV, D)] * 2,
        ),
        out_shape=[shape, shape],
        compiler_params=params(24),
        cost_estimate=cost(4 * PAIR * D * local * SLOTS, 8 * PAIR * D),
        name="combine_part",
    )(place, slot_rows, slot_rows, slots, slots)


def spread_kernel(dp_ref, slot_ref, out_ref):
    for i in range(2):
        for j, pick in enumerate(picks(slot_ref[i], F32)):
            out_ref[i, j : j + 1, :] = jnp.sum(pick * dp_ref[j], 0, keepdims=True)


def spread_back(dp_slots, slots, after=()):
    blocks, local, _ = slots.shape
    return ordered(
        spread_kernel,
        after,
        dict(
            grid=(blocks // 2,),
            in_specs=[
                pl.BlockSpec((local, SLOTS, HD), lambda i: (0, i, 0)),
                pl.BlockSpec((2, local, TOK_DEV), lambda i: (i, 0, 0)),
            ],
            out_specs=pl.BlockSpec((2, local, TOK_DEV), lambda i: (i, 0, 0)),
        ),
        out_shape=jax.ShapeDtypeStruct(slots.shape, F32),
        compiler_params=params(24),
        name="spread_back",
    )(dp_slots, slots)


def slope_kernel(g_ref, wd_ref, out_ref):
    out_ref[0] = nt(g_ref[0], wd_ref[0])


def slopes(grads, w_down, after=()):
    local, count, _ = grads.shape
    hidden = w_down.shape[1]
    chunk = hidden // 2
    return ordered(
        slope_kernel,
        after,
        dict(
            grid=(local, 2),
            in_specs=[
                pl.BlockSpec((1, count, D), lambda j, f: (j, 0, 0)),
                pl.BlockSpec((1, chunk, D), lambda j, f: (j, f, 0)),
            ],
            out_specs=pl.BlockSpec((1, count, chunk), lambda j, f: (j, 0, f)),
        ),
        out_shape=jax.ShapeDtypeStruct((local, count, hidden), F32),
        compiler_params=params(24),
        cost_estimate=cost(2 * local * count * hidden * D, 2 * local * hidden * D),
        name="slopes",
    )(grads, w_down)


def expert_kernel(first_ref, x_ref, h_ref, wg_ref, wu_ref, wr_ref, *rest, full):
    if full:
        (act_ref, dg_ref, du_ref, gate_ref, z_ref, dp_ref, z_s, dp_s) = rest
    else:
        (act_ref, dg_ref, du_ref, gate_ref) = rest
    step, steps = pl.program_id(1), pl.num_programs(1)
    rows = x_ref[0]

    @pl.when(step == 0)
    def _():
        logits = nn(rows, wr_ref[...])
        lane = lax.broadcasted_iota(jnp.int32, logits.shape, 1)
        logits = jnp.where(lane < EXPERTS, logits, NEG_FILL)
        powers = jnp.exp(logits - jnp.max(logits, -1, keepdims=True))
        mine = jnp.where(lane == first_ref[0] + pl.program_id(0), powers, 0.0)
        gate = jnp.sum(mine, -1, keepdims=True) / jnp.sum(powers, -1, keepdims=True)
        gate_ref[0] = jnp.broadcast_to(gate, gate_ref.shape[1:])
        if full:
            z_s[...] = jnp.zeros_like(z_s)
            dp_s[...] = jnp.zeros_like(dp_s)

    gate = gate_ref[0, :, 0:1]
    gate_pre = nn(rows, wg_ref[0])
    up_pre = nn(rows, wu_ref[0])
    slope = h_ref[0]
    sig = jax.nn.sigmoid(gate_pre)
    silu = gate_pre * sig
    act = (silu * up_pre).astype(BF16)
    grad_act = slope * gate
    grad_gate = (grad_act * up_pre * sig * (1.0 + gate_pre * (1.0 - sig))).astype(BF16)
    grad_up = (grad_act * silu).astype(BF16)
    act_ref[0] = act
    dg_ref[0] = grad_gate
    du_ref[0] = grad_up
    if full:
        dp_s[...] += jnp.broadcast_to(
            jnp.sum(act.astype(F32) * slope, -1, keepdims=True), dp_s.shape
        )
        z_s[...] += nt(grad_gate, wg_ref[0]) + nt(grad_up, wu_ref[0])

        @pl.when(step == steps - 1)
        def _():
            z_ref[0] = z_s[...].astype(BF16)
            dp_ref[0] = dp_s[...]


def experts(first, rows, slope, w_gate, w_up, router, full, after=()):
    local, count, _ = rows.shape
    hidden = w_gate.shape[2]
    chunk = hidden // 2
    row_spec = pl.BlockSpec((1, count, D), lambda j, f, s: (j, 0, 0))
    mid_spec = pl.BlockSpec((1, count, chunk), lambda j, f, s: (j, 0, f))
    lane_spec = pl.BlockSpec((1, count, HD), lambda j, f, s: (j, 0, 0))
    in_w = pl.BlockSpec((1, D, chunk), lambda j, f, s: (j, 0, f))
    mid_shape = jax.ShapeDtypeStruct((local, count, hidden), BF16)
    lane_shape = jax.ShapeDtypeStruct((local, count, HD), F32)
    out_specs = [mid_spec, mid_spec, mid_spec, lane_spec]
    out_shape = [mid_shape, mid_shape, mid_shape, lane_shape]
    scratch = []
    if full:
        out_specs += [row_spec, lane_spec]
        out_shape += [jax.ShapeDtypeStruct((local, count, D), BF16), lane_shape]
        scratch += [pltpu.VMEM((count, D), F32), pltpu.VMEM((count, HD), F32)]
    unit = 2 * local * count * hidden * D
    return ordered(
        functools.partial(expert_kernel, full=full),
        after,
        dict(
            num_scalar_prefetch=1,
            grid=(local, 2),
            in_specs=[
                row_spec, mid_spec, in_w, in_w,
                pl.BlockSpec((D, HD), lambda j, f, s: (0, 0)),
            ],
            out_specs=out_specs,
            scratch_shapes=scratch,
        ),
        out_shape=out_shape,
        compiler_params=params(40),
        cost_estimate=cost((4 if full else 2) * unit, 4 * local * hidden * D + 8 * local * count * D),
        name="experts_full" if full else "experts_half",
    )(first, rows, slope, w_gate, w_up, router)


def down_kernel(act_ref, gate_ref, wd_ref, out_ref):
    out_ref[0] = (nn(act_ref[0], wd_ref[0]) * gate_ref[0, :, 0:1]).astype(BF16)


def down(act, gate, w_down, after=()):
    local, count, hidden = act.shape
    chunk = D // 2
    return ordered(
        down_kernel,
        after,
        dict(
            grid=(local, 2),
            in_specs=[
                pl.BlockSpec((1, count, hidden), lambda j, f: (j, 0, 0)),
                pl.BlockSpec((1, count, HD), lambda j, f: (j, 0, 0)),
                pl.BlockSpec((1, hidden, chunk), lambda j, f: (j, 0, f)),
            ],
            out_specs=pl.BlockSpec((1, count, chunk), lambda j, f: (j, 0, f)),
        ),
        out_shape=jax.ShapeDtypeStruct((local, count, D), BF16),
        compiler_params=params(24),
        cost_estimate=cost(2 * local * count * hidden * D, 2 * local * hidden * D),
        name="down",
    )(act, gate, w_down)


def weights_kernel(
    half_ref, xa, xb, dga, dgb, dua, dub, aa, ab, ga, gb, gate_a, gate_b, gate_ref, up_ref, down_ref
):
    gate_ref[0] = tn(xa[0], dga[0]) + tn(xb[0], dgb[0])
    up_ref[0] = tn(xa[0], dua[0]) + tn(xb[0], dub[0])
    grad_a = (ga[0].astype(F32) * gate_a[0, :, 0:1]).astype(BF16)
    grad_b = (gb[0].astype(F32) * gate_b[0, :, 0:1]).astype(BF16)
    down_ref[0] = tn(aa[0], grad_a) + tn(ab[0], grad_b)


def weight_grads(half, x_pair, dg_pair, du_pair, act_pair, g_pair, gate_pair, after=()):
    local, count, _ = x_pair[0].shape
    hidden = dg_pair[0].shape[2]
    x_spec = pl.BlockSpec((1, count, D // 2), lambda j, f, s: (j, 0, s[0]))
    d_spec = pl.BlockSpec((1, count, hidden // 2), lambda j, f, s: (j, 0, f))
    a_spec = pl.BlockSpec((1, count, hidden // 2), lambda j, f, s: (j, 0, s[0]))
    g_spec = pl.BlockSpec((1, count, D // 2), lambda j, f, s: (j, 0, f))
    lane_spec = pl.BlockSpec((1, count, HD), lambda j, f, s: (j, 0, 0))
    unit = 2 * local * count * hidden * D
    return ordered(
        weights_kernel,
        after,
        dict(
            num_scalar_prefetch=1,
            grid=(local, 2),
            in_specs=[x_spec] * 2 + [d_spec] * 4 + [a_spec] * 2 + [g_spec] * 2 + [lane_spec] * 2,
            out_specs=[
                pl.BlockSpec((1, D // 2, hidden // 2), lambda j, f, s: (j, 0, f)),
                pl.BlockSpec((1, D // 2, hidden // 2), lambda j, f, s: (j, 0, f)),
                pl.BlockSpec((1, hidden // 2, D // 2), lambda j, f, s: (j, 0, f)),
            ],
        ),
        out_shape=[
            jax.ShapeDtypeStruct((local, D // 2, hidden), F32),
            jax.ShapeDtypeStruct((local, D // 2, hidden), F32),
            jax.ShapeDtypeStruct((local, hidden // 2, D), F32),
        ],
        compiler_params=params(44),
        cost_estimate=cost(3 * unit, 6 * local * hidden * D + 8 * local * count * D),
        name="weight_grads",
    )(half, *x_pair, *dg_pair, *du_pair, *act_pair, *g_pair, *gate_pair)


def swap(value, axis):
    return lax.ppermute(value, axis, [(0, 1), (1, 0)])


def total_over_ep(value):
    value = value + swap(value, "core")
    value = value + swap(value, "x")
    value = value + lax.ppermute(value, "z", [(0, 1), (1, 0), (2, 3), (3, 2)])
    return value + lax.ppermute(value, "z", [(0, 2), (2, 0), (1, 3), (3, 1)])


def gather_rows(value):
    return lax.all_gather(value, EP, axis=0, tiled=True)


def reduce_rows(value):
    return lax.psum_scatter(value, EP, scatter_dimension=0, tiled=True)


CHIP_ORDER = ((0, 1, 2, 3), (1, 0, 2, 3), (2, 1, 3, 0), (3, 2, 1, 0))


def chip_places():
    z, x = lax.axis_index("z"), lax.axis_index("x")
    order = jnp.asarray(CHIP_ORDER, jnp.int32)[z]
    return [[order[s] * 2 + (x if r == 0 else 1 - x) for r in range(2)] for s in range(4)]


def shift(value, pairs):
    return lax.ppermute(value, "z", pairs)


def choose_kernel(flag_ref, *refs):
    out_ref = refs[-1]
    for i in range(len(refs) - 1):

        @pl.when(flag_ref[i] == 1)
        def _(i=i):
            out_ref[...] = refs[i][...]


def choose(flags, options, after=()):
    return ordered(
        choose_kernel,
        after,
        dict(
            num_scalar_prefetch=1,
            grid=(1,),
            in_specs=[whole(*BLOCK_SHAPE)] * len(options),
            out_specs=whole(*BLOCK_SHAPE),
        ),
        out_shape=jax.ShapeDtypeStruct(BLOCK_SHAPE, BF16),
        compiler_params=params(16),
        cost_estimate=cost(TOK_DEV * D, 2 * (len(options) + 1) * TOK_DEV * D),
        name="choose",
    )(flags, *options)


def gather_steps(block, use, work):
    z = lax.axis_index("z")
    flags = lambda *tests: jnp.stack([jnp.asarray(test, jnp.int32) for test in tests])
    below1 = shift(block, [(0, 1), (1, 2), (2, 3)])
    above1 = shift(block, [(3, 2), (2, 1), (1, 0)])
    across0 = swap(block, "x")
    far00 = swap(block, "core")
    last = work(0, block)
    column1 = choose(flags(z == 0, z != 0), [above1, below1], [last])
    below2 = shift(below1, [(1, 2), (2, 3)])
    above2 = shift(above1, [(2, 1), (1, 0)])
    across1 = swap(column1, "x")
    far01, far10 = swap(across0, "core"), swap(column1, "core")
    last = use(0, 0, block, far00, [column1])
    last = use(0, 1, across0, far01, [last])
    last = use(1, 0, column1, far10, [last])
    last = work(1, last)
    column2 = choose(
        flags(z == 0, z == 3, (z == 1) | (z == 2)), [above2, below2, above1], [last]
    )
    below3 = shift(below2, [(2, 3)])
    above3 = shift(above2, [(1, 0)])
    across2 = swap(column2, "x")
    far11, far20 = swap(across1, "core"), swap(column2, "core")
    last = use(1, 1, across1, far11, [column2])
    last = use(2, 0, column2, far20, [last])
    last = work(2, last)
    column3 = choose(
        flags(z == 0, z == 1, z == 2, z == 3), [above3, above2, below2, below3], [last]
    )
    across3 = swap(column3, "x")
    far21, far30 = swap(across2, "core"), swap(column3, "core")
    last = use(2, 1, across2, far21, [column3])
    last = use(3, 0, column3, far30, [last])
    last = work(3, last)
    far31 = swap(across3, "core")
    return use(3, 1, across3, far31, [last])


def sum_kernel(*refs):
    out_ref = refs[-1]
    total = refs[0][...].astype(F32)
    for ref in refs[1:-1]:
        total = total + ref[...].astype(F32)
    out_ref[...] = total.astype(out_ref.dtype)


def sum_blocks(terms, after=(), dtype=BF16):
    specs, arrays = [], []
    for term in terms:
        if isinstance(term, tuple):
            arrays.append(term[0])
            specs.append(pl.BlockSpec((None,) + BLOCK_SHAPE, lambda i, n=term[1]: (n, 0, 0)))
        else:
            arrays.append(term)
            specs.append(whole(*BLOCK_SHAPE))
    return ordered(
        sum_kernel,
        after,
        dict(grid=(1,), in_specs=specs, out_specs=whole(*BLOCK_SHAPE)),
        out_shape=jax.ShapeDtypeStruct(BLOCK_SHAPE, dtype),
        compiler_params=params(16),
        cost_estimate=cost(len(terms) * TOK_DEV * D, 2 * (len(terms) + 1) * TOK_DEV * D),
        name="sum_blocks",
    )(*arrays)


def pass_on(place, near_up, far_up, near_down, far_down, below, above, after=()):
    def kernel(place_ref, nu, fu, nd, fd, below_ref, above_ref, up_ref, down_ref):
        z = place_ref[0]

        def store(out_ref, source_ref, arrived_ref):
            total = source_ref[...].astype(F32) + arrived_ref[...].astype(F32)
            out_ref[...] = total.astype(BF16)

        for edge, near, far, arrived, out_ref in (
            (0, nu, fu, below_ref, up_ref),
            (3, nd, fd, above_ref, down_ref),
        ):
            pl.when(z == edge)(functools.partial(store, out_ref, near, arrived))
            pl.when(z != edge)(functools.partial(store, out_ref, far, arrived))

    shape = jax.ShapeDtypeStruct(BLOCK_SHAPE, BF16)
    return ordered(
        kernel,
        after,
        dict(
            num_scalar_prefetch=1,
            grid=(1,),
            in_specs=[whole(*BLOCK_SHAPE)] * 6,
            out_specs=[whole(*BLOCK_SHAPE)] * 2,
        ),
        out_shape=[shape, shape],
        compiler_params=params(24),
        cost_estimate=cost(4 * TOK_DEV * D, 16 * TOK_DEV * D),
        name="pass_on",
    )(place, near_up, far_up, near_down, far_down, below, above)


def reduce_steps(parts, work):
    place = lax.axis_index("z").reshape(1).astype(jnp.int32)
    own, near = {}, {}
    last = None
    for s in (3, 2, 1, 0):
        own[s], other = parts(s, [] if last is None else [last])
        near[s] = swap(other, "core")
        last = own[s]
    crossed = {}
    for s in (3, 2, 1, 0):
        last = sum_blocks([(own[s], 1), (near[s], 1)], [last])
        crossed[s] = swap(last, "x")
    last = work(0, last)
    low = {}
    low[3] = last = sum_blocks([(own[3], 0), (near[3], 0), crossed[3]], [last])
    up3 = shift(low[3], [(0, 1)])
    down3 = shift(low[3], [(3, 2)])
    last = work(1, last)
    low[2] = last = sum_blocks([(own[2], 0), (near[2], 0), crossed[2]], [last])
    up2, down2 = pass_on(place, low[2], low[3], low[2], low[3], up3, down3)
    last = work(2, up2)
    up2 = shift(up2, [(0, 1), (1, 2)])
    down2 = shift(down2, [(3, 2), (2, 1)])
    low[1] = last = sum_blocks([(own[1], 0), (near[1], 0), crossed[1]], [last])
    up1, down1 = pass_on(place, low[1], low[2], low[1], low[1], up2, down2)
    last = work(3, up1)
    up1 = shift(up1, [(0, 1), (1, 2), (2, 3)])
    down1 = shift(down1, [(3, 2), (2, 1), (1, 0)])
    return sum_blocks([(own[0], 0), (near[0], 0), crossed[0], up1, down1], [last], F32)


def expert_slots(routes_all, first, local):
    rows = routes_all.shape[0]
    ids = first + jnp.arange(local, dtype=jnp.int32)
    named = jnp.any(routes_all[None, :, :] == ids[:, None, None], -1).reshape(
        local, rows // TOK_DEV, TOK_DEV
    )
    places = jnp.arange(TOK_DEV, dtype=jnp.int32)
    upto = (places[:, None] <= places[None, :]).astype(BF16)
    rank = jnp.einsum(
        "ebt,ts->ebs", named.astype(BF16), upto, preferred_element_type=F32
    ).astype(jnp.int32)
    base = (jnp.arange(rows // TOK_DEV, dtype=jnp.int32) % 2) * CAP
    slots = jnp.where(named, rank - 1 + base[None, :, None], -1)
    return jnp.transpose(slots, (1, 0, 2))


def fast_shards(
    tokens, w_query, w_key, w_value, w_output, w_router, attn_gain, query_gain, key_gain,
    moe_gain, w_gate, w_up, w_down, routes, cotangent,
):
    group = lax.axis_index("grp")
    place = lax.axis_index(EP)
    members = lax.axis_size(EP)
    seq = TOK_DEV * members
    local = w_gate.shape[0]
    wide = w_query.shape[0]
    first = (place * local).reshape(1).astype(jnp.int32)

    core = lax.axis_index("core").astype(jnp.int32)
    chips = chip_places()
    small = jnp.concatenate(
        [
            w_router,
            routes.reshape(-1, EXPERTS).astype(BF16),
            jnp.stack([attn_gain, query_gain, key_gain, moe_gain]),
            jnp.zeros((12, EXPERTS), BF16),
        ],
        0,
    ).reshape(16, 3 * HD)
    columns = jnp.stack([w_query, w_key, w_value], 1).reshape(wide, 3, HEADS, HD)
    columns = jnp.transpose(columns, (2, 0, 1, 3)).reshape(HEADS, wide, 3 * HD)
    columns = jnp.concatenate([columns, jnp.broadcast_to(small, (HEADS,) + small.shape)], 1)
    mine = lax.all_to_all(columns, EP, 0, 0, tiled=True)
    other = swap(mine, "grp")
    both = jnp.where(group == 0, jnp.stack([mine, other]), jnp.stack([other, mine]))
    w_head = both[:, :, :wide].reshape(D, 3 * HD)
    small_all = both[:, :, wide:].reshape(2 * members, -1, EXPERTS)
    route_rows = TOK_DEV * TOPK // EXPERTS
    router_full = small_all[:, :wide].reshape(D, EXPERTS)
    routes_all = (
        small_all[:, wide : wide + route_rows].reshape(2, seq, TOPK).astype(jnp.int32)
    )
    gains = jnp.transpose(
        small_all[:, wide + route_rows : wide + route_rows + 4], (1, 0, 2)
    ).reshape(4, D).astype(F32)
    router_wide = jnp.concatenate([router_full, jnp.zeros((D, HD - EXPERTS), BF16)], 1)
    head_gains = lax.dynamic_slice(gains, (0, place * HD), (4, HD))
    gain_q, gain_k = head_gains[1:2], head_gains[2:3]
    attn_row, moe_row = gains[0:1], gains[3:4]

    out_pair = jnp.where(
        group == 0,
        jnp.concatenate([w_output, swap(w_output, "grp")]),
        jnp.concatenate([swap(w_output, "grp"), w_output]),
    )
    output_full = jnp.transpose(
        gather_rows(out_pair).reshape(members, 2, wide, D), (1, 0, 2, 3)
    ).reshape(D, D)
    cot_own = gather_rows(cotangent)
    cot_other = gather_rows(swap(cotangent, "grp"))

    slots_own = expert_slots(lax.dynamic_index_in_dim(routes_all, group, 0, False), first, local)
    slots_other = expert_slots(
        lax.dynamic_index_in_dim(routes_all, 1 - group, 0, False), first, local
    )

    positions = jnp.arange(seq, dtype=jnp.int32)
    half_dim = HD // 2
    frequency = jnp.exp(-(2.0 * jnp.arange(half_dim, dtype=F32) / HD) * math.log(10000.0))
    angles = positions.astype(F32)[:, None] * frequency[None, :]
    cosine = jnp.concatenate([jnp.cos(angles)] * 2, 1)
    sine = jnp.concatenate([-jnp.sin(angles), jnp.sin(angles)], 1)

    kept = [None]

    def use_tokens(s, r, own, far, after):
        spot = jnp.stack([chips[s][r], core])
        kept[0] = project(spot, own, far, w_head, attn_row, kept[0], seq, after)
        return kept[0][2]

    def idle(_, last):
        return last

    gather_steps(tokens, use_tokens, idle)
    normed_all, qkv, stat = kept[0]
    stat = total_over_ep(stat)
    q16, k16, v16, attn_float, att_head, lse = attend(qkv, stat, gain_q, gain_k, cosine, sine)
    attended = lax.all_to_all(att_head.reshape(members, TOK_DEV, HD), EP, 0, 0, tiled=True)
    attended = jnp.transpose(attended, (1, 0, 2)).reshape(TOK_DEV, D)
    inputs = tokens.astype(F32)
    branch_attn = nn(attended, output_full)
    hidden = inputs + branch_attn
    moe_inv = inv_rms(hidden)
    mixed = (hidden * moe_inv * moe_row).astype(BF16)

    early = {}

    def early_work(step, last):
        if step == 1:
            early["g"] = plain_dispatch(cot_own, slots_own, [last])
            return early["g"]
        if step == 2:
            early["slope"] = slopes(early["g"], w_down, [last])
            return early["slope"]
        return last

    rows = [None]

    def use_mixed(s, r, own, far, after):
        spot = jnp.stack([chips[s][r], core, place.astype(jnp.int32)])
        rows[0] = dispatch(spot, own, far, slots_own, rows[0], after)
        return rows[0][0]

    gather_steps(mixed, use_mixed, early_work)
    x_own, mixed_columns = rows[0]
    mixed_other = gather_rows(swap(mixed, "grp"))
    g_own, slope_own = early["g"], early["slope"]
    route_probs = jax.nn.softmax(nn(mixed, router_full), -1)
    act_a, dg_a, du_a, gate_a, z_rows, dp_slots = experts(
        first, x_own, slope_own, w_gate, w_up, router_wide, True
    )

    def place_of(s):
        return jnp.stack([chips[s][0], chips[s][1], core])

    late = {}

    def late_work(step, last):
        if step == 0:
            dp_part = spread_back(dp_slots, slots_own, [last])
            late["dp"] = lax.all_to_all(dp_part, EP, 0, 0, tiled=True).reshape(EXPERTS, TOK_DEV).T
            return dp_part
        if step == 1:
            late["y"] = down(act_a, gate_a, w_down, [last])
            return late["y"]
        if step == 2:
            return last
        late["g"] = plain_dispatch(cot_other, slots_other, [last])
        late["slope"] = slopes(late["g"], w_down, [late["g"]])
        return late["slope"]

    grad_mixed = reduce_steps(
        lambda s, after: combine_part(place_of(s), z_rows, slots_own, after), late_work
    )
    dp = late["dp"]
    branch_part = combine(late["y"], slots_own)
    branch_moe = reduce_rows(branch_part).astype(F32)
    output = (hidden + branch_moe).astype(BF16)

    grad_logits = (
        route_probs * (dp - jnp.sum(route_probs * dp, -1, keepdims=True))
    ).astype(BF16)
    grad_mixed = grad_mixed + nt(grad_logits, router_full)
    grad_hid_norm, moe_gain_part = norm_back(grad_mixed, hidden, moe_inv, moe_row)
    grad_hidden = cotangent.astype(F32) + grad_hid_norm
    grad_branch = grad_hidden.astype(BF16)
    grad_out = nt(grad_branch, output_full).astype(BF16).reshape(TOK_DEV, HEADS, HD)
    grad_out = jnp.transpose(grad_out, (1, 0, 2))
    grad_att_head = lax.all_to_all(grad_out, EP, 0, 0, tiled=True).reshape(seq, HD)

    wide_branch = jnp.concatenate(
        [grad_branch, grad_logits, jnp.zeros((TOK_DEV, HD - EXPERTS), BF16)], 1
    )
    branch_all = gather_rows(wide_branch)
    dnq, dnk, dv16, means, gain_parts = attend_back(
        q16, k16, v16, grad_att_head, attn_float, lse, qkv, stat, gain_q, gain_k, cosine, sine
    )
    means = total_over_ep(means)
    qkv_grads = finish(dnq, dnk, dv16, qkv, stat, means, gain_q, gain_k)
    half = group.reshape(1).astype(jnp.int32)

    def last_work(step, last):
        if step == 0:
            late["dw"] = dw_product(normed_all, qkv_grads, [last])
            return late["dw"]
        if step == 1:
            late["x"] = plain_dispatch(mixed_other, slots_other, [last])
            return late["x"]
        if step == 2:
            late["mid"] = experts(
                first, late["x"], late["slope"], w_gate, w_up, router_wide, False, [last]
            )
            return late["mid"][3]
        act_b, dg_b, du_b, gate_b = late["mid"]
        late["grads"] = weight_grads(
            half, (x_own, late["x"]), (dg_a, dg_b), (du_a, du_b), (act_a, act_b),
            (g_own, late["g"]), (gate_a, gate_b), [last],
        )
        return late["grads"][0]

    grad_normed = reduce_steps(
        lambda s, after: normed_part(place_of(s), qkv_grads, w_head, after), last_work
    )
    dw_head = late["dw"]
    gate_grad, up_grad, down_grad = late["grads"]
    attn_inv = inv_rms(inputs)
    scaled = grad_normed * attn_row
    grad_tok = attn_inv * (
        scaled - inputs * attn_inv * attn_inv * jnp.mean(scaled * inputs, -1, keepdims=True)
    )
    tokens_grad = (grad_hidden + grad_tok).astype(BF16)

    dw_keep = lax.dynamic_slice_in_dim(dw_head, group * (D // 2), D // 2, 0)
    dw_send = lax.dynamic_slice_in_dim(dw_head, (1 - group) * (D // 2), D // 2, 0)
    dw_half = (dw_keep + swap(dw_send.astype(BF16), "grp").astype(F32)).astype(BF16)
    gain_parts = gain_parts + swap(gain_parts, "grp")
    sums = jnp.stack(
        [jnp.sum(inputs * inputs), jnp.sum(branch_attn * branch_attn), jnp.sum(branch_moe * branch_moe)]
    )
    extra = jnp.concatenate(
        [gain_parts.reshape(1, 2 * HD), sums[None, :], jnp.zeros((1, HD - 3), F32)], 1
    )
    high = extra.astype(BF16)
    low = (extra - high.astype(F32)).astype(BF16)
    moe_high = moe_gain_part.astype(BF16)
    moe_low = (moe_gain_part - moe_high.astype(F32)).astype(BF16)
    moe_rows = jnp.concatenate(
        [moe_high.reshape(members, 1, HD), moe_low.reshape(members, 1, HD),
         jnp.zeros((members, 1, HD), BF16)], 2,
    )
    extra = jnp.broadcast_to(jnp.stack([high[0], low[0]])[None], (members, 2, 3 * HD))
    extra = jnp.concatenate([extra, moe_rows, jnp.zeros((members, 13, 3 * HD), BF16)], 1)
    payload = jnp.concatenate(
        [
            dw_half.reshape(members, wide, 3 * HD),
            extra,
        ],
        1,
    )
    arrived = lax.all_to_all(payload, EP, 0, 0, tiled=True).astype(F32)
    dense = jnp.transpose(
        arrived[:, :wide].reshape(HEADS, wide, 3, HD), (2, 1, 0, 3)
    ).reshape(3, wide, D)
    extras = arrived[:, wide] + arrived[:, wide + 1]
    rms_stats = jnp.sqrt(jnp.sum(extras[:, 2 * HD : 2 * HD + 3], 0) / (seq * D)).reshape(1, 3)
    flat = group * members + place
    head_row = lax.dynamic_slice(
        extras[:, : 2 * HD].reshape(HEADS, 2, HD // wide, wide),
        (flat // (HD // wide), 0, flat % (HD // wide), 0),
        (1, 2, 1, wide),
    ).reshape(2, wide)
    attn_gain_grad = (
        jnp.sum(
            w_query.astype(F32) * dense[0]
            + w_key.astype(F32) * dense[1]
            + w_value.astype(F32) * dense[2],
            -1,
        )
        / attn_gain.astype(F32)
    )

    moe_sums = jnp.sum(arrived[:, wide + 2], 0)
    moe_part = (moe_sums[:HD] + moe_sums[HD : 2 * HD]).reshape(2, wide, 1)
    out_part = tn(att_head, branch_all[:, :D]).reshape(2, wide, D)
    router_part = tn(mixed_columns, branch_all[:, D : D + EXPERTS]).reshape(2, wide, EXPERTS)
    out_part = jnp.concatenate(
        [out_part, router_part, moe_part, jnp.zeros((2, wide, HD - EXPERTS - 1), F32)], 2
    )
    out_keep = lax.dynamic_index_in_dim(out_part, group, 0, False)
    out_send = lax.dynamic_index_in_dim(out_part, 1 - group, 0, False).astype(BF16)
    out_sum = (out_keep + swap(out_send, "grp").astype(F32)).astype(BF16)
    owners = [(g * members + e, 2 * e + g) for g in range(2) for e in range(members)]
    owned = lax.ppermute(out_sum, ALL, owners).astype(F32)
    output_grad = owned[:, :D]
    router_grad, moe_gain_grad = owned[:, D : D + EXPERTS], owned[:, D + EXPERTS]

    return (
        output, tokens_grad, dense[0], dense[1], dense[2], output_grad, router_grad,
        attn_gain_grad, head_row[0], head_row[1], moe_gain_grad, gate_grad, up_grad, down_grad,
        rms_stats,
    )


def fast_solution(mesh, sides):
    inner = jax.sharding.Mesh(mesh.devices.reshape((2,) + sides), ALL)
    rows = P(ALL, None)
    expert = P(EP, None, None)
    return jax.shard_map(
        fast_shards,
        mesh=inner,
        in_specs=(rows,) * 6 + (P(ALL),) * 4 + (expert,) * 3 + (rows,) * 2,
        out_specs=(rows,) * 7 + (P(ALL),) * 4 + (P(EP, "grp", None),) * 3 + (P("grp", None),),
        check_vma=False,
    )


def solution(mesh):
    sides = SIDES.get(mesh.shape["ep"])
    if sides is not None and mesh.shape["grp"] == 2:
        return fast_solution(mesh, sides)
    return jax.shard_map(
        shards,
        mesh=mesh,
        in_specs=(
            P(("grp", "ep"), None),
            P(("grp", "ep"), None),
            P(("grp", "ep"), None),
            P(("grp", "ep"), None),
            P(("grp", "ep"), None),
            P(("grp", "ep"), None),
            P(("grp", "ep")),
            P(("grp", "ep")),
            P(("grp", "ep")),
            P(("grp", "ep")),
            P("ep", None, None),
            P("ep", None, None),
            P("ep", None, None),
            P(("grp", "ep"), None),
            P(("grp", "ep"), None),
        ),
        out_specs=(
            P(("grp", "ep"), None),
            P(("grp", "ep"), None),
            P(("grp", "ep"), None),
            P(("grp", "ep"), None),
            P(("grp", "ep"), None),
            P(("grp", "ep"), None),
            P(("grp", "ep"), None),
            P(("grp", "ep")),
            P(("grp", "ep")),
            P(("grp", "ep")),
            P(("grp", "ep")),
            P("ep", "grp", None),
            P("ep", "grp", None),
            P("ep", "grp", None),
            P("grp", None),
        ),
        check_vma=False,
    )
```

```python
import functools
import math

import jax
import jax.numpy as jnp
from jax import lax
from jax.experimental import pallas as pl
from jax.experimental.pallas import tpu as pltpu
from jax.sharding import PartitionSpec as P

D = 2048
HEADS = 16
HD = 128
EXPERTS = 64
TOPK = 8
TOK_DEV = 128
BLOCK = 256
CAP = 24


EPSILON = 1e-05
NEG_FILL = -1e30


def inv_rms(values):
    return lax.rsqrt(jnp.mean(values * values, -1, keepdims=True) + EPSILON)


def norm_back(grad_out, values, inverse, gain_vec):
    scaled = grad_out * gain_vec
    grad_in = inverse * (
        scaled - values * inverse * inverse * jnp.mean(scaled * values, -1, keepdims=True)
    )
    return (grad_in, jnp.sum(grad_out * values * inverse, 0))


def rope_tables(positions):
    half_dim = HD // 2
    frequency = jnp.exp(-(2.0 * jnp.arange(half_dim, dtype=jnp.float32) / HD) * math.log(10000.0))
    angles = positions.astype(jnp.float32)[:, None] * frequency[None, :]
    return (jnp.cos(angles)[:, None, :], jnp.sin(angles)[:, None, :])


def rotate(values, cosine, sine_tab):
    half_dim = HD // 2
    first_half = values[..., :half_dim]
    second_half = values[..., half_dim:]
    return jnp.concatenate(
        [
            first_half * cosine - second_half * sine_tab,
            second_half * cosine + first_half * sine_tab,
        ],
        -1,
    )


def rotate_back(grad_in, cosine, sine_tab):
    half_dim = HD // 2
    first_half = grad_in[..., :half_dim]
    second_half = grad_in[..., half_dim:]
    return jnp.concatenate(
        [
            first_half * cosine + second_half * sine_tab,
            second_half * cosine - first_half * sine_tab,
        ],
        -1,
    )


def fold_keys(state_now, key_piece, queries, query_pos):
    keys_in, values_in = key_piece
    piece_rows = keys_in.shape[0]
    blk_rows = math.gcd(piece_rows, 1024)
    key_blocks = keys_in.reshape(piece_rows // blk_rows, blk_rows, HEADS, HD)
    value_blocks = values_in.reshape(piece_rows // blk_rows, blk_rows, HEADS, HD)
    last_block = query_pos[-1] // BLOCK

    def block_step(state_in, block_items):
        key_blk, value_blk, block_num = block_items
        key_start = block_num * blk_rows

        def block_compute(state_cur):
            top_now, total_now, acc_now = state_cur
            key_pos = key_start + jnp.arange(blk_rows, dtype=jnp.int32)
            scores = jnp.einsum(
                "qhd,khd->hqk", queries, key_blk, preferred_element_type=jnp.float32
            ) * HD ** (-0.5)
            allowed = (key_pos // BLOCK)[None, None, :] <= (query_pos // BLOCK)[None, :, None]
            scores = jnp.where(allowed, scores, NEG_FILL)
            top_new = jnp.maximum(top_now, jnp.max(scores, -1, keepdims=True))
            weights = jnp.where(allowed, jnp.exp(scores - top_new), 0.0)
            rescale = jnp.exp(top_now - top_new)
            total_new = total_now * rescale + jnp.sum(weights, -1, keepdims=True)
            acc_new = acc_now * jnp.transpose(rescale, (1, 0, 2)) + jnp.einsum(
                "hqk,khd->qhd",
                weights.astype(jnp.bfloat16),
                value_blk,
                preferred_element_type=jnp.float32,
            )
            return (top_new, total_new, acc_new)

        def block_passing(state_cur):
            return state_cur

        return (
            lax.cond(key_start // BLOCK <= last_block, block_compute, block_passing, state_in),
            None,
        )

    state_out, unused = lax.scan(
        block_step,
        state_now,
        (key_blocks, value_blocks, jnp.arange(piece_rows // blk_rows, dtype=jnp.int32)),
    )
    return state_out


def score_grads(queries, grad_attended, row_delta, log_sum, query_pos, key_blk, value_blk, key_pos):
    scores = jnp.einsum(
        "qhd,khd->hqk", queries, key_blk, preferred_element_type=jnp.float32
    ) * HD ** (-0.5)
    allowed = (key_pos // BLOCK)[None, None, :] <= (query_pos // BLOCK)[None, :, None]
    prob_vals = jnp.where(allowed, jnp.exp(scores - log_sum), 0.0)
    grad_probs = jnp.einsum(
        "qhd,khd->hqk", grad_attended, value_blk, preferred_element_type=jnp.float32
    )
    grad_scores = (prob_vals * (grad_probs - row_delta)).astype(jnp.bfloat16)
    return (prob_vals, grad_scores)


def shards(
    tokens,
    w_query,
    w_key,
    w_value,
    w_output,
    w_router,
    attn_gain,
    query_gain,
    key_gain,
    moe_gain,
    w_gate,
    w_up,
    w_down,
    routes,
    cotangent,
):
    gathered = (
        lax.all_gather(w_query, ("grp", "ep"), axis=0, tiled=True),
        lax.all_gather(w_key, ("grp", "ep"), axis=0, tiled=True),
        lax.all_gather(w_value, ("grp", "ep"), axis=0, tiled=True),
        lax.all_gather(w_output, ("grp", "ep"), axis=0, tiled=True),
        lax.all_gather(w_router, ("grp", "ep"), axis=0, tiled=True),
        lax.all_gather(attn_gain, ("grp", "ep"), axis=0, tiled=True),
        lax.all_gather(query_gain, ("grp", "ep"), axis=0, tiled=True),
        lax.all_gather(key_gain, ("grp", "ep"), axis=0, tiled=True),
        lax.all_gather(moe_gain, ("grp", "ep"), axis=0, tiled=True),
    )
    query_full, key_full, value_full, output_full, router_full = (
        gathered[0],
        gathered[1],
        gathered[2],
        gathered[3],
        gathered[4],
    )
    attn_scale = gathered[5].astype(jnp.float32)
    query_scale = gathered[6].astype(jnp.float32)
    key_scale = gathered[7].astype(jnp.float32)
    moe_scale = gathered[8].astype(jnp.float32)
    ep_count = lax.axis_size("ep")
    exp_local = EXPERTS // ep_count
    score_scale = HD ** (-0.5)
    inputs = tokens.astype(jnp.float32)
    positions = lax.axis_index("ep") * TOK_DEV + jnp.arange(TOK_DEV, dtype=jnp.int32)
    cosine, sine_tab = rope_tables(positions)
    attn_inv = inv_rms(inputs)
    normed = (inputs * attn_inv * attn_scale).astype(jnp.bfloat16)
    query_raw = jnp.dot(normed, query_full, preferred_element_type=jnp.float32)
    key_raw = jnp.dot(normed, key_full, preferred_element_type=jnp.float32)
    values16 = jnp.dot(normed, value_full, preferred_element_type=jnp.float32).astype(jnp.bfloat16)
    query_inv = inv_rms(query_raw)
    queries16 = rotate(
        (query_raw * query_inv * query_scale).reshape(TOK_DEV, HEADS, HD), cosine, sine_tab
    ).astype(jnp.bfloat16)
    key_inv = inv_rms(key_raw)
    keys16 = (
        rotate((key_raw * key_inv * key_scale).reshape(TOK_DEV, HEADS, HD), cosine, sine_tab)
        .astype(jnp.bfloat16)
        .reshape(TOK_DEV, D)
    )
    start_state = (
        jnp.full((HEADS, TOK_DEV, 1), NEG_FILL, jnp.float32),
        jnp.zeros((HEADS, TOK_DEV, 1), jnp.float32),
        jnp.zeros((TOK_DEV, HEADS, HD), jnp.float32),
    )
    folded = fold_keys(
        start_state,
        (
            lax.all_gather(keys16, "ep", axis=0, tiled=True),
            lax.all_gather(values16, "ep", axis=0, tiled=True),
        ),
        queries16,
        positions,
    )
    top_score, total_weight, acc_sum = folded
    log_sum = top_score + jnp.log(total_weight)
    attn_float = acc_sum / jnp.transpose(total_weight, (1, 0, 2))
    attended16 = attn_float.reshape(TOK_DEV, D).astype(jnp.bfloat16)
    branch_attn = jnp.dot(attended16, output_full, preferred_element_type=jnp.float32)
    hidden = inputs + branch_attn
    moe_inv = inv_rms(hidden)
    mixed_in = (hidden * moe_inv * moe_scale).astype(jnp.bfloat16)
    logits = jnp.dot(mixed_in, router_full, preferred_element_type=jnp.float32)
    route_probs = jax.nn.softmax(logits, -1)
    chosen = (routes[:, :, None] == jnp.arange(EXPERTS, dtype=jnp.int32)[None, None, :]).astype(
        jnp.float32
    )
    gate_vals = jnp.sum(chosen * route_probs[:, None, :], -1)
    pair_expert = routes.reshape(-1)
    one_hot = (pair_expert[:, None] == jnp.arange(EXPERTS, dtype=jnp.int32)[None, :]).astype(
        jnp.int32
    )
    pair_rank = jnp.sum(jnp.cumsum(one_hot, 0) * one_hot, 1) - 1
    slot_index = pair_expert * CAP + pair_rank
    pair_token = jnp.arange(TOK_DEV * TOPK, dtype=jnp.int32) // TOPK
    send_rows = jnp.zeros((EXPERTS * CAP, D), jnp.bfloat16).at[slot_index].set(mixed_in[pair_token])
    send_rows = send_rows.reshape(ep_count, exp_local, CAP, D)
    received = lax.all_to_all(send_rows, "ep", split_axis=0, concat_axis=0, tiled=True)
    gate_pre = jnp.einsum("secd,edf->secf", received, w_gate, preferred_element_type=jnp.float32)
    up_pre = jnp.einsum("secd,edf->secf", received, w_up, preferred_element_type=jnp.float32)
    activation = (jax.nn.silu(gate_pre) * up_pre).astype(jnp.bfloat16)
    expert_out = jnp.einsum(
        "secf,efd->secd", activation, w_down, preferred_element_type=jnp.float32
    ).astype(jnp.bfloat16)
    expert_out, gate_pre, up_pre, activation, received = (
        expert_out,
        gate_pre,
        up_pre,
        activation,
        received,
    )
    returned = lax.all_to_all(expert_out, "ep", split_axis=0, concat_axis=0, tiled=True).reshape(
        EXPERTS * CAP, D
    )
    pair_out = returned[slot_index].astype(jnp.float32).reshape(TOK_DEV, TOPK, D)
    branch_moe = jnp.sum(gate_vals[:, :, None] * pair_out, 1)
    output = (hidden + branch_moe).astype(jnp.bfloat16)
    local_sums = jnp.stack(
        [
            jnp.sum(inputs * inputs),
            jnp.sum(branch_attn * branch_attn),
            jnp.sum(branch_moe * branch_moe),
        ]
    )
    seq_sums = lax.psum(local_sums, "ep")
    rms_stats = jnp.sqrt(seq_sums / (TOK_DEV * ep_count * D)).reshape(1, 3)
    grad_out = cotangent.astype(jnp.float32)
    grad_gates = jnp.sum(pair_out * grad_out[:, None, :], -1)
    grad_pairs = (
        (gate_vals[:, :, None] * grad_out[:, None, :])
        .astype(jnp.bfloat16)
        .reshape(TOK_DEV * TOPK, D)
    )
    send_grads = jnp.zeros((EXPERTS * CAP, D), jnp.bfloat16).at[slot_index].set(grad_pairs)
    send_grads = send_grads.reshape(ep_count, exp_local, CAP, D)
    grad_received = lax.all_to_all(send_grads, "ep", split_axis=0, concat_axis=0, tiled=True)
    grad_activation = jnp.einsum(
        "secd,efd->secf", grad_received, w_down, preferred_element_type=jnp.float32
    )
    grad_down = jnp.einsum(
        "secf,secd->efd", activation, grad_received, preferred_element_type=jnp.float32
    )
    sig_gate = jax.nn.sigmoid(gate_pre)
    grad_gate_pre = (
        grad_activation * up_pre * sig_gate * (1.0 + gate_pre * (1.0 - sig_gate))
    ).astype(jnp.bfloat16)
    grad_up_pre = (grad_activation * gate_pre * sig_gate).astype(jnp.bfloat16)
    grad_gate_w = jnp.einsum(
        "secd,secf->edf", received, grad_gate_pre, preferred_element_type=jnp.float32
    )
    grad_up_w = jnp.einsum(
        "secd,secf->edf", received, grad_up_pre, preferred_element_type=jnp.float32
    )
    grad_inputs = (
        jnp.einsum("secf,edf->secd", grad_gate_pre, w_gate, preferred_element_type=jnp.float32)
        + jnp.einsum("secf,edf->secd", grad_up_pre, w_up, preferred_element_type=jnp.float32)
    ).astype(jnp.bfloat16)
    grad_back = lax.all_to_all(grad_inputs, "ep", split_axis=0, concat_axis=0, tiled=True).reshape(
        EXPERTS * CAP, D
    )
    grad_mixed = jnp.sum(grad_back[slot_index].astype(jnp.float32).reshape(TOK_DEV, TOPK, D), 1)
    spread = jnp.sum(chosen * grad_gates[:, :, None], 1)
    grad_logits = (
        route_probs * (spread - jnp.sum(route_probs * spread, -1, keepdims=True))
    ).astype(jnp.bfloat16)
    router_grad = jnp.einsum("td,te->de", mixed_in, grad_logits, preferred_element_type=jnp.float32)
    grad_mixed = grad_mixed + jnp.einsum(
        "te,de->td", grad_logits, router_full, preferred_element_type=jnp.float32
    )
    grad_hid_norm, moe_gain_grad = norm_back(grad_mixed, hidden, moe_inv, moe_scale)
    grad_hidden = grad_out + grad_hid_norm
    grad_branch = grad_hidden.astype(jnp.bfloat16)
    output_grad = jnp.einsum(
        "td,tf->df", attended16, grad_branch, preferred_element_type=jnp.float32
    )
    grad_attended = jnp.einsum(
        "tf,df->td", grad_branch, output_full, preferred_element_type=jnp.float32
    ).astype(jnp.bfloat16)
    grad_attended = grad_attended.reshape(TOK_DEV, HEADS, HD)
    row_delta = jnp.transpose(jnp.sum(grad_attended.astype(jnp.float32) * attn_float, -1), (1, 0))[
        :, :, None
    ]
    gathered_keys, gathered_values = (
        lax.all_gather(keys16, "ep", axis=0, tiled=True),
        lax.all_gather(values16, "ep", axis=0, tiled=True),
    )
    total_rows = gathered_keys.shape[0]
    blk_rows = math.gcd(total_rows, 1024)
    last_query_block = positions[-1] // BLOCK

    def query_step(grad_now, block_num):
        begin_row = block_num * blk_rows

        def query_compute(grad_cur):
            key_blk = lax.dynamic_slice_in_dim(gathered_keys, begin_row, blk_rows, 0).reshape(
                blk_rows, HEADS, HD
            )
            value_blk = lax.dynamic_slice_in_dim(gathered_values, begin_row, blk_rows, 0).reshape(
                blk_rows, HEADS, HD
            )
            key_pos = begin_row + jnp.arange(blk_rows, dtype=jnp.int32)
            prob_vals, grad_scores = score_grads(
                queries16, grad_attended, row_delta, log_sum, positions, key_blk, value_blk, key_pos
            )
            return (
                grad_cur
                + jnp.einsum(
                    "hqk,khd->qhd", grad_scores, key_blk, preferred_element_type=jnp.float32
                )
                * score_scale
            )

        def query_passing(grad_cur):
            return grad_cur

        return (
            lax.cond(
                begin_row // BLOCK <= last_query_block, query_compute, query_passing, grad_now
            ),
            None,
        )

    grad_queries, unused = lax.scan(
        query_step,
        jnp.zeros((TOK_DEV, HEADS, HD), jnp.float32),
        jnp.arange(total_rows // blk_rows, dtype=jnp.int32),
    )
    all_queries, all_grad_att = (
        lax.all_gather(queries16, "ep", axis=0, tiled=True),
        lax.all_gather(grad_attended, "ep", axis=0, tiled=True),
    )
    all_delta, all_log_sum = (
        lax.all_gather(row_delta, "ep", axis=1, tiled=True),
        lax.all_gather(log_sum, "ep", axis=1, tiled=True),
    )
    query_rows = all_queries.shape[0]
    query_blk_rows = math.gcd(query_rows, 1024)
    own_keys = keys16.reshape(TOK_DEV, HEADS, HD)
    own_values = values16.reshape(TOK_DEV, HEADS, HD)
    first_key_block = positions[0] // BLOCK

    def key_step(grads_now, block_num):
        begin_row = block_num * query_blk_rows

        def key_compute(grads_cur):
            query_blk = lax.dynamic_slice_in_dim(all_queries, begin_row, query_blk_rows, 0)
            grad_att_blk = lax.dynamic_slice_in_dim(all_grad_att, begin_row, query_blk_rows, 0)
            delta_blk = lax.dynamic_slice_in_dim(all_delta, begin_row, query_blk_rows, 1)
            log_blk = lax.dynamic_slice_in_dim(all_log_sum, begin_row, query_blk_rows, 1)
            query_pos = begin_row + jnp.arange(query_blk_rows, dtype=jnp.int32)
            prob_vals, grad_scores = score_grads(
                query_blk,
                grad_att_blk,
                delta_blk,
                log_blk,
                query_pos,
                own_keys,
                own_values,
                positions,
            )
            key_part = (
                jnp.einsum(
                    "hqk,qhd->khd", grad_scores, query_blk, preferred_element_type=jnp.float32
                )
                * score_scale
            )
            value_part = jnp.einsum(
                "hqk,qhd->khd",
                prob_vals.astype(jnp.bfloat16),
                grad_att_blk,
                preferred_element_type=jnp.float32,
            )
            return (grads_cur[0] + key_part, grads_cur[1] + value_part)

        def key_passing(grads_cur):
            return grads_cur

        return (
            lax.cond(
                (begin_row + query_blk_rows - 1) // BLOCK >= first_key_block,
                key_compute,
                key_passing,
                grads_now,
            ),
            None,
        )

    key_start = (
        jnp.zeros((TOK_DEV, HEADS, HD), jnp.float32),
        jnp.zeros((TOK_DEV, HEADS, HD), jnp.float32),
    )
    key_value_grads, unused = lax.scan(
        key_step, key_start, jnp.arange(query_rows // query_blk_rows, dtype=jnp.int32)
    )
    grad_keys16 = key_value_grads[0].astype(jnp.bfloat16)
    grad_values16 = key_value_grads[1].reshape(TOK_DEV, D).astype(jnp.bfloat16)
    grad_keys = lax.optimization_barrier(grad_keys16).astype(jnp.float32)
    grad_queries = lax.optimization_barrier(grad_queries.astype(jnp.bfloat16)).astype(jnp.float32)
    grad_query_rot = rotate_back(grad_queries, cosine, sine_tab).reshape(TOK_DEV, D)
    grad_query_raw, query_gain_grad = norm_back(grad_query_rot, query_raw, query_inv, query_scale)
    grad_query16 = grad_query_raw.astype(jnp.bfloat16)
    grad_key_rot = rotate_back(grad_keys, cosine, sine_tab).reshape(TOK_DEV, D)
    grad_key_raw, key_gain_grad = norm_back(grad_key_rot, key_raw, key_inv, key_scale)
    grad_key16 = grad_key_raw.astype(jnp.bfloat16)
    query_grad = jnp.einsum("td,tf->df", normed, grad_query16, preferred_element_type=jnp.float32)
    key_grad = jnp.einsum("td,tf->df", normed, grad_key16, preferred_element_type=jnp.float32)
    value_grad = jnp.einsum("td,tf->df", normed, grad_values16, preferred_element_type=jnp.float32)
    grad_normed = (
        jnp.einsum("tf,df->td", grad_query16, query_full, preferred_element_type=jnp.float32)
        + jnp.einsum("tf,df->td", grad_key16, key_full, preferred_element_type=jnp.float32)
        + jnp.einsum("tf,df->td", grad_values16, value_full, preferred_element_type=jnp.float32)
    )
    grad_tok_norm, attn_gain_grad = norm_back(grad_normed, inputs, attn_inv, attn_scale)
    tokens_grad = (grad_hidden + grad_tok_norm).astype(jnp.bfloat16)
    dense_sums = (
        lax.psum_scatter(query_grad, ("grp", "ep"), scatter_dimension=0, tiled=True),
        lax.psum_scatter(key_grad, ("grp", "ep"), scatter_dimension=0, tiled=True),
        lax.psum_scatter(value_grad, ("grp", "ep"), scatter_dimension=0, tiled=True),
        lax.psum_scatter(output_grad, ("grp", "ep"), scatter_dimension=0, tiled=True),
        lax.psum_scatter(router_grad, ("grp", "ep"), scatter_dimension=0, tiled=True),
        lax.psum_scatter(attn_gain_grad, ("grp", "ep"), scatter_dimension=0, tiled=True),
        lax.psum_scatter(query_gain_grad, ("grp", "ep"), scatter_dimension=0, tiled=True),
        lax.psum_scatter(key_gain_grad, ("grp", "ep"), scatter_dimension=0, tiled=True),
        lax.psum_scatter(moe_gain_grad, ("grp", "ep"), scatter_dimension=0, tiled=True),
    )
    expert_sums = (
        lax.psum_scatter(
            grad_gate_w.astype(jnp.bfloat16), "grp", scatter_dimension=1, tiled=True
        ).astype(jnp.float32),
        lax.psum_scatter(
            grad_up_w.astype(jnp.bfloat16), "grp", scatter_dimension=1, tiled=True
        ).astype(jnp.float32),
        lax.psum_scatter(
            grad_down.astype(jnp.bfloat16), "grp", scatter_dimension=1, tiled=True
        ).astype(jnp.float32),
    )
    return (
        output,
        tokens_grad,
        dense_sums[0],
        dense_sums[1],
        dense_sums[2],
        dense_sums[3],
        dense_sums[4],
        dense_sums[5],
        dense_sums[6],
        dense_sums[7],
        dense_sums[8],
        expert_sums[0],
        expert_sums[1],
        expert_sums[2],
        rms_stats,
    )


F32 = jnp.float32
BF16 = jnp.bfloat16
EP = ("z", "x", "core")
ALL = ("grp", "z", "x", "core")
PAIR = 2 * TOK_DEV
SLOTS = 2 * CAP
COST = 0.1
SIDES = {16: (4, 2, 2)}


def nt(left, right):
    return lax.dot_general(left, right, (((1,), (1,)), ((), ())), preferred_element_type=F32)


def nn(left, right):
    return lax.dot_general(left, right, (((1,), (0,)), ((), ())), preferred_element_type=F32)


def tn(left, right):
    return lax.dot_general(left, right, (((0,), (0,)), ((), ())), preferred_element_type=F32)


def as_row(column):
    return jnp.broadcast_to(column, (column.shape[0], 128)).T[0:1]


def as_column(row):
    return jnp.broadcast_to(row, (128, row.shape[1])).T


def inv_of(sum_row):
    return as_column(lax.rsqrt(sum_row / D + EPSILON))


def params(mebibytes):
    return pltpu.CompilerParams(vmem_limit_bytes=mebibytes * 1024 * 1024)


def cost(flops, moved):
    return pl.CostEstimate(flops=int(flops * COST), bytes_accessed=int(moved * COST), transcendentals=0)


def whole(*dims):
    return pl.BlockSpec(dims, lambda *_: (0,) * len(dims))


class Order:
    marks = []

    @classmethod
    def mark_of(cls, array):
        for known, mark in cls.marks:
            if known is array:
                return mark
        return array


MARK = (8, 128)


def ordered(kernel, after, specs, **settings):
    after = [Order.mark_of(array) for array in after]
    inputs = len(specs["in_specs"])
    prefetch = specs.pop("num_scalar_prefetch", 0)
    extra = len(after)
    single = not isinstance(specs["out_specs"], list)
    outputs = [specs["out_specs"]] if single else specs["out_specs"]
    shapes = settings.pop("out_shape")
    shapes = [shapes] if single else list(shapes)
    last = prefetch + inputs + extra + len(outputs)

    def body(*refs):
        refs[last][...] = jnp.zeros(MARK, F32)
        kernel(*refs[: prefetch + inputs], *refs[prefetch + inputs + extra : last], *refs[last + 1 :])

    specs["in_specs"] = list(specs["in_specs"]) + [pl.BlockSpec(memory_space=pl.ANY)] * extra
    specs["out_specs"] = outputs + [pl.BlockSpec(MARK, lambda *_: (0, 0))]
    call = pl.pallas_call(
        body,
        grid_spec=pltpu.PrefetchScalarGridSpec(num_scalar_prefetch=prefetch, **specs),
        out_shape=shapes + [jax.ShapeDtypeStruct(MARK, F32)],
        **settings,
    )

    def run(*args):
        *results, mark = call(*args, *after)
        Order.marks.extend((result, mark) for result in results)
        return results[0] if single else results

    return run


ANYWHERE = pl.BlockSpec(memory_space=pl.ANY)


def in_hbm(dims, kind):
    return pltpu.HBM(dims, kind)


BLOCK_SHAPE = (TOK_DEV, D)


def project_kernel(place_ref, own_ref, other_ref, w_ref, gain_ref, *refs):
    normed_ref, qkv_ref, stat_ref = refs[-3:]
    core = place_ref[1]
    for side, tok_ref in ((core, own_ref), (1 - core, other_ref)):
        here = pl.ds(pl.multiple_of(side * TOK_DEV, TOK_DEV), TOK_DEV)
        rows = tok_ref[...].astype(F32)
        inverse = lax.rsqrt(jnp.mean(rows * rows, -1, keepdims=True) + EPSILON)
        normed = (rows * inverse * gain_ref[...]).astype(BF16)
        normed_ref[here, :] = normed
        out = nn(normed, w_ref[...])
        qkv_ref[here, :] = out
        for part in range(2):
            piece = out[:, part * HD : (part + 1) * HD]
            stat_ref[part : part + 1, here] = as_row(jnp.sum(piece * piece, -1, keepdims=True))


def project(chip_core, own, other, w_head, gain_row, buffers, seq, after=()):
    kept = [] if buffers is None else list(buffers)
    return ordered(
        project_kernel,
        after,
        dict(
            num_scalar_prefetch=1,
            grid=(1,),
            in_specs=[whole(TOK_DEV, D), whole(TOK_DEV, D), whole(D, 3 * HD), whole(1, D)]
            + [ANYWHERE] * len(kept),
            out_specs=[
                pl.BlockSpec((PAIR, D), lambda i, s: (s[0], 0)),
                pl.BlockSpec((PAIR, 3 * HD), lambda i, s: (s[0], 0)),
                pl.BlockSpec((2, PAIR), lambda i, s: (0, s[0])),
            ],
        ),
        out_shape=[
            in_hbm((seq, D), BF16),
            in_hbm((seq, 3 * HD), F32),
            jax.ShapeDtypeStruct((2, seq), F32),
        ],
        input_output_aliases={5 + i: i for i in range(len(kept))},
        compiler_params=params(24),
        cost_estimate=cost(2 * PAIR * D * 3 * HD, 10 * PAIR * D),
        name="project",
    )(chip_core, own, other, w_head, gain_row, *kept)


def attend_kernel(
    qkv_ref, stat_ref, gq_ref, gk_ref, cos_ref, sin_ref,
    q_ref, k_ref, v_ref, of_ref, att_ref, lse_ref, vt_ref,
):
    blocks = q_ref.shape[0] // BLOCK
    for i in range(blocks):
        rows = slice(i * BLOCK, (i + 1) * BLOCK)
        cosine, sine = cos_ref[rows, :], sin_ref[rows, :]
        for part, gain_ref, out_ref in ((0, gq_ref, q_ref), (1, gk_ref, k_ref)):
            raw = qkv_ref[rows, part * HD : (part + 1) * HD]
            scaled = raw * inv_of(stat_ref[part : part + 1, rows]) * gain_ref[...]
            turned = scaled * cosine + pltpu.roll(scaled, HD // 2, 1) * sine
            out_ref[rows, :] = turned.astype(BF16)
        value = qkv_ref[rows, 2 * HD :]
        v_ref[rows, :] = value.astype(BF16)
        vt_ref[:, rows] = value.T.astype(BF16)
    for i in range(blocks):
        rows = slice(i * BLOCK, (i + 1) * BLOCK)
        reach = (i + 1) * BLOCK
        scores = nt(k_ref[0:reach, :], q_ref[rows, :]) * HD ** (-0.5)
        top = jnp.max(scores, 0, keepdims=True)
        weights = jnp.exp(scores - top)
        total = jnp.sum(weights, 0, keepdims=True)
        probs = (weights * (1.0 / total)).astype(BF16)
        out = nn(vt_ref[:, 0:reach], probs).T
        of_ref[rows, :] = out
        att_ref[rows, :] = out.astype(BF16)
        lse_ref[:, rows] = top + jnp.log(total)


def attend(qkv, stat, gain_q, gain_k, cosine, sine):
    rows = qkv.shape[0]
    shape = lambda kind: jax.ShapeDtypeStruct((rows, HD), kind)
    return ordered(
        attend_kernel,
        (),
        dict(
            grid=(1,),
            in_specs=[
                whole(rows, 3 * HD), whole(2, rows), whole(1, HD), whole(1, HD), whole(rows, HD), whole(rows, HD),
            ],
            out_specs=[whole(rows, HD)] * 5 + [whole(1, rows)],
            scratch_shapes=[pltpu.VMEM((HD, rows), BF16)],
        ),
        out_shape=[shape(BF16), shape(BF16), shape(BF16), shape(F32), shape(BF16),
                   jax.ShapeDtypeStruct((1, rows), F32)],
        compiler_params=params(48),
        cost_estimate=cost(8 * rows * rows * HD, 10 * rows * 384),
        name="attend",
    )(qkv, stat, gain_q, gain_k, cosine, sine)


def attend_back_kernel(
    q_ref, k_ref, v_ref, do_ref, of_ref, lse_ref, qkv_ref, stat_ref, gq_ref, gk_ref,
    cos_ref, sin_ref, dnq_ref, dnk_ref, dv_ref, means_ref, gains_ref, dk_acc, dv_acc,
):
    blocks = q_ref.shape[0] // BLOCK
    scale = HD ** (-0.5)
    dk_acc[...] = jnp.zeros_like(dk_acc)
    dv_acc[...] = jnp.zeros_like(dv_acc)

    def turn_back(grad, rows, part, gain_ref, out_ref):
        grad = grad.astype(BF16).astype(F32)
        grad = grad * cos_ref[rows, :] - pltpu.roll(grad, HD // 2, 1) * sin_ref[rows, :]
        raw = qkv_ref[rows, part * HD : (part + 1) * HD]
        out_ref[rows, :] = grad
        means_ref[part : part + 1, rows] = jnp.sum((grad * gain_ref[...] * raw).T, 0, keepdims=True)
        inverse = inv_of(stat_ref[part : part + 1, rows])
        return jnp.sum(grad * raw * inverse, 0, keepdims=True)

    gain_q = jnp.zeros((1, HD), F32)
    gain_k = jnp.zeros((1, HD), F32)
    for i in range(blocks):
        rows = slice(i * BLOCK, (i + 1) * BLOCK)
        reach = (i + 1) * BLOCK
        queries, grads = q_ref[rows, :], do_ref[rows, :]
        delta = jnp.sum((grads.astype(F32) * of_ref[rows, :]).T, 0, keepdims=True)
        scores = nt(k_ref[0:reach, :], queries) * scale
        probs = jnp.exp(scores - lse_ref[:, rows])
        slopes = nt(v_ref[0:reach, :], grads)
        grad_scores = (probs * (slopes - delta)).astype(BF16)
        dv_acc[0:reach, :] += nn(probs.astype(BF16), grads)
        dk_acc[0:reach, :] += nn(grad_scores, queries)
        gain_q += turn_back(tn(grad_scores, k_ref[0:reach, :]) * scale, rows, 0, gq_ref, dnq_ref)
    for i in range(blocks):
        rows = slice(i * BLOCK, (i + 1) * BLOCK)
        dv_ref[rows, :] = dv_acc[rows, :].astype(BF16)
        gain_k += turn_back(dk_acc[rows, :] * scale, rows, 1, gk_ref, dnk_ref)
    gains_ref[0:1, :] = gain_q
    gains_ref[1:2, :] = gain_k


def attend_back(q, k, v, grad, out, lse, qkv, stat, gain_q, gain_k, cosine, sine, after=()):
    rows = q.shape[0]
    shape = lambda kind: jax.ShapeDtypeStruct((rows, HD), kind)
    return ordered(
        attend_back_kernel,
        after,
        dict(
            grid=(1,),
            in_specs=[whole(rows, HD)] * 5
            + [whole(1, rows), whole(rows, 3 * HD), whole(2, rows), whole(1, HD), whole(1, HD)]
            + [whole(rows, HD)] * 2,
            out_specs=[whole(rows, HD)] * 3 + [whole(2, rows), whole(2, HD)],
            scratch_shapes=[pltpu.VMEM((rows, HD), F32), pltpu.VMEM((rows, HD), F32)],
        ),
        out_shape=[shape(F32), shape(F32), shape(BF16),
                   jax.ShapeDtypeStruct((2, rows), F32), jax.ShapeDtypeStruct((2, HD), F32)],
        compiler_params=params(48),
        cost_estimate=cost(20 * rows * rows * HD, 20 * rows * 384),
        name="attend_back",
    )(q, k, v, grad, out, lse, qkv, stat, gain_q, gain_k, cosine, sine)


def finish_kernel(
    dnq_ref, dnk_ref, dv_ref, qkv_ref, stat_ref, means_ref, gq_ref, gk_ref, out_ref
):
    for part, dn_ref, g_ref in ((0, dnq_ref, gq_ref), (1, dnk_ref, gk_ref)):
        raw = qkv_ref[:, part * HD : (part + 1) * HD]
        inverse = inv_of(stat_ref[part : part + 1, :])
        mean = as_column(means_ref[part : part + 1, :] / D)
        grad = inverse * (dn_ref[...] * g_ref[...] - raw * inverse * inverse * mean)
        out_ref[:, part * HD : (part + 1) * HD] = grad.astype(BF16)
    out_ref[:, 2 * HD :] = dv_ref[...]


def finish(dnq, dnk, dv, qkv, stat, means, gain_q, gain_k, after=()):
    rows = dnq.shape[0]
    head = pl.BlockSpec((PAIR, HD), lambda i: (i, 0))
    line = pl.BlockSpec((2, PAIR), lambda i: (0, i))
    full = pl.BlockSpec((PAIR, 3 * HD), lambda i: (i, 0))
    return ordered(
        finish_kernel,
        after,
        dict(
        grid=(rows // PAIR,),
        in_specs=[head, head, head, full, line, line, whole(1, HD), whole(1, HD)],
        out_specs=full,
        ),
        out_shape=jax.ShapeDtypeStruct((rows, 3 * HD), BF16),
        compiler_params=params(24),
        cost_estimate=cost(20 * rows * 3 * HD, 12 * rows * 3 * HD),
        name="finish",
    )(dnq, dnk, dv, qkv, stat, means, gain_q, gain_k)


def sort_cores(core, first, second, own_ref, other_ref, at):
    at = (0, at)

    @pl.when(core == 0)
    def _():
        own_ref[at] = first
        other_ref[at] = second

    @pl.when(core == 1)
    def _():
        own_ref[at] = second
        other_ref[at] = first


def normed_part_kernel(
    place_ref, a_ref, b_ref, w_ref, ya_ref, yb_ref, a_slot, b_slot, own_ref, other_ref
):
    core = place_ref[4]
    here, there = own_ref.at[:, :, :, D:], other_ref.at[:, :, :, D:]
    for at, (g_ref, y_ref, slot_ref) in enumerate(((a_ref, ya_ref, a_slot), (b_ref, yb_ref, b_slot))):
        out = nt(g_ref[...], w_ref[...]).astype(BF16)
        sort_cores(
            core, out[:TOK_DEV], out[TOK_DEV:], own_ref.at[:, :, :, :D], other_ref.at[:, :, :, :D], at
        )
        first, second = combine_chip(y_ref, slot_ref)
        sort_cores(core, first, second, here, there, at)


def normed_part(place, grads, w_head, y_rows, slots, after=()):
    blocks = jax.ShapeDtypeStruct((2, 2, TOK_DEV, 2 * D), BF16)
    return ordered(
        normed_part_kernel,
        after,
        dict(
            num_scalar_prefetch=1,
            grid=(2,),
            in_specs=[
                pl.BlockSpec((PAIR, 3 * HD), lambda i, s: (s[2 * i], 0)),
                pl.BlockSpec((PAIR, 3 * HD), lambda i, s: (s[2 * i + 1], 0)),
                whole(D, 3 * HD),
            ]
            + chip_specs(y_rows, slots),
            out_specs=[pl.BlockSpec((1, 2, TOK_DEV, 2 * D), lambda i, s: (i, 0, 0, 0))] * 2,
        ),
        out_shape=[blocks, blocks],
        compiler_params=params(32),
        cost_estimate=cost(8 * PAIR * D * 3 * HD, 24 * PAIR * D),
        name="normed_part",
    )(place, grads, grads, w_head, y_rows, y_rows, slots, slots)


def dw_kernel(normed_ref, grad_ref, out_ref):
    @pl.when(pl.program_id(0) == 0)
    def _():
        out_ref[...] = jnp.zeros_like(out_ref)

    out_ref[...] += tn(normed_ref[...], grad_ref[...])


def dw_product(normed, grads, after=()):
    rows = normed.shape[0]
    return ordered(
        dw_kernel,
        after,
        dict(
            grid=(rows // 512,),
            in_specs=[
                pl.BlockSpec((512, D), lambda i: (i, 0)),
                pl.BlockSpec((512, 3 * HD), lambda i: (i, 0)),
            ],
            out_specs=whole(D, 3 * HD),
        ),
        out_shape=jax.ShapeDtypeStruct((D, 3 * HD), F32),
        compiler_params=params(32),
        cost_estimate=cost(2 * rows * D * 3 * HD, 3 * rows * D),
        name="dw_product",
    )(normed, grads)


def picks(slots, dtype):
    shape = (SLOTS, slots.shape[1])
    numbers = lax.broadcasted_iota(jnp.int32, shape, 0)
    return [(numbers == slots[j : j + 1, :]).astype(dtype) for j in range(slots.shape[0])]


def pick_matrix(slots):
    return jnp.concatenate(picks(slots, F32), 0).astype(BF16)


def dispatch_kernel(place_ref, own_ref, other_ref, own_slot, other_slot, *refs):
    out_ref, column_ref, stack_ref = refs[-3:]
    stack_ref[0] = own_ref[...]
    core = place_ref[1]
    lanes = pl.ds(pl.multiple_of(place_ref[2] * HD, HD), HD)
    out = nn(pick_matrix(own_slot[0]), own_ref[...])
    out = (out + nn(pick_matrix(other_slot[0]), other_ref[...])).astype(BF16)
    for j in range(out_ref.shape[0]):
        out_ref[j] = out[j * SLOTS : (j + 1) * SLOTS]
    for side, row_ref in ((core, own_ref), (1 - core, other_ref)):
        column_ref[pl.ds(pl.multiple_of(side * TOK_DEV, TOK_DEV), TOK_DEV), :] = row_ref[:, lanes]


def dispatch(place, own, other, slots, buffers, after=()):
    blocks, local, _ = slots.shape
    kept = [] if buffers is None else list(buffers)
    return ordered(
        dispatch_kernel,
        after,
        dict(
            num_scalar_prefetch=1,
            grid=(1,),
            in_specs=[
                whole(*BLOCK_SHAPE),
                whole(*BLOCK_SHAPE),
                pl.BlockSpec((1, local, TOK_DEV), lambda i, s: (2 * s[0] + s[1], 0, 0)),
                pl.BlockSpec((1, local, TOK_DEV), lambda i, s: (2 * s[0] + 1 - s[1], 0, 0)),
            ]
            + [ANYWHERE] * len(kept),
            out_specs=[
                pl.BlockSpec((local, SLOTS, D), lambda i, s: (0, s[0], 0)),
                pl.BlockSpec((PAIR, HD), lambda i, s: (s[0], 0)),
                pl.BlockSpec((1, TOK_DEV, D), lambda i, s: (s[0], 0, 0)),
            ],
        ),
        out_shape=[
            in_hbm((local, blocks // 2 * SLOTS, D), BF16),
            in_hbm((blocks * TOK_DEV, HD), BF16),
            in_hbm((blocks // 2, TOK_DEV, D), BF16),
        ],
        input_output_aliases={5 + i: i for i in range(len(kept))},
        compiler_params=params(24),
        cost_estimate=cost(2 * PAIR * D * local * SLOTS, 4 * PAIR * D),
        name="dispatch",
    )(place, own, other, slots, slots, *kept)


def stack_kernel(place_ref, row_ref, out_ref):
    out_ref[0] = row_ref[0, 0]


def stack_of_core(core, rows, after=()):
    chips = rows.shape[0]
    return ordered(
        stack_kernel,
        after,
        dict(
            num_scalar_prefetch=1,
            grid=(chips,),
            in_specs=[pl.BlockSpec((1, 1, TOK_DEV, D), lambda i, s: (i, s[0], 0, 0))],
            out_specs=pl.BlockSpec((1, TOK_DEV, D), lambda i, s: (i, 0, 0)),
        ),
        out_shape=in_hbm((chips, TOK_DEV, D), BF16),
        compiler_params=params(16),
        cost_estimate=cost(0, 4 * chips * TOK_DEV * D),
        name="stack_of_core",
    )(core.reshape(1), rows)


def stack_dispatch_kernel(place_ref, own_ref, other_ref, own_slot, other_slot, out_ref):
    out = nn(pick_matrix(own_slot[0]), own_ref[0])
    out = (out + nn(pick_matrix(other_slot[0]), other_ref[0])).astype(BF16)
    for j in range(out_ref.shape[0]):
        out_ref[j] = out[j * SLOTS : (j + 1) * SLOTS]


def stack_dispatch(places, stacks, slots, after=()):
    chips = stacks.shape[1]
    blocks, local, _ = slots.shape
    row_shape = (None, 1, TOK_DEV, D)
    return ordered(
        stack_dispatch_kernel,
        after,
        dict(
            num_scalar_prefetch=1,
            grid=(chips,),
            in_specs=[
                pl.BlockSpec(row_shape, lambda i, s: (2 - 2 * s[chips + 1] + s[chips], i, 0, 0)),
                pl.BlockSpec(row_shape, lambda i, s: (3 - 2 * s[chips + 1] - s[chips], i, 0, 0)),
                pl.BlockSpec((1, local, TOK_DEV), lambda i, s: (2 * s[i] + s[chips], 0, 0)),
                pl.BlockSpec((1, local, TOK_DEV), lambda i, s: (2 * s[i] + 1 - s[chips], 0, 0)),
            ],
            out_specs=pl.BlockSpec((local, SLOTS, D), lambda i, s: (0, s[i], 0)),
        ),
        out_shape=in_hbm((local, blocks // 2 * SLOTS, D), BF16),
        compiler_params=params(24),
        cost_estimate=cost(2 * chips * PAIR * D * local * SLOTS, 4 * chips * PAIR * D),
        name="stack_dispatch",
    )(places, stacks, stacks, slots, slots)


def plain_dispatch_kernel(row_ref, slot_ref, out_ref):
    out = sum(nn(pick_matrix(slot_ref[i]), row_ref[i]) for i in range(2)).astype(BF16)
    for j in range(out_ref.shape[0]):
        out_ref[j] = out[j * SLOTS : (j + 1) * SLOTS]


def plain_dispatch(rows, slots, after=(), part=0, parts=1):
    blocks, local, _ = slots.shape
    rows = rows.reshape(blocks, parts, TOK_DEV, D)
    return ordered(
        plain_dispatch_kernel,
        after,
        dict(
            grid=(blocks // 2,),
            in_specs=[
                pl.BlockSpec((2, None, TOK_DEV, D), lambda i: (i, part, 0, 0)),
                pl.BlockSpec((2, local, TOK_DEV), lambda i: (i, 0, 0)),
            ],
            out_specs=pl.BlockSpec((local, SLOTS, D), lambda i: (0, i, 0)),
        ),
        out_shape=in_hbm((local, blocks // 2 * SLOTS, D), BF16),
        compiler_params=params(24),
        cost_estimate=cost(2 * blocks * TOK_DEV * D * local * SLOTS, 4 * blocks * TOK_DEV * D),
        name="plain_dispatch",
    )(rows, slots)


def combine_chip(row_ref, slot_ref):
    rows = jnp.concatenate([row_ref[j] for j in range(row_ref.shape[0])], 0)
    return [tn(pick_matrix(slot_ref[i]), rows).astype(BF16) for i in range(2)]


def combine_part_kernel(place_ref, a_ref, b_ref, a_slot, b_slot, own_ref, other_ref):
    for at, (row_ref, slot_ref) in enumerate(((a_ref, a_slot), (b_ref, b_slot))):
        first, second = combine_chip(row_ref, slot_ref)
        sort_cores(place_ref[4], first, second, own_ref, other_ref, at)


def chip_specs(slot_rows, slots):
    local, width = slots.shape[1], slot_rows.shape[2]
    rows = [
        pl.BlockSpec((local, SLOTS, width), lambda i, s, n=n: (0, s[2 * i + n], 0)) for n in (0, 1)
    ]
    spots = [
        pl.BlockSpec((2, local, TOK_DEV), lambda i, s, n=n: (s[2 * i + n], 0, 0)) for n in (0, 1)
    ]
    return rows + spots


def combine_part(place, slot_rows, slots, after=()):
    local, width = slots.shape[1], slot_rows.shape[2]
    shape = jax.ShapeDtypeStruct((2, 2, TOK_DEV, width), BF16)
    return ordered(
        combine_part_kernel,
        after,
        dict(
            num_scalar_prefetch=1,
            grid=(2,),
            in_specs=chip_specs(slot_rows, slots),
            out_specs=[pl.BlockSpec((1, 2, TOK_DEV, width), lambda i, s: (i, 0, 0, 0))] * 2,
        ),
        out_shape=[shape, shape],
        compiler_params=params(24),
        cost_estimate=cost(4 * PAIR * D * local * SLOTS, 8 * PAIR * D),
        name="combine_part",
    )(place, slot_rows, slot_rows, slots, slots)


def slope_kernel(g_ref, wd_ref, out_ref):
    out_ref[0] = nt(g_ref[0], wd_ref[0])


def slopes(grads, w_down, after=()):
    local, count, _ = grads.shape
    hidden = w_down.shape[1]
    chunk = hidden // 2
    return ordered(
        slope_kernel,
        after,
        dict(
            grid=(local, 2),
            in_specs=[
                pl.BlockSpec((1, count, D), lambda j, f: (j, 0, 0)),
                pl.BlockSpec((1, chunk, D), lambda j, f: (j, f, 0)),
            ],
            out_specs=pl.BlockSpec((1, count, chunk), lambda j, f: (j, 0, f)),
        ),
        out_shape=in_hbm((local, count, hidden), F32),
        compiler_params=params(24),
        cost_estimate=cost(2 * local * count * hidden * D, 2 * local * hidden * D),
        name="slopes",
    )(grads, w_down)


def expert_kernel(first_ref, x_ref, h_ref, wg_ref, wu_ref, wr_ref, *rest, full, offset):
    if full:
        (act_ref, dg_ref, du_ref, gate_ref, z_ref, z_s, dp_s) = rest
    else:
        (act_ref, dg_ref, du_ref, gate_ref) = rest
    step, steps = pl.program_id(1), pl.num_programs(1)
    rows = x_ref[0]

    @pl.when(step == 0)
    def _():
        logits = nn(rows, wr_ref[...])
        lane = lax.broadcasted_iota(jnp.int32, logits.shape, 1)
        logits = jnp.where(lane < EXPERTS, logits, NEG_FILL)
        powers = jnp.exp(logits - jnp.max(logits, -1, keepdims=True))
        mine = jnp.where(lane == first_ref[0] + offset + pl.program_id(0), powers, 0.0)
        gate = jnp.sum(mine, -1, keepdims=True) / jnp.sum(powers, -1, keepdims=True)
        gate_ref[0] = jnp.broadcast_to(gate, gate_ref.shape[1:])
        if full:
            z_s[...] = jnp.zeros_like(z_s)
            dp_s[...] = jnp.zeros_like(dp_s)

    gate = gate_ref[0, :, 0:1]
    gate_pre = nn(rows, wg_ref[0])
    up_pre = nn(rows, wu_ref[0])
    slope = h_ref[0]
    sig = jax.nn.sigmoid(gate_pre)
    silu = gate_pre * sig
    act = (silu * up_pre).astype(BF16)
    grad_act = slope * gate
    grad_gate = (grad_act * up_pre * sig * (1.0 + gate_pre * (1.0 - sig))).astype(BF16)
    grad_up = (grad_act * silu).astype(BF16)
    act_ref[0] = act
    dg_ref[0] = grad_gate
    du_ref[0] = grad_up
    if full:
        dp_s[...] += jnp.broadcast_to(
            jnp.sum(act.astype(F32) * slope, -1, keepdims=True), dp_s.shape
        )
        z_s[...] += nt(grad_gate, wg_ref[0]) + nt(grad_up, wu_ref[0])

        @pl.when(step == steps - 1)
        def _():
            z_ref[0, :, :D] = z_s[...].astype(BF16)
            lane = lax.broadcasted_iota(jnp.int32, dp_s.shape, 1)
            mine = first_ref[0] + offset + pl.program_id(0)
            high = dp_s[...].astype(BF16).astype(F32)
            parts = jnp.where(lane == mine, high, 0.0)
            parts = jnp.where(lane == mine + EXPERTS, dp_s[...] - high, parts)
            z_ref[0, :, D:] = parts.astype(BF16)


def experts(first, rows, slope, w_gate, w_up, router, full, only=None, after=()):
    local, count, _ = rows.shape
    offset, number = (0, local) if only is None else only
    hidden = w_gate.shape[2]
    chunk = hidden // 2
    row_spec = pl.BlockSpec((1, count, D), lambda j, f, s: (j, 0, 0))
    mid_spec = pl.BlockSpec((1, count, chunk), lambda j, f, s: (j, 0, f))
    lane_spec = pl.BlockSpec((1, count, HD), lambda j, f, s: (j, 0, 0))
    in_w = pl.BlockSpec((1, D, chunk), lambda j, f, s: (j + offset, 0, f))
    mid_shape = in_hbm((number, count, hidden), BF16)
    lane_shape = jax.ShapeDtypeStruct((number, count, HD), F32)
    out_specs = [mid_spec, mid_spec, mid_spec, lane_spec]
    out_shape = [mid_shape, mid_shape, mid_shape, lane_shape]
    scratch = []
    if full:
        out_specs += [pl.BlockSpec((1, count, D + HD), lambda j, f, s: (j, 0, 0))]
        out_shape += [in_hbm((number, count, D + HD), BF16)]
        scratch += [pltpu.VMEM((count, D), F32), pltpu.VMEM((count, HD), F32)]
    unit = 2 * number * count * hidden * D
    return ordered(
        functools.partial(expert_kernel, full=full, offset=offset),
        after,
        dict(
            num_scalar_prefetch=1,
            grid=(number, 2),
            in_specs=[
                pl.BlockSpec((1, count, D), lambda j, f, s: (j + offset, 0, 0)),
                pl.BlockSpec((1, count, chunk), lambda j, f, s: (j + offset, 0, f)),
                in_w,
                in_w,
                pl.BlockSpec((D, HD), lambda j, f, s: (0, 0)),
            ],
            out_specs=out_specs,
            scratch_shapes=scratch,
        ),
        out_shape=out_shape,
        compiler_params=params(56),
        cost_estimate=cost((4 if full else 2) * unit, 4 * number * hidden * D + 8 * number * count * D),
        name="experts_full" if full else "experts_half",
    )(first, rows, slope, w_gate, w_up, router)


def down_kernel(act_ref, gate_ref, wd_ref, out_ref):
    out_ref[0] = (nn(act_ref[0], wd_ref[0]) * gate_ref[0, :, 0:1]).astype(BF16)


def down(act, gate, w_down, after=()):
    local, count, hidden = act.shape
    chunk = D // 2
    return ordered(
        down_kernel,
        after,
        dict(
            grid=(local, 2),
            in_specs=[
                pl.BlockSpec((1, count, hidden), lambda j, f: (j, 0, 0)),
                pl.BlockSpec((1, count, HD), lambda j, f: (j, 0, 0)),
                pl.BlockSpec((1, hidden, chunk), lambda j, f: (j, 0, f)),
            ],
            out_specs=pl.BlockSpec((1, count, chunk), lambda j, f: (j, 0, f)),
        ),
        out_shape=jax.ShapeDtypeStruct((local, count, D), BF16),
        compiler_params=params(24),
        cost_estimate=cost(2 * local * count * hidden * D, 2 * local * hidden * D),
        name="down",
    )(act, gate, w_down)


def weights_kernel(
    half_ref, xa, xb, dga, dgb, dua, dub, aa, ab, ga, gb, gate_a, gate_b, *refs
):
    gate_ref, up_ref, down_ref = refs[-3:]
    rows = jnp.concatenate([xa[0], xb[0]], 0)
    gate_ref[0] = tn(rows, jnp.concatenate([dga[0], dgb[0]], 0))
    up_ref[0] = tn(rows, jnp.concatenate([dua[0], dub[0]], 0))
    grad_a = (ga[0].astype(F32) * gate_a[0, :, 0:1]).astype(BF16)
    grad_b = (gb[0].astype(F32) * gate_b[0, :, 0:1]).astype(BF16)
    down_ref[0] = tn(
        jnp.concatenate([aa[0], ab[0]], 0), jnp.concatenate([grad_a, grad_b], 0)
    )


def weight_grads(only, half, x_pair, dg_pair, du_pair, act_pair, g_pair, gate_pair, buffers, after=()):
    local, count, _ = x_pair[0].shape
    start, number = only
    hidden = dg_pair[0].shape[2]
    kept = [] if buffers is None else list(buffers)
    chunk = hidden // 2

    def spec(width, by_half, single):
        at = 0 if single else start
        if by_half is None:
            return pl.BlockSpec((1, count, width), lambda j, f, s: (j + at, 0, 0))
        if by_half:
            return pl.BlockSpec((1, count, width), lambda j, f, s: (j + at, 0, s[0]))
        return pl.BlockSpec((1, count, width), lambda j, f, s: (j + at, 0, f))

    in_specs = [
        spec(D // 2, True, False), spec(D // 2, True, False),
        spec(chunk, False, False), spec(chunk, False, True),
        spec(chunk, False, False), spec(chunk, False, True),
        spec(chunk, True, False), spec(chunk, True, True),
        spec(D // 2, False, False), spec(D // 2, False, False),
        spec(HD, None, False), spec(HD, None, True),
    ]
    unit = 2 * number * count * hidden * D
    return ordered(
        weights_kernel,
        after,
        dict(
            num_scalar_prefetch=1,
            grid=(number, 2),
            in_specs=in_specs + [ANYWHERE] * len(kept),
            out_specs=[
                pl.BlockSpec((1, D // 2, chunk), lambda j, f, s: (j + start, 0, f)),
                pl.BlockSpec((1, D // 2, chunk), lambda j, f, s: (j + start, 0, f)),
                pl.BlockSpec((1, chunk, D // 2), lambda j, f, s: (j + start, 0, f)),
            ],
        ),
        out_shape=[
            in_hbm((local, D // 2, hidden), F32),
            in_hbm((local, D // 2, hidden), F32),
            in_hbm((local, hidden // 2, D), F32),
        ],
        input_output_aliases={13 + i: i for i in range(len(kept))},
        compiler_params=params(56),
        cost_estimate=cost(3 * unit, 6 * number * hidden * D + 8 * number * count * D),
        name="weight_grads",
    )(half, *x_pair, *dg_pair, *du_pair, *act_pair, *g_pair, *gate_pair, *kept)


def softmax_of(mixed, router):
    logits = nn(mixed, router)
    lane = lax.broadcasted_iota(jnp.int32, logits.shape, 1)
    logits = jnp.where(lane < EXPERTS, logits, NEG_FILL)
    powers = jnp.exp(logits - jnp.max(logits, -1, keepdims=True))
    return powers / jnp.sum(powers, -1, keepdims=True)


def pair_kernel(group_ref, near_ref, far_ref, out_ref):
    out_ref[group_ref[0]] = near_ref[...]
    out_ref[1 - group_ref[0]] = far_ref[...]


def pair_up(group, near, far, after=()):
    return ordered(
        pair_kernel,
        after,
        dict(
            num_scalar_prefetch=1,
            grid=(1,),
            in_specs=[whole(*near.shape)] * 2,
            out_specs=whole(2, *near.shape),
        ),
        out_shape=jax.ShapeDtypeStruct((2,) + near.shape, near.dtype),
        compiler_params=params(16),
        name="pair_up",
    )(group.reshape(1).astype(jnp.int32), near, far)


def out_kernel(att_ref, w_ref, tok_ref, gain_ref, hidden_ref, mixed_ref, sums_ref, acc_ref):
    step, steps = pl.program_id(0), pl.num_programs(0)
    heads = jnp.concatenate([att_ref[i] for i in range(att_ref.shape[0])], 1)
    part = nn(heads, w_ref[...].reshape(heads.shape[1], D))

    @pl.when(step == 0)
    def _():
        acc_ref[...] = part

    @pl.when(step > 0)
    def _():
        acc_ref[...] += part

    @pl.when(step == steps - 1)
    def _():
        branch = acc_ref[...]
        hidden = tok_ref[...].astype(F32) + branch
        hidden_ref[...] = hidden
        mixed_ref[...] = (hidden * inv_rms(hidden) * gain_ref[...]).astype(BF16)
        total = jnp.sum(jnp.sum(branch * branch, -1, keepdims=True), 0, keepdims=True)
        sums_ref[...] = jnp.broadcast_to(total, sums_ref.shape)


def out_rows_spec(weights, heads):
    members, groups, rows, _ = weights.shape
    count = heads * HD // rows
    steps = members // count
    return pl.BlockSpec((count, None, rows, D), lambda i: (i % steps, i // steps, 0, 0))


def project_out(att, weights, tokens, gain_row, after=()):
    chunk = 4
    return ordered(
        out_kernel,
        after,
        dict(
        grid=(HEADS // chunk,),
        in_specs=[
            pl.BlockSpec((chunk, TOK_DEV, HD), lambda i, *_: (i, 0, 0)),
            out_rows_spec(weights, chunk),
            whole(*BLOCK_SHAPE),
            whole(1, D),
        ],
        out_specs=[whole(*BLOCK_SHAPE), whole(*BLOCK_SHAPE), whole(1, HD)],
        scratch_shapes=[pltpu.VMEM(BLOCK_SHAPE, F32)],
        ),
        out_shape=[
            jax.ShapeDtypeStruct(BLOCK_SHAPE, F32),
            jax.ShapeDtypeStruct(BLOCK_SHAPE, BF16),
            jax.ShapeDtypeStruct((1, HD), F32),
        ],
        compiler_params=params(24),
        cost_estimate=cost(2 * TOK_DEV * D * D, 2 * D * D),
        name="project_out",
    )(att, weights, tokens, gain_row)


def token_back_kernel(
    a, b, c, d, e, mixed_ref, hidden_ref, cot_ref, router_ref, gain_ref,
    grad_ref, wide_ref,
):
    probs = softmax_of(mixed_ref[...], router_ref[...])
    grad = sum(ref[...].astype(F32) for ref in (a, b, c, d, e))
    dp = grad[:, D : D + HD] + pltpu.roll(grad[:, D : D + HD], EXPERTS, 1)
    logits = (probs * (dp - jnp.sum(probs * dp, -1, keepdims=True))).astype(BF16)
    grad = grad[:, :D] + nt(logits, router_ref[...])
    hidden = hidden_ref[...]
    inverse = inv_rms(hidden)
    scaled = grad * gain_ref[...]
    mean = jnp.mean(scaled * hidden, -1, keepdims=True)
    result = cot_ref[...].astype(F32) + inverse * (scaled - hidden * inverse * inverse * mean)
    grad_ref[...] = result
    wide_ref[:, :D] = result.astype(BF16)
    wide_ref[:, D : D + HD] = logits
    wide_ref[:, D + HD :] = jnp.zeros((TOK_DEV, HD), BF16)
    part = jnp.sum(grad * hidden * inverse, 0, keepdims=True)
    high = part.astype(BF16).astype(F32)
    rows = lax.broadcasted_iota(jnp.int32, (2 * HEADS, HD), 0)
    spread = jnp.zeros((2 * HEADS, HD), F32)
    for i in range(HEADS):
        lanes = slice(i * HD, (i + 1) * HD)
        spread = jnp.where(rows == i, high[:, lanes], spread)
        spread = jnp.where(rows == HEADS + i, part[:, lanes] - high[:, lanes], spread)
    wide_ref[: 2 * HEADS, D + HD :] = spread.astype(BF16)


def term_specs(terms):
    specs, arrays = [], []
    for term in terms:
        if isinstance(term, tuple):
            arrays.append(term[0])
            shape = (None, None) + term[0].shape[2:]
            specs.append(pl.BlockSpec(shape, lambda i, n=term[1]: n + (0, 0)))
        else:
            arrays.append(term)
            specs.append(whole(*term.shape))
    return specs, arrays


def token_back(terms, mixed, hidden, cotangent, router, gain_row, after=()):
    specs, arrays = term_specs(terms)
    return ordered(
        token_back_kernel,
        after,
        dict(
            grid=(1,),
            in_specs=specs
            + [whole(*BLOCK_SHAPE)] * 3
            + [whole(D, HD), whole(1, D)],
            out_specs=[whole(*BLOCK_SHAPE), whole(TOK_DEV, D + 2 * HD)],
        ),
        out_shape=[
            jax.ShapeDtypeStruct(BLOCK_SHAPE, F32),
            jax.ShapeDtypeStruct((TOK_DEV, D + 2 * HD), BF16),
        ],
        compiler_params=params(40),
        cost_estimate=cost(30 * TOK_DEV * D, 20 * TOK_DEV * D),
        name="token_back",
    )(*arrays, mixed, hidden, cotangent, router, gain_row)


def out_back_kernel(grad_ref, w_ref, out_ref):
    out = nt(grad_ref[...], w_ref[...].reshape(-1, D)).astype(BF16)
    for i in range(out_ref.shape[0]):
        out_ref[i] = out[:, i * HD : (i + 1) * HD]


def out_back(wide, weights):
    chunk = 4
    return ordered(
        out_back_kernel,
        (),
        dict(
        grid=(HEADS // chunk,),
        in_specs=[
            pl.BlockSpec(BLOCK_SHAPE, lambda i: (0, 0)),
            out_rows_spec(weights, chunk),
        ],
        out_specs=pl.BlockSpec((chunk, TOK_DEV, HD), lambda i: (i, 0, 0)),
        ),
        out_shape=jax.ShapeDtypeStruct((HEADS, TOK_DEV, HD), BF16),
        compiler_params=params(24),
        cost_estimate=cost(2 * TOK_DEV * D * D, 2 * D * D),
        name="out_back",
    )(wide, weights)


def tokens_grad_kernel(
    a, b, c, d, e, tok_ref, gain_ref, grad_ref, hidden_ref, before_ref, out_ref, result_ref, sums_ref
):
    total = sum(ref[...].astype(F32) for ref in (a, b, c, d, e))
    grad, branch = total[:, :D], total[:, D:]
    inputs = tok_ref[...].astype(F32)
    inverse = inv_rms(inputs)
    scaled = grad * gain_ref[...]
    mean = jnp.mean(scaled * inputs, -1, keepdims=True)
    result = grad_ref[...] + inverse * (scaled - inputs * inverse * inverse * mean)
    out_ref[...] = result.astype(BF16)
    result_ref[...] = (hidden_ref[...] + branch).astype(BF16)
    lane = lax.broadcasted_iota(jnp.int32, sums_ref.shape, 1)
    sums = jnp.where(lane == 1, before_ref[...], 0.0)
    for place, values in ((0, inputs), (2, branch)):
        square = jnp.sum(jnp.sum(values * values, -1, keepdims=True), 0, keepdims=True)
        sums = jnp.where(lane == place, square, sums)
    sums_ref[...] = sums


def final_tokens(terms, tokens, gain_row, grad_hidden, hidden, branch_sums, after=()):
    specs, arrays = term_specs(terms)
    return ordered(
        tokens_grad_kernel,
        after,
        dict(
            grid=(1,),
            in_specs=specs
            + [whole(*BLOCK_SHAPE), whole(1, D), whole(*BLOCK_SHAPE), whole(*BLOCK_SHAPE), whole(1, HD)],
            out_specs=[whole(*BLOCK_SHAPE), whole(*BLOCK_SHAPE), whole(1, HD)],
        ),
        out_shape=[
            jax.ShapeDtypeStruct(BLOCK_SHAPE, BF16),
            jax.ShapeDtypeStruct(BLOCK_SHAPE, BF16),
            jax.ShapeDtypeStruct((1, HD), F32),
        ],
        compiler_params=params(40),
        cost_estimate=cost(30 * TOK_DEV * D, 20 * TOK_DEV * D),
        name="final_tokens",
    )(*arrays, tokens, gain_row, grad_hidden, hidden, branch_sums)


def owner_rows_kernel(place_ref, att_ref, mixed_ref, wide_ref, out_ref, moe_ref):
    step, steps = pl.program_id(0), pl.num_programs(0)

    @pl.when(step == 0)
    def _():
        out_ref[...] = jnp.zeros_like(out_ref)
        moe_ref[...] = jnp.zeros_like(moe_ref)

    out_ref[:, :D] += tn(att_ref[...], wide_ref[:, :D])
    out_ref[:, D:] += tn(mixed_ref[...], wide_ref[:, D : D + HD])
    tail = wide_ref[:, D + HD :].astype(F32)
    rows = lax.broadcasted_iota(jnp.int32, tail.shape, 0) % TOK_DEV
    mine = (rows == place_ref[0]) | (rows == place_ref[0] + HEADS)
    moe_ref[...] += jnp.sum(jnp.where(mine, tail, 0.0), 0, keepdims=True)

    @pl.when(step == steps - 1)
    def _():
        lane = lax.broadcasted_iota(jnp.int32, (HD, HD), 1)
        out_ref[:, D:] = jnp.where(lane == EXPERTS, as_column(moe_ref[...]), out_ref[:, D:])


def owner_rows(place, att, mixed_columns, wide_all, after=()):
    rows, width = wide_all.shape
    chunk = rows // 4
    return ordered(
        owner_rows_kernel,
        after,
        dict(
            num_scalar_prefetch=1,
            grid=(4,),
            in_specs=[
                pl.BlockSpec((chunk, HD), lambda i, s: (i, 0)),
                pl.BlockSpec((chunk, HD), lambda i, s: (i, 0)),
                pl.BlockSpec((chunk, width), lambda i, s: (i, 0)),
            ],
            out_specs=whole(HD, D + HD),
            scratch_shapes=[pltpu.VMEM((1, HD), F32)],
        ),
        out_shape=jax.ShapeDtypeStruct((HD, D + HD), F32),
        compiler_params=params(24),
        cost_estimate=cost(2 * rows * D * HD, 2 * rows * D),
        name="owner_rows",
    )(place.reshape(1).astype(jnp.int32), att, mixed_columns, wide_all)


def unpack_kernel(in_ref, wq_ref, wk_ref, wv_ref, gain_ref, q_ref, k_ref, v_ref, sums_ref):
    heads = in_ref.shape[0]
    total = jnp.zeros((q_ref.shape[0], 1), F32)
    for part, (w_ref, out_ref) in enumerate(((wq_ref, q_ref), (wk_ref, k_ref), (wv_ref, v_ref))):
        for h in range(heads):
            piece = in_ref[h, : q_ref.shape[0], part * HD : (part + 1) * HD].astype(F32)
            lanes = slice(h * HD, (h + 1) * HD)
            out_ref[:, lanes] = piece
            total += jnp.sum(w_ref[:, lanes].astype(F32) * piece, -1, keepdims=True)
    sums_ref[...] = jnp.broadcast_to(total / gain_ref[...], sums_ref.shape)


def unpack(arrived, weights, gain, after=()):
    rows = weights[0].shape[0]
    shape = jax.ShapeDtypeStruct((rows, D), F32)
    return ordered(
        unpack_kernel,
        after,
        dict(
            grid=(1,),
            in_specs=[whole(*arrived.shape)] + [whole(rows, D)] * 3 + [whole(rows, 1)],
            out_specs=[whole(rows, D)] * 3 + [whole(rows, HD)],
        ),
        out_shape=[shape] * 3 + [jax.ShapeDtypeStruct((rows, HD), F32)],
        compiler_params=params(24),
        cost_estimate=cost(6 * rows * D, 20 * rows * D),
        name="unpack",
    )(arrived, *weights, gain.astype(F32).reshape(rows, 1))


def tie_kernel(in_ref, out_ref):
    out_ref[...] = in_ref[...]


def tie(array, after):
    return ordered(
        tie_kernel,
        after,
        dict(grid=(1,), in_specs=[whole(*array.shape)], out_specs=whole(*array.shape)),
        out_shape=jax.ShapeDtypeStruct(array.shape, array.dtype),
        compiler_params=params(16),
        name="tie",
    )(array)


def swap(value, axis):
    return lax.ppermute(value, axis, [(0, 1), (1, 0)])


def total_over_ep(value):
    value = value + swap(value, "core")
    value = value + swap(value, "x")
    value = value + lax.ppermute(value, "z", [(0, 1), (1, 0), (2, 3), (3, 2)])
    return value + lax.ppermute(value, "z", [(0, 2), (2, 0), (1, 3), (3, 1)])


def of_groups(value):
    return lax.all_gather(value, ("grp", "core"))


def gather_rows(value):
    return lax.all_gather(value, EP, axis=0, tiled=True)


def reduce_rows(value):
    return lax.psum_scatter(value, EP, scatter_dimension=0, tiled=True)


CHIP_ORDER = ((0, 1, 2, 3), (1, 0, 2, 3), (2, 1, 3, 0), (3, 2, 1, 0))


def chip_places():
    z, x = lax.axis_index("z"), lax.axis_index("x")
    order = jnp.asarray(CHIP_ORDER, jnp.int32)[z]
    return [[order[s] * 2 + (x if r == 0 else 1 - x) for r in range(2)] for s in range(4)]


def shift(value, pairs):
    return lax.ppermute(value, "z", pairs)


def choose_kernel(flag_ref, *refs):
    out_ref = refs[-1]
    for i in range(len(refs) - 1):

        @pl.when(flag_ref[i] == 1)
        def _(i=i):
            out_ref[...] = refs[i][...]


def choose(flags, options, after=()):
    return ordered(
        choose_kernel,
        after,
        dict(
            num_scalar_prefetch=1,
            grid=(1,),
            in_specs=[whole(*BLOCK_SHAPE)] * len(options),
            out_specs=whole(*BLOCK_SHAPE),
        ),
        out_shape=jax.ShapeDtypeStruct(BLOCK_SHAPE, BF16),
        compiler_params=params(16),
        cost_estimate=cost(TOK_DEV * D, 2 * (len(options) + 1) * TOK_DEV * D),
        name="choose",
    )(flags, *options)


def gather_steps(block, use, work):
    z = lax.axis_index("z")
    flags = lambda *tests: jnp.stack([jnp.asarray(test, jnp.int32) for test in tests])
    below1 = shift(block, [(0, 1), (1, 2), (2, 3)])
    above1 = shift(block, [(3, 2), (2, 1), (1, 0)])
    across0 = swap(block, "x")
    far00 = swap(block, "core")
    last = work(0, block)
    column1 = choose(flags(z == 0, z != 0), [above1, below1], [last])
    below2 = shift(below1, [(1, 2), (2, 3)])
    above2 = shift(above1, [(2, 1), (1, 0)])
    across1 = swap(column1, "x")
    far01, far10 = swap(across0, "core"), swap(column1, "core")
    last = use(0, 0, block, far00, [column1])
    last = use(0, 1, across0, far01, [last])
    last = use(1, 0, column1, far10, [last])
    last = work(1, last)
    column2 = choose(
        flags(z == 0, z == 3, (z == 1) | (z == 2)), [above2, below2, above1], [last]
    )
    below3 = shift(below2, [(2, 3)])
    above3 = shift(above2, [(1, 0)])
    across2 = swap(column2, "x")
    far11, far20 = swap(across1, "core"), swap(column2, "core")
    last = use(1, 1, across1, far11, [column2])
    last = use(2, 0, column2, far20, [last])
    last = work(2, last)
    column3 = choose(
        flags(z == 0, z == 1, z == 2, z == 3), [above3, above2, below2, below3], [last]
    )
    across3 = swap(column3, "x")
    far21, far30 = swap(across2, "core"), swap(column3, "core")
    last = use(2, 1, across2, far21, [column3])
    last = use(3, 0, column3, far30, [last])
    last = work(3, last)
    far31 = swap(across3, "core")
    return use(3, 1, across3, far31, [last])


def sum_kernel(*refs):
    out_ref = refs[-1]
    total = refs[0][...].astype(F32)
    for ref in refs[1:-1]:
        total = total + ref[...].astype(F32)
    out_ref[...] = total.astype(out_ref.dtype)


def sum_blocks(terms, after=(), dtype=BF16):
    specs, arrays = term_specs(terms)
    return ordered(
        sum_kernel,
        after,
        dict(grid=(1,), in_specs=specs, out_specs=whole(*arrays[0].shape[-2:])),
        out_shape=jax.ShapeDtypeStruct(arrays[0].shape[-2:], dtype),
        compiler_params=params(16),
        cost_estimate=cost(len(terms) * TOK_DEV * D, 2 * (len(terms) + 1) * TOK_DEV * D),
        name="sum_blocks",
    )(*arrays)


def pass_on(place, near_up, far_up, near_down, far_down, below, above, after=()):
    def kernel(place_ref, nu, fu, nd, fd, below_ref, above_ref, up_ref, down_ref):
        z = place_ref[0]

        def store(out_ref, source_ref, arrived_ref):
            total = source_ref[...].astype(F32) + arrived_ref[...].astype(F32)
            out_ref[...] = total.astype(BF16)

        for edge, near, far, arrived, out_ref in (
            (0, nu, fu, below_ref, up_ref),
            (3, nd, fd, above_ref, down_ref),
        ):
            pl.when(z == edge)(functools.partial(store, out_ref, near, arrived))
            pl.when(z != edge)(functools.partial(store, out_ref, far, arrived))

    shape = jax.ShapeDtypeStruct(below.shape, BF16)
    return ordered(
        kernel,
        after,
        dict(
            num_scalar_prefetch=1,
            grid=(1,),
            in_specs=[whole(*below.shape)] * 6,
            out_specs=[whole(*below.shape)] * 2,
        ),
        out_shape=[shape, shape],
        compiler_params=params(24),
        cost_estimate=cost(4 * TOK_DEV * D, 16 * TOK_DEV * D),
        name="pass_on",
    )(place, near_up, far_up, near_down, far_down, below, above)


def reduce_steps(parts, work):
    place = lax.axis_index("z").reshape(1).astype(jnp.int32)
    last, sources = [], {}
    for s in (3, 1):
        own, other = parts(s, last)
        near = swap(other, "core")
        last = [own]
        for i in range(2):
            sources[s - i] = lambda r, i=i, own=own, near=near: [(own, (i, r)), (near, (i, r))]
    crossed = {}
    last = last[0]
    for s in (3, 2, 1, 0):
        last = sum_blocks(sources[s](1), [last])
        crossed[s] = swap(last, "x")
    last = work(0, last)
    low = {}
    low[3] = last = sum_blocks(sources[3](0) + [crossed[3]], [last])
    up3 = shift(low[3], [(0, 1)])
    down3 = shift(low[3], [(3, 2)])
    last = work(1, last)
    low[2] = last = sum_blocks(sources[2](0) + [crossed[2]], [last])
    up2, down2 = pass_on(place, low[2], low[3], low[2], low[3], up3, down3)
    last = work(2, up2)
    up2 = shift(up2, [(0, 1), (1, 2)])
    down2 = shift(down2, [(3, 2), (2, 1)])
    low[1] = last = sum_blocks(sources[1](0) + [crossed[1]], [last])
    up1, down1 = pass_on(place, low[1], low[2], low[1], low[1], up2, down2)
    last = work(3, up1)
    up1 = shift(up1, [(0, 1), (1, 2), (2, 3)])
    down1 = shift(down1, [(3, 2), (2, 1), (1, 0)])
    return sources[0](0) + [crossed[0], up1, down1], last


def expert_slots(routes_all, first, local):
    rows = routes_all.shape[0]
    ids = first + jnp.arange(local, dtype=jnp.int32)
    named = jnp.any(routes_all[None, :, :] == ids[:, None, None], -1).reshape(
        local, rows // TOK_DEV, TOK_DEV
    )
    places = jnp.arange(TOK_DEV, dtype=jnp.int32)
    upto = (places[:, None] <= places[None, :]).astype(BF16)
    rank = jnp.einsum(
        "ebt,ts->ebs", named.astype(BF16), upto, preferred_element_type=F32
    ).astype(jnp.int32)
    base = (jnp.arange(rows // TOK_DEV, dtype=jnp.int32) % 2) * CAP
    slots = jnp.where(named, rank - 1 + base[None, :, None], -1)
    return jnp.transpose(slots, (1, 0, 2))


def fast_shards(
    tokens, w_query, w_key, w_value, w_output, w_router, attn_gain, query_gain, key_gain,
    moe_gain, w_gate, w_up, w_down, routes, cotangent,
):
    Order.marks.clear()
    group = lax.axis_index("grp")
    place = lax.axis_index(EP)
    members = lax.axis_size(EP)
    seq = TOK_DEV * members
    local = w_gate.shape[0]
    wide = w_query.shape[0]
    first = (place * local).reshape(1).astype(jnp.int32)

    core = lax.axis_index("core").astype(jnp.int32)
    chips = chip_places()
    small = jnp.concatenate(
        [
            w_router,
            routes.reshape(-1, EXPERTS).astype(BF16),
            jnp.stack([attn_gain, query_gain, key_gain, moe_gain]),
            jnp.zeros((12, EXPERTS), BF16),
        ],
        0,
    ).reshape(16, 3 * HD)
    columns = jnp.stack([w_query, w_key, w_value], 1).reshape(wide, 3, HEADS, HD)
    columns = jnp.transpose(columns, (2, 0, 1, 3)).reshape(HEADS, wide, 3 * HD)
    columns = jnp.concatenate([columns, jnp.broadcast_to(small, (HEADS,) + small.shape)], 1)
    mine = lax.all_to_all(columns, EP, 0, 0, tiled=True)
    other = swap(mine, "grp")
    both = jnp.where(group == 0, jnp.stack([mine, other]), jnp.stack([other, mine]))
    w_head = both[:, :, :wide].reshape(D, 3 * HD)
    small_all = both[:, :, wide:].reshape(2 * members, -1, EXPERTS)
    route_rows = TOK_DEV * TOPK // EXPERTS
    router_full = small_all[:, :wide].reshape(D, EXPERTS)
    routes_all = (
        small_all[:, wide : wide + route_rows].reshape(2, seq, TOPK).astype(jnp.int32)
    )
    gains = jnp.transpose(
        small_all[:, wide + route_rows : wide + route_rows + 4], (1, 0, 2)
    ).reshape(4, D).astype(F32)
    router_wide = jnp.concatenate([router_full, jnp.zeros((D, HD - EXPERTS), BF16)], 1)
    head_gains = lax.dynamic_slice(gains, (0, place * HD), (4, HD))
    gain_q, gain_k = head_gains[1:2], head_gains[2:3]
    attn_row, moe_row = gains[0:1], gains[3:4]

    far_out = swap(w_output, "grp")

    slots_own = expert_slots(lax.dynamic_index_in_dim(routes_all, group, 0, False), first, local)
    slots_other = expert_slots(
        lax.dynamic_index_in_dim(routes_all, 1 - group, 0, False), first, local
    )

    positions = jnp.arange(seq, dtype=jnp.int32)
    half_dim = HD // 2
    frequency = jnp.exp(-(2.0 * jnp.arange(half_dim, dtype=F32) / HD) * math.log(10000.0))
    angles = positions.astype(F32)[:, None] * frequency[None, :]
    cosine = jnp.concatenate([jnp.cos(angles)] * 2, 1)
    sine = jnp.concatenate([-jnp.sin(angles), jnp.sin(angles)], 1)

    kept = [None]

    def use_tokens(s, r, own, far, after):
        spot = jnp.stack([chips[s][r], core])
        kept[0] = project(spot, own, far, w_head, attn_row, kept[0], seq, after)
        return kept[0][2]

    def start_work(step, last):
        if step == 3:
            kept.append(pair_up(group, w_output, far_out, [last, mine]))
            return kept[1]
        return last

    gather_steps(tokens, use_tokens, start_work)
    output_full = gather_rows(kept[1][None])
    cot_own = gather_rows(cotangent)
    normed_all, qkv, stat = kept[0]
    stat = total_over_ep(stat)
    q16, k16, v16, attn_float, att_head, lse = attend(qkv, stat, gain_q, gain_k, cosine, sine)
    attended = lax.all_to_all(att_head.reshape(members, TOK_DEV, HD), EP, 0, 0, tiled=True)
    g_own = plain_dispatch(cot_own, slots_own, [att_head])
    cot_stack = stack_of_core(core, cot_own.reshape(members // 2, 2, TOK_DEV, D), [g_own])
    slope_own = slopes(g_own, w_down, [cot_stack])
    hidden, mixed, branch_sums = project_out(attended, output_full, tokens, moe_row, [slope_own])
    def early_work(_, last):
        return last

    rows = [None]

    def use_mixed(s, r, own, far, after):
        spot = jnp.stack([chips[s][r], core, place.astype(jnp.int32)])
        rows[0] = dispatch(spot, own, far, slots_own, rows[0], after)
        return rows[0][0]

    gather_steps(mixed, use_mixed, early_work)
    x_own, mixed_columns, mixed_stack = rows[0]
    sides = jnp.stack([core, group.astype(jnp.int32)])
    cot_near = of_groups(cot_stack)
    mixed_near = of_groups(mixed_stack)
    every = jnp.concatenate([jnp.arange(members // 2, dtype=jnp.int32), sides])
    act_a, dg_a, du_a, gate_a, z_rows = experts(
        first, x_own, slope_own, w_gate, w_up, router_wide, True
    )

    def place_of(s):
        return jnp.stack([chips[s][0], chips[s][1], chips[s - 1][0], chips[s - 1][1], core])

    late = {}

    def late_work(step, last):
        if step == 1:
            late["y"] = down(act_a, gate_a, w_down, [last])
            return late["y"]
        if step == 2:
            late["g"] = stack_dispatch(every, cot_near, slots_other, [last])
            return late["g"]
        if step == 3:
            late["slope"] = slopes(late["g"], w_down, [last])
            return late["slope"]
        return last

    terms, last = reduce_steps(
        lambda s, after: combine_part(place_of(s), z_rows, slots_own, after), late_work
    )
    grad_hidden, wide_branch = token_back(
        terms, mixed, hidden, cotangent, router_wide, moe_row, [last]
    )
    grad_out = out_back(wide_branch, output_full)
    grad_att_head = lax.all_to_all(grad_out, EP, 0, 0, tiled=True).reshape(seq, HD)
    branch_all = gather_rows(wide_branch)

    def expert_other(only, last):
        late[only] = experts(
            first, late["x"], late["slope"], w_gate, w_up, router_wide, False, only, [last]
        )
        return late[only][3]

    groups = [(0, local // 2), (local // 2, local - local // 2)]
    late["x"] = stack_dispatch(every, mixed_near, slots_other, [grad_out])
    last = expert_other(groups[0], late["x"])

    dnq, dnk, dv16, means, gain_parts = attend_back(
        q16, k16, v16, grad_att_head, attn_float, lse, qkv, stat, gain_q, gain_k, cosine, sine, [last],
    )
    means = total_over_ep(means)
    qkv_grads = finish(dnq, dnk, dv16, qkv, stat, means, gain_q, gain_k)
    half = group.reshape(1).astype(jnp.int32)

    def expert_grads(only, last):
        act_b, dg_b, du_b, gate_b = late[only]
        late["grads"] = weight_grads(
            only, half, (x_own, late["x"]), (dg_a, dg_b), (du_a, du_b), (act_a, act_b),
            (g_own, late["g"]), (gate_a, gate_b), late.get("grads"), [last],
        )
        return late["grads"][0]

    def last_work(step, last):
        if step == 0:
            late["dw"] = dw_product(normed_all, qkv_grads, [last])
            return late["dw"]
        if step == 1:
            return expert_other(groups[1], last)
        if step == 2:
            return expert_grads(groups[0], last)
        return last

    terms, last = reduce_steps(
        lambda s, after: normed_part(place_of(s), qkv_grads, w_head, late["y"], slots_own, after),
        last_work,
    )
    tokens_grad, output, sums = final_tokens(
        terms, tokens, attn_row, grad_hidden, hidden, branch_sums, [last]
    )
    dw_head = late["dw"]
    last = tokens_grad
    last = expert_grads(groups[1], last)
    gate_grad, up_grad, down_grad = late["grads"]
    rms_stats = jnp.sqrt(total_over_ep(sums)[:, :3] / (seq * D))

    dw_keep = lax.dynamic_slice_in_dim(dw_head, group * (D // 2), D // 2, 0)
    dw_send = lax.dynamic_slice_in_dim(dw_head, (1 - group) * (D // 2), D // 2, 0)
    dw_half = (dw_keep + swap(dw_send.astype(BF16), "grp").astype(F32)).astype(BF16)
    gain_parts = gain_parts + swap(gain_parts, "grp")
    extra = gain_parts.reshape(1, 2 * HD)
    high = extra.astype(BF16)
    low = (extra - high.astype(F32)).astype(BF16)
    extra = jnp.pad(jnp.concatenate([high, low], 0), ((0, 14), (0, HD)))
    payload = jnp.concatenate(
        [
            dw_half.reshape(members, wide, 3 * HD),
            jnp.broadcast_to(extra, (members,) + extra.shape),
        ],
        1,
    )
    arrived = lax.all_to_all(payload, EP, 0, 0, tiled=True)
    *dense, attn_sums = unpack(arrived, (w_query, w_key, w_value), attn_gain, [last])
    attn_gain_grad = attn_sums[:, 0]
    extras = arrived[:, wide].astype(F32) + arrived[:, wide + 1].astype(F32)
    flat = group * members + place
    head_row = lax.dynamic_slice(
        extras[:, : 2 * HD].reshape(HEADS, 2, HD // wide, wide),
        (flat // (HD // wide), 0, flat % (HD // wide), 0),
        (1, 2, 1, wide),
    ).reshape(2, wide)

    out_part = owner_rows(place, att_head, mixed_columns, branch_all, [last])
    out_part = out_part.reshape(2, wide, D + HD)
    out_keep = lax.dynamic_index_in_dim(out_part, group, 0, False)
    out_send = lax.dynamic_index_in_dim(out_part, 1 - group, 0, False).astype(BF16)
    out_sum = (out_keep + swap(out_send, "grp").astype(F32)).astype(BF16)
    owners = [(g * members + e, 2 * e + g) for g in range(2) for e in range(members)]
    owned = lax.ppermute(out_sum, ALL, owners).astype(F32)
    output_grad = owned[:, :D]
    router_grad, moe_gain_grad = owned[:, D : D + EXPERTS], owned[:, D + EXPERTS]

    return (
        output, tokens_grad, dense[0], dense[1], dense[2], output_grad, router_grad,
        attn_gain_grad, head_row[0], head_row[1], moe_gain_grad, gate_grad, up_grad, down_grad,
        rms_stats,
    )


def fast_solution(mesh, sides):
    inner = jax.sharding.Mesh(mesh.devices.reshape((2,) + sides), ALL)
    rows = P(ALL, None)
    expert = P(EP, None, None)
    return jax.shard_map(
        fast_shards,
        mesh=inner,
        in_specs=(rows,) * 6 + (P(ALL),) * 4 + (expert,) * 3 + (rows,) * 2,
        out_specs=(rows,) * 7 + (P(ALL),) * 4 + (P(EP, "grp", None),) * 3 + (P("grp", None),),
        check_vma=False,
    )


def solution(mesh):
    sides = SIDES.get(mesh.shape["ep"])
    if sides is not None and mesh.shape["grp"] == 2:
        return fast_solution(mesh, sides)
    return jax.shard_map(
        shards,
        mesh=mesh,
        in_specs=(
            P(("grp", "ep"), None),
            P(("grp", "ep"), None),
            P(("grp", "ep"), None),
            P(("grp", "ep"), None),
            P(("grp", "ep"), None),
            P(("grp", "ep"), None),
            P(("grp", "ep")),
            P(("grp", "ep")),
            P(("grp", "ep")),
            P(("grp", "ep")),
            P("ep", None, None),
            P("ep", None, None),
            P("ep", None, None),
            P(("grp", "ep"), None),
            P(("grp", "ep"), None),
        ),
        out_specs=(
            P(("grp", "ep"), None),
            P(("grp", "ep"), None),
            P(("grp", "ep"), None),
            P(("grp", "ep"), None),
            P(("grp", "ep"), None),
            P(("grp", "ep"), None),
            P(("grp", "ep"), None),
            P(("grp", "ep")),
            P(("grp", "ep")),
            P(("grp", "ep")),
            P(("grp", "ep")),
            P("ep", "grp", None),
            P("ep", "grp", None),
            P("ep", "grp", None),
            P("grp", None),
        ),
        check_vma=False,
    )
```

```python
import functools
import math

import jax
import jax.numpy as jnp
from jax import lax
from jax.experimental import pallas as pl
from jax.experimental.pallas import tpu as pltpu
from jax.sharding import PartitionSpec as P

D = 2048
HEADS = 16
HD = 128
EXPERTS = 64
TOPK = 8
TOK_DEV = 128
BLOCK = 256
CAP = 24


EPSILON = 1e-05
NEG_FILL = -1e30


def inv_rms(values):
    return lax.rsqrt(jnp.mean(values * values, -1, keepdims=True) + EPSILON)


def norm_back(grad_out, values, inverse, gain_vec):
    scaled = grad_out * gain_vec
    grad_in = inverse * (
        scaled - values * inverse * inverse * jnp.mean(scaled * values, -1, keepdims=True)
    )
    return (grad_in, jnp.sum(grad_out * values * inverse, 0))


def rope_tables(positions):
    half_dim = HD // 2
    frequency = jnp.exp(-(2.0 * jnp.arange(half_dim, dtype=jnp.float32) / HD) * math.log(10000.0))
    angles = positions.astype(jnp.float32)[:, None] * frequency[None, :]
    return (jnp.cos(angles)[:, None, :], jnp.sin(angles)[:, None, :])


def rotate(values, cosine, sine_tab):
    half_dim = HD // 2
    first_half = values[..., :half_dim]
    second_half = values[..., half_dim:]
    return jnp.concatenate(
        [
            first_half * cosine - second_half * sine_tab,
            second_half * cosine + first_half * sine_tab,
        ],
        -1,
    )


def rotate_back(grad_in, cosine, sine_tab):
    half_dim = HD // 2
    first_half = grad_in[..., :half_dim]
    second_half = grad_in[..., half_dim:]
    return jnp.concatenate(
        [
            first_half * cosine + second_half * sine_tab,
            second_half * cosine - first_half * sine_tab,
        ],
        -1,
    )


def fold_keys(state_now, key_piece, queries, query_pos):
    keys_in, values_in = key_piece
    piece_rows = keys_in.shape[0]
    blk_rows = math.gcd(piece_rows, 1024)
    key_blocks = keys_in.reshape(piece_rows // blk_rows, blk_rows, HEADS, HD)
    value_blocks = values_in.reshape(piece_rows // blk_rows, blk_rows, HEADS, HD)
    last_block = query_pos[-1] // BLOCK

    def block_step(state_in, block_items):
        key_blk, value_blk, block_num = block_items
        key_start = block_num * blk_rows

        def block_compute(state_cur):
            top_now, total_now, acc_now = state_cur
            key_pos = key_start + jnp.arange(blk_rows, dtype=jnp.int32)
            scores = jnp.einsum(
                "qhd,khd->hqk", queries, key_blk, preferred_element_type=jnp.float32
            ) * HD ** (-0.5)
            allowed = (key_pos // BLOCK)[None, None, :] <= (query_pos // BLOCK)[None, :, None]
            scores = jnp.where(allowed, scores, NEG_FILL)
            top_new = jnp.maximum(top_now, jnp.max(scores, -1, keepdims=True))
            weights = jnp.where(allowed, jnp.exp(scores - top_new), 0.0)
            rescale = jnp.exp(top_now - top_new)
            total_new = total_now * rescale + jnp.sum(weights, -1, keepdims=True)
            acc_new = acc_now * jnp.transpose(rescale, (1, 0, 2)) + jnp.einsum(
                "hqk,khd->qhd",
                weights.astype(jnp.bfloat16),
                value_blk,
                preferred_element_type=jnp.float32,
            )
            return (top_new, total_new, acc_new)

        def block_passing(state_cur):
            return state_cur

        return (
            lax.cond(key_start // BLOCK <= last_block, block_compute, block_passing, state_in),
            None,
        )

    state_out, unused = lax.scan(
        block_step,
        state_now,
        (key_blocks, value_blocks, jnp.arange(piece_rows // blk_rows, dtype=jnp.int32)),
    )
    return state_out


def score_grads(queries, grad_attended, row_delta, log_sum, query_pos, key_blk, value_blk, key_pos):
    scores = jnp.einsum(
        "qhd,khd->hqk", queries, key_blk, preferred_element_type=jnp.float32
    ) * HD ** (-0.5)
    allowed = (key_pos // BLOCK)[None, None, :] <= (query_pos // BLOCK)[None, :, None]
    prob_vals = jnp.where(allowed, jnp.exp(scores - log_sum), 0.0)
    grad_probs = jnp.einsum(
        "qhd,khd->hqk", grad_attended, value_blk, preferred_element_type=jnp.float32
    )
    grad_scores = (prob_vals * (grad_probs - row_delta)).astype(jnp.bfloat16)
    return (prob_vals, grad_scores)


def shards(
    tokens,
    w_query,
    w_key,
    w_value,
    w_output,
    w_router,
    attn_gain,
    query_gain,
    key_gain,
    moe_gain,
    w_gate,
    w_up,
    w_down,
    routes,
    cotangent,
):
    gathered = (
        lax.all_gather(w_query, ("grp", "ep"), axis=0, tiled=True),
        lax.all_gather(w_key, ("grp", "ep"), axis=0, tiled=True),
        lax.all_gather(w_value, ("grp", "ep"), axis=0, tiled=True),
        lax.all_gather(w_output, ("grp", "ep"), axis=0, tiled=True),
        lax.all_gather(w_router, ("grp", "ep"), axis=0, tiled=True),
        lax.all_gather(attn_gain, ("grp", "ep"), axis=0, tiled=True),
        lax.all_gather(query_gain, ("grp", "ep"), axis=0, tiled=True),
        lax.all_gather(key_gain, ("grp", "ep"), axis=0, tiled=True),
        lax.all_gather(moe_gain, ("grp", "ep"), axis=0, tiled=True),
    )
    query_full, key_full, value_full, output_full, router_full = (
        gathered[0],
        gathered[1],
        gathered[2],
        gathered[3],
        gathered[4],
    )
    attn_scale = gathered[5].astype(jnp.float32)
    query_scale = gathered[6].astype(jnp.float32)
    key_scale = gathered[7].astype(jnp.float32)
    moe_scale = gathered[8].astype(jnp.float32)
    ep_count = lax.axis_size("ep")
    exp_local = EXPERTS // ep_count
    score_scale = HD ** (-0.5)
    inputs = tokens.astype(jnp.float32)
    positions = lax.axis_index("ep") * TOK_DEV + jnp.arange(TOK_DEV, dtype=jnp.int32)
    cosine, sine_tab = rope_tables(positions)
    attn_inv = inv_rms(inputs)
    normed = (inputs * attn_inv * attn_scale).astype(jnp.bfloat16)
    query_raw = jnp.dot(normed, query_full, preferred_element_type=jnp.float32)
    key_raw = jnp.dot(normed, key_full, preferred_element_type=jnp.float32)
    values16 = jnp.dot(normed, value_full, preferred_element_type=jnp.float32).astype(jnp.bfloat16)
    query_inv = inv_rms(query_raw)
    queries16 = rotate(
        (query_raw * query_inv * query_scale).reshape(TOK_DEV, HEADS, HD), cosine, sine_tab
    ).astype(jnp.bfloat16)
    key_inv = inv_rms(key_raw)
    keys16 = (
        rotate((key_raw * key_inv * key_scale).reshape(TOK_DEV, HEADS, HD), cosine, sine_tab)
        .astype(jnp.bfloat16)
        .reshape(TOK_DEV, D)
    )
    start_state = (
        jnp.full((HEADS, TOK_DEV, 1), NEG_FILL, jnp.float32),
        jnp.zeros((HEADS, TOK_DEV, 1), jnp.float32),
        jnp.zeros((TOK_DEV, HEADS, HD), jnp.float32),
    )
    folded = fold_keys(
        start_state,
        (
            lax.all_gather(keys16, "ep", axis=0, tiled=True),
            lax.all_gather(values16, "ep", axis=0, tiled=True),
        ),
        queries16,
        positions,
    )
    top_score, total_weight, acc_sum = folded
    log_sum = top_score + jnp.log(total_weight)
    attn_float = acc_sum / jnp.transpose(total_weight, (1, 0, 2))
    attended16 = attn_float.reshape(TOK_DEV, D).astype(jnp.bfloat16)
    branch_attn = jnp.dot(attended16, output_full, preferred_element_type=jnp.float32)
    hidden = inputs + branch_attn
    moe_inv = inv_rms(hidden)
    mixed_in = (hidden * moe_inv * moe_scale).astype(jnp.bfloat16)
    logits = jnp.dot(mixed_in, router_full, preferred_element_type=jnp.float32)
    route_probs = jax.nn.softmax(logits, -1)
    chosen = (routes[:, :, None] == jnp.arange(EXPERTS, dtype=jnp.int32)[None, None, :]).astype(
        jnp.float32
    )
    gate_vals = jnp.sum(chosen * route_probs[:, None, :], -1)
    pair_expert = routes.reshape(-1)
    one_hot = (pair_expert[:, None] == jnp.arange(EXPERTS, dtype=jnp.int32)[None, :]).astype(
        jnp.int32
    )
    pair_rank = jnp.sum(jnp.cumsum(one_hot, 0) * one_hot, 1) - 1
    slot_index = pair_expert * CAP + pair_rank
    pair_token = jnp.arange(TOK_DEV * TOPK, dtype=jnp.int32) // TOPK
    send_rows = jnp.zeros((EXPERTS * CAP, D), jnp.bfloat16).at[slot_index].set(mixed_in[pair_token])
    send_rows = send_rows.reshape(ep_count, exp_local, CAP, D)
    received = lax.all_to_all(send_rows, "ep", split_axis=0, concat_axis=0, tiled=True)
    gate_pre = jnp.einsum("secd,edf->secf", received, w_gate, preferred_element_type=jnp.float32)
    up_pre = jnp.einsum("secd,edf->secf", received, w_up, preferred_element_type=jnp.float32)
    activation = (jax.nn.silu(gate_pre) * up_pre).astype(jnp.bfloat16)
    expert_out = jnp.einsum(
        "secf,efd->secd", activation, w_down, preferred_element_type=jnp.float32
    ).astype(jnp.bfloat16)
    expert_out, gate_pre, up_pre, activation, received = (
        expert_out,
        gate_pre,
        up_pre,
        activation,
        received,
    )
    returned = lax.all_to_all(expert_out, "ep", split_axis=0, concat_axis=0, tiled=True).reshape(
        EXPERTS * CAP, D
    )
    pair_out = returned[slot_index].astype(jnp.float32).reshape(TOK_DEV, TOPK, D)
    branch_moe = jnp.sum(gate_vals[:, :, None] * pair_out, 1)
    output = (hidden + branch_moe).astype(jnp.bfloat16)
    local_sums = jnp.stack(
        [
            jnp.sum(inputs * inputs),
            jnp.sum(branch_attn * branch_attn),
            jnp.sum(branch_moe * branch_moe),
        ]
    )
    seq_sums = lax.psum(local_sums, "ep")
    rms_stats = jnp.sqrt(seq_sums / (TOK_DEV * ep_count * D)).reshape(1, 3)
    grad_out = cotangent.astype(jnp.float32)
    grad_gates = jnp.sum(pair_out * grad_out[:, None, :], -1)
    grad_pairs = (
        (gate_vals[:, :, None] * grad_out[:, None, :])
        .astype(jnp.bfloat16)
        .reshape(TOK_DEV * TOPK, D)
    )
    send_grads = jnp.zeros((EXPERTS * CAP, D), jnp.bfloat16).at[slot_index].set(grad_pairs)
    send_grads = send_grads.reshape(ep_count, exp_local, CAP, D)
    grad_received = lax.all_to_all(send_grads, "ep", split_axis=0, concat_axis=0, tiled=True)
    grad_activation = jnp.einsum(
        "secd,efd->secf", grad_received, w_down, preferred_element_type=jnp.float32
    )
    grad_down = jnp.einsum(
        "secf,secd->efd", activation, grad_received, preferred_element_type=jnp.float32
    )
    sig_gate = jax.nn.sigmoid(gate_pre)
    grad_gate_pre = (
        grad_activation * up_pre * sig_gate * (1.0 + gate_pre * (1.0 - sig_gate))
    ).astype(jnp.bfloat16)
    grad_up_pre = (grad_activation * gate_pre * sig_gate).astype(jnp.bfloat16)
    grad_gate_w = jnp.einsum(
        "secd,secf->edf", received, grad_gate_pre, preferred_element_type=jnp.float32
    )
    grad_up_w = jnp.einsum(
        "secd,secf->edf", received, grad_up_pre, preferred_element_type=jnp.float32
    )
    grad_inputs = (
        jnp.einsum("secf,edf->secd", grad_gate_pre, w_gate, preferred_element_type=jnp.float32)
        + jnp.einsum("secf,edf->secd", grad_up_pre, w_up, preferred_element_type=jnp.float32)
    ).astype(jnp.bfloat16)
    grad_back = lax.all_to_all(grad_inputs, "ep", split_axis=0, concat_axis=0, tiled=True).reshape(
        EXPERTS * CAP, D
    )
    grad_mixed = jnp.sum(grad_back[slot_index].astype(jnp.float32).reshape(TOK_DEV, TOPK, D), 1)
    spread = jnp.sum(chosen * grad_gates[:, :, None], 1)
    grad_logits = (
        route_probs * (spread - jnp.sum(route_probs * spread, -1, keepdims=True))
    ).astype(jnp.bfloat16)
    router_grad = jnp.einsum("td,te->de", mixed_in, grad_logits, preferred_element_type=jnp.float32)
    grad_mixed = grad_mixed + jnp.einsum(
        "te,de->td", grad_logits, router_full, preferred_element_type=jnp.float32
    )
    grad_hid_norm, moe_gain_grad = norm_back(grad_mixed, hidden, moe_inv, moe_scale)
    grad_hidden = grad_out + grad_hid_norm
    grad_branch = grad_hidden.astype(jnp.bfloat16)
    output_grad = jnp.einsum(
        "td,tf->df", attended16, grad_branch, preferred_element_type=jnp.float32
    )
    grad_attended = jnp.einsum(
        "tf,df->td", grad_branch, output_full, preferred_element_type=jnp.float32
    ).astype(jnp.bfloat16)
    grad_attended = grad_attended.reshape(TOK_DEV, HEADS, HD)
    row_delta = jnp.transpose(jnp.sum(grad_attended.astype(jnp.float32) * attn_float, -1), (1, 0))[
        :, :, None
    ]
    gathered_keys, gathered_values = (
        lax.all_gather(keys16, "ep", axis=0, tiled=True),
        lax.all_gather(values16, "ep", axis=0, tiled=True),
    )
    total_rows = gathered_keys.shape[0]
    blk_rows = math.gcd(total_rows, 1024)
    last_query_block = positions[-1] // BLOCK

    def query_step(grad_now, block_num):
        begin_row = block_num * blk_rows

        def query_compute(grad_cur):
            key_blk = lax.dynamic_slice_in_dim(gathered_keys, begin_row, blk_rows, 0).reshape(
                blk_rows, HEADS, HD
            )
            value_blk = lax.dynamic_slice_in_dim(gathered_values, begin_row, blk_rows, 0).reshape(
                blk_rows, HEADS, HD
            )
            key_pos = begin_row + jnp.arange(blk_rows, dtype=jnp.int32)
            prob_vals, grad_scores = score_grads(
                queries16, grad_attended, row_delta, log_sum, positions, key_blk, value_blk, key_pos
            )
            return (
                grad_cur
                + jnp.einsum(
                    "hqk,khd->qhd", grad_scores, key_blk, preferred_element_type=jnp.float32
                )
                * score_scale
            )

        def query_passing(grad_cur):
            return grad_cur

        return (
            lax.cond(
                begin_row // BLOCK <= last_query_block, query_compute, query_passing, grad_now
            ),
            None,
        )

    grad_queries, unused = lax.scan(
        query_step,
        jnp.zeros((TOK_DEV, HEADS, HD), jnp.float32),
        jnp.arange(total_rows // blk_rows, dtype=jnp.int32),
    )
    all_queries, all_grad_att = (
        lax.all_gather(queries16, "ep", axis=0, tiled=True),
        lax.all_gather(grad_attended, "ep", axis=0, tiled=True),
    )
    all_delta, all_log_sum = (
        lax.all_gather(row_delta, "ep", axis=1, tiled=True),
        lax.all_gather(log_sum, "ep", axis=1, tiled=True),
    )
    query_rows = all_queries.shape[0]
    query_blk_rows = math.gcd(query_rows, 1024)
    own_keys = keys16.reshape(TOK_DEV, HEADS, HD)
    own_values = values16.reshape(TOK_DEV, HEADS, HD)
    first_key_block = positions[0] // BLOCK

    def key_step(grads_now, block_num):
        begin_row = block_num * query_blk_rows

        def key_compute(grads_cur):
            query_blk = lax.dynamic_slice_in_dim(all_queries, begin_row, query_blk_rows, 0)
            grad_att_blk = lax.dynamic_slice_in_dim(all_grad_att, begin_row, query_blk_rows, 0)
            delta_blk = lax.dynamic_slice_in_dim(all_delta, begin_row, query_blk_rows, 1)
            log_blk = lax.dynamic_slice_in_dim(all_log_sum, begin_row, query_blk_rows, 1)
            query_pos = begin_row + jnp.arange(query_blk_rows, dtype=jnp.int32)
            prob_vals, grad_scores = score_grads(
                query_blk,
                grad_att_blk,
                delta_blk,
                log_blk,
                query_pos,
                own_keys,
                own_values,
                positions,
            )
            key_part = (
                jnp.einsum(
                    "hqk,qhd->khd", grad_scores, query_blk, preferred_element_type=jnp.float32
                )
                * score_scale
            )
            value_part = jnp.einsum(
                "hqk,qhd->khd",
                prob_vals.astype(jnp.bfloat16),
                grad_att_blk,
                preferred_element_type=jnp.float32,
            )
            return (grads_cur[0] + key_part, grads_cur[1] + value_part)

        def key_passing(grads_cur):
            return grads_cur

        return (
            lax.cond(
                (begin_row + query_blk_rows - 1) // BLOCK >= first_key_block,
                key_compute,
                key_passing,
                grads_now,
            ),
            None,
        )

    key_start = (
        jnp.zeros((TOK_DEV, HEADS, HD), jnp.float32),
        jnp.zeros((TOK_DEV, HEADS, HD), jnp.float32),
    )
    key_value_grads, unused = lax.scan(
        key_step, key_start, jnp.arange(query_rows // query_blk_rows, dtype=jnp.int32)
    )
    grad_keys16 = key_value_grads[0].astype(jnp.bfloat16)
    grad_values16 = key_value_grads[1].reshape(TOK_DEV, D).astype(jnp.bfloat16)
    grad_keys = lax.optimization_barrier(grad_keys16).astype(jnp.float32)
    grad_queries = lax.optimization_barrier(grad_queries.astype(jnp.bfloat16)).astype(jnp.float32)
    grad_query_rot = rotate_back(grad_queries, cosine, sine_tab).reshape(TOK_DEV, D)
    grad_query_raw, query_gain_grad = norm_back(grad_query_rot, query_raw, query_inv, query_scale)
    grad_query16 = grad_query_raw.astype(jnp.bfloat16)
    grad_key_rot = rotate_back(grad_keys, cosine, sine_tab).reshape(TOK_DEV, D)
    grad_key_raw, key_gain_grad = norm_back(grad_key_rot, key_raw, key_inv, key_scale)
    grad_key16 = grad_key_raw.astype(jnp.bfloat16)
    query_grad = jnp.einsum("td,tf->df", normed, grad_query16, preferred_element_type=jnp.float32)
    key_grad = jnp.einsum("td,tf->df", normed, grad_key16, preferred_element_type=jnp.float32)
    value_grad = jnp.einsum("td,tf->df", normed, grad_values16, preferred_element_type=jnp.float32)
    grad_normed = (
        jnp.einsum("tf,df->td", grad_query16, query_full, preferred_element_type=jnp.float32)
        + jnp.einsum("tf,df->td", grad_key16, key_full, preferred_element_type=jnp.float32)
        + jnp.einsum("tf,df->td", grad_values16, value_full, preferred_element_type=jnp.float32)
    )
    grad_tok_norm, attn_gain_grad = norm_back(grad_normed, inputs, attn_inv, attn_scale)
    tokens_grad = (grad_hidden + grad_tok_norm).astype(jnp.bfloat16)
    dense_sums = (
        lax.psum_scatter(query_grad, ("grp", "ep"), scatter_dimension=0, tiled=True),
        lax.psum_scatter(key_grad, ("grp", "ep"), scatter_dimension=0, tiled=True),
        lax.psum_scatter(value_grad, ("grp", "ep"), scatter_dimension=0, tiled=True),
        lax.psum_scatter(output_grad, ("grp", "ep"), scatter_dimension=0, tiled=True),
        lax.psum_scatter(router_grad, ("grp", "ep"), scatter_dimension=0, tiled=True),
        lax.psum_scatter(attn_gain_grad, ("grp", "ep"), scatter_dimension=0, tiled=True),
        lax.psum_scatter(query_gain_grad, ("grp", "ep"), scatter_dimension=0, tiled=True),
        lax.psum_scatter(key_gain_grad, ("grp", "ep"), scatter_dimension=0, tiled=True),
        lax.psum_scatter(moe_gain_grad, ("grp", "ep"), scatter_dimension=0, tiled=True),
    )
    expert_sums = (
        lax.psum_scatter(
            grad_gate_w.astype(jnp.bfloat16), "grp", scatter_dimension=1, tiled=True
        ).astype(jnp.float32),
        lax.psum_scatter(
            grad_up_w.astype(jnp.bfloat16), "grp", scatter_dimension=1, tiled=True
        ).astype(jnp.float32),
        lax.psum_scatter(
            grad_down.astype(jnp.bfloat16), "grp", scatter_dimension=1, tiled=True
        ).astype(jnp.float32),
    )
    return (
        output,
        tokens_grad,
        dense_sums[0],
        dense_sums[1],
        dense_sums[2],
        dense_sums[3],
        dense_sums[4],
        dense_sums[5],
        dense_sums[6],
        dense_sums[7],
        dense_sums[8],
        expert_sums[0],
        expert_sums[1],
        expert_sums[2],
        rms_stats,
    )


F32 = jnp.float32
BF16 = jnp.bfloat16
EP = ("z", "x", "core")
ALL = ("grp", "z", "x", "core")
PAIR = 2 * TOK_DEV
SLOTS = 2 * CAP
COST = 0.1
SIDES = {16: (4, 2, 2)}


def nt(left, right):
    return lax.dot_general(left, right, (((1,), (1,)), ((), ())), preferred_element_type=F32)


def nn(left, right):
    return lax.dot_general(left, right, (((1,), (0,)), ((), ())), preferred_element_type=F32)


def tn(left, right):
    return lax.dot_general(left, right, (((0,), (0,)), ((), ())), preferred_element_type=F32)


def as_row(column):
    return jnp.broadcast_to(column, (column.shape[0], 128)).T[0:1]


def as_column(row):
    return jnp.broadcast_to(row, (128, row.shape[1])).T


def inv_of(sum_row):
    return as_column(lax.rsqrt(sum_row / D + EPSILON))


def params(mebibytes):
    return pltpu.CompilerParams(vmem_limit_bytes=mebibytes * 1024 * 1024)


def cost(flops, moved):
    return pl.CostEstimate(flops=int(flops * COST), bytes_accessed=int(moved * COST), transcendentals=0)


def whole(*dims):
    return pl.BlockSpec(dims, lambda *_: (0,) * len(dims))


class Order:
    marks = []

    @classmethod
    def mark_of(cls, array):
        for known, mark in cls.marks:
            if known is array:
                return mark
        return array


MARK = (8, 128)


def ordered(kernel, after, specs, **settings):
    after = [Order.mark_of(array) for array in after]
    inputs = len(specs["in_specs"])
    prefetch = specs.pop("num_scalar_prefetch", 0)
    extra = len(after)
    single = not isinstance(specs["out_specs"], list)
    outputs = [specs["out_specs"]] if single else specs["out_specs"]
    shapes = settings.pop("out_shape")
    shapes = [shapes] if single else list(shapes)
    last = prefetch + inputs + extra + len(outputs)

    def body(*refs):
        refs[last][...] = jnp.zeros(MARK, F32)
        kernel(*refs[: prefetch + inputs], *refs[prefetch + inputs + extra : last], *refs[last + 1 :])

    specs["in_specs"] = list(specs["in_specs"]) + [pl.BlockSpec(memory_space=pl.ANY)] * extra
    specs["out_specs"] = outputs + [pl.BlockSpec(MARK, lambda *_: (0, 0))]
    call = pl.pallas_call(
        body,
        grid_spec=pltpu.PrefetchScalarGridSpec(num_scalar_prefetch=prefetch, **specs),
        out_shape=shapes + [jax.ShapeDtypeStruct(MARK, F32)],
        **settings,
    )

    def run(*args):
        *results, mark = call(*args, *after)
        Order.marks.extend((result, mark) for result in results)
        return results[0] if single else results

    return run


ANYWHERE = pl.BlockSpec(memory_space=pl.ANY)


def in_hbm(dims, kind):
    return pltpu.HBM(dims, kind)


BLOCK_SHAPE = (TOK_DEV, D)


def project_kernel(place_ref, own_ref, other_ref, w_ref, gain_ref, *refs):
    normed_ref, qkv_ref, stat_ref = refs[-3:]
    core = place_ref[1]
    for side, tok_ref in ((core, own_ref), (1 - core, other_ref)):
        here = pl.ds(pl.multiple_of(side * TOK_DEV, TOK_DEV), TOK_DEV)
        rows = tok_ref[...].astype(F32)
        inverse = lax.rsqrt(jnp.mean(rows * rows, -1, keepdims=True) + EPSILON)
        normed = (rows * inverse * gain_ref[...]).astype(BF16)
        normed_ref[here, :] = normed
        out = nn(normed, w_ref[...])
        qkv_ref[here, :] = out
        for part in range(2):
            piece = out[:, part * HD : (part + 1) * HD]
            stat_ref[part : part + 1, here] = as_row(jnp.sum(piece * piece, -1, keepdims=True))


def project(chip_core, own, other, w_head, gain_row, buffers, seq, after=()):
    kept = [] if buffers is None else list(buffers)
    return ordered(
        project_kernel,
        after,
        dict(
            num_scalar_prefetch=1,
            grid=(1,),
            in_specs=[whole(TOK_DEV, D), whole(TOK_DEV, D), whole(D, 3 * HD), whole(1, D)]
            + [ANYWHERE] * len(kept),
            out_specs=[
                pl.BlockSpec((PAIR, D), lambda i, s: (s[0], 0)),
                pl.BlockSpec((PAIR, 3 * HD), lambda i, s: (s[0], 0)),
                pl.BlockSpec((2, PAIR), lambda i, s: (0, s[0])),
            ],
        ),
        out_shape=[
            in_hbm((seq, D), BF16),
            in_hbm((seq, 3 * HD), F32),
            jax.ShapeDtypeStruct((2, seq), F32),
        ],
        input_output_aliases={5 + i: i for i in range(len(kept))},
        compiler_params=params(24),
        cost_estimate=cost(2 * PAIR * D * 3 * HD, 10 * PAIR * D),
        name="project",
    )(chip_core, own, other, w_head, gain_row, *kept)


def attend_kernel(
    qkv_ref, stat_ref, gq_ref, gk_ref, cos_ref, sin_ref,
    q_ref, k_ref, v_ref, of_ref, att_ref, lse_ref, vt_ref,
):
    blocks = q_ref.shape[0] // BLOCK
    for i in range(blocks):
        rows = slice(i * BLOCK, (i + 1) * BLOCK)
        cosine, sine = cos_ref[rows, :], sin_ref[rows, :]
        for part, gain_ref, out_ref in ((0, gq_ref, q_ref), (1, gk_ref, k_ref)):
            raw = qkv_ref[rows, part * HD : (part + 1) * HD]
            scaled = raw * inv_of(stat_ref[part : part + 1, rows]) * gain_ref[...]
            turned = scaled * cosine + pltpu.roll(scaled, HD // 2, 1) * sine
            out_ref[rows, :] = turned.astype(BF16)
        value = qkv_ref[rows, 2 * HD :]
        v_ref[rows, :] = value.astype(BF16)
        vt_ref[:, rows] = value.T.astype(BF16)
    for i in range(blocks):
        rows = slice(i * BLOCK, (i + 1) * BLOCK)
        reach = (i + 1) * BLOCK
        scores = nt(k_ref[0:reach, :], q_ref[rows, :]) * HD ** (-0.5)
        top = jnp.max(scores, 0, keepdims=True)
        weights = jnp.exp(scores - top)
        total = jnp.sum(weights, 0, keepdims=True)
        probs = (weights * (1.0 / total)).astype(BF16)
        out = nn(vt_ref[:, 0:reach], probs).T
        of_ref[rows, :] = out
        att_ref[rows, :] = out.astype(BF16)
        lse_ref[:, rows] = top + jnp.log(total)


def attend(qkv, stat, gain_q, gain_k, cosine, sine):
    rows = qkv.shape[0]
    shape = lambda kind: jax.ShapeDtypeStruct((rows, HD), kind)
    return ordered(
        attend_kernel,
        (),
        dict(
            grid=(1,),
            in_specs=[
                whole(rows, 3 * HD), whole(2, rows), whole(1, HD), whole(1, HD), whole(rows, HD), whole(rows, HD),
            ],
            out_specs=[whole(rows, HD)] * 5 + [whole(1, rows)],
            scratch_shapes=[pltpu.VMEM((HD, rows), BF16)],
        ),
        out_shape=[shape(BF16), shape(BF16), shape(BF16), shape(F32), shape(BF16),
                   jax.ShapeDtypeStruct((1, rows), F32)],
        compiler_params=params(48),
        cost_estimate=cost(8 * rows * rows * HD, 10 * rows * 384),
        name="attend",
    )(qkv, stat, gain_q, gain_k, cosine, sine)


def attend_back_kernel(
    q_ref, k_ref, v_ref, do_ref, of_ref, lse_ref, qkv_ref, stat_ref, gq_ref, gk_ref,
    cos_ref, sin_ref, dnq_ref, dnk_ref, dv_ref, means_ref, gains_ref, dk_acc, dv_acc,
):
    blocks = q_ref.shape[0] // BLOCK
    scale = HD ** (-0.5)
    dk_acc[...] = jnp.zeros_like(dk_acc)
    dv_acc[...] = jnp.zeros_like(dv_acc)

    def turn_back(grad, rows, part, gain_ref, out_ref):
        grad = grad.astype(BF16).astype(F32)
        grad = grad * cos_ref[rows, :] - pltpu.roll(grad, HD // 2, 1) * sin_ref[rows, :]
        raw = qkv_ref[rows, part * HD : (part + 1) * HD]
        out_ref[rows, :] = grad
        means_ref[part : part + 1, rows] = jnp.sum((grad * gain_ref[...] * raw).T, 0, keepdims=True)
        inverse = inv_of(stat_ref[part : part + 1, rows])
        return jnp.sum(grad * raw * inverse, 0, keepdims=True)

    gain_q = jnp.zeros((1, HD), F32)
    gain_k = jnp.zeros((1, HD), F32)
    for i in range(blocks):
        rows = slice(i * BLOCK, (i + 1) * BLOCK)
        reach = (i + 1) * BLOCK
        queries, grads = q_ref[rows, :], do_ref[rows, :]
        delta = jnp.sum((grads.astype(F32) * of_ref[rows, :]).T, 0, keepdims=True)
        scores = nt(k_ref[0:reach, :], queries) * scale
        probs = jnp.exp(scores - lse_ref[:, rows])
        slopes = nt(v_ref[0:reach, :], grads)
        grad_scores = (probs * (slopes - delta)).astype(BF16)
        dv_acc[0:reach, :] += nn(probs.astype(BF16), grads)
        dk_acc[0:reach, :] += nn(grad_scores, queries)
        gain_q += turn_back(tn(grad_scores, k_ref[0:reach, :]) * scale, rows, 0, gq_ref, dnq_ref)
    for i in range(blocks):
        rows = slice(i * BLOCK, (i + 1) * BLOCK)
        dv_ref[rows, :] = dv_acc[rows, :].astype(BF16)
        gain_k += turn_back(dk_acc[rows, :] * scale, rows, 1, gk_ref, dnk_ref)
    gains_ref[0:1, :] = gain_q
    gains_ref[1:2, :] = gain_k


def attend_back(q, k, v, grad, out, lse, qkv, stat, gain_q, gain_k, cosine, sine, after=()):
    rows = q.shape[0]
    shape = lambda kind: jax.ShapeDtypeStruct((rows, HD), kind)
    return ordered(
        attend_back_kernel,
        after,
        dict(
            grid=(1,),
            in_specs=[whole(rows, HD)] * 5
            + [whole(1, rows), whole(rows, 3 * HD), whole(2, rows), whole(1, HD), whole(1, HD)]
            + [whole(rows, HD)] * 2,
            out_specs=[whole(rows, HD)] * 3 + [whole(2, rows), whole(2, HD)],
            scratch_shapes=[pltpu.VMEM((rows, HD), F32), pltpu.VMEM((rows, HD), F32)],
        ),
        out_shape=[shape(F32), shape(F32), shape(BF16),
                   jax.ShapeDtypeStruct((2, rows), F32), jax.ShapeDtypeStruct((2, HD), F32)],
        compiler_params=params(48),
        cost_estimate=cost(20 * rows * rows * HD, 20 * rows * 384),
        name="attend_back",
    )(q, k, v, grad, out, lse, qkv, stat, gain_q, gain_k, cosine, sine)


def finish_kernel(
    dnq_ref, dnk_ref, dv_ref, qkv_ref, stat_ref, means_ref, gq_ref, gk_ref, out_ref
):
    for part, dn_ref, g_ref in ((0, dnq_ref, gq_ref), (1, dnk_ref, gk_ref)):
        raw = qkv_ref[:, part * HD : (part + 1) * HD]
        inverse = inv_of(stat_ref[part : part + 1, :])
        mean = as_column(means_ref[part : part + 1, :] / D)
        grad = inverse * (dn_ref[...] * g_ref[...] - raw * inverse * inverse * mean)
        out_ref[:, part * HD : (part + 1) * HD] = grad.astype(BF16)
    out_ref[:, 2 * HD :] = dv_ref[...]


def finish(dnq, dnk, dv, qkv, stat, means, gain_q, gain_k, after=()):
    rows = dnq.shape[0]
    head = pl.BlockSpec((PAIR, HD), lambda i: (i, 0))
    line = pl.BlockSpec((2, PAIR), lambda i: (0, i))
    full = pl.BlockSpec((PAIR, 3 * HD), lambda i: (i, 0))
    return ordered(
        finish_kernel,
        after,
        dict(
        grid=(rows // PAIR,),
        in_specs=[head, head, head, full, line, line, whole(1, HD), whole(1, HD)],
        out_specs=full,
        ),
        out_shape=jax.ShapeDtypeStruct((rows, 3 * HD), BF16),
        compiler_params=params(24),
        cost_estimate=cost(20 * rows * 3 * HD, 12 * rows * 3 * HD),
        name="finish",
    )(dnq, dnk, dv, qkv, stat, means, gain_q, gain_k)


def sort_cores(core, first, second, own_ref, other_ref, at):
    at = (0, at)

    @pl.when(core == 0)
    def _():
        own_ref[at] = first
        other_ref[at] = second

    @pl.when(core == 1)
    def _():
        own_ref[at] = second
        other_ref[at] = first


def normed_part_kernel(place_ref, a_ref, b_ref, w_ref, own_ref, other_ref):
    for at, g_ref in enumerate((a_ref, b_ref)):
        out = nt(g_ref[...], w_ref[...]).astype(BF16)
        sort_cores(place_ref[4], out[:TOK_DEV], out[TOK_DEV:], own_ref, other_ref, at)


def normed_part(place, grads, w_head, after=()):
    blocks = jax.ShapeDtypeStruct((2, 2, TOK_DEV, D), BF16)
    return ordered(
        normed_part_kernel,
        after,
        dict(
            num_scalar_prefetch=1,
            grid=(2,),
            in_specs=[
                pl.BlockSpec((PAIR, 3 * HD), lambda i, s: (s[2 * i], 0)),
                pl.BlockSpec((PAIR, 3 * HD), lambda i, s: (s[2 * i + 1], 0)),
                whole(D, 3 * HD),
            ],
            out_specs=[pl.BlockSpec((1, 2, TOK_DEV, D), lambda i, s: (i, 0, 0, 0))] * 2,
        ),
        out_shape=[blocks, blocks],
        compiler_params=params(24),
        cost_estimate=cost(8 * PAIR * D * 3 * HD, 16 * PAIR * D),
        name="normed_part",
    )(place, grads, grads, w_head)


def dw_kernel(normed_ref, grad_ref, out_ref):
    @pl.when(pl.program_id(0) == 0)
    def _():
        out_ref[...] = jnp.zeros_like(out_ref)

    out_ref[...] += tn(normed_ref[...], grad_ref[...])


def dw_product(normed, grads, after=()):
    rows = normed.shape[0]
    return ordered(
        dw_kernel,
        after,
        dict(
            grid=(rows // 512,),
            in_specs=[
                pl.BlockSpec((512, D), lambda i: (i, 0)),
                pl.BlockSpec((512, 3 * HD), lambda i: (i, 0)),
            ],
            out_specs=whole(D, 3 * HD),
        ),
        out_shape=jax.ShapeDtypeStruct((D, 3 * HD), F32),
        compiler_params=params(32),
        cost_estimate=cost(2 * rows * D * 3 * HD, 3 * rows * D),
        name="dw_product",
    )(normed, grads)


def picks(slots, dtype):
    shape = (SLOTS, slots.shape[1])
    numbers = lax.broadcasted_iota(jnp.int32, shape, 0)
    return [(numbers == slots[j : j + 1, :]).astype(dtype) for j in range(slots.shape[0])]


def pick_matrix(slots):
    return jnp.concatenate(picks(slots, F32), 0).astype(BF16)


def dispatch_kernel(place_ref, own_ref, other_ref, own_slot, other_slot, *refs):
    out_ref, column_ref, stack_ref = refs[-3:]
    stack_ref[0] = own_ref[...]
    core = place_ref[1]
    lanes = pl.ds(pl.multiple_of(place_ref[2] * HD, HD), HD)
    out = nn(pick_matrix(own_slot[0]), own_ref[...])
    out = (out + nn(pick_matrix(other_slot[0]), other_ref[...])).astype(BF16)
    for j in range(out_ref.shape[0]):
        out_ref[j] = out[j * SLOTS : (j + 1) * SLOTS]
    for side, row_ref in ((core, own_ref), (1 - core, other_ref)):
        column_ref[pl.ds(pl.multiple_of(side * TOK_DEV, TOK_DEV), TOK_DEV), :] = row_ref[:, lanes]


def dispatch(place, own, other, slots, buffers, after=()):
    blocks, local, _ = slots.shape
    kept = [] if buffers is None else list(buffers)
    return ordered(
        dispatch_kernel,
        after,
        dict(
            num_scalar_prefetch=1,
            grid=(1,),
            in_specs=[
                whole(*BLOCK_SHAPE),
                whole(*BLOCK_SHAPE),
                pl.BlockSpec((1, local, TOK_DEV), lambda i, s: (2 * s[0] + s[1], 0, 0)),
                pl.BlockSpec((1, local, TOK_DEV), lambda i, s: (2 * s[0] + 1 - s[1], 0, 0)),
            ]
            + [ANYWHERE] * len(kept),
            out_specs=[
                pl.BlockSpec((local, SLOTS, D), lambda i, s: (0, s[0], 0)),
                pl.BlockSpec((PAIR, HD), lambda i, s: (s[0], 0)),
                pl.BlockSpec((1, TOK_DEV, D), lambda i, s: (s[0], 0, 0)),
            ],
        ),
        out_shape=[
            in_hbm((local, blocks // 2 * SLOTS, D), BF16),
            in_hbm((blocks * TOK_DEV, HD), BF16),
            in_hbm((blocks // 2, TOK_DEV, D), BF16),
        ],
        input_output_aliases={5 + i: i for i in range(len(kept))},
        compiler_params=params(24),
        cost_estimate=cost(2 * PAIR * D * local * SLOTS, 4 * PAIR * D),
        name="dispatch",
    )(place, own, other, slots, slots, *kept)


def stack_kernel(place_ref, row_ref, out_ref):
    out_ref[0] = row_ref[0, 0]


def stack_of_core(core, rows, after=()):
    chips = rows.shape[0]
    return ordered(
        stack_kernel,
        after,
        dict(
            num_scalar_prefetch=1,
            grid=(chips,),
            in_specs=[pl.BlockSpec((1, 1, TOK_DEV, D), lambda i, s: (i, s[0], 0, 0))],
            out_specs=pl.BlockSpec((1, TOK_DEV, D), lambda i, s: (i, 0, 0)),
        ),
        out_shape=in_hbm((chips, TOK_DEV, D), BF16),
        compiler_params=params(16),
        cost_estimate=cost(0, 4 * chips * TOK_DEV * D),
        name="stack_of_core",
    )(core.reshape(1), rows)


def stack_dispatch_kernel(place_ref, own_ref, other_ref, own_slot, other_slot, out_ref):
    out = nn(pick_matrix(own_slot[0]), own_ref[0])
    out = (out + nn(pick_matrix(other_slot[0]), other_ref[0])).astype(BF16)
    for j in range(out_ref.shape[0]):
        out_ref[j] = out[j * SLOTS : (j + 1) * SLOTS]


def stack_dispatch(places, stacks, slots, after=()):
    chips = stacks.shape[1]
    blocks, local, _ = slots.shape
    row_shape = (None, 1, TOK_DEV, D)
    return ordered(
        stack_dispatch_kernel,
        after,
        dict(
            num_scalar_prefetch=1,
            grid=(chips,),
            in_specs=[
                pl.BlockSpec(row_shape, lambda i, s: (2 - 2 * s[chips + 1] + s[chips], i, 0, 0)),
                pl.BlockSpec(row_shape, lambda i, s: (3 - 2 * s[chips + 1] - s[chips], i, 0, 0)),
                pl.BlockSpec((1, local, TOK_DEV), lambda i, s: (2 * s[i] + s[chips], 0, 0)),
                pl.BlockSpec((1, local, TOK_DEV), lambda i, s: (2 * s[i] + 1 - s[chips], 0, 0)),
            ],
            out_specs=pl.BlockSpec((local, SLOTS, D), lambda i, s: (0, s[i], 0)),
        ),
        out_shape=in_hbm((local, blocks // 2 * SLOTS, D), BF16),
        compiler_params=params(24),
        cost_estimate=cost(2 * chips * PAIR * D * local * SLOTS, 4 * chips * PAIR * D),
        name="stack_dispatch",
    )(places, stacks, stacks, slots, slots)


def plain_dispatch_kernel(row_ref, slot_ref, out_ref):
    out = sum(nn(pick_matrix(slot_ref[i]), row_ref[i]) for i in range(2)).astype(BF16)
    for j in range(out_ref.shape[0]):
        out_ref[j] = out[j * SLOTS : (j + 1) * SLOTS]


def plain_dispatch(rows, slots, after=(), part=0, parts=1):
    blocks, local, _ = slots.shape
    rows = rows.reshape(blocks, parts, TOK_DEV, D)
    return ordered(
        plain_dispatch_kernel,
        after,
        dict(
            grid=(blocks // 2,),
            in_specs=[
                pl.BlockSpec((2, None, TOK_DEV, D), lambda i: (i, part, 0, 0)),
                pl.BlockSpec((2, local, TOK_DEV), lambda i: (i, 0, 0)),
            ],
            out_specs=pl.BlockSpec((local, SLOTS, D), lambda i: (0, i, 0)),
        ),
        out_shape=in_hbm((local, blocks // 2 * SLOTS, D), BF16),
        compiler_params=params(24),
        cost_estimate=cost(2 * blocks * TOK_DEV * D * local * SLOTS, 4 * blocks * TOK_DEV * D),
        name="plain_dispatch",
    )(rows, slots)


def combine_chip(row_ref, slot_ref):
    rows = jnp.concatenate([row_ref[j] for j in range(row_ref.shape[0])], 0)
    return [tn(pick_matrix(slot_ref[i]), rows).astype(BF16) for i in range(2)]


def combine_kernel(row_ref, slot_ref, out_ref):
    first, second = combine_chip(row_ref, slot_ref)
    out_ref[:TOK_DEV] = first
    out_ref[TOK_DEV:] = second


def combine(slot_rows, slots, after=()):
    blocks, local, _ = slots.shape
    rows = blocks * TOK_DEV
    return ordered(
        combine_kernel,
        after,
        dict(
            grid=(blocks // 2,),
            in_specs=[
                pl.BlockSpec((local, SLOTS, D), lambda i: (0, i, 0)),
                pl.BlockSpec((2, local, TOK_DEV), lambda i: (i, 0, 0)),
            ],
            out_specs=pl.BlockSpec((PAIR, D), lambda i: (i, 0)),
        ),
        out_shape=jax.ShapeDtypeStruct((rows, D), BF16),
        compiler_params=params(24),
        cost_estimate=cost(2 * rows * D * local * SLOTS, 4 * rows * D),
        name="combine",
    )(slot_rows, slots)


def combine_part_kernel(place_ref, a_ref, b_ref, a_slot, b_slot, own_ref, other_ref):
    for at, (row_ref, slot_ref) in enumerate(((a_ref, a_slot), (b_ref, b_slot))):
        first, second = combine_chip(row_ref, slot_ref)
        sort_cores(place_ref[4], first, second, own_ref, other_ref, at)


def chip_specs(slot_rows, slots):
    local, width = slots.shape[1], slot_rows.shape[2]
    rows = [
        pl.BlockSpec((local, SLOTS, width), lambda i, s, n=n: (0, s[2 * i + n], 0)) for n in (0, 1)
    ]
    spots = [
        pl.BlockSpec((2, local, TOK_DEV), lambda i, s, n=n: (s[2 * i + n], 0, 0)) for n in (0, 1)
    ]
    return rows + spots


def combine_part(place, slot_rows, slots, after=()):
    local, width = slots.shape[1], slot_rows.shape[2]
    shape = jax.ShapeDtypeStruct((2, 2, TOK_DEV, width), BF16)
    return ordered(
        combine_part_kernel,
        after,
        dict(
            num_scalar_prefetch=1,
            grid=(2,),
            in_specs=chip_specs(slot_rows, slots),
            out_specs=[pl.BlockSpec((1, 2, TOK_DEV, width), lambda i, s: (i, 0, 0, 0))] * 2,
        ),
        out_shape=[shape, shape],
        compiler_params=params(24),
        cost_estimate=cost(4 * PAIR * D * local * SLOTS, 8 * PAIR * D),
        name="combine_part",
    )(place, slot_rows, slot_rows, slots, slots)


def slope_kernel(g_ref, wd_ref, out_ref):
    out_ref[0] = nt(g_ref[0], wd_ref[0])


def slopes(grads, w_down, after=()):
    local, count, _ = grads.shape
    hidden = w_down.shape[1]
    chunk = hidden // 2
    return ordered(
        slope_kernel,
        after,
        dict(
            grid=(local, 2),
            in_specs=[
                pl.BlockSpec((1, count, D), lambda j, f: (j, 0, 0)),
                pl.BlockSpec((1, chunk, D), lambda j, f: (j, f, 0)),
            ],
            out_specs=pl.BlockSpec((1, count, chunk), lambda j, f: (j, 0, f)),
        ),
        out_shape=in_hbm((local, count, hidden), F32),
        compiler_params=params(24),
        cost_estimate=cost(2 * local * count * hidden * D, 2 * local * hidden * D),
        name="slopes",
    )(grads, w_down)


def expert_kernel(first_ref, x_ref, h_ref, wg_ref, wu_ref, wr_ref, *rest, full, offset):
    if full:
        (act_ref, dg_ref, du_ref, gate_ref, z_ref, z_s, dp_s) = rest
    else:
        (act_ref, dg_ref, du_ref, gate_ref) = rest
    step, steps = pl.program_id(1), pl.num_programs(1)
    rows = x_ref[0]

    @pl.when(step == 0)
    def _():
        logits = nn(rows, wr_ref[...])
        lane = lax.broadcasted_iota(jnp.int32, logits.shape, 1)
        logits = jnp.where(lane < EXPERTS, logits, NEG_FILL)
        powers = jnp.exp(logits - jnp.max(logits, -1, keepdims=True))
        mine = jnp.where(lane == first_ref[0] + offset + pl.program_id(0), powers, 0.0)
        gate = jnp.sum(mine, -1, keepdims=True) / jnp.sum(powers, -1, keepdims=True)
        gate_ref[0] = jnp.broadcast_to(gate, gate_ref.shape[1:])
        if full:
            z_s[...] = jnp.zeros_like(z_s)
            dp_s[...] = jnp.zeros_like(dp_s)

    gate = gate_ref[0, :, 0:1]
    gate_pre = nn(rows, wg_ref[0])
    up_pre = nn(rows, wu_ref[0])
    slope = h_ref[0]
    sig = jax.nn.sigmoid(gate_pre)
    silu = gate_pre * sig
    act = (silu * up_pre).astype(BF16)
    grad_act = slope * gate
    grad_gate = (grad_act * up_pre * sig * (1.0 + gate_pre * (1.0 - sig))).astype(BF16)
    grad_up = (grad_act * silu).astype(BF16)
    act_ref[0] = act
    dg_ref[0] = grad_gate
    du_ref[0] = grad_up
    if full:
        dp_s[...] += jnp.broadcast_to(
            jnp.sum(act.astype(F32) * slope, -1, keepdims=True), dp_s.shape
        )
        z_s[...] += nt(grad_gate, wg_ref[0]) + nt(grad_up, wu_ref[0])

        @pl.when(step == steps - 1)
        def _():
            z_ref[0, :, :D] = z_s[...].astype(BF16)
            lane = lax.broadcasted_iota(jnp.int32, dp_s.shape, 1)
            mine = first_ref[0] + offset + pl.program_id(0)
            high = dp_s[...].astype(BF16).astype(F32)
            parts = jnp.where(lane == mine, high, 0.0)
            parts = jnp.where(lane == mine + EXPERTS, dp_s[...] - high, parts)
            z_ref[0, :, D:] = parts.astype(BF16)


def experts(first, rows, slope, w_gate, w_up, router, full, only=None, after=()):
    local, count, _ = rows.shape
    offset, number = (0, local) if only is None else only
    hidden = w_gate.shape[2]
    chunk = hidden // 2
    row_spec = pl.BlockSpec((1, count, D), lambda j, f, s: (j, 0, 0))
    mid_spec = pl.BlockSpec((1, count, chunk), lambda j, f, s: (j, 0, f))
    lane_spec = pl.BlockSpec((1, count, HD), lambda j, f, s: (j, 0, 0))
    in_w = pl.BlockSpec((1, D, chunk), lambda j, f, s: (j + offset, 0, f))
    mid_shape = in_hbm((number, count, hidden), BF16)
    lane_shape = jax.ShapeDtypeStruct((number, count, HD), F32)
    out_specs = [mid_spec, mid_spec, mid_spec, lane_spec]
    out_shape = [mid_shape, mid_shape, mid_shape, lane_shape]
    scratch = []
    if full:
        out_specs += [pl.BlockSpec((1, count, D + HD), lambda j, f, s: (j, 0, 0))]
        out_shape += [in_hbm((number, count, D + HD), BF16)]
        scratch += [pltpu.VMEM((count, D), F32), pltpu.VMEM((count, HD), F32)]
    unit = 2 * number * count * hidden * D
    return ordered(
        functools.partial(expert_kernel, full=full, offset=offset),
        after,
        dict(
            num_scalar_prefetch=1,
            grid=(number, 2),
            in_specs=[
                pl.BlockSpec((1, count, D), lambda j, f, s: (j + offset, 0, 0)),
                pl.BlockSpec((1, count, chunk), lambda j, f, s: (j + offset, 0, f)),
                in_w,
                in_w,
                pl.BlockSpec((D, HD), lambda j, f, s: (0, 0)),
            ],
            out_specs=out_specs,
            scratch_shapes=scratch,
        ),
        out_shape=out_shape,
        compiler_params=params(56),
        cost_estimate=cost((4 if full else 2) * unit, 4 * number * hidden * D + 8 * number * count * D),
        name="experts_full" if full else "experts_half",
    )(first, rows, slope, w_gate, w_up, router)


def down_kernel(act_ref, gate_ref, wd_ref, out_ref):
    out_ref[0] = (nn(act_ref[0], wd_ref[0]) * gate_ref[0, :, 0:1]).astype(BF16)


def down(act, gate, w_down, after=()):
    local, count, hidden = act.shape
    chunk = D // 2
    return ordered(
        down_kernel,
        after,
        dict(
            grid=(local, 2),
            in_specs=[
                pl.BlockSpec((1, count, hidden), lambda j, f: (j, 0, 0)),
                pl.BlockSpec((1, count, HD), lambda j, f: (j, 0, 0)),
                pl.BlockSpec((1, hidden, chunk), lambda j, f: (j, 0, f)),
            ],
            out_specs=pl.BlockSpec((1, count, chunk), lambda j, f: (j, 0, f)),
        ),
        out_shape=jax.ShapeDtypeStruct((local, count, D), BF16),
        compiler_params=params(24),
        cost_estimate=cost(2 * local * count * hidden * D, 2 * local * hidden * D),
        name="down",
    )(act, gate, w_down)


def weights_kernel(
    half_ref, xa, xb, dga, dgb, dua, dub, aa, ab, ga, gb, gate_a, gate_b, *refs
):
    gate_ref, up_ref, down_ref = refs[-3:]
    rows = jnp.concatenate([xa[0], xb[0]], 0)
    gate_ref[0] = tn(rows, jnp.concatenate([dga[0], dgb[0]], 0))
    up_ref[0] = tn(rows, jnp.concatenate([dua[0], dub[0]], 0))
    grad_a = (ga[0].astype(F32) * gate_a[0, :, 0:1]).astype(BF16)
    grad_b = (gb[0].astype(F32) * gate_b[0, :, 0:1]).astype(BF16)
    down_ref[0] = tn(
        jnp.concatenate([aa[0], ab[0]], 0), jnp.concatenate([grad_a, grad_b], 0)
    )


def weight_grads(only, half, x_pair, dg_pair, du_pair, act_pair, g_pair, gate_pair, buffers, after=()):
    local, count, _ = x_pair[0].shape
    start, number = only
    hidden = dg_pair[0].shape[2]
    kept = [] if buffers is None else list(buffers)
    chunk = hidden // 2

    def spec(width, by_half, single):
        at = 0 if single else start
        if by_half is None:
            return pl.BlockSpec((1, count, width), lambda j, f, s: (j + at, 0, 0))
        if by_half:
            return pl.BlockSpec((1, count, width), lambda j, f, s: (j + at, 0, s[0]))
        return pl.BlockSpec((1, count, width), lambda j, f, s: (j + at, 0, f))

    in_specs = [
        spec(D // 2, True, False), spec(D // 2, True, False),
        spec(chunk, False, False), spec(chunk, False, True),
        spec(chunk, False, False), spec(chunk, False, True),
        spec(chunk, True, False), spec(chunk, True, True),
        spec(D // 2, False, False), spec(D // 2, False, False),
        spec(HD, None, False), spec(HD, None, True),
    ]
    unit = 2 * number * count * hidden * D
    return ordered(
        weights_kernel,
        after,
        dict(
            num_scalar_prefetch=1,
            grid=(number, 2),
            in_specs=in_specs + [ANYWHERE] * len(kept),
            out_specs=[
                pl.BlockSpec((1, D // 2, chunk), lambda j, f, s: (j + start, 0, f)),
                pl.BlockSpec((1, D // 2, chunk), lambda j, f, s: (j + start, 0, f)),
                pl.BlockSpec((1, chunk, D // 2), lambda j, f, s: (j + start, 0, f)),
            ],
        ),
        out_shape=[
            in_hbm((local, D // 2, hidden), F32),
            in_hbm((local, D // 2, hidden), F32),
            in_hbm((local, hidden // 2, D), F32),
        ],
        input_output_aliases={13 + i: i for i in range(len(kept))},
        compiler_params=params(56),
        cost_estimate=cost(3 * unit, 6 * number * hidden * D + 8 * number * count * D),
        name="weight_grads",
    )(half, *x_pair, *dg_pair, *du_pair, *act_pair, *g_pair, *gate_pair, *kept)


def softmax_of(mixed, router):
    logits = nn(mixed, router)
    lane = lax.broadcasted_iota(jnp.int32, logits.shape, 1)
    logits = jnp.where(lane < EXPERTS, logits, NEG_FILL)
    powers = jnp.exp(logits - jnp.max(logits, -1, keepdims=True))
    return powers / jnp.sum(powers, -1, keepdims=True)


def pair_kernel(group_ref, near_ref, far_ref, out_ref):
    out_ref[group_ref[0]] = near_ref[...]
    out_ref[1 - group_ref[0]] = far_ref[...]


def pair_up(group, near, far, after=()):
    return ordered(
        pair_kernel,
        after,
        dict(
            num_scalar_prefetch=1,
            grid=(1,),
            in_specs=[whole(*near.shape)] * 2,
            out_specs=whole(2, *near.shape),
        ),
        out_shape=jax.ShapeDtypeStruct((2,) + near.shape, near.dtype),
        compiler_params=params(16),
        name="pair_up",
    )(group.reshape(1).astype(jnp.int32), near, far)


def out_kernel(att_ref, w_ref, tok_ref, gain_ref, hidden_ref, mixed_ref, sums_ref, acc_ref):
    step, steps = pl.program_id(0), pl.num_programs(0)
    heads = jnp.concatenate([att_ref[i] for i in range(att_ref.shape[0])], 1)
    part = nn(heads, w_ref[...].reshape(heads.shape[1], D))

    @pl.when(step == 0)
    def _():
        acc_ref[...] = part

    @pl.when(step > 0)
    def _():
        acc_ref[...] += part

    @pl.when(step == steps - 1)
    def _():
        branch = acc_ref[...]
        hidden = tok_ref[...].astype(F32) + branch
        hidden_ref[...] = hidden
        mixed_ref[...] = (hidden * inv_rms(hidden) * gain_ref[...]).astype(BF16)
        total = jnp.sum(jnp.sum(branch * branch, -1, keepdims=True), 0, keepdims=True)
        sums_ref[...] = jnp.broadcast_to(total, sums_ref.shape)


def out_rows_spec(weights, heads):
    members, groups, rows, _ = weights.shape
    count = heads * HD // rows
    steps = members // count
    return pl.BlockSpec((count, None, rows, D), lambda i: (i % steps, i // steps, 0, 0))


def project_out(att, weights, tokens, gain_row, after=()):
    chunk = 4
    return ordered(
        out_kernel,
        after,
        dict(
        grid=(HEADS // chunk,),
        in_specs=[
            pl.BlockSpec((chunk, TOK_DEV, HD), lambda i, *_: (i, 0, 0)),
            out_rows_spec(weights, chunk),
            whole(*BLOCK_SHAPE),
            whole(1, D),
        ],
        out_specs=[whole(*BLOCK_SHAPE), whole(*BLOCK_SHAPE), whole(1, HD)],
        scratch_shapes=[pltpu.VMEM(BLOCK_SHAPE, F32)],
        ),
        out_shape=[
            jax.ShapeDtypeStruct(BLOCK_SHAPE, F32),
            jax.ShapeDtypeStruct(BLOCK_SHAPE, BF16),
            jax.ShapeDtypeStruct((1, HD), F32),
        ],
        compiler_params=params(24),
        cost_estimate=cost(2 * TOK_DEV * D * D, 2 * D * D),
        name="project_out",
    )(att, weights, tokens, gain_row)


def token_back_kernel(
    a, b, c, d, e, mixed_ref, hidden_ref, cot_ref, router_ref, gain_ref,
    grad_ref, wide_ref,
):
    probs = softmax_of(mixed_ref[...], router_ref[...])
    grad = sum(ref[...].astype(F32) for ref in (a, b, c, d, e))
    dp = grad[:, D : D + HD] + pltpu.roll(grad[:, D : D + HD], EXPERTS, 1)
    logits = (probs * (dp - jnp.sum(probs * dp, -1, keepdims=True))).astype(BF16)
    grad = grad[:, :D] + nt(logits, router_ref[...])
    hidden = hidden_ref[...]
    inverse = inv_rms(hidden)
    scaled = grad * gain_ref[...]
    mean = jnp.mean(scaled * hidden, -1, keepdims=True)
    result = cot_ref[...].astype(F32) + inverse * (scaled - hidden * inverse * inverse * mean)
    grad_ref[...] = result
    wide_ref[:, :D] = result.astype(BF16)
    wide_ref[:, D : D + HD] = logits
    wide_ref[:, D + HD :] = jnp.zeros((TOK_DEV, HD), BF16)
    part = jnp.sum(grad * hidden * inverse, 0, keepdims=True)
    high = part.astype(BF16).astype(F32)
    rows = lax.broadcasted_iota(jnp.int32, (2 * HEADS, HD), 0)
    spread = jnp.zeros((2 * HEADS, HD), F32)
    for i in range(HEADS):
        lanes = slice(i * HD, (i + 1) * HD)
        spread = jnp.where(rows == i, high[:, lanes], spread)
        spread = jnp.where(rows == HEADS + i, part[:, lanes] - high[:, lanes], spread)
    wide_ref[: 2 * HEADS, D + HD :] = spread.astype(BF16)


def term_specs(terms):
    specs, arrays = [], []
    for term in terms:
        if isinstance(term, tuple):
            arrays.append(term[0])
            shape = (None, None) + term[0].shape[2:]
            specs.append(pl.BlockSpec(shape, lambda i, n=term[1]: n + (0, 0)))
        else:
            arrays.append(term)
            specs.append(whole(*term.shape))
    return specs, arrays


def token_back(terms, mixed, hidden, cotangent, router, gain_row, after=()):
    specs, arrays = term_specs(terms)
    return ordered(
        token_back_kernel,
        after,
        dict(
            grid=(1,),
            in_specs=specs
            + [whole(*BLOCK_SHAPE)] * 3
            + [whole(D, HD), whole(1, D)],
            out_specs=[whole(*BLOCK_SHAPE), whole(TOK_DEV, D + 2 * HD)],
        ),
        out_shape=[
            jax.ShapeDtypeStruct(BLOCK_SHAPE, F32),
            jax.ShapeDtypeStruct((TOK_DEV, D + 2 * HD), BF16),
        ],
        compiler_params=params(40),
        cost_estimate=cost(30 * TOK_DEV * D, 20 * TOK_DEV * D),
        name="token_back",
    )(*arrays, mixed, hidden, cotangent, router, gain_row)


def out_back_kernel(grad_ref, w_ref, out_ref):
    out = nt(grad_ref[...], w_ref[...].reshape(-1, D)).astype(BF16)
    for i in range(out_ref.shape[0]):
        out_ref[i] = out[:, i * HD : (i + 1) * HD]


def out_back(wide, weights):
    chunk = 4
    return ordered(
        out_back_kernel,
        (),
        dict(
        grid=(HEADS // chunk,),
        in_specs=[
            pl.BlockSpec(BLOCK_SHAPE, lambda i: (0, 0)),
            out_rows_spec(weights, chunk),
        ],
        out_specs=pl.BlockSpec((chunk, TOK_DEV, HD), lambda i: (i, 0, 0)),
        ),
        out_shape=jax.ShapeDtypeStruct((HEADS, TOK_DEV, HD), BF16),
        compiler_params=params(24),
        cost_estimate=cost(2 * TOK_DEV * D * D, 2 * D * D),
        name="out_back",
    )(wide, weights)


def tokens_grad_kernel(
    a, b, c, d, e, tok_ref, gain_ref, grad_ref, out_ref
):
    grad = sum(ref[...].astype(F32) for ref in (a, b, c, d, e))
    inputs = tok_ref[...].astype(F32)
    inverse = inv_rms(inputs)
    scaled = grad * gain_ref[...]
    mean = jnp.mean(scaled * inputs, -1, keepdims=True)
    result = grad_ref[...] + inverse * (scaled - inputs * inverse * inverse * mean)
    out_ref[...] = result.astype(BF16)


def final_tokens(terms, tokens, gain_row, grad_hidden, after=()):
    specs, arrays = term_specs(terms)
    return ordered(
        tokens_grad_kernel,
        after,
        dict(
            grid=(1,),
            in_specs=specs
            + [whole(*BLOCK_SHAPE), whole(1, D), whole(*BLOCK_SHAPE)],
            out_specs=whole(*BLOCK_SHAPE),
        ),
        out_shape=jax.ShapeDtypeStruct(BLOCK_SHAPE, BF16),
        compiler_params=params(40),
        cost_estimate=cost(30 * TOK_DEV * D, 20 * TOK_DEV * D),
        name="final_tokens",
    )(*arrays, tokens, gain_row, grad_hidden)


def owner_rows_kernel(place_ref, att_ref, mixed_ref, wide_ref, out_ref, moe_ref):
    step, steps = pl.program_id(0), pl.num_programs(0)

    @pl.when(step == 0)
    def _():
        out_ref[...] = jnp.zeros_like(out_ref)
        moe_ref[...] = jnp.zeros_like(moe_ref)

    out_ref[:, :D] += tn(att_ref[...], wide_ref[:, :D])
    out_ref[:, D:] += tn(mixed_ref[...], wide_ref[:, D : D + HD])
    tail = wide_ref[:, D + HD :].astype(F32)
    rows = lax.broadcasted_iota(jnp.int32, tail.shape, 0) % TOK_DEV
    mine = (rows == place_ref[0]) | (rows == place_ref[0] + HEADS)
    moe_ref[...] += jnp.sum(jnp.where(mine, tail, 0.0), 0, keepdims=True)

    @pl.when(step == steps - 1)
    def _():
        lane = lax.broadcasted_iota(jnp.int32, (HD, HD), 1)
        out_ref[:, D:] = jnp.where(lane == EXPERTS, as_column(moe_ref[...]), out_ref[:, D:])


def owner_rows(place, att, mixed_columns, wide_all, after=()):
    rows, width = wide_all.shape
    chunk = rows // 4
    return ordered(
        owner_rows_kernel,
        after,
        dict(
            num_scalar_prefetch=1,
            grid=(4,),
            in_specs=[
                pl.BlockSpec((chunk, HD), lambda i, s: (i, 0)),
                pl.BlockSpec((chunk, HD), lambda i, s: (i, 0)),
                pl.BlockSpec((chunk, width), lambda i, s: (i, 0)),
            ],
            out_specs=whole(HD, D + HD),
            scratch_shapes=[pltpu.VMEM((1, HD), F32)],
        ),
        out_shape=jax.ShapeDtypeStruct((HD, D + HD), F32),
        compiler_params=params(24),
        cost_estimate=cost(2 * rows * D * HD, 2 * rows * D),
        name="owner_rows",
    )(place.reshape(1).astype(jnp.int32), att, mixed_columns, wide_all)


def unpack_kernel(in_ref, wq_ref, wk_ref, wv_ref, gain_ref, q_ref, k_ref, v_ref, sums_ref):
    heads = in_ref.shape[0]
    total = jnp.zeros((q_ref.shape[0], 1), F32)
    for part, (w_ref, out_ref) in enumerate(((wq_ref, q_ref), (wk_ref, k_ref), (wv_ref, v_ref))):
        for h in range(heads):
            piece = in_ref[h, : q_ref.shape[0], part * HD : (part + 1) * HD].astype(F32)
            lanes = slice(h * HD, (h + 1) * HD)
            out_ref[:, lanes] = piece
            total += jnp.sum(w_ref[:, lanes].astype(F32) * piece, -1, keepdims=True)
    sums_ref[...] = jnp.broadcast_to(total / gain_ref[...], sums_ref.shape)


def unpack(arrived, weights, gain, after=()):
    rows = weights[0].shape[0]
    shape = jax.ShapeDtypeStruct((rows, D), F32)
    return ordered(
        unpack_kernel,
        after,
        dict(
            grid=(1,),
            in_specs=[whole(*arrived.shape)] + [whole(rows, D)] * 3 + [whole(rows, 1)],
            out_specs=[whole(rows, D)] * 3 + [whole(rows, HD)],
        ),
        out_shape=[shape] * 3 + [jax.ShapeDtypeStruct((rows, HD), F32)],
        compiler_params=params(24),
        cost_estimate=cost(6 * rows * D, 20 * rows * D),
        name="unpack",
    )(arrived, *weights, gain.astype(F32).reshape(rows, 1))


def tie_kernel(in_ref, out_ref):
    out_ref[...] = in_ref[...]


def tie(array, after):
    return ordered(
        tie_kernel,
        after,
        dict(grid=(1,), in_specs=[whole(*array.shape)], out_specs=whole(*array.shape)),
        out_shape=jax.ShapeDtypeStruct(array.shape, array.dtype),
        compiler_params=params(16),
        name="tie",
    )(array)


def swap(value, axis):
    return lax.ppermute(value, axis, [(0, 1), (1, 0)])


def total_over_ep(value):
    value = value + swap(value, "core")
    value = value + swap(value, "x")
    value = value + lax.ppermute(value, "z", [(0, 1), (1, 0), (2, 3), (3, 2)])
    return value + lax.ppermute(value, "z", [(0, 2), (2, 0), (1, 3), (3, 1)])


def of_groups(value):
    return lax.all_gather(value, ("grp", "core"))


def gather_rows(value):
    return lax.all_gather(value, EP, axis=0, tiled=True)


def reduce_rows(value):
    return lax.psum_scatter(value, EP, scatter_dimension=0, tiled=True)


CHIP_ORDER = ((0, 1, 2, 3), (1, 0, 2, 3), (2, 1, 3, 0), (3, 2, 1, 0))


def chip_places():
    z, x = lax.axis_index("z"), lax.axis_index("x")
    order = jnp.asarray(CHIP_ORDER, jnp.int32)[z]
    return [[order[s] * 2 + (x if r == 0 else 1 - x) for r in range(2)] for s in range(4)]


def shift(value, pairs):
    return lax.ppermute(value, "z", pairs)


def choose_kernel(flag_ref, *refs):
    out_ref = refs[-1]
    for i in range(len(refs) - 1):

        @pl.when(flag_ref[i] == 1)
        def _(i=i):
            out_ref[...] = refs[i][...]


def choose(flags, options, after=()):
    return ordered(
        choose_kernel,
        after,
        dict(
            num_scalar_prefetch=1,
            grid=(1,),
            in_specs=[whole(*BLOCK_SHAPE)] * len(options),
            out_specs=whole(*BLOCK_SHAPE),
        ),
        out_shape=jax.ShapeDtypeStruct(BLOCK_SHAPE, BF16),
        compiler_params=params(16),
        cost_estimate=cost(TOK_DEV * D, 2 * (len(options) + 1) * TOK_DEV * D),
        name="choose",
    )(flags, *options)


def gather_steps(block, use, work):
    z = lax.axis_index("z")
    flags = lambda *tests: jnp.stack([jnp.asarray(test, jnp.int32) for test in tests])

    def use_now(arrived, last):
        for s, r, own, far in arrived:
            last = use(s, r, own, far, [last])
        return last

    below1 = shift(block, [(0, 1), (1, 2), (2, 3)])
    above1 = shift(block, [(3, 2), (2, 1), (1, 0)])
    across0 = swap(block, "x")
    far00 = swap(block, "core")
    last = work(0, block)
    column1 = last = choose(flags(z == 0, z != 0), [above1, below1], [last])
    below2 = shift(below1, [(1, 2), (2, 3)])
    above2 = shift(above1, [(2, 1), (1, 0)])
    across1 = swap(column1, "x")
    far01, far10 = swap(across0, "core"), swap(column1, "core")
    last = use_now([(0, 0, block, far00), (0, 1, across0, far01), (1, 0, column1, far10)], last)
    last = work(1, last)
    column2 = last = choose(
        flags(z == 0, z == 3, (z == 1) | (z == 2)), [above2, below2, above1], [last]
    )
    below3 = shift(below2, [(2, 3)])
    above3 = shift(above2, [(1, 0)])
    across2 = swap(column2, "x")
    far11, far20 = swap(across1, "core"), swap(column2, "core")
    last = use_now([(1, 1, across1, far11), (2, 0, column2, far20)], last)
    last = work(2, last)
    column3 = last = choose(
        flags(z == 0, z == 1, z == 2, z == 3), [above3, above2, below2, below3], [last]
    )
    across3 = swap(column3, "x")
    far21, far30 = swap(across2, "core"), swap(column3, "core")
    last = use_now([(2, 1, across2, far21), (3, 0, column3, far30)], last)
    last = work(3, last)
    far31 = swap(across3, "core")
    return use_now([(3, 1, across3, far31)], last)


def sum_kernel(*refs):
    out_ref = refs[-1]
    total = refs[0][...].astype(F32)
    for ref in refs[1:-1]:
        total = total + ref[...].astype(F32)
    out_ref[...] = total.astype(out_ref.dtype)


def sum_blocks(terms, after=(), dtype=BF16):
    specs, arrays = term_specs(terms)
    return ordered(
        sum_kernel,
        after,
        dict(grid=(1,), in_specs=specs, out_specs=whole(*arrays[0].shape[-2:])),
        out_shape=jax.ShapeDtypeStruct(arrays[0].shape[-2:], dtype),
        compiler_params=params(16),
        cost_estimate=cost(len(terms) * TOK_DEV * D, 2 * (len(terms) + 1) * TOK_DEV * D),
        name="sum_blocks",
    )(*arrays)


def pass_on(place, near_up, far_up, near_down, far_down, below, above, after=()):
    def kernel(place_ref, nu, fu, nd, fd, below_ref, above_ref, up_ref, down_ref):
        z = place_ref[0]

        def store(out_ref, source_ref, arrived_ref):
            total = source_ref[...].astype(F32) + arrived_ref[...].astype(F32)
            out_ref[...] = total.astype(BF16)

        for edge, near, far, arrived, out_ref in (
            (0, nu, fu, below_ref, up_ref),
            (3, nd, fd, above_ref, down_ref),
        ):
            pl.when(z == edge)(functools.partial(store, out_ref, near, arrived))
            pl.when(z != edge)(functools.partial(store, out_ref, far, arrived))

    shape = jax.ShapeDtypeStruct(below.shape, BF16)
    return ordered(
        kernel,
        after,
        dict(
            num_scalar_prefetch=1,
            grid=(1,),
            in_specs=[whole(*below.shape)] * 6,
            out_specs=[whole(*below.shape)] * 2,
        ),
        out_shape=[shape, shape],
        compiler_params=params(24),
        cost_estimate=cost(4 * TOK_DEV * D, 16 * TOK_DEV * D),
        name="pass_on",
    )(place, near_up, far_up, near_down, far_down, below, above)


def reduce_steps(parts, work):
    place = lax.axis_index("z").reshape(1).astype(jnp.int32)
    last, sources = [], {}
    for s in (3, 1):
        own, other = parts(s, last)
        near = swap(other, "core")
        last = [own]
        for i in range(2):
            sources[s - i] = lambda r, i=i, own=own, near=near: [(own, (i, r)), (near, (i, r))]
    crossed = {}
    last = last[0]
    for s in (3, 2, 1, 0):
        last = sum_blocks(sources[s](1), [last])
        crossed[s] = swap(last, "x")
    last = work(0, last)
    low = {}
    low[3] = last = sum_blocks(sources[3](0) + [crossed[3]], [last])
    up3 = shift(low[3], [(0, 1)])
    down3 = shift(low[3], [(3, 2)])
    last = work(1, last)
    low[2] = last = sum_blocks(sources[2](0) + [crossed[2]], [last])
    up2, down2 = pass_on(place, low[2], low[3], low[2], low[3], up3, down3)
    last = work(2, up2)
    up2 = shift(up2, [(0, 1), (1, 2)])
    down2 = shift(down2, [(3, 2), (2, 1)])
    low[1] = last = sum_blocks(sources[1](0) + [crossed[1]], [last])
    up1, down1 = pass_on(place, low[1], low[2], low[1], low[1], up2, down2)
    last = work(3, up1)
    up1 = shift(up1, [(0, 1), (1, 2), (2, 3)])
    down1 = shift(down1, [(3, 2), (2, 1), (1, 0)])
    return sources[0](0) + [crossed[0], up1, down1], last


def expert_slots(routes_all, first, local):
    rows = routes_all.shape[0]
    ids = first + jnp.arange(local, dtype=jnp.int32)
    named = jnp.any(routes_all[None, :, :] == ids[:, None, None], -1).reshape(
        local, rows // TOK_DEV, TOK_DEV
    )
    places = jnp.arange(TOK_DEV, dtype=jnp.int32)
    upto = (places[:, None] <= places[None, :]).astype(BF16)
    rank = jnp.einsum(
        "ebt,ts->ebs", named.astype(BF16), upto, preferred_element_type=F32
    ).astype(jnp.int32)
    base = (jnp.arange(rows // TOK_DEV, dtype=jnp.int32) % 2) * CAP
    slots = jnp.where(named, rank - 1 + base[None, :, None], -1)
    return jnp.transpose(slots, (1, 0, 2))


def fast_shards(
    tokens, w_query, w_key, w_value, w_output, w_router, attn_gain, query_gain, key_gain,
    moe_gain, w_gate, w_up, w_down, routes, cotangent,
):
    Order.marks.clear()
    group = lax.axis_index("grp")
    place = lax.axis_index(EP)
    members = lax.axis_size(EP)
    seq = TOK_DEV * members
    local = w_gate.shape[0]
    wide = w_query.shape[0]
    first = (place * local).reshape(1).astype(jnp.int32)

    core = lax.axis_index("core").astype(jnp.int32)
    chips = chip_places()
    small = jnp.concatenate(
        [
            w_router,
            routes.reshape(-1, EXPERTS).astype(BF16),
            jnp.stack([attn_gain, query_gain, key_gain, moe_gain]),
            jnp.zeros((12, EXPERTS), BF16),
        ],
        0,
    ).reshape(16, 3 * HD)
    columns = jnp.stack([w_query, w_key, w_value], 1).reshape(wide, 3, HEADS, HD)
    columns = jnp.transpose(columns, (2, 0, 1, 3)).reshape(HEADS, wide, 3 * HD)
    columns = jnp.concatenate([columns, jnp.broadcast_to(small, (HEADS,) + small.shape)], 1)
    mine = lax.all_to_all(columns, EP, 0, 0, tiled=True)
    other = swap(mine, "grp")
    both = jnp.where(group == 0, jnp.stack([mine, other]), jnp.stack([other, mine]))
    w_head = both[:, :, :wide].reshape(D, 3 * HD)
    small_all = both[:, :, wide:].reshape(2 * members, -1, EXPERTS)
    route_rows = TOK_DEV * TOPK // EXPERTS
    router_full = small_all[:, :wide].reshape(D, EXPERTS)
    routes_all = (
        small_all[:, wide : wide + route_rows].reshape(2, seq, TOPK).astype(jnp.int32)
    )
    gains = jnp.transpose(
        small_all[:, wide + route_rows : wide + route_rows + 4], (1, 0, 2)
    ).reshape(4, D).astype(F32)
    router_wide = jnp.concatenate([router_full, jnp.zeros((D, HD - EXPERTS), BF16)], 1)
    head_gains = lax.dynamic_slice(gains, (0, place * HD), (4, HD))
    gain_q, gain_k = head_gains[1:2], head_gains[2:3]
    attn_row, moe_row = gains[0:1], gains[3:4]

    far_out = swap(w_output, "grp")

    slots_own = expert_slots(lax.dynamic_index_in_dim(routes_all, group, 0, False), first, local)
    slots_other = expert_slots(
        lax.dynamic_index_in_dim(routes_all, 1 - group, 0, False), first, local
    )

    positions = jnp.arange(seq, dtype=jnp.int32)
    half_dim = HD // 2
    frequency = jnp.exp(-(2.0 * jnp.arange(half_dim, dtype=F32) / HD) * math.log(10000.0))
    angles = positions.astype(F32)[:, None] * frequency[None, :]
    cosine = jnp.concatenate([jnp.cos(angles)] * 2, 1)
    sine = jnp.concatenate([-jnp.sin(angles), jnp.sin(angles)], 1)

    kept = [None]

    def use_tokens(s, r, own, far, after):
        spot = jnp.stack([chips[s][r], core])
        kept[0] = project(spot, own, far, w_head, attn_row, kept[0], seq, after)
        return kept[0][2]

    def start_work(step, last):
        if step == 3:
            kept.append(pair_up(group, w_output, far_out, [last, mine]))
            return kept[1]
        return last

    gather_steps(tokens, use_tokens, start_work)
    output_full = gather_rows(kept[1][None])
    cot_own = gather_rows(cotangent)
    normed_all, qkv, stat = kept[0]
    stat = total_over_ep(stat)
    q16, k16, v16, attn_float, att_head, lse = attend(qkv, stat, gain_q, gain_k, cosine, sine)
    attended = lax.all_to_all(att_head.reshape(members, TOK_DEV, HD), EP, 0, 0, tiled=True)
    g_own = plain_dispatch(cot_own, slots_own, [att_head])
    cot_stack = stack_of_core(core, cot_own.reshape(members // 2, 2, TOK_DEV, D), [g_own])
    hidden, mixed, branch_sums = project_out(attended, output_full, tokens, moe_row, [cot_stack])
    early = {}

    def early_work(step, last):
        if step == 2:
            early["slope"] = slopes(g_own, w_down, [last])
            return early["slope"]
        return last

    rows = [None]

    def use_mixed(s, r, own, far, after):
        spot = jnp.stack([chips[s][r], core, place.astype(jnp.int32)])
        rows[0] = dispatch(spot, own, far, slots_own, rows[0], after)
        return rows[0][0]

    gather_steps(mixed, use_mixed, early_work)
    x_own, mixed_columns, mixed_stack = rows[0]
    slope_own = early["slope"]
    sides = jnp.stack([core, group.astype(jnp.int32)])
    cot_near = of_groups(cot_stack)
    mixed_near = of_groups(mixed_stack)
    every = jnp.concatenate([jnp.arange(members // 2, dtype=jnp.int32), sides])
    act_a, dg_a, du_a, gate_a, z_rows = experts(
        first, x_own, slope_own, w_gate, w_up, router_wide, True
    )

    def place_of(s):
        return jnp.stack([chips[s][0], chips[s][1], chips[s - 1][0], chips[s - 1][1], core])

    late = {}

    def late_work(step, last):
        if step == 1:
            late["y"] = down(act_a, gate_a, w_down, [last])
            return late["y"]
        if step == 2:
            late["branch"] = combine(late["y"], slots_own, [last])
            late["g"] = stack_dispatch(every, cot_near, slots_other, [late["branch"]])
            return late["g"]
        if step == 3:
            late["slope"] = slopes(late["g"], w_down, [last])
            return late["slope"]
        return last

    terms, last = reduce_steps(
        lambda s, after: combine_part(place_of(s), z_rows, slots_own, after), late_work
    )
    branch_moe = reduce_rows(late["branch"]).astype(F32)
    output = (hidden + branch_moe).astype(BF16)
    grad_hidden, wide_branch = token_back(
        terms, mixed, hidden, cotangent, router_wide, moe_row, [last]
    )
    grad_out = out_back(wide_branch, output_full)
    grad_att_head = lax.all_to_all(grad_out, EP, 0, 0, tiled=True).reshape(seq, HD)
    branch_all = gather_rows(wide_branch)

    def expert_other(only, last):
        late[only] = experts(
            first, late["x"], late["slope"], w_gate, w_up, router_wide, False, only, [last]
        )
        return late[only][3]

    groups = [(0, local // 2), (local // 2, local - local // 2)]
    late["x"] = stack_dispatch(every, mixed_near, slots_other, [grad_out])
    last = expert_other(groups[0], late["x"])

    dnq, dnk, dv16, means, gain_parts = attend_back(
        q16, k16, v16, grad_att_head, attn_float, lse, qkv, stat, gain_q, gain_k, cosine, sine, [last],
    )
    means = total_over_ep(means)
    qkv_grads = finish(dnq, dnk, dv16, qkv, stat, means, gain_q, gain_k)
    half = group.reshape(1).astype(jnp.int32)

    def expert_grads(only, last):
        act_b, dg_b, du_b, gate_b = late[only]
        late["grads"] = weight_grads(
            only, half, (x_own, late["x"]), (dg_a, dg_b), (du_a, du_b), (act_a, act_b),
            (g_own, late["g"]), (gate_a, gate_b), late.get("grads"), [last],
        )
        return late["grads"][0]

    def last_work(step, last):
        if step == 0:
            late["dw"] = dw_product(normed_all, qkv_grads, [last])
            return late["dw"]
        if step == 1:
            return expert_other(groups[1], last)
        if step == 2:
            return expert_grads(groups[0], last)
        return last

    terms, last = reduce_steps(
        lambda s, after: normed_part(place_of(s), qkv_grads, w_head, after),
        last_work,
    )
    tokens_grad = final_tokens(terms, tokens, attn_row, grad_hidden, [last])
    dw_head = late["dw"]
    last = tokens_grad
    last = expert_grads(groups[1], last)
    gate_grad, up_grad, down_grad = late["grads"]
    inputs = tokens.astype(F32)
    sums = jnp.stack(
        [jnp.sum(inputs * inputs), branch_sums[0, 0], jnp.sum(branch_moe * branch_moe)]
    )
    sums = jnp.pad(sums[None, :], ((0, 0), (0, HD - 3)))
    rms_stats = jnp.sqrt(total_over_ep(sums)[:, :3] / (seq * D))

    dw_keep = lax.dynamic_slice_in_dim(dw_head, group * (D // 2), D // 2, 0)
    dw_send = lax.dynamic_slice_in_dim(dw_head, (1 - group) * (D // 2), D // 2, 0)
    dw_half = (dw_keep + swap(dw_send.astype(BF16), "grp").astype(F32)).astype(BF16)
    gain_parts = gain_parts + swap(gain_parts, "grp")
    extra = gain_parts.reshape(1, 2 * HD)
    high = extra.astype(BF16)
    low = (extra - high.astype(F32)).astype(BF16)
    extra = jnp.pad(jnp.concatenate([high, low], 0), ((0, 14), (0, HD)))
    payload = jnp.concatenate(
        [
            dw_half.reshape(members, wide, 3 * HD),
            jnp.broadcast_to(extra, (members,) + extra.shape),
        ],
        1,
    )
    arrived = lax.all_to_all(payload, EP, 0, 0, tiled=True)
    *dense, attn_sums = unpack(arrived, (w_query, w_key, w_value), attn_gain, [last])
    attn_gain_grad = attn_sums[:, 0]
    extras = arrived[:, wide].astype(F32) + arrived[:, wide + 1].astype(F32)
    flat = group * members + place
    head_row = lax.dynamic_slice(
        extras[:, : 2 * HD].reshape(HEADS, 2, HD // wide, wide),
        (flat // (HD // wide), 0, flat % (HD // wide), 0),
        (1, 2, 1, wide),
    ).reshape(2, wide)

    out_part = owner_rows(place, att_head, mixed_columns, branch_all, [last])
    out_part = out_part.reshape(2, wide, D + HD)
    out_keep = lax.dynamic_index_in_dim(out_part, group, 0, False)
    out_send = lax.dynamic_index_in_dim(out_part, 1 - group, 0, False).astype(BF16)
    out_sum = (out_keep + swap(out_send, "grp").astype(F32)).astype(BF16)
    owners = [(g * members + e, 2 * e + g) for g in range(2) for e in range(members)]
    owned = lax.ppermute(out_sum, ALL, owners).astype(F32)
    output_grad = owned[:, :D]
    router_grad, moe_gain_grad = owned[:, D : D + EXPERTS], owned[:, D + EXPERTS]

    return (
        output, tokens_grad, dense[0], dense[1], dense[2], output_grad, router_grad,
        attn_gain_grad, head_row[0], head_row[1], moe_gain_grad, gate_grad, up_grad, down_grad,
        rms_stats,
    )


def fast_solution(mesh, sides):
    inner = jax.sharding.Mesh(mesh.devices.reshape((2,) + sides), ALL)
    rows = P(ALL, None)
    expert = P(EP, None, None)
    return jax.shard_map(
        fast_shards,
        mesh=inner,
        in_specs=(rows,) * 6 + (P(ALL),) * 4 + (expert,) * 3 + (rows,) * 2,
        out_specs=(rows,) * 7 + (P(ALL),) * 4 + (P(EP, "grp", None),) * 3 + (P("grp", None),),
        check_vma=False,
    )


def solution(mesh):
    sides = SIDES.get(mesh.shape["ep"])
    if sides is not None and mesh.shape["grp"] == 2:
        return fast_solution(mesh, sides)
    return jax.shard_map(
        shards,
        mesh=mesh,
        in_specs=(
            P(("grp", "ep"), None),
            P(("grp", "ep"), None),
            P(("grp", "ep"), None),
            P(("grp", "ep"), None),
            P(("grp", "ep"), None),
            P(("grp", "ep"), None),
            P(("grp", "ep")),
            P(("grp", "ep")),
            P(("grp", "ep")),
            P(("grp", "ep")),
            P("ep", None, None),
            P("ep", None, None),
            P("ep", None, None),
            P(("grp", "ep"), None),
            P(("grp", "ep"), None),
        ),
        out_specs=(
            P(("grp", "ep"), None),
            P(("grp", "ep"), None),
            P(("grp", "ep"), None),
            P(("grp", "ep"), None),
            P(("grp", "ep"), None),
            P(("grp", "ep"), None),
            P(("grp", "ep"), None),
            P(("grp", "ep")),
            P(("grp", "ep")),
            P(("grp", "ep")),
            P(("grp", "ep")),
            P("ep", "grp", None),
            P("ep", "grp", None),
            P("ep", "grp", None),
            P("grp", None),
        ),
        check_vma=False,
    )
```

```python
import functools
import math

import jax
import jax.numpy as jnp
from jax import lax
from jax.experimental import pallas as pl
from jax.experimental.pallas import tpu as pltpu
from jax.sharding import PartitionSpec as P

D = 2048
HEADS = 16
HD = 128
EXPERTS = 64
TOPK = 8
TOK_DEV = 128
BLOCK = 256
CAP = 24


EPSILON = 1e-05
NEG_FILL = -1e30


def inv_rms(values):
    return lax.rsqrt(jnp.mean(values * values, -1, keepdims=True) + EPSILON)


def norm_back(grad_out, values, inverse, gain_vec):
    scaled = grad_out * gain_vec
    grad_in = inverse * (
        scaled - values * inverse * inverse * jnp.mean(scaled * values, -1, keepdims=True)
    )
    return (grad_in, jnp.sum(grad_out * values * inverse, 0))


def rope_tables(positions):
    half_dim = HD // 2
    frequency = jnp.exp(-(2.0 * jnp.arange(half_dim, dtype=jnp.float32) / HD) * math.log(10000.0))
    angles = positions.astype(jnp.float32)[:, None] * frequency[None, :]
    return (jnp.cos(angles)[:, None, :], jnp.sin(angles)[:, None, :])


def rotate(values, cosine, sine_tab):
    half_dim = HD // 2
    first_half = values[..., :half_dim]
    second_half = values[..., half_dim:]
    return jnp.concatenate(
        [
            first_half * cosine - second_half * sine_tab,
            second_half * cosine + first_half * sine_tab,
        ],
        -1,
    )


def rotate_back(grad_in, cosine, sine_tab):
    half_dim = HD // 2
    first_half = grad_in[..., :half_dim]
    second_half = grad_in[..., half_dim:]
    return jnp.concatenate(
        [
            first_half * cosine + second_half * sine_tab,
            second_half * cosine - first_half * sine_tab,
        ],
        -1,
    )


def fold_keys(state_now, key_piece, queries, query_pos):
    keys_in, values_in = key_piece
    piece_rows = keys_in.shape[0]
    blk_rows = math.gcd(piece_rows, 1024)
    key_blocks = keys_in.reshape(piece_rows // blk_rows, blk_rows, HEADS, HD)
    value_blocks = values_in.reshape(piece_rows // blk_rows, blk_rows, HEADS, HD)
    last_block = query_pos[-1] // BLOCK

    def block_step(state_in, block_items):
        key_blk, value_blk, block_num = block_items
        key_start = block_num * blk_rows

        def block_compute(state_cur):
            top_now, total_now, acc_now = state_cur
            key_pos = key_start + jnp.arange(blk_rows, dtype=jnp.int32)
            scores = jnp.einsum(
                "qhd,khd->hqk", queries, key_blk, preferred_element_type=jnp.float32
            ) * HD ** (-0.5)
            allowed = (key_pos // BLOCK)[None, None, :] <= (query_pos // BLOCK)[None, :, None]
            scores = jnp.where(allowed, scores, NEG_FILL)
            top_new = jnp.maximum(top_now, jnp.max(scores, -1, keepdims=True))
            weights = jnp.where(allowed, jnp.exp(scores - top_new), 0.0)
            rescale = jnp.exp(top_now - top_new)
            total_new = total_now * rescale + jnp.sum(weights, -1, keepdims=True)
            acc_new = acc_now * jnp.transpose(rescale, (1, 0, 2)) + jnp.einsum(
                "hqk,khd->qhd",
                weights.astype(jnp.bfloat16),
                value_blk,
                preferred_element_type=jnp.float32,
            )
            return (top_new, total_new, acc_new)

        def block_passing(state_cur):
            return state_cur

        return (
            lax.cond(key_start // BLOCK <= last_block, block_compute, block_passing, state_in),
            None,
        )

    state_out, unused = lax.scan(
        block_step,
        state_now,
        (key_blocks, value_blocks, jnp.arange(piece_rows // blk_rows, dtype=jnp.int32)),
    )
    return state_out


def score_grads(queries, grad_attended, row_delta, log_sum, query_pos, key_blk, value_blk, key_pos):
    scores = jnp.einsum(
        "qhd,khd->hqk", queries, key_blk, preferred_element_type=jnp.float32
    ) * HD ** (-0.5)
    allowed = (key_pos // BLOCK)[None, None, :] <= (query_pos // BLOCK)[None, :, None]
    prob_vals = jnp.where(allowed, jnp.exp(scores - log_sum), 0.0)
    grad_probs = jnp.einsum(
        "qhd,khd->hqk", grad_attended, value_blk, preferred_element_type=jnp.float32
    )
    grad_scores = (prob_vals * (grad_probs - row_delta)).astype(jnp.bfloat16)
    return (prob_vals, grad_scores)


def shards(
    tokens,
    w_query,
    w_key,
    w_value,
    w_output,
    w_router,
    attn_gain,
    query_gain,
    key_gain,
    moe_gain,
    w_gate,
    w_up,
    w_down,
    routes,
    cotangent,
):
    gathered = (
        lax.all_gather(w_query, ("grp", "ep"), axis=0, tiled=True),
        lax.all_gather(w_key, ("grp", "ep"), axis=0, tiled=True),
        lax.all_gather(w_value, ("grp", "ep"), axis=0, tiled=True),
        lax.all_gather(w_output, ("grp", "ep"), axis=0, tiled=True),
        lax.all_gather(w_router, ("grp", "ep"), axis=0, tiled=True),
        lax.all_gather(attn_gain, ("grp", "ep"), axis=0, tiled=True),
        lax.all_gather(query_gain, ("grp", "ep"), axis=0, tiled=True),
        lax.all_gather(key_gain, ("grp", "ep"), axis=0, tiled=True),
        lax.all_gather(moe_gain, ("grp", "ep"), axis=0, tiled=True),
    )
    query_full, key_full, value_full, output_full, router_full = (
        gathered[0],
        gathered[1],
        gathered[2],
        gathered[3],
        gathered[4],
    )
    attn_scale = gathered[5].astype(jnp.float32)
    query_scale = gathered[6].astype(jnp.float32)
    key_scale = gathered[7].astype(jnp.float32)
    moe_scale = gathered[8].astype(jnp.float32)
    ep_count = lax.axis_size("ep")
    exp_local = EXPERTS // ep_count
    score_scale = HD ** (-0.5)
    inputs = tokens.astype(jnp.float32)
    positions = lax.axis_index("ep") * TOK_DEV + jnp.arange(TOK_DEV, dtype=jnp.int32)
    cosine, sine_tab = rope_tables(positions)
    attn_inv = inv_rms(inputs)
    normed = (inputs * attn_inv * attn_scale).astype(jnp.bfloat16)
    query_raw = jnp.dot(normed, query_full, preferred_element_type=jnp.float32)
    key_raw = jnp.dot(normed, key_full, preferred_element_type=jnp.float32)
    values16 = jnp.dot(normed, value_full, preferred_element_type=jnp.float32).astype(jnp.bfloat16)
    query_inv = inv_rms(query_raw)
    queries16 = rotate(
        (query_raw * query_inv * query_scale).reshape(TOK_DEV, HEADS, HD), cosine, sine_tab
    ).astype(jnp.bfloat16)
    key_inv = inv_rms(key_raw)
    keys16 = (
        rotate((key_raw * key_inv * key_scale).reshape(TOK_DEV, HEADS, HD), cosine, sine_tab)
        .astype(jnp.bfloat16)
        .reshape(TOK_DEV, D)
    )
    start_state = (
        jnp.full((HEADS, TOK_DEV, 1), NEG_FILL, jnp.float32),
        jnp.zeros((HEADS, TOK_DEV, 1), jnp.float32),
        jnp.zeros((TOK_DEV, HEADS, HD), jnp.float32),
    )
    folded = fold_keys(
        start_state,
        (
            lax.all_gather(keys16, "ep", axis=0, tiled=True),
            lax.all_gather(values16, "ep", axis=0, tiled=True),
        ),
        queries16,
        positions,
    )
    top_score, total_weight, acc_sum = folded
    log_sum = top_score + jnp.log(total_weight)
    attn_float = acc_sum / jnp.transpose(total_weight, (1, 0, 2))
    attended16 = attn_float.reshape(TOK_DEV, D).astype(jnp.bfloat16)
    branch_attn = jnp.dot(attended16, output_full, preferred_element_type=jnp.float32)
    hidden = inputs + branch_attn
    moe_inv = inv_rms(hidden)
    mixed_in = (hidden * moe_inv * moe_scale).astype(jnp.bfloat16)
    logits = jnp.dot(mixed_in, router_full, preferred_element_type=jnp.float32)
    route_probs = jax.nn.softmax(logits, -1)
    chosen = (routes[:, :, None] == jnp.arange(EXPERTS, dtype=jnp.int32)[None, None, :]).astype(
        jnp.float32
    )
    gate_vals = jnp.sum(chosen * route_probs[:, None, :], -1)
    pair_expert = routes.reshape(-1)
    one_hot = (pair_expert[:, None] == jnp.arange(EXPERTS, dtype=jnp.int32)[None, :]).astype(
        jnp.int32
    )
    pair_rank = jnp.sum(jnp.cumsum(one_hot, 0) * one_hot, 1) - 1
    slot_index = pair_expert * CAP + pair_rank
    pair_token = jnp.arange(TOK_DEV * TOPK, dtype=jnp.int32) // TOPK
    send_rows = jnp.zeros((EXPERTS * CAP, D), jnp.bfloat16).at[slot_index].set(mixed_in[pair_token])
    send_rows = send_rows.reshape(ep_count, exp_local, CAP, D)
    received = lax.all_to_all(send_rows, "ep", split_axis=0, concat_axis=0, tiled=True)
    gate_pre = jnp.einsum("secd,edf->secf", received, w_gate, preferred_element_type=jnp.float32)
    up_pre = jnp.einsum("secd,edf->secf", received, w_up, preferred_element_type=jnp.float32)
    activation = (jax.nn.silu(gate_pre) * up_pre).astype(jnp.bfloat16)
    expert_out = jnp.einsum(
        "secf,efd->secd", activation, w_down, preferred_element_type=jnp.float32
    ).astype(jnp.bfloat16)
    expert_out, gate_pre, up_pre, activation, received = (
        expert_out,
        gate_pre,
        up_pre,
        activation,
        received,
    )
    returned = lax.all_to_all(expert_out, "ep", split_axis=0, concat_axis=0, tiled=True).reshape(
        EXPERTS * CAP, D
    )
    pair_out = returned[slot_index].astype(jnp.float32).reshape(TOK_DEV, TOPK, D)
    branch_moe = jnp.sum(gate_vals[:, :, None] * pair_out, 1)
    output = (hidden + branch_moe).astype(jnp.bfloat16)
    local_sums = jnp.stack(
        [
            jnp.sum(inputs * inputs),
            jnp.sum(branch_attn * branch_attn),
            jnp.sum(branch_moe * branch_moe),
        ]
    )
    seq_sums = lax.psum(local_sums, "ep")
    rms_stats = jnp.sqrt(seq_sums / (TOK_DEV * ep_count * D)).reshape(1, 3)
    grad_out = cotangent.astype(jnp.float32)
    grad_gates = jnp.sum(pair_out * grad_out[:, None, :], -1)
    grad_pairs = (
        (gate_vals[:, :, None] * grad_out[:, None, :])
        .astype(jnp.bfloat16)
        .reshape(TOK_DEV * TOPK, D)
    )
    send_grads = jnp.zeros((EXPERTS * CAP, D), jnp.bfloat16).at[slot_index].set(grad_pairs)
    send_grads = send_grads.reshape(ep_count, exp_local, CAP, D)
    grad_received = lax.all_to_all(send_grads, "ep", split_axis=0, concat_axis=0, tiled=True)
    grad_activation = jnp.einsum(
        "secd,efd->secf", grad_received, w_down, preferred_element_type=jnp.float32
    )
    grad_down = jnp.einsum(
        "secf,secd->efd", activation, grad_received, preferred_element_type=jnp.float32
    )
    sig_gate = jax.nn.sigmoid(gate_pre)
    grad_gate_pre = (
        grad_activation * up_pre * sig_gate * (1.0 + gate_pre * (1.0 - sig_gate))
    ).astype(jnp.bfloat16)
    grad_up_pre = (grad_activation * gate_pre * sig_gate).astype(jnp.bfloat16)
    grad_gate_w = jnp.einsum(
        "secd,secf->edf", received, grad_gate_pre, preferred_element_type=jnp.float32
    )
    grad_up_w = jnp.einsum(
        "secd,secf->edf", received, grad_up_pre, preferred_element_type=jnp.float32
    )
    grad_inputs = (
        jnp.einsum("secf,edf->secd", grad_gate_pre, w_gate, preferred_element_type=jnp.float32)
        + jnp.einsum("secf,edf->secd", grad_up_pre, w_up, preferred_element_type=jnp.float32)
    ).astype(jnp.bfloat16)
    grad_back = lax.all_to_all(grad_inputs, "ep", split_axis=0, concat_axis=0, tiled=True).reshape(
        EXPERTS * CAP, D
    )
    grad_mixed = jnp.sum(grad_back[slot_index].astype(jnp.float32).reshape(TOK_DEV, TOPK, D), 1)
    spread = jnp.sum(chosen * grad_gates[:, :, None], 1)
    grad_logits = (
        route_probs * (spread - jnp.sum(route_probs * spread, -1, keepdims=True))
    ).astype(jnp.bfloat16)
    router_grad = jnp.einsum("td,te->de", mixed_in, grad_logits, preferred_element_type=jnp.float32)
    grad_mixed = grad_mixed + jnp.einsum(
        "te,de->td", grad_logits, router_full, preferred_element_type=jnp.float32
    )
    grad_hid_norm, moe_gain_grad = norm_back(grad_mixed, hidden, moe_inv, moe_scale)
    grad_hidden = grad_out + grad_hid_norm
    grad_branch = grad_hidden.astype(jnp.bfloat16)
    output_grad = jnp.einsum(
        "td,tf->df", attended16, grad_branch, preferred_element_type=jnp.float32
    )
    grad_attended = jnp.einsum(
        "tf,df->td", grad_branch, output_full, preferred_element_type=jnp.float32
    ).astype(jnp.bfloat16)
    grad_attended = grad_attended.reshape(TOK_DEV, HEADS, HD)
    row_delta = jnp.transpose(jnp.sum(grad_attended.astype(jnp.float32) * attn_float, -1), (1, 0))[
        :, :, None
    ]
    gathered_keys, gathered_values = (
        lax.all_gather(keys16, "ep", axis=0, tiled=True),
        lax.all_gather(values16, "ep", axis=0, tiled=True),
    )
    total_rows = gathered_keys.shape[0]
    blk_rows = math.gcd(total_rows, 1024)
    last_query_block = positions[-1] // BLOCK

    def query_step(grad_now, block_num):
        begin_row = block_num * blk_rows

        def query_compute(grad_cur):
            key_blk = lax.dynamic_slice_in_dim(gathered_keys, begin_row, blk_rows, 0).reshape(
                blk_rows, HEADS, HD
            )
            value_blk = lax.dynamic_slice_in_dim(gathered_values, begin_row, blk_rows, 0).reshape(
                blk_rows, HEADS, HD
            )
            key_pos = begin_row + jnp.arange(blk_rows, dtype=jnp.int32)
            prob_vals, grad_scores = score_grads(
                queries16, grad_attended, row_delta, log_sum, positions, key_blk, value_blk, key_pos
            )
            return (
                grad_cur
                + jnp.einsum(
                    "hqk,khd->qhd", grad_scores, key_blk, preferred_element_type=jnp.float32
                )
                * score_scale
            )

        def query_passing(grad_cur):
            return grad_cur

        return (
            lax.cond(
                begin_row // BLOCK <= last_query_block, query_compute, query_passing, grad_now
            ),
            None,
        )

    grad_queries, unused = lax.scan(
        query_step,
        jnp.zeros((TOK_DEV, HEADS, HD), jnp.float32),
        jnp.arange(total_rows // blk_rows, dtype=jnp.int32),
    )
    all_queries, all_grad_att = (
        lax.all_gather(queries16, "ep", axis=0, tiled=True),
        lax.all_gather(grad_attended, "ep", axis=0, tiled=True),
    )
    all_delta, all_log_sum = (
        lax.all_gather(row_delta, "ep", axis=1, tiled=True),
        lax.all_gather(log_sum, "ep", axis=1, tiled=True),
    )
    query_rows = all_queries.shape[0]
    query_blk_rows = math.gcd(query_rows, 1024)
    own_keys = keys16.reshape(TOK_DEV, HEADS, HD)
    own_values = values16.reshape(TOK_DEV, HEADS, HD)
    first_key_block = positions[0] // BLOCK

    def key_step(grads_now, block_num):
        begin_row = block_num * query_blk_rows

        def key_compute(grads_cur):
            query_blk = lax.dynamic_slice_in_dim(all_queries, begin_row, query_blk_rows, 0)
            grad_att_blk = lax.dynamic_slice_in_dim(all_grad_att, begin_row, query_blk_rows, 0)
            delta_blk = lax.dynamic_slice_in_dim(all_delta, begin_row, query_blk_rows, 1)
            log_blk = lax.dynamic_slice_in_dim(all_log_sum, begin_row, query_blk_rows, 1)
            query_pos = begin_row + jnp.arange(query_blk_rows, dtype=jnp.int32)
            prob_vals, grad_scores = score_grads(
                query_blk,
                grad_att_blk,
                delta_blk,
                log_blk,
                query_pos,
                own_keys,
                own_values,
                positions,
            )
            key_part = (
                jnp.einsum(
                    "hqk,qhd->khd", grad_scores, query_blk, preferred_element_type=jnp.float32
                )
                * score_scale
            )
            value_part = jnp.einsum(
                "hqk,qhd->khd",
                prob_vals.astype(jnp.bfloat16),
                grad_att_blk,
                preferred_element_type=jnp.float32,
            )
            return (grads_cur[0] + key_part, grads_cur[1] + value_part)

        def key_passing(grads_cur):
            return grads_cur

        return (
            lax.cond(
                (begin_row + query_blk_rows - 1) // BLOCK >= first_key_block,
                key_compute,
                key_passing,
                grads_now,
            ),
            None,
        )

    key_start = (
        jnp.zeros((TOK_DEV, HEADS, HD), jnp.float32),
        jnp.zeros((TOK_DEV, HEADS, HD), jnp.float32),
    )
    key_value_grads, unused = lax.scan(
        key_step, key_start, jnp.arange(query_rows // query_blk_rows, dtype=jnp.int32)
    )
    grad_keys16 = key_value_grads[0].astype(jnp.bfloat16)
    grad_values16 = key_value_grads[1].reshape(TOK_DEV, D).astype(jnp.bfloat16)
    grad_keys = lax.optimization_barrier(grad_keys16).astype(jnp.float32)
    grad_queries = lax.optimization_barrier(grad_queries.astype(jnp.bfloat16)).astype(jnp.float32)
    grad_query_rot = rotate_back(grad_queries, cosine, sine_tab).reshape(TOK_DEV, D)
    grad_query_raw, query_gain_grad = norm_back(grad_query_rot, query_raw, query_inv, query_scale)
    grad_query16 = grad_query_raw.astype(jnp.bfloat16)
    grad_key_rot = rotate_back(grad_keys, cosine, sine_tab).reshape(TOK_DEV, D)
    grad_key_raw, key_gain_grad = norm_back(grad_key_rot, key_raw, key_inv, key_scale)
    grad_key16 = grad_key_raw.astype(jnp.bfloat16)
    query_grad = jnp.einsum("td,tf->df", normed, grad_query16, preferred_element_type=jnp.float32)
    key_grad = jnp.einsum("td,tf->df", normed, grad_key16, preferred_element_type=jnp.float32)
    value_grad = jnp.einsum("td,tf->df", normed, grad_values16, preferred_element_type=jnp.float32)
    grad_normed = (
        jnp.einsum("tf,df->td", grad_query16, query_full, preferred_element_type=jnp.float32)
        + jnp.einsum("tf,df->td", grad_key16, key_full, preferred_element_type=jnp.float32)
        + jnp.einsum("tf,df->td", grad_values16, value_full, preferred_element_type=jnp.float32)
    )
    grad_tok_norm, attn_gain_grad = norm_back(grad_normed, inputs, attn_inv, attn_scale)
    tokens_grad = (grad_hidden + grad_tok_norm).astype(jnp.bfloat16)
    dense_sums = (
        lax.psum_scatter(query_grad, ("grp", "ep"), scatter_dimension=0, tiled=True),
        lax.psum_scatter(key_grad, ("grp", "ep"), scatter_dimension=0, tiled=True),
        lax.psum_scatter(value_grad, ("grp", "ep"), scatter_dimension=0, tiled=True),
        lax.psum_scatter(output_grad, ("grp", "ep"), scatter_dimension=0, tiled=True),
        lax.psum_scatter(router_grad, ("grp", "ep"), scatter_dimension=0, tiled=True),
        lax.psum_scatter(attn_gain_grad, ("grp", "ep"), scatter_dimension=0, tiled=True),
        lax.psum_scatter(query_gain_grad, ("grp", "ep"), scatter_dimension=0, tiled=True),
        lax.psum_scatter(key_gain_grad, ("grp", "ep"), scatter_dimension=0, tiled=True),
        lax.psum_scatter(moe_gain_grad, ("grp", "ep"), scatter_dimension=0, tiled=True),
    )
    expert_sums = (
        lax.psum_scatter(
            grad_gate_w.astype(jnp.bfloat16), "grp", scatter_dimension=1, tiled=True
        ).astype(jnp.float32),
        lax.psum_scatter(
            grad_up_w.astype(jnp.bfloat16), "grp", scatter_dimension=1, tiled=True
        ).astype(jnp.float32),
        lax.psum_scatter(
            grad_down.astype(jnp.bfloat16), "grp", scatter_dimension=1, tiled=True
        ).astype(jnp.float32),
    )
    return (
        output,
        tokens_grad,
        dense_sums[0],
        dense_sums[1],
        dense_sums[2],
        dense_sums[3],
        dense_sums[4],
        dense_sums[5],
        dense_sums[6],
        dense_sums[7],
        dense_sums[8],
        expert_sums[0],
        expert_sums[1],
        expert_sums[2],
        rms_stats,
    )


F32 = jnp.float32
BF16 = jnp.bfloat16
EP = ("z", "x", "core")
ALL = ("grp", "z", "x", "core")
PAIR = 2 * TOK_DEV
SLOTS = 2 * CAP
COST = 0.1
SIDES = {16: (4, 2, 2)}


def nt(left, right):
    return lax.dot_general(left, right, (((1,), (1,)), ((), ())), preferred_element_type=F32)


def nn(left, right):
    return lax.dot_general(left, right, (((1,), (0,)), ((), ())), preferred_element_type=F32)


def tn(left, right):
    return lax.dot_general(left, right, (((0,), (0,)), ((), ())), preferred_element_type=F32)


def as_row(column):
    return jnp.broadcast_to(column, (column.shape[0], 128)).T[0:1]


def as_column(row):
    return jnp.broadcast_to(row, (128, row.shape[1])).T


def inv_of(sum_row):
    return as_column(lax.rsqrt(sum_row / D + EPSILON))


def params(mebibytes):
    return pltpu.CompilerParams(vmem_limit_bytes=mebibytes * 1024 * 1024)


def cost(flops, moved):
    return pl.CostEstimate(flops=int(flops * COST), bytes_accessed=int(moved * COST), transcendentals=0)


def whole(*dims):
    return pl.BlockSpec(dims, lambda *_: (0,) * len(dims))


class Order:
    marks = []

    @classmethod
    def mark_of(cls, array):
        for known, mark in cls.marks:
            if known is array:
                return mark
        return array


MARK = (8, 128)


def ordered(kernel, after, specs, **settings):
    after = [Order.mark_of(array) for array in after]
    inputs = len(specs["in_specs"])
    prefetch = specs.pop("num_scalar_prefetch", 0)
    extra = len(after)
    single = not isinstance(specs["out_specs"], list)
    outputs = [specs["out_specs"]] if single else specs["out_specs"]
    shapes = settings.pop("out_shape")
    shapes = [shapes] if single else list(shapes)
    last = prefetch + inputs + extra + len(outputs)

    def body(*refs):
        refs[last][...] = jnp.zeros(MARK, F32)
        kernel(*refs[: prefetch + inputs], *refs[prefetch + inputs + extra : last], *refs[last + 1 :])

    specs["in_specs"] = list(specs["in_specs"]) + [pl.BlockSpec(memory_space=pl.ANY)] * extra
    specs["out_specs"] = outputs + [pl.BlockSpec(MARK, lambda *_: (0, 0))]
    call = pl.pallas_call(
        body,
        grid_spec=pltpu.PrefetchScalarGridSpec(num_scalar_prefetch=prefetch, **specs),
        out_shape=shapes + [jax.ShapeDtypeStruct(MARK, F32)],
        **settings,
    )

    def run(*args):
        *results, mark = call(*args, *after)
        Order.marks.extend((result, mark) for result in results)
        return results[0] if single else results

    return run


ANYWHERE = pl.BlockSpec(memory_space=pl.ANY)


def in_hbm(dims, kind):
    return pltpu.HBM(dims, kind)


BLOCK_SHAPE = (TOK_DEV, D)


def project_kernel(place_ref, own_ref, other_ref, w_ref, gain_ref, *refs):
    normed_ref, qkv_ref, stat_ref = refs[-3:]
    core = place_ref[1]
    for side, tok_ref in ((core, own_ref), (1 - core, other_ref)):
        here = pl.ds(pl.multiple_of(side * TOK_DEV, TOK_DEV), TOK_DEV)
        rows = tok_ref[...].astype(F32)
        inverse = lax.rsqrt(jnp.mean(rows * rows, -1, keepdims=True) + EPSILON)
        normed = (rows * inverse * gain_ref[...]).astype(BF16)
        normed_ref[here, :] = normed
        out = nn(normed, w_ref[...])
        qkv_ref[here, :] = out
        for part in range(2):
            piece = out[:, part * HD : (part + 1) * HD]
            stat_ref[part : part + 1, here] = as_row(jnp.sum(piece * piece, -1, keepdims=True))


def project(chip_core, own, other, w_head, gain_row, buffers, seq, after=()):
    kept = [] if buffers is None else list(buffers)
    return ordered(
        project_kernel,
        after,
        dict(
            num_scalar_prefetch=1,
            grid=(1,),
            in_specs=[whole(TOK_DEV, D), whole(TOK_DEV, D), whole(D, 3 * HD), whole(1, D)]
            + [ANYWHERE] * len(kept),
            out_specs=[
                pl.BlockSpec((PAIR, D), lambda i, s: (s[0], 0)),
                pl.BlockSpec((PAIR, 3 * HD), lambda i, s: (s[0], 0)),
                pl.BlockSpec((2, PAIR), lambda i, s: (0, s[0])),
            ],
        ),
        out_shape=[
            in_hbm((seq, D), BF16),
            in_hbm((seq, 3 * HD), F32),
            jax.ShapeDtypeStruct((2, seq), F32),
        ],
        input_output_aliases={5 + i: i for i in range(len(kept))},
        compiler_params=params(24),
        cost_estimate=cost(2 * PAIR * D * 3 * HD, 10 * PAIR * D),
        name="project",
    )(chip_core, own, other, w_head, gain_row, *kept)


def attend_kernel(
    qkv_ref, stat_ref, gq_ref, gk_ref, cos_ref, sin_ref,
    q_ref, k_ref, v_ref, of_ref, att_ref, lse_ref, vt_ref,
):
    blocks = q_ref.shape[0] // BLOCK
    for i in range(blocks):
        rows = slice(i * BLOCK, (i + 1) * BLOCK)
        cosine, sine = cos_ref[rows, :], sin_ref[rows, :]
        for part, gain_ref, out_ref in ((0, gq_ref, q_ref), (1, gk_ref, k_ref)):
            raw = qkv_ref[rows, part * HD : (part + 1) * HD]
            scaled = raw * inv_of(stat_ref[part : part + 1, rows]) * gain_ref[...]
            turned = scaled * cosine + pltpu.roll(scaled, HD // 2, 1) * sine
            out_ref[rows, :] = turned.astype(BF16)
        value = qkv_ref[rows, 2 * HD :]
        v_ref[rows, :] = value.astype(BF16)
        vt_ref[:, rows] = value.T.astype(BF16)
    for i in range(blocks):
        rows = slice(i * BLOCK, (i + 1) * BLOCK)
        reach = (i + 1) * BLOCK
        scores = nt(k_ref[0:reach, :], q_ref[rows, :]) * HD ** (-0.5)
        top = jnp.max(scores, 0, keepdims=True)
        weights = jnp.exp(scores - top)
        total = jnp.sum(weights, 0, keepdims=True)
        probs = (weights * (1.0 / total)).astype(BF16)
        out = nn(vt_ref[:, 0:reach], probs).T
        of_ref[rows, :] = out
        att_ref[rows, :] = out.astype(BF16)
        lse_ref[:, rows] = top + jnp.log(total)


def attend(qkv, stat, gain_q, gain_k, cosine, sine):
    rows = qkv.shape[0]
    shape = lambda kind: jax.ShapeDtypeStruct((rows, HD), kind)
    return ordered(
        attend_kernel,
        (),
        dict(
            grid=(1,),
            in_specs=[
                whole(rows, 3 * HD), whole(2, rows), whole(1, HD), whole(1, HD), whole(rows, HD), whole(rows, HD),
            ],
            out_specs=[whole(rows, HD)] * 5 + [whole(1, rows)],
            scratch_shapes=[pltpu.VMEM((HD, rows), BF16)],
        ),
        out_shape=[shape(BF16), shape(BF16), shape(BF16), shape(F32), shape(BF16),
                   jax.ShapeDtypeStruct((1, rows), F32)],
        compiler_params=params(48),
        cost_estimate=cost(8 * rows * rows * HD, 10 * rows * 384),
        name="attend",
    )(qkv, stat, gain_q, gain_k, cosine, sine)


def attend_back_kernel(
    q_ref, k_ref, v_ref, do_ref, of_ref, lse_ref, qkv_ref, stat_ref, gq_ref, gk_ref,
    cos_ref, sin_ref, dnq_ref, dnk_ref, dv_ref, means_ref, gains_ref, dk_acc, dv_acc,
):
    blocks = q_ref.shape[0] // BLOCK
    scale = HD ** (-0.5)
    dk_acc[...] = jnp.zeros_like(dk_acc)
    dv_acc[...] = jnp.zeros_like(dv_acc)

    def turn_back(grad, rows, part, gain_ref, out_ref):
        grad = grad.astype(BF16).astype(F32)
        grad = grad * cos_ref[rows, :] - pltpu.roll(grad, HD // 2, 1) * sin_ref[rows, :]
        raw = qkv_ref[rows, part * HD : (part + 1) * HD]
        out_ref[rows, :] = grad
        means_ref[part : part + 1, rows] = jnp.sum((grad * gain_ref[...] * raw).T, 0, keepdims=True)
        inverse = inv_of(stat_ref[part : part + 1, rows])
        return jnp.sum(grad * raw * inverse, 0, keepdims=True)

    gain_q = jnp.zeros((1, HD), F32)
    gain_k = jnp.zeros((1, HD), F32)
    for i in range(blocks):
        rows = slice(i * BLOCK, (i + 1) * BLOCK)
        reach = (i + 1) * BLOCK
        queries, grads = q_ref[rows, :], do_ref[rows, :]
        delta = jnp.sum((grads.astype(F32) * of_ref[rows, :]).T, 0, keepdims=True)
        scores = nt(k_ref[0:reach, :], queries) * scale
        probs = jnp.exp(scores - lse_ref[:, rows])
        slopes = nt(v_ref[0:reach, :], grads)
        grad_scores = (probs * (slopes - delta)).astype(BF16)
        dv_acc[0:reach, :] += nn(probs.astype(BF16), grads)
        dk_acc[0:reach, :] += nn(grad_scores, queries)
        gain_q += turn_back(tn(grad_scores, k_ref[0:reach, :]) * scale, rows, 0, gq_ref, dnq_ref)
    for i in range(blocks):
        rows = slice(i * BLOCK, (i + 1) * BLOCK)
        dv_ref[rows, :] = dv_acc[rows, :].astype(BF16)
        gain_k += turn_back(dk_acc[rows, :] * scale, rows, 1, gk_ref, dnk_ref)
    gains_ref[0:1, :] = gain_q
    gains_ref[1:2, :] = gain_k


def attend_back(q, k, v, grad, out, lse, qkv, stat, gain_q, gain_k, cosine, sine, after=()):
    rows = q.shape[0]
    shape = lambda kind: jax.ShapeDtypeStruct((rows, HD), kind)
    return ordered(
        attend_back_kernel,
        after,
        dict(
            grid=(1,),
            in_specs=[whole(rows, HD)] * 5
            + [whole(1, rows), whole(rows, 3 * HD), whole(2, rows), whole(1, HD), whole(1, HD)]
            + [whole(rows, HD)] * 2,
            out_specs=[whole(rows, HD)] * 3 + [whole(2, rows), whole(2, HD)],
            scratch_shapes=[pltpu.VMEM((rows, HD), F32), pltpu.VMEM((rows, HD), F32)],
        ),
        out_shape=[shape(F32), shape(F32), shape(BF16),
                   jax.ShapeDtypeStruct((2, rows), F32), jax.ShapeDtypeStruct((2, HD), F32)],
        compiler_params=params(48),
        cost_estimate=cost(20 * rows * rows * HD, 20 * rows * 384),
        name="attend_back",
    )(q, k, v, grad, out, lse, qkv, stat, gain_q, gain_k, cosine, sine)


def finish_kernel(
    dnq_ref, dnk_ref, dv_ref, qkv_ref, stat_ref, means_ref, gq_ref, gk_ref, out_ref
):
    for part, dn_ref, g_ref in ((0, dnq_ref, gq_ref), (1, dnk_ref, gk_ref)):
        raw = qkv_ref[:, part * HD : (part + 1) * HD]
        inverse = inv_of(stat_ref[part : part + 1, :])
        mean = as_column(means_ref[part : part + 1, :] / D)
        grad = inverse * (dn_ref[...] * g_ref[...] - raw * inverse * inverse * mean)
        out_ref[:, part * HD : (part + 1) * HD] = grad.astype(BF16)
    out_ref[:, 2 * HD :] = dv_ref[...]


def finish(dnq, dnk, dv, qkv, stat, means, gain_q, gain_k, after=()):
    rows = dnq.shape[0]
    head = pl.BlockSpec((PAIR, HD), lambda i: (i, 0))
    line = pl.BlockSpec((2, PAIR), lambda i: (0, i))
    full = pl.BlockSpec((PAIR, 3 * HD), lambda i: (i, 0))
    return ordered(
        finish_kernel,
        after,
        dict(
        grid=(rows // PAIR,),
        in_specs=[head, head, head, full, line, line, whole(1, HD), whole(1, HD)],
        out_specs=full,
        ),
        out_shape=jax.ShapeDtypeStruct((rows, 3 * HD), BF16),
        compiler_params=params(24),
        cost_estimate=cost(20 * rows * 3 * HD, 12 * rows * 3 * HD),
        name="finish",
    )(dnq, dnk, dv, qkv, stat, means, gain_q, gain_k)


def sort_cores(core, first, second, own_ref, other_ref, at):
    at = (0, at)

    @pl.when(core == 0)
    def _():
        own_ref[at] = first
        other_ref[at] = second

    @pl.when(core == 1)
    def _():
        own_ref[at] = second
        other_ref[at] = first


def normed_part_kernel(place_ref, a_ref, b_ref, w_ref, own_ref, other_ref):
    for at, g_ref in enumerate((a_ref, b_ref)):
        out = nt(g_ref[...], w_ref[...]).astype(BF16)
        sort_cores(place_ref[4], out[:TOK_DEV], out[TOK_DEV:], own_ref, other_ref, at)


def normed_part(place, grads, w_head, after=()):
    blocks = jax.ShapeDtypeStruct((2, 2, TOK_DEV, D), BF16)
    return ordered(
        normed_part_kernel,
        after,
        dict(
            num_scalar_prefetch=1,
            grid=(2,),
            in_specs=[
                pl.BlockSpec((PAIR, 3 * HD), lambda i, s: (s[2 * i], 0)),
                pl.BlockSpec((PAIR, 3 * HD), lambda i, s: (s[2 * i + 1], 0)),
                whole(D, 3 * HD),
            ],
            out_specs=[pl.BlockSpec((1, 2, TOK_DEV, D), lambda i, s: (i, 0, 0, 0))] * 2,
        ),
        out_shape=[blocks, blocks],
        compiler_params=params(24),
        cost_estimate=cost(8 * PAIR * D * 3 * HD, 16 * PAIR * D),
        name="normed_part",
    )(place, grads, grads, w_head)


def dw_kernel(normed_ref, grad_ref, out_ref):
    @pl.when(pl.program_id(0) == 0)
    def _():
        out_ref[...] = jnp.zeros_like(out_ref)

    out_ref[...] += tn(normed_ref[...], grad_ref[...])


def dw_product(normed, grads, after=()):
    rows = normed.shape[0]
    return ordered(
        dw_kernel,
        after,
        dict(
            grid=(rows // 512,),
            in_specs=[
                pl.BlockSpec((512, D), lambda i: (i, 0)),
                pl.BlockSpec((512, 3 * HD), lambda i: (i, 0)),
            ],
            out_specs=whole(D, 3 * HD),
        ),
        out_shape=jax.ShapeDtypeStruct((D, 3 * HD), F32),
        compiler_params=params(32),
        cost_estimate=cost(2 * rows * D * 3 * HD, 3 * rows * D),
        name="dw_product",
    )(normed, grads)


def picks(slots, dtype):
    shape = (SLOTS, slots.shape[1])
    numbers = lax.broadcasted_iota(jnp.int32, shape, 0)
    return [(numbers == slots[j : j + 1, :]).astype(dtype) for j in range(slots.shape[0])]


def pick_matrix(slots):
    return jnp.concatenate(picks(slots, F32), 0).astype(BF16)


def dispatch_kernel(place_ref, own_ref, other_ref, own_slot, other_slot, *refs):
    out_ref, column_ref, stack_ref = refs[-3:]
    stack_ref[0] = own_ref[...]
    core = place_ref[1]
    lanes = pl.ds(pl.multiple_of(place_ref[2] * HD, HD), HD)
    out = nn(pick_matrix(own_slot[0]), own_ref[...])
    out = (out + nn(pick_matrix(other_slot[0]), other_ref[...])).astype(BF16)
    for j in range(out_ref.shape[0]):
        out_ref[j] = out[j * SLOTS : (j + 1) * SLOTS]
    for side, row_ref in ((core, own_ref), (1 - core, other_ref)):
        column_ref[pl.ds(pl.multiple_of(side * TOK_DEV, TOK_DEV), TOK_DEV), :] = row_ref[:, lanes]


def dispatch(place, own, other, slots, buffers, after=()):
    blocks, local, _ = slots.shape
    kept = [] if buffers is None else list(buffers)
    return ordered(
        dispatch_kernel,
        after,
        dict(
            num_scalar_prefetch=1,
            grid=(1,),
            in_specs=[
                whole(*BLOCK_SHAPE),
                whole(*BLOCK_SHAPE),
                pl.BlockSpec((1, local, TOK_DEV), lambda i, s: (2 * s[0] + s[1], 0, 0)),
                pl.BlockSpec((1, local, TOK_DEV), lambda i, s: (2 * s[0] + 1 - s[1], 0, 0)),
            ]
            + [ANYWHERE] * len(kept),
            out_specs=[
                pl.BlockSpec((local, SLOTS, D), lambda i, s: (0, s[0], 0)),
                pl.BlockSpec((PAIR, HD), lambda i, s: (s[0], 0)),
                pl.BlockSpec((1, TOK_DEV, D), lambda i, s: (s[0], 0, 0)),
            ],
        ),
        out_shape=[
            in_hbm((local, blocks // 2 * SLOTS, D), BF16),
            in_hbm((blocks * TOK_DEV, HD), BF16),
            in_hbm((blocks // 2, TOK_DEV, D), BF16),
        ],
        input_output_aliases={5 + i: i for i in range(len(kept))},
        compiler_params=params(24),
        cost_estimate=cost(2 * PAIR * D * local * SLOTS, 4 * PAIR * D),
        name="dispatch",
    )(place, own, other, slots, slots, *kept)


def stack_kernel(place_ref, row_ref, out_ref):
    out_ref[0] = row_ref[0, 0]


def stack_of_core(core, rows, after=()):
    chips = rows.shape[0]
    return ordered(
        stack_kernel,
        after,
        dict(
            num_scalar_prefetch=1,
            grid=(chips,),
            in_specs=[pl.BlockSpec((1, 1, TOK_DEV, D), lambda i, s: (i, s[0], 0, 0))],
            out_specs=pl.BlockSpec((1, TOK_DEV, D), lambda i, s: (i, 0, 0)),
        ),
        out_shape=in_hbm((chips, TOK_DEV, D), BF16),
        compiler_params=params(16),
        cost_estimate=cost(0, 4 * chips * TOK_DEV * D),
        name="stack_of_core",
    )(core.reshape(1), rows)


def stack_dispatch_kernel(place_ref, own_ref, other_ref, own_slot, other_slot, out_ref):
    out = nn(pick_matrix(own_slot[0]), own_ref[0])
    out = (out + nn(pick_matrix(other_slot[0]), other_ref[0])).astype(BF16)
    for j in range(out_ref.shape[0]):
        out_ref[j] = out[j * SLOTS : (j + 1) * SLOTS]


def stack_dispatch(places, stacks, slots, after=()):
    chips = stacks.shape[1]
    blocks, local, _ = slots.shape
    row_shape = (None, 1, TOK_DEV, D)
    return ordered(
        stack_dispatch_kernel,
        after,
        dict(
            num_scalar_prefetch=1,
            grid=(chips,),
            in_specs=[
                pl.BlockSpec(row_shape, lambda i, s: (2 - 2 * s[chips + 1] + s[chips], i, 0, 0)),
                pl.BlockSpec(row_shape, lambda i, s: (3 - 2 * s[chips + 1] - s[chips], i, 0, 0)),
                pl.BlockSpec((1, local, TOK_DEV), lambda i, s: (2 * s[i] + s[chips], 0, 0)),
                pl.BlockSpec((1, local, TOK_DEV), lambda i, s: (2 * s[i] + 1 - s[chips], 0, 0)),
            ],
            out_specs=pl.BlockSpec((local, SLOTS, D), lambda i, s: (0, s[i], 0)),
        ),
        out_shape=in_hbm((local, blocks // 2 * SLOTS, D), BF16),
        compiler_params=params(24),
        cost_estimate=cost(2 * chips * PAIR * D * local * SLOTS, 4 * chips * PAIR * D),
        name="stack_dispatch",
    )(places, stacks, stacks, slots, slots)


def plain_dispatch_kernel(row_ref, slot_ref, out_ref):
    out = sum(nn(pick_matrix(slot_ref[i]), row_ref[i]) for i in range(2)).astype(BF16)
    for j in range(out_ref.shape[0]):
        out_ref[j] = out[j * SLOTS : (j + 1) * SLOTS]


def plain_dispatch(rows, slots, after=(), part=0, parts=1):
    blocks, local, _ = slots.shape
    rows = rows.reshape(blocks, parts, TOK_DEV, D)
    return ordered(
        plain_dispatch_kernel,
        after,
        dict(
            grid=(blocks // 2,),
            in_specs=[
                pl.BlockSpec((2, None, TOK_DEV, D), lambda i: (i, part, 0, 0)),
                pl.BlockSpec((2, local, TOK_DEV), lambda i: (i, 0, 0)),
            ],
            out_specs=pl.BlockSpec((local, SLOTS, D), lambda i: (0, i, 0)),
        ),
        out_shape=in_hbm((local, blocks // 2 * SLOTS, D), BF16),
        compiler_params=params(24),
        cost_estimate=cost(2 * blocks * TOK_DEV * D * local * SLOTS, 4 * blocks * TOK_DEV * D),
        name="plain_dispatch",
    )(rows, slots)


def combine_chip(row_ref, slot_ref):
    rows = jnp.concatenate([row_ref[j] for j in range(row_ref.shape[0])], 0)
    return [tn(pick_matrix(slot_ref[i]), rows).astype(BF16) for i in range(2)]


def combine_kernel(row_ref, slot_ref, out_ref):
    first, second = combine_chip(row_ref, slot_ref)
    out_ref[:TOK_DEV] = first
    out_ref[TOK_DEV:] = second


def combine(slot_rows, slots, after=()):
    blocks, local, _ = slots.shape
    rows = blocks * TOK_DEV
    return ordered(
        combine_kernel,
        after,
        dict(
            grid=(blocks // 2,),
            in_specs=[
                pl.BlockSpec((local, SLOTS, D), lambda i: (0, i, 0)),
                pl.BlockSpec((2, local, TOK_DEV), lambda i: (i, 0, 0)),
            ],
            out_specs=pl.BlockSpec((PAIR, D), lambda i: (i, 0)),
        ),
        out_shape=jax.ShapeDtypeStruct((rows, D), BF16),
        compiler_params=params(24),
        cost_estimate=cost(2 * rows * D * local * SLOTS, 4 * rows * D),
        name="combine",
    )(slot_rows, slots)


def combine_part_kernel(place_ref, a_ref, b_ref, a_slot, b_slot, own_ref, other_ref):
    for at, (row_ref, slot_ref) in enumerate(((a_ref, a_slot), (b_ref, b_slot))):
        first, second = combine_chip(row_ref, slot_ref)
        sort_cores(place_ref[4], first, second, own_ref, other_ref, at)


def chip_specs(slot_rows, slots):
    local, width = slots.shape[1], slot_rows.shape[2]
    rows = [
        pl.BlockSpec((local, SLOTS, width), lambda i, s, n=n: (0, s[2 * i + n], 0)) for n in (0, 1)
    ]
    spots = [
        pl.BlockSpec((2, local, TOK_DEV), lambda i, s, n=n: (s[2 * i + n], 0, 0)) for n in (0, 1)
    ]
    return rows + spots


def combine_part(place, slot_rows, slots, after=()):
    local, width = slots.shape[1], slot_rows.shape[2]
    shape = jax.ShapeDtypeStruct((2, 2, TOK_DEV, width), BF16)
    return ordered(
        combine_part_kernel,
        after,
        dict(
            num_scalar_prefetch=1,
            grid=(2,),
            in_specs=chip_specs(slot_rows, slots),
            out_specs=[pl.BlockSpec((1, 2, TOK_DEV, width), lambda i, s: (i, 0, 0, 0))] * 2,
        ),
        out_shape=[shape, shape],
        compiler_params=params(24),
        cost_estimate=cost(4 * PAIR * D * local * SLOTS, 8 * PAIR * D),
        name="combine_part",
    )(place, slot_rows, slot_rows, slots, slots)


def slope_kernel(g_ref, wd_ref, out_ref):
    out_ref[0] = nt(g_ref[0], wd_ref[0])


def slopes(grads, w_down, after=()):
    local, count, _ = grads.shape
    hidden = w_down.shape[1]
    chunk = hidden // 2
    return ordered(
        slope_kernel,
        after,
        dict(
            grid=(local, 2),
            in_specs=[
                pl.BlockSpec((1, count, D), lambda j, f: (j, 0, 0)),
                pl.BlockSpec((1, chunk, D), lambda j, f: (j, f, 0)),
            ],
            out_specs=pl.BlockSpec((1, count, chunk), lambda j, f: (j, 0, f)),
        ),
        out_shape=in_hbm((local, count, hidden), F32),
        compiler_params=params(24),
        cost_estimate=cost(2 * local * count * hidden * D, 2 * local * hidden * D),
        name="slopes",
    )(grads, w_down)


def expert_kernel(first_ref, x_ref, h_ref, wg_ref, wu_ref, wr_ref, *rest, full, offset):
    if full:
        (act_ref, dg_ref, du_ref, gate_ref, z_ref, z_s, dp_s) = rest
    else:
        (act_ref, dg_ref, du_ref, gate_ref) = rest
    step, steps = pl.program_id(1), pl.num_programs(1)
    rows = x_ref[0]

    @pl.when(step == 0)
    def _():
        logits = nn(rows, wr_ref[...])
        lane = lax.broadcasted_iota(jnp.int32, logits.shape, 1)
        logits = jnp.where(lane < EXPERTS, logits, NEG_FILL)
        powers = jnp.exp(logits - jnp.max(logits, -1, keepdims=True))
        mine = jnp.where(lane == first_ref[0] + offset + pl.program_id(0), powers, 0.0)
        gate = jnp.sum(mine, -1, keepdims=True) / jnp.sum(powers, -1, keepdims=True)
        gate_ref[0] = jnp.broadcast_to(gate, gate_ref.shape[1:])
        if full:
            z_s[...] = jnp.zeros_like(z_s)
            dp_s[...] = jnp.zeros_like(dp_s)

    gate = gate_ref[0, :, 0:1]
    gate_pre = nn(rows, wg_ref[0])
    up_pre = nn(rows, wu_ref[0])
    slope = h_ref[0]
    sig = jax.nn.sigmoid(gate_pre)
    silu = gate_pre * sig
    act = (silu * up_pre).astype(BF16)
    grad_act = slope * gate
    grad_gate = (grad_act * up_pre * sig * (1.0 + gate_pre * (1.0 - sig))).astype(BF16)
    grad_up = (grad_act * silu).astype(BF16)
    act_ref[0] = act
    dg_ref[0] = grad_gate
    du_ref[0] = grad_up
    if full:
        dp_s[...] += jnp.broadcast_to(
            jnp.sum(act.astype(F32) * slope, -1, keepdims=True), dp_s.shape
        )
        z_s[...] += nt(grad_gate, wg_ref[0]) + nt(grad_up, wu_ref[0])

        @pl.when(step == steps - 1)
        def _():
            z_ref[0, :, :D] = z_s[...].astype(BF16)
            lane = lax.broadcasted_iota(jnp.int32, dp_s.shape, 1)
            mine = first_ref[0] + offset + pl.program_id(0)
            high = dp_s[...].astype(BF16).astype(F32)
            parts = jnp.where(lane == mine, high, 0.0)
            parts = jnp.where(lane == mine + EXPERTS, dp_s[...] - high, parts)
            z_ref[0, :, D:] = parts.astype(BF16)


def experts(first, rows, slope, w_gate, w_up, router, full, only=None, after=()):
    local, count, _ = rows.shape
    offset, number = (0, local) if only is None else only
    hidden = w_gate.shape[2]
    chunk = hidden // 2
    row_spec = pl.BlockSpec((1, count, D), lambda j, f, s: (j, 0, 0))
    mid_spec = pl.BlockSpec((1, count, chunk), lambda j, f, s: (j, 0, f))
    lane_spec = pl.BlockSpec((1, count, HD), lambda j, f, s: (j, 0, 0))
    in_w = pl.BlockSpec((1, D, chunk), lambda j, f, s: (j + offset, 0, f))
    mid_shape = in_hbm((number, count, hidden), BF16)
    lane_shape = jax.ShapeDtypeStruct((number, count, HD), F32)
    out_specs = [mid_spec, mid_spec, mid_spec, lane_spec]
    out_shape = [mid_shape, mid_shape, mid_shape, lane_shape]
    scratch = []
    if full:
        out_specs += [pl.BlockSpec((1, count, D + HD), lambda j, f, s: (j, 0, 0))]
        out_shape += [in_hbm((number, count, D + HD), BF16)]
        scratch += [pltpu.VMEM((count, D), F32), pltpu.VMEM((count, HD), F32)]
    unit = 2 * number * count * hidden * D
    return ordered(
        functools.partial(expert_kernel, full=full, offset=offset),
        after,
        dict(
            num_scalar_prefetch=1,
            grid=(number, 2),
            in_specs=[
                pl.BlockSpec((1, count, D), lambda j, f, s: (j + offset, 0, 0)),
                pl.BlockSpec((1, count, chunk), lambda j, f, s: (j + offset, 0, f)),
                in_w,
                in_w,
                pl.BlockSpec((D, HD), lambda j, f, s: (0, 0)),
            ],
            out_specs=out_specs,
            scratch_shapes=scratch,
        ),
        out_shape=out_shape,
        compiler_params=params(56),
        cost_estimate=cost((4 if full else 2) * unit, 4 * number * hidden * D + 8 * number * count * D),
        name="experts_full" if full else "experts_half",
    )(first, rows, slope, w_gate, w_up, router)


def down_kernel(act_ref, gate_ref, wd_ref, out_ref):
    out_ref[0] = (nn(act_ref[0], wd_ref[0]) * gate_ref[0, :, 0:1]).astype(BF16)


def down(act, gate, w_down, after=()):
    local, count, hidden = act.shape
    chunk = D // 2
    return ordered(
        down_kernel,
        after,
        dict(
            grid=(local, 2),
            in_specs=[
                pl.BlockSpec((1, count, hidden), lambda j, f: (j, 0, 0)),
                pl.BlockSpec((1, count, HD), lambda j, f: (j, 0, 0)),
                pl.BlockSpec((1, hidden, chunk), lambda j, f: (j, 0, f)),
            ],
            out_specs=pl.BlockSpec((1, count, chunk), lambda j, f: (j, 0, f)),
        ),
        out_shape=jax.ShapeDtypeStruct((local, count, D), BF16),
        compiler_params=params(24),
        cost_estimate=cost(2 * local * count * hidden * D, 2 * local * hidden * D),
        name="down",
    )(act, gate, w_down)


def weights_kernel(
    half_ref, xa, xb, dga, dgb, dua, dub, aa, ab, ga, gb, gate_a, gate_b, *refs
):
    gate_ref, up_ref, down_ref = refs[-3:]
    rows = jnp.concatenate([xa[0], xb[0]], 0)
    gate_ref[0] = tn(rows, jnp.concatenate([dga[0], dgb[0]], 0))
    up_ref[0] = tn(rows, jnp.concatenate([dua[0], dub[0]], 0))
    grad_a = (ga[0].astype(F32) * gate_a[0, :, 0:1]).astype(BF16)
    grad_b = (gb[0].astype(F32) * gate_b[0, :, 0:1]).astype(BF16)
    down_ref[0] = tn(
        jnp.concatenate([aa[0], ab[0]], 0), jnp.concatenate([grad_a, grad_b], 0)
    )


def weight_grads(only, half, x_pair, dg_pair, du_pair, act_pair, g_pair, gate_pair, buffers, after=()):
    local, count, _ = x_pair[0].shape
    start, number = only
    hidden = dg_pair[0].shape[2]
    kept = [] if buffers is None else list(buffers)
    chunk = hidden // 2

    def spec(width, by_half, single):
        at = 0 if single else start
        if by_half is None:
            return pl.BlockSpec((1, count, width), lambda j, f, s: (j + at, 0, 0))
        if by_half:
            return pl.BlockSpec((1, count, width), lambda j, f, s: (j + at, 0, s[0]))
        return pl.BlockSpec((1, count, width), lambda j, f, s: (j + at, 0, f))

    in_specs = [
        spec(D // 2, True, False), spec(D // 2, True, False),
        spec(chunk, False, False), spec(chunk, False, True),
        spec(chunk, False, False), spec(chunk, False, True),
        spec(chunk, True, False), spec(chunk, True, True),
        spec(D // 2, False, False), spec(D // 2, False, False),
        spec(HD, None, False), spec(HD, None, True),
    ]
    unit = 2 * number * count * hidden * D
    return ordered(
        weights_kernel,
        after,
        dict(
            num_scalar_prefetch=1,
            grid=(number, 2),
            in_specs=in_specs + [ANYWHERE] * len(kept),
            out_specs=[
                pl.BlockSpec((1, D // 2, chunk), lambda j, f, s: (j + start, 0, f)),
                pl.BlockSpec((1, D // 2, chunk), lambda j, f, s: (j + start, 0, f)),
                pl.BlockSpec((1, chunk, D // 2), lambda j, f, s: (j + start, 0, f)),
            ],
        ),
        out_shape=[
            in_hbm((local, D // 2, hidden), F32),
            in_hbm((local, D // 2, hidden), F32),
            in_hbm((local, hidden // 2, D), F32),
        ],
        input_output_aliases={13 + i: i for i in range(len(kept))},
        compiler_params=params(56),
        cost_estimate=cost(3 * unit, 6 * number * hidden * D + 8 * number * count * D),
        name="weight_grads",
    )(half, *x_pair, *dg_pair, *du_pair, *act_pair, *g_pair, *gate_pair, *kept)


def softmax_of(mixed, router):
    logits = nn(mixed, router)
    lane = lax.broadcasted_iota(jnp.int32, logits.shape, 1)
    logits = jnp.where(lane < EXPERTS, logits, NEG_FILL)
    powers = jnp.exp(logits - jnp.max(logits, -1, keepdims=True))
    return powers / jnp.sum(powers, -1, keepdims=True)


def pair_kernel(group_ref, near_ref, far_ref, out_ref):
    out_ref[group_ref[0]] = near_ref[...]
    out_ref[1 - group_ref[0]] = far_ref[...]


def pair_up(group, near, far, after=()):
    return ordered(
        pair_kernel,
        after,
        dict(
            num_scalar_prefetch=1,
            grid=(1,),
            in_specs=[whole(*near.shape)] * 2,
            out_specs=whole(2, *near.shape),
        ),
        out_shape=jax.ShapeDtypeStruct((2,) + near.shape, near.dtype),
        compiler_params=params(16),
        name="pair_up",
    )(group.reshape(1).astype(jnp.int32), near, far)


def out_kernel(att_ref, w_ref, tok_ref, gain_ref, hidden_ref, mixed_ref, sums_ref, acc_ref):
    step, steps = pl.program_id(0), pl.num_programs(0)
    heads = jnp.concatenate([att_ref[i] for i in range(att_ref.shape[0])], 1)
    part = nn(heads, w_ref[...].reshape(heads.shape[1], D))

    @pl.when(step == 0)
    def _():
        acc_ref[...] = part

    @pl.when(step > 0)
    def _():
        acc_ref[...] += part

    @pl.when(step == steps - 1)
    def _():
        branch = acc_ref[...]
        hidden = tok_ref[...].astype(F32) + branch
        hidden_ref[...] = hidden
        mixed_ref[...] = (hidden * inv_rms(hidden) * gain_ref[...]).astype(BF16)
        total = jnp.sum(jnp.sum(branch * branch, -1, keepdims=True), 0, keepdims=True)
        sums_ref[...] = jnp.broadcast_to(total, sums_ref.shape)


def out_rows_spec(weights, heads):
    members, groups, rows, _ = weights.shape
    count = heads * HD // rows
    steps = members // count
    return pl.BlockSpec((count, None, rows, D), lambda i: (i % steps, i // steps, 0, 0))


def project_out(att, weights, tokens, gain_row, after=()):
    chunk = 4
    return ordered(
        out_kernel,
        after,
        dict(
        grid=(HEADS // chunk,),
        in_specs=[
            pl.BlockSpec((chunk, TOK_DEV, HD), lambda i, *_: (i, 0, 0)),
            out_rows_spec(weights, chunk),
            whole(*BLOCK_SHAPE),
            whole(1, D),
        ],
        out_specs=[whole(*BLOCK_SHAPE), whole(*BLOCK_SHAPE), whole(1, HD)],
        scratch_shapes=[pltpu.VMEM(BLOCK_SHAPE, F32)],
        ),
        out_shape=[
            jax.ShapeDtypeStruct(BLOCK_SHAPE, F32),
            jax.ShapeDtypeStruct(BLOCK_SHAPE, BF16),
            jax.ShapeDtypeStruct((1, HD), F32),
        ],
        compiler_params=params(24),
        cost_estimate=cost(2 * TOK_DEV * D * D, 2 * D * D),
        name="project_out",
    )(att, weights, tokens, gain_row)


def token_back_kernel(
    a, b, c, d, e, mixed_ref, hidden_ref, cot_ref, router_ref, gain_ref,
    grad_ref, wide_ref,
):
    probs = softmax_of(mixed_ref[...], router_ref[...])
    grad = sum(ref[...].astype(F32) for ref in (a, b, c, d, e))
    dp = grad[:, D : D + HD] + pltpu.roll(grad[:, D : D + HD], EXPERTS, 1)
    logits = (probs * (dp - jnp.sum(probs * dp, -1, keepdims=True))).astype(BF16)
    grad = grad[:, :D] + nt(logits, router_ref[...])
    hidden = hidden_ref[...]
    inverse = inv_rms(hidden)
    scaled = grad * gain_ref[...]
    mean = jnp.mean(scaled * hidden, -1, keepdims=True)
    result = cot_ref[...].astype(F32) + inverse * (scaled - hidden * inverse * inverse * mean)
    grad_ref[...] = result
    wide_ref[:, :D] = result.astype(BF16)
    wide_ref[:, D : D + HD] = logits
    wide_ref[:, D + HD :] = jnp.zeros((TOK_DEV, HD), BF16)
    part = jnp.sum(grad * hidden * inverse, 0, keepdims=True)
    high = part.astype(BF16).astype(F32)
    rows = lax.broadcasted_iota(jnp.int32, (2 * HEADS, HD), 0)
    spread = jnp.zeros((2 * HEADS, HD), F32)
    for i in range(HEADS):
        lanes = slice(i * HD, (i + 1) * HD)
        spread = jnp.where(rows == i, high[:, lanes], spread)
        spread = jnp.where(rows == HEADS + i, part[:, lanes] - high[:, lanes], spread)
    wide_ref[: 2 * HEADS, D + HD :] = spread.astype(BF16)


def term_specs(terms):
    specs, arrays = [], []
    for term in terms:
        if isinstance(term, tuple):
            arrays.append(term[0])
            shape = (None, None) + term[0].shape[2:]
            specs.append(pl.BlockSpec(shape, lambda i, n=term[1]: n + (0, 0)))
        else:
            arrays.append(term)
            specs.append(whole(*term.shape))
    return specs, arrays


def token_back(terms, mixed, hidden, cotangent, router, gain_row, after=()):
    specs, arrays = term_specs(terms)
    return ordered(
        token_back_kernel,
        after,
        dict(
            grid=(1,),
            in_specs=specs
            + [whole(*BLOCK_SHAPE)] * 3
            + [whole(D, HD), whole(1, D)],
            out_specs=[whole(*BLOCK_SHAPE), whole(TOK_DEV, D + 2 * HD)],
        ),
        out_shape=[
            jax.ShapeDtypeStruct(BLOCK_SHAPE, F32),
            jax.ShapeDtypeStruct((TOK_DEV, D + 2 * HD), BF16),
        ],
        compiler_params=params(40),
        cost_estimate=cost(30 * TOK_DEV * D, 20 * TOK_DEV * D),
        name="token_back",
    )(*arrays, mixed, hidden, cotangent, router, gain_row)


def out_back_kernel(grad_ref, w_ref, out_ref):
    out = nt(grad_ref[...], w_ref[...].reshape(-1, D)).astype(BF16)
    for i in range(out_ref.shape[0]):
        out_ref[i] = out[:, i * HD : (i + 1) * HD]


def out_back(wide, weights):
    chunk = 4
    return ordered(
        out_back_kernel,
        (),
        dict(
        grid=(HEADS // chunk,),
        in_specs=[
            pl.BlockSpec(BLOCK_SHAPE, lambda i: (0, 0)),
            out_rows_spec(weights, chunk),
        ],
        out_specs=pl.BlockSpec((chunk, TOK_DEV, HD), lambda i: (i, 0, 0)),
        ),
        out_shape=jax.ShapeDtypeStruct((HEADS, TOK_DEV, HD), BF16),
        compiler_params=params(24),
        cost_estimate=cost(2 * TOK_DEV * D * D, 2 * D * D),
        name="out_back",
    )(wide, weights)


def tokens_grad_kernel(
    a, b, c, d, e, tok_ref, gain_ref, grad_ref, out_ref
):
    grad = sum(ref[...].astype(F32) for ref in (a, b, c, d, e))
    inputs = tok_ref[...].astype(F32)
    inverse = inv_rms(inputs)
    scaled = grad * gain_ref[...]
    mean = jnp.mean(scaled * inputs, -1, keepdims=True)
    result = grad_ref[...] + inverse * (scaled - inputs * inverse * inverse * mean)
    out_ref[...] = result.astype(BF16)


def final_tokens(terms, tokens, gain_row, grad_hidden, after=()):
    specs, arrays = term_specs(terms)
    return ordered(
        tokens_grad_kernel,
        after,
        dict(
            grid=(1,),
            in_specs=specs
            + [whole(*BLOCK_SHAPE), whole(1, D), whole(*BLOCK_SHAPE)],
            out_specs=whole(*BLOCK_SHAPE),
        ),
        out_shape=jax.ShapeDtypeStruct(BLOCK_SHAPE, BF16),
        compiler_params=params(40),
        cost_estimate=cost(30 * TOK_DEV * D, 20 * TOK_DEV * D),
        name="final_tokens",
    )(*arrays, tokens, gain_row, grad_hidden)


def owner_rows_kernel(place_ref, att_ref, mixed_ref, wide_ref, out_ref, moe_ref):
    step, steps = pl.program_id(0), pl.num_programs(0)

    @pl.when(step == 0)
    def _():
        out_ref[...] = jnp.zeros_like(out_ref)
        moe_ref[...] = jnp.zeros_like(moe_ref)

    out_ref[:, :D] += tn(att_ref[...], wide_ref[:, :D])
    out_ref[:, D:] += tn(mixed_ref[...], wide_ref[:, D : D + HD])
    tail = wide_ref[:, D + HD :].astype(F32)
    rows = lax.broadcasted_iota(jnp.int32, tail.shape, 0) % TOK_DEV
    mine = (rows == place_ref[0]) | (rows == place_ref[0] + HEADS)
    moe_ref[...] += jnp.sum(jnp.where(mine, tail, 0.0), 0, keepdims=True)

    @pl.when(step == steps - 1)
    def _():
        lane = lax.broadcasted_iota(jnp.int32, (HD, HD), 1)
        out_ref[:, D:] = jnp.where(lane == EXPERTS, as_column(moe_ref[...]), out_ref[:, D:])


def owner_rows(place, att, mixed_columns, wide_all, after=()):
    rows, width = wide_all.shape
    chunk = rows // 4
    return ordered(
        owner_rows_kernel,
        after,
        dict(
            num_scalar_prefetch=1,
            grid=(4,),
            in_specs=[
                pl.BlockSpec((chunk, HD), lambda i, s: (i, 0)),
                pl.BlockSpec((chunk, HD), lambda i, s: (i, 0)),
                pl.BlockSpec((chunk, width), lambda i, s: (i, 0)),
            ],
            out_specs=whole(HD, D + HD),
            scratch_shapes=[pltpu.VMEM((1, HD), F32)],
        ),
        out_shape=jax.ShapeDtypeStruct((HD, D + HD), F32),
        compiler_params=params(24),
        cost_estimate=cost(2 * rows * D * HD, 2 * rows * D),
        name="owner_rows",
    )(place.reshape(1).astype(jnp.int32), att, mixed_columns, wide_all)


def unpack_kernel(in_ref, wq_ref, wk_ref, wv_ref, gain_ref, q_ref, k_ref, v_ref, sums_ref):
    heads = in_ref.shape[0] // 2
    total = jnp.zeros((q_ref.shape[0], 1), F32)
    for part, (w_ref, out_ref) in enumerate(((wq_ref, q_ref), (wk_ref, k_ref), (wv_ref, v_ref))):
        for h in range(heads):
            spot = (slice(0, q_ref.shape[0]), slice(part * HD, (part + 1) * HD))
            piece = in_ref[(h,) + spot].astype(F32) + in_ref[(heads + h,) + spot].astype(F32)
            lanes = slice(h * HD, (h + 1) * HD)
            out_ref[:, lanes] = piece
            total += jnp.sum(w_ref[:, lanes].astype(F32) * piece, -1, keepdims=True)
    sums_ref[...] = jnp.broadcast_to(total / gain_ref[...], sums_ref.shape)


def unpack(arrived, weights, gain, after=()):
    rows = weights[0].shape[0]
    shape = jax.ShapeDtypeStruct((rows, D), F32)
    return ordered(
        unpack_kernel,
        after,
        dict(
            grid=(1,),
            in_specs=[whole(*arrived.shape)] + [whole(rows, D)] * 3 + [whole(rows, 1)],
            out_specs=[whole(rows, D)] * 3 + [whole(rows, HD)],
        ),
        out_shape=[shape] * 3 + [jax.ShapeDtypeStruct((rows, HD), F32)],
        compiler_params=params(24),
        cost_estimate=cost(6 * rows * D, 20 * rows * D),
        name="unpack",
    )(arrived, *weights, gain.astype(F32).reshape(rows, 1))


def tie_kernel(in_ref, out_ref):
    out_ref[...] = in_ref[...]


def tie(array, after):
    return ordered(
        tie_kernel,
        after,
        dict(grid=(1,), in_specs=[whole(*array.shape)], out_specs=whole(*array.shape)),
        out_shape=jax.ShapeDtypeStruct(array.shape, array.dtype),
        compiler_params=params(16),
        name="tie",
    )(array)


def swap(value, axis):
    return lax.ppermute(value, axis, [(0, 1), (1, 0)])


def total_over_ep(value):
    value = value + swap(value, "core")
    value = value + swap(value, "x")
    value = value + lax.ppermute(value, "z", [(0, 1), (1, 0), (2, 3), (3, 2)])
    return value + lax.ppermute(value, "z", [(0, 2), (2, 0), (1, 3), (3, 1)])


def of_groups(value):
    return lax.all_gather(value, ("grp", "core"))


def gather_rows(value):
    return lax.all_gather(value, EP, axis=0, tiled=True)


def reduce_rows(value):
    return lax.psum_scatter(value, EP, scatter_dimension=0, tiled=True)


CHIP_ORDER = ((0, 1, 2, 3), (1, 0, 2, 3), (2, 1, 3, 0), (3, 2, 1, 0))


def chip_places():
    z, x = lax.axis_index("z"), lax.axis_index("x")
    order = jnp.asarray(CHIP_ORDER, jnp.int32)[z]
    return [[order[s] * 2 + (x if r == 0 else 1 - x) for r in range(2)] for s in range(4)]


def shift(value, pairs):
    return lax.ppermute(value, "z", pairs)


def choose_kernel(flag_ref, *refs):
    out_ref = refs[-1]
    for i in range(len(refs) - 1):

        @pl.when(flag_ref[i] == 1)
        def _(i=i):
            out_ref[...] = refs[i][...]


def choose(flags, options, after=()):
    return ordered(
        choose_kernel,
        after,
        dict(
            num_scalar_prefetch=1,
            grid=(1,),
            in_specs=[whole(*BLOCK_SHAPE)] * len(options),
            out_specs=whole(*BLOCK_SHAPE),
        ),
        out_shape=jax.ShapeDtypeStruct(BLOCK_SHAPE, BF16),
        compiler_params=params(16),
        cost_estimate=cost(TOK_DEV * D, 2 * (len(options) + 1) * TOK_DEV * D),
        name="choose",
    )(flags, *options)


def gather_steps(block, use, work):
    z = lax.axis_index("z")
    flags = lambda *tests: jnp.stack([jnp.asarray(test, jnp.int32) for test in tests])

    def use_now(arrived, last):
        for s, r, own, far in arrived:
            last = use(s, r, own, far, [last])
        return last

    below1 = shift(block, [(0, 1), (1, 2), (2, 3)])
    above1 = shift(block, [(3, 2), (2, 1), (1, 0)])
    across0 = swap(block, "x")
    far00 = swap(block, "core")
    last = work(0, block)
    column1 = last = choose(flags(z == 0, z != 0), [above1, below1], [last])
    below2 = shift(below1, [(1, 2), (2, 3)])
    above2 = shift(above1, [(2, 1), (1, 0)])
    across1 = swap(column1, "x")
    far01, far10 = swap(across0, "core"), swap(column1, "core")
    last = use_now([(0, 0, block, far00), (0, 1, across0, far01), (1, 0, column1, far10)], last)
    last = work(1, last)
    column2 = last = choose(
        flags(z == 0, z == 3, (z == 1) | (z == 2)), [above2, below2, above1], [last]
    )
    below3 = shift(below2, [(2, 3)])
    above3 = shift(above2, [(1, 0)])
    across2 = swap(column2, "x")
    far11, far20 = swap(across1, "core"), swap(column2, "core")
    last = use_now([(1, 1, across1, far11), (2, 0, column2, far20)], last)
    last = work(2, last)
    column3 = last = choose(
        flags(z == 0, z == 1, z == 2, z == 3), [above3, above2, below2, below3], [last]
    )
    across3 = swap(column3, "x")
    far21, far30 = swap(across2, "core"), swap(column3, "core")
    last = use_now([(2, 1, across2, far21), (3, 0, column3, far30)], last)
    last = work(3, last)
    far31 = swap(across3, "core")
    return use_now([(3, 1, across3, far31)], last)


def sum_kernel(*refs):
    out_ref = refs[-1]
    total = refs[0][...].astype(F32)
    for ref in refs[1:-1]:
        total = total + ref[...].astype(F32)
    out_ref[...] = total.astype(out_ref.dtype)


def sum_blocks(terms, after=(), dtype=BF16):
    specs, arrays = term_specs(terms)
    return ordered(
        sum_kernel,
        after,
        dict(grid=(1,), in_specs=specs, out_specs=whole(*arrays[0].shape[-2:])),
        out_shape=jax.ShapeDtypeStruct(arrays[0].shape[-2:], dtype),
        compiler_params=params(16),
        cost_estimate=cost(len(terms) * TOK_DEV * D, 2 * (len(terms) + 1) * TOK_DEV * D),
        name="sum_blocks",
    )(*arrays)


def pass_on(place, near_up, far_up, near_down, far_down, below, above, after=()):
    def kernel(place_ref, nu, fu, nd, fd, below_ref, above_ref, up_ref, down_ref):
        z = place_ref[0]

        def store(out_ref, source_ref, arrived_ref):
            total = source_ref[...].astype(F32) + arrived_ref[...].astype(F32)
            out_ref[...] = total.astype(BF16)

        for edge, near, far, arrived, out_ref in (
            (0, nu, fu, below_ref, up_ref),
            (3, nd, fd, above_ref, down_ref),
        ):
            pl.when(z == edge)(functools.partial(store, out_ref, near, arrived))
            pl.when(z != edge)(functools.partial(store, out_ref, far, arrived))

    shape = jax.ShapeDtypeStruct(below.shape, BF16)
    return ordered(
        kernel,
        after,
        dict(
            num_scalar_prefetch=1,
            grid=(1,),
            in_specs=[whole(*below.shape)] * 6,
            out_specs=[whole(*below.shape)] * 2,
        ),
        out_shape=[shape, shape],
        compiler_params=params(24),
        cost_estimate=cost(4 * TOK_DEV * D, 16 * TOK_DEV * D),
        name="pass_on",
    )(place, near_up, far_up, near_down, far_down, below, above)


def reduce_steps(parts, work):
    place = lax.axis_index("z").reshape(1).astype(jnp.int32)
    last, sources = [], {}
    for s in (3, 1):
        own, other = parts(s, last)
        near = swap(other, "core")
        last = [own]
        for i in range(2):
            sources[s - i] = lambda r, i=i, own=own, near=near: [(own, (i, r)), (near, (i, r))]
    crossed = {}
    last = last[0]
    for s in (3, 2, 1, 0):
        last = sum_blocks(sources[s](1), [last])
        crossed[s] = swap(last, "x")
    last = work(0, last)
    low = {}
    low[3] = last = sum_blocks(sources[3](0) + [crossed[3]], [last])
    up3 = shift(low[3], [(0, 1)])
    down3 = shift(low[3], [(3, 2)])
    last = work(1, last)
    low[2] = last = sum_blocks(sources[2](0) + [crossed[2]], [last])
    up2, down2 = pass_on(place, low[2], low[3], low[2], low[3], up3, down3)
    last = work(2, up2)
    up2 = shift(up2, [(0, 1), (1, 2)])
    down2 = shift(down2, [(3, 2), (2, 1)])
    low[1] = last = sum_blocks(sources[1](0) + [crossed[1]], [last])
    up1, down1 = pass_on(place, low[1], low[2], low[1], low[1], up2, down2)
    last = work(3, up1)
    up1 = shift(up1, [(0, 1), (1, 2), (2, 3)])
    down1 = shift(down1, [(3, 2), (2, 1), (1, 0)])
    return sources[0](0) + [crossed[0], up1, down1], last


def expert_slots(routes_all, first, local):
    rows = routes_all.shape[0]
    ids = first + jnp.arange(local, dtype=jnp.int32)
    named = jnp.any(routes_all[None, :, :] == ids[:, None, None], -1).reshape(
        local, rows // TOK_DEV, TOK_DEV
    )
    places = jnp.arange(TOK_DEV, dtype=jnp.int32)
    upto = (places[:, None] <= places[None, :]).astype(BF16)
    rank = jnp.einsum(
        "ebt,ts->ebs", named.astype(BF16), upto, preferred_element_type=F32
    ).astype(jnp.int32)
    base = (jnp.arange(rows // TOK_DEV, dtype=jnp.int32) % 2) * CAP
    slots = jnp.where(named, rank - 1 + base[None, :, None], -1)
    return jnp.transpose(slots, (1, 0, 2))


def fast_shards(
    tokens, w_query, w_key, w_value, w_output, w_router, attn_gain, query_gain, key_gain,
    moe_gain, w_gate, w_up, w_down, routes, cotangent,
):
    Order.marks.clear()
    group = lax.axis_index("grp")
    place = lax.axis_index(EP)
    members = lax.axis_size(EP)
    seq = TOK_DEV * members
    local = w_gate.shape[0]
    wide = w_query.shape[0]
    first = (place * local).reshape(1).astype(jnp.int32)

    core = lax.axis_index("core").astype(jnp.int32)
    chips = chip_places()
    small = jnp.concatenate(
        [
            w_router,
            routes.reshape(-1, EXPERTS).astype(BF16),
            jnp.stack([attn_gain, query_gain, key_gain, moe_gain]),
            jnp.zeros((12, EXPERTS), BF16),
        ],
        0,
    ).reshape(16, 3 * HD)
    columns = jnp.stack([w_query, w_key, w_value], 1).reshape(wide, 3, HEADS, HD)
    columns = jnp.transpose(columns, (2, 0, 1, 3)).reshape(HEADS, wide, 3 * HD)
    columns = jnp.concatenate([columns, jnp.broadcast_to(small, (HEADS,) + small.shape)], 1)
    mine = lax.all_to_all(columns, EP, 0, 0, tiled=True)
    other = swap(mine, "grp")
    both = jnp.where(group == 0, jnp.stack([mine, other]), jnp.stack([other, mine]))
    w_head = both[:, :, :wide].reshape(D, 3 * HD)
    small_all = both[:, :, wide:].reshape(2 * members, -1, EXPERTS)
    route_rows = TOK_DEV * TOPK // EXPERTS
    router_full = small_all[:, :wide].reshape(D, EXPERTS)
    routes_all = (
        small_all[:, wide : wide + route_rows].reshape(2, seq, TOPK).astype(jnp.int32)
    )
    gains = jnp.transpose(
        small_all[:, wide + route_rows : wide + route_rows + 4], (1, 0, 2)
    ).reshape(4, D).astype(F32)
    router_wide = jnp.concatenate([router_full, jnp.zeros((D, HD - EXPERTS), BF16)], 1)
    head_gains = lax.dynamic_slice(gains, (0, place * HD), (4, HD))
    gain_q, gain_k = head_gains[1:2], head_gains[2:3]
    attn_row, moe_row = gains[0:1], gains[3:4]

    far_out = swap(w_output, "grp")

    slots_own = expert_slots(lax.dynamic_index_in_dim(routes_all, group, 0, False), first, local)
    slots_other = expert_slots(
        lax.dynamic_index_in_dim(routes_all, 1 - group, 0, False), first, local
    )

    positions = jnp.arange(seq, dtype=jnp.int32)
    half_dim = HD // 2
    frequency = jnp.exp(-(2.0 * jnp.arange(half_dim, dtype=F32) / HD) * math.log(10000.0))
    angles = positions.astype(F32)[:, None] * frequency[None, :]
    cosine = jnp.concatenate([jnp.cos(angles)] * 2, 1)
    sine = jnp.concatenate([-jnp.sin(angles), jnp.sin(angles)], 1)

    kept = [None]

    def use_tokens(s, r, own, far, after):
        spot = jnp.stack([chips[s][r], core])
        kept[0] = project(spot, own, far, w_head, attn_row, kept[0], seq, after)
        return kept[0][2]

    def start_work(step, last):
        if step == 3:
            kept.append(pair_up(group, w_output, far_out, [last, mine]))
            return kept[1]
        return last

    gather_steps(tokens, use_tokens, start_work)
    output_full = gather_rows(kept[1][None])
    cot_own = gather_rows(cotangent)
    normed_all, qkv, stat = kept[0]
    stat = total_over_ep(stat)
    q16, k16, v16, attn_float, att_head, lse = attend(qkv, stat, gain_q, gain_k, cosine, sine)
    attended = lax.all_to_all(att_head.reshape(members, TOK_DEV, HD), EP, 0, 0, tiled=True)
    g_own = plain_dispatch(cot_own, slots_own, [att_head])
    cot_stack = stack_of_core(core, cot_own.reshape(members // 2, 2, TOK_DEV, D), [g_own])
    hidden, mixed, branch_sums = project_out(attended, output_full, tokens, moe_row, [cot_stack])
    early = {}

    def early_work(step, last):
        if step == 2:
            early["slope"] = slopes(g_own, w_down, [last])
            return early["slope"]
        return last

    rows = [None]

    def use_mixed(s, r, own, far, after):
        spot = jnp.stack([chips[s][r], core, place.astype(jnp.int32)])
        rows[0] = dispatch(spot, own, far, slots_own, rows[0], after)
        return rows[0][0]

    gather_steps(mixed, use_mixed, early_work)
    x_own, mixed_columns, mixed_stack = rows[0]
    slope_own = early["slope"]
    sides = jnp.stack([core, group.astype(jnp.int32)])
    cot_near = of_groups(cot_stack)
    mixed_near = of_groups(mixed_stack)
    every = jnp.concatenate([jnp.arange(members // 2, dtype=jnp.int32), sides])
    act_a, dg_a, du_a, gate_a, z_rows = experts(
        first, x_own, slope_own, w_gate, w_up, router_wide, True
    )

    def place_of(s):
        return jnp.stack([chips[s][0], chips[s][1], chips[s - 1][0], chips[s - 1][1], core])

    late = {}

    def late_work(step, last):
        if step == 1:
            late["y"] = down(act_a, gate_a, w_down, [last])
            return late["y"]
        if step == 2:
            late["branch"] = combine(late["y"], slots_own, [last])
            late["g"] = stack_dispatch(every, cot_near, slots_other, [late["branch"]])
            return late["g"]
        if step == 3:
            late["slope"] = slopes(late["g"], w_down, [last])
            return late["slope"]
        return last

    terms, last = reduce_steps(
        lambda s, after: combine_part(place_of(s), z_rows, slots_own, after), late_work
    )
    branch_moe = reduce_rows(late["branch"]).astype(F32)
    output = (hidden + branch_moe).astype(BF16)
    grad_hidden, wide_branch = token_back(
        terms, mixed, hidden, cotangent, router_wide, moe_row, [last]
    )
    grad_out = out_back(wide_branch, output_full)
    grad_att_head = lax.all_to_all(grad_out, EP, 0, 0, tiled=True).reshape(seq, HD)
    branch_all = gather_rows(wide_branch)

    def expert_other(only, last):
        late[only] = experts(
            first, late["x"], late["slope"], w_gate, w_up, router_wide, False, only, [last]
        )
        return late[only][3]

    groups = [(0, local // 2), (local // 2, local - local // 2)]
    late["x"] = stack_dispatch(every, mixed_near, slots_other, [grad_out])
    last = expert_other(groups[0], late["x"])

    dnq, dnk, dv16, means, gain_parts = attend_back(
        q16, k16, v16, grad_att_head, attn_float, lse, qkv, stat, gain_q, gain_k, cosine, sine, [last],
    )
    means = total_over_ep(means)
    qkv_grads = finish(dnq, dnk, dv16, qkv, stat, means, gain_q, gain_k)
    half = group.reshape(1).astype(jnp.int32)

    def expert_grads(only, last):
        act_b, dg_b, du_b, gate_b = late[only]
        late["grads"] = weight_grads(
            only, half, (x_own, late["x"]), (dg_a, dg_b), (du_a, du_b), (act_a, act_b),
            (g_own, late["g"]), (gate_a, gate_b), late.get("grads"), [last],
        )
        return late["grads"][0]

    def last_work(step, last):
        if step == 1:
            return expert_other(groups[1], last)
        if step == 3:
            late["dw"] = dw_product(normed_all, qkv_grads, [last])
            return late["dw"]
        return last

    terms, last = reduce_steps(
        lambda s, after: normed_part(place_of(s), qkv_grads, w_head, after),
        last_work,
    )
    tokens_grad = final_tokens(terms, tokens, attn_row, grad_hidden, [last])
    dw_head = late["dw"]
    last = tokens_grad
    last = expert_grads(groups[0], last)
    out_part = owner_rows(place, att_head, mixed_columns, branch_all, [last])
    last = expert_grads(groups[1], out_part)
    gate_grad, up_grad, down_grad = late["grads"]
    inputs = tokens.astype(F32)
    sums = jnp.stack(
        [jnp.sum(inputs * inputs), branch_sums[0, 0], jnp.sum(branch_moe * branch_moe)]
    )

    extra = jnp.concatenate([gain_parts.reshape(1, 2 * HD), sums[None, :]], 1)
    high = extra.astype(BF16)
    low = (extra - high.astype(F32)).astype(BF16)
    extra = jnp.pad(jnp.concatenate([high, low], 0), ((0, 14), (0, HD - 3)))
    everyone = 2 * members
    payload = jnp.concatenate(
        [
            dw_head.astype(BF16).reshape(everyone, wide, 3 * HD),
            jnp.broadcast_to(extra, (everyone,) + extra.shape),
        ],
        1,
    )
    arrived = lax.all_to_all(payload, ALL, 0, 0, tiled=True)
    *dense, attn_sums = unpack(arrived, (w_query, w_key, w_value), attn_gain, [last])
    attn_gain_grad = attn_sums[:, 0]
    extras = arrived[:, wide].astype(F32) + arrived[:, wide + 1].astype(F32)
    seq_sums = lax.dynamic_slice(extras, (group * members, 2 * HD), (members, 3))
    rms_stats = jnp.sqrt(jnp.sum(seq_sums, 0, keepdims=True) / (seq * D))
    extras = extras[:members] + extras[members:]
    flat = group * members + place
    head_row = lax.dynamic_slice(
        extras[:, : 2 * HD].reshape(HEADS, 2, HD // wide, wide),
        (flat // (HD // wide), 0, flat % (HD // wide), 0),
        (1, 2, 1, wide),
    ).reshape(2, wide)

    out_part = out_part.reshape(2, wide, D + HD)
    out_keep = lax.dynamic_index_in_dim(out_part, group, 0, False)
    out_send = lax.dynamic_index_in_dim(out_part, 1 - group, 0, False).astype(BF16)
    out_sum = (out_keep + swap(out_send, "grp").astype(F32)).astype(BF16)
    owners = [(g * members + e, 2 * e + g) for g in range(2) for e in range(members)]
    owned = lax.ppermute(out_sum, ALL, owners).astype(F32)
    output_grad = owned[:, :D]
    router_grad, moe_gain_grad = owned[:, D : D + EXPERTS], owned[:, D + EXPERTS]

    return (
        output, tokens_grad, dense[0], dense[1], dense[2], output_grad, router_grad,
        attn_gain_grad, head_row[0], head_row[1], moe_gain_grad, gate_grad, up_grad, down_grad,
        rms_stats,
    )


def fast_solution(mesh, sides):
    inner = jax.sharding.Mesh(mesh.devices.reshape((2,) + sides), ALL)
    rows = P(ALL, None)
    expert = P(EP, None, None)
    return jax.shard_map(
        fast_shards,
        mesh=inner,
        in_specs=(rows,) * 6 + (P(ALL),) * 4 + (expert,) * 3 + (rows,) * 2,
        out_specs=(rows,) * 7 + (P(ALL),) * 4 + (P(EP, "grp", None),) * 3 + (P("grp", None),),
        check_vma=False,
    )


def solution(mesh):
    sides = SIDES.get(mesh.shape["ep"])
    if sides is not None and mesh.shape["grp"] == 2:
        return fast_solution(mesh, sides)
    return jax.shard_map(
        shards,
        mesh=mesh,
        in_specs=(
            P(("grp", "ep"), None),
            P(("grp", "ep"), None),
            P(("grp", "ep"), None),
            P(("grp", "ep"), None),
            P(("grp", "ep"), None),
            P(("grp", "ep"), None),
            P(("grp", "ep")),
            P(("grp", "ep")),
            P(("grp", "ep")),
            P(("grp", "ep")),
            P("ep", None, None),
            P("ep", None, None),
            P("ep", None, None),
            P(("grp", "ep"), None),
            P(("grp", "ep"), None),
        ),
        out_specs=(
            P(("grp", "ep"), None),
            P(("grp", "ep"), None),
            P(("grp", "ep"), None),
            P(("grp", "ep"), None),
            P(("grp", "ep"), None),
            P(("grp", "ep"), None),
            P(("grp", "ep"), None),
            P(("grp", "ep")),
            P(("grp", "ep")),
            P(("grp", "ep")),
            P(("grp", "ep")),
            P("ep", "grp", None),
            P("ep", "grp", None),
            P("ep", "grp", None),
            P("grp", None),
        ),
        check_vma=False,
    )
```

```python
import functools
import math

import jax
import jax.numpy as jnp
from jax import lax
from jax.experimental import pallas as pl
from jax.experimental.pallas import tpu as pltpu
from jax.sharding import PartitionSpec as P

D = 2048
HEADS = 16
HD = 128
EXPERTS = 64
TOPK = 8
TOK_DEV = 128
BLOCK = 256
CAP = 24


EPSILON = 1e-05
NEG_FILL = -1e30


def inv_rms(values):
    return lax.rsqrt(jnp.mean(values * values, -1, keepdims=True) + EPSILON)


def norm_back(grad_out, values, inverse, gain_vec):
    scaled = grad_out * gain_vec
    grad_in = inverse * (
        scaled - values * inverse * inverse * jnp.mean(scaled * values, -1, keepdims=True)
    )
    return (grad_in, jnp.sum(grad_out * values * inverse, 0))


def rope_tables(positions):
    half_dim = HD // 2
    frequency = jnp.exp(-(2.0 * jnp.arange(half_dim, dtype=jnp.float32) / HD) * math.log(10000.0))
    angles = positions.astype(jnp.float32)[:, None] * frequency[None, :]
    return (jnp.cos(angles)[:, None, :], jnp.sin(angles)[:, None, :])


def rotate(values, cosine, sine_tab):
    half_dim = HD // 2
    first_half = values[..., :half_dim]
    second_half = values[..., half_dim:]
    return jnp.concatenate(
        [
            first_half * cosine - second_half * sine_tab,
            second_half * cosine + first_half * sine_tab,
        ],
        -1,
    )


def rotate_back(grad_in, cosine, sine_tab):
    half_dim = HD // 2
    first_half = grad_in[..., :half_dim]
    second_half = grad_in[..., half_dim:]
    return jnp.concatenate(
        [
            first_half * cosine + second_half * sine_tab,
            second_half * cosine - first_half * sine_tab,
        ],
        -1,
    )


def fold_keys(state_now, key_piece, queries, query_pos):
    keys_in, values_in = key_piece
    piece_rows = keys_in.shape[0]
    blk_rows = math.gcd(piece_rows, 1024)
    key_blocks = keys_in.reshape(piece_rows // blk_rows, blk_rows, HEADS, HD)
    value_blocks = values_in.reshape(piece_rows // blk_rows, blk_rows, HEADS, HD)
    last_block = query_pos[-1] // BLOCK

    def block_step(state_in, block_items):
        key_blk, value_blk, block_num = block_items
        key_start = block_num * blk_rows

        def block_compute(state_cur):
            top_now, total_now, acc_now = state_cur
            key_pos = key_start + jnp.arange(blk_rows, dtype=jnp.int32)
            scores = jnp.einsum(
                "qhd,khd->hqk", queries, key_blk, preferred_element_type=jnp.float32
            ) * HD ** (-0.5)
            allowed = (key_pos // BLOCK)[None, None, :] <= (query_pos // BLOCK)[None, :, None]
            scores = jnp.where(allowed, scores, NEG_FILL)
            top_new = jnp.maximum(top_now, jnp.max(scores, -1, keepdims=True))
            weights = jnp.where(allowed, jnp.exp(scores - top_new), 0.0)
            rescale = jnp.exp(top_now - top_new)
            total_new = total_now * rescale + jnp.sum(weights, -1, keepdims=True)
            acc_new = acc_now * jnp.transpose(rescale, (1, 0, 2)) + jnp.einsum(
                "hqk,khd->qhd",
                weights.astype(jnp.bfloat16),
                value_blk,
                preferred_element_type=jnp.float32,
            )
            return (top_new, total_new, acc_new)

        def block_passing(state_cur):
            return state_cur

        return (
            lax.cond(key_start // BLOCK <= last_block, block_compute, block_passing, state_in),
            None,
        )

    state_out, unused = lax.scan(
        block_step,
        state_now,
        (key_blocks, value_blocks, jnp.arange(piece_rows // blk_rows, dtype=jnp.int32)),
    )
    return state_out


def score_grads(queries, grad_attended, row_delta, log_sum, query_pos, key_blk, value_blk, key_pos):
    scores = jnp.einsum(
        "qhd,khd->hqk", queries, key_blk, preferred_element_type=jnp.float32
    ) * HD ** (-0.5)
    allowed = (key_pos // BLOCK)[None, None, :] <= (query_pos // BLOCK)[None, :, None]
    prob_vals = jnp.where(allowed, jnp.exp(scores - log_sum), 0.0)
    grad_probs = jnp.einsum(
        "qhd,khd->hqk", grad_attended, value_blk, preferred_element_type=jnp.float32
    )
    grad_scores = (prob_vals * (grad_probs - row_delta)).astype(jnp.bfloat16)
    return (prob_vals, grad_scores)


def shards(
    tokens,
    w_query,
    w_key,
    w_value,
    w_output,
    w_router,
    attn_gain,
    query_gain,
    key_gain,
    moe_gain,
    w_gate,
    w_up,
    w_down,
    routes,
    cotangent,
):
    gathered = (
        lax.all_gather(w_query, ("grp", "ep"), axis=0, tiled=True),
        lax.all_gather(w_key, ("grp", "ep"), axis=0, tiled=True),
        lax.all_gather(w_value, ("grp", "ep"), axis=0, tiled=True),
        lax.all_gather(w_output, ("grp", "ep"), axis=0, tiled=True),
        lax.all_gather(w_router, ("grp", "ep"), axis=0, tiled=True),
        lax.all_gather(attn_gain, ("grp", "ep"), axis=0, tiled=True),
        lax.all_gather(query_gain, ("grp", "ep"), axis=0, tiled=True),
        lax.all_gather(key_gain, ("grp", "ep"), axis=0, tiled=True),
        lax.all_gather(moe_gain, ("grp", "ep"), axis=0, tiled=True),
    )
    query_full, key_full, value_full, output_full, router_full = (
        gathered[0],
        gathered[1],
        gathered[2],
        gathered[3],
        gathered[4],
    )
    attn_scale = gathered[5].astype(jnp.float32)
    query_scale = gathered[6].astype(jnp.float32)
    key_scale = gathered[7].astype(jnp.float32)
    moe_scale = gathered[8].astype(jnp.float32)
    ep_count = lax.axis_size("ep")
    exp_local = EXPERTS // ep_count
    score_scale = HD ** (-0.5)
    inputs = tokens.astype(jnp.float32)
    positions = lax.axis_index("ep") * TOK_DEV + jnp.arange(TOK_DEV, dtype=jnp.int32)
    cosine, sine_tab = rope_tables(positions)
    attn_inv = inv_rms(inputs)
    normed = (inputs * attn_inv * attn_scale).astype(jnp.bfloat16)
    query_raw = jnp.dot(normed, query_full, preferred_element_type=jnp.float32)
    key_raw = jnp.dot(normed, key_full, preferred_element_type=jnp.float32)
    values16 = jnp.dot(normed, value_full, preferred_element_type=jnp.float32).astype(jnp.bfloat16)
    query_inv = inv_rms(query_raw)
    queries16 = rotate(
        (query_raw * query_inv * query_scale).reshape(TOK_DEV, HEADS, HD), cosine, sine_tab
    ).astype(jnp.bfloat16)
    key_inv = inv_rms(key_raw)
    keys16 = (
        rotate((key_raw * key_inv * key_scale).reshape(TOK_DEV, HEADS, HD), cosine, sine_tab)
        .astype(jnp.bfloat16)
        .reshape(TOK_DEV, D)
    )
    start_state = (
        jnp.full((HEADS, TOK_DEV, 1), NEG_FILL, jnp.float32),
        jnp.zeros((HEADS, TOK_DEV, 1), jnp.float32),
        jnp.zeros((TOK_DEV, HEADS, HD), jnp.float32),
    )
    folded = fold_keys(
        start_state,
        (
            lax.all_gather(keys16, "ep", axis=0, tiled=True),
            lax.all_gather(values16, "ep", axis=0, tiled=True),
        ),
        queries16,
        positions,
    )
    top_score, total_weight, acc_sum = folded
    log_sum = top_score + jnp.log(total_weight)
    attn_float = acc_sum / jnp.transpose(total_weight, (1, 0, 2))
    attended16 = attn_float.reshape(TOK_DEV, D).astype(jnp.bfloat16)
    branch_attn = jnp.dot(attended16, output_full, preferred_element_type=jnp.float32)
    hidden = inputs + branch_attn
    moe_inv = inv_rms(hidden)
    mixed_in = (hidden * moe_inv * moe_scale).astype(jnp.bfloat16)
    logits = jnp.dot(mixed_in, router_full, preferred_element_type=jnp.float32)
    route_probs = jax.nn.softmax(logits, -1)
    chosen = (routes[:, :, None] == jnp.arange(EXPERTS, dtype=jnp.int32)[None, None, :]).astype(
        jnp.float32
    )
    gate_vals = jnp.sum(chosen * route_probs[:, None, :], -1)
    pair_expert = routes.reshape(-1)
    one_hot = (pair_expert[:, None] == jnp.arange(EXPERTS, dtype=jnp.int32)[None, :]).astype(
        jnp.int32
    )
    pair_rank = jnp.sum(jnp.cumsum(one_hot, 0) * one_hot, 1) - 1
    slot_index = pair_expert * CAP + pair_rank
    pair_token = jnp.arange(TOK_DEV * TOPK, dtype=jnp.int32) // TOPK
    send_rows = jnp.zeros((EXPERTS * CAP, D), jnp.bfloat16).at[slot_index].set(mixed_in[pair_token])
    send_rows = send_rows.reshape(ep_count, exp_local, CAP, D)
    received = lax.all_to_all(send_rows, "ep", split_axis=0, concat_axis=0, tiled=True)
    gate_pre = jnp.einsum("secd,edf->secf", received, w_gate, preferred_element_type=jnp.float32)
    up_pre = jnp.einsum("secd,edf->secf", received, w_up, preferred_element_type=jnp.float32)
    activation = (jax.nn.silu(gate_pre) * up_pre).astype(jnp.bfloat16)
    expert_out = jnp.einsum(
        "secf,efd->secd", activation, w_down, preferred_element_type=jnp.float32
    ).astype(jnp.bfloat16)
    expert_out, gate_pre, up_pre, activation, received = (
        expert_out,
        gate_pre,
        up_pre,
        activation,
        received,
    )
    returned = lax.all_to_all(expert_out, "ep", split_axis=0, concat_axis=0, tiled=True).reshape(
        EXPERTS * CAP, D
    )
    pair_out = returned[slot_index].astype(jnp.float32).reshape(TOK_DEV, TOPK, D)
    branch_moe = jnp.sum(gate_vals[:, :, None] * pair_out, 1)
    output = (hidden + branch_moe).astype(jnp.bfloat16)
    local_sums = jnp.stack(
        [
            jnp.sum(inputs * inputs),
            jnp.sum(branch_attn * branch_attn),
            jnp.sum(branch_moe * branch_moe),
        ]
    )
    seq_sums = lax.psum(local_sums, "ep")
    rms_stats = jnp.sqrt(seq_sums / (TOK_DEV * ep_count * D)).reshape(1, 3)
    grad_out = cotangent.astype(jnp.float32)
    grad_gates = jnp.sum(pair_out * grad_out[:, None, :], -1)
    grad_pairs = (
        (gate_vals[:, :, None] * grad_out[:, None, :])
        .astype(jnp.bfloat16)
        .reshape(TOK_DEV * TOPK, D)
    )
    send_grads = jnp.zeros((EXPERTS * CAP, D), jnp.bfloat16).at[slot_index].set(grad_pairs)
    send_grads = send_grads.reshape(ep_count, exp_local, CAP, D)
    grad_received = lax.all_to_all(send_grads, "ep", split_axis=0, concat_axis=0, tiled=True)
    grad_activation = jnp.einsum(
        "secd,efd->secf", grad_received, w_down, preferred_element_type=jnp.float32
    )
    grad_down = jnp.einsum(
        "secf,secd->efd", activation, grad_received, preferred_element_type=jnp.float32
    )
    sig_gate = jax.nn.sigmoid(gate_pre)
    grad_gate_pre = (
        grad_activation * up_pre * sig_gate * (1.0 + gate_pre * (1.0 - sig_gate))
    ).astype(jnp.bfloat16)
    grad_up_pre = (grad_activation * gate_pre * sig_gate).astype(jnp.bfloat16)
    grad_gate_w = jnp.einsum(
        "secd,secf->edf", received, grad_gate_pre, preferred_element_type=jnp.float32
    )
    grad_up_w = jnp.einsum(
        "secd,secf->edf", received, grad_up_pre, preferred_element_type=jnp.float32
    )
    grad_inputs = (
        jnp.einsum("secf,edf->secd", grad_gate_pre, w_gate, preferred_element_type=jnp.float32)
        + jnp.einsum("secf,edf->secd", grad_up_pre, w_up, preferred_element_type=jnp.float32)
    ).astype(jnp.bfloat16)
    grad_back = lax.all_to_all(grad_inputs, "ep", split_axis=0, concat_axis=0, tiled=True).reshape(
        EXPERTS * CAP, D
    )
    grad_mixed = jnp.sum(grad_back[slot_index].astype(jnp.float32).reshape(TOK_DEV, TOPK, D), 1)
    spread = jnp.sum(chosen * grad_gates[:, :, None], 1)
    grad_logits = (
        route_probs * (spread - jnp.sum(route_probs * spread, -1, keepdims=True))
    ).astype(jnp.bfloat16)
    router_grad = jnp.einsum("td,te->de", mixed_in, grad_logits, preferred_element_type=jnp.float32)
    grad_mixed = grad_mixed + jnp.einsum(
        "te,de->td", grad_logits, router_full, preferred_element_type=jnp.float32
    )
    grad_hid_norm, moe_gain_grad = norm_back(grad_mixed, hidden, moe_inv, moe_scale)
    grad_hidden = grad_out + grad_hid_norm
    grad_branch = grad_hidden.astype(jnp.bfloat16)
    output_grad = jnp.einsum(
        "td,tf->df", attended16, grad_branch, preferred_element_type=jnp.float32
    )
    grad_attended = jnp.einsum(
        "tf,df->td", grad_branch, output_full, preferred_element_type=jnp.float32
    ).astype(jnp.bfloat16)
    grad_attended = grad_attended.reshape(TOK_DEV, HEADS, HD)
    row_delta = jnp.transpose(jnp.sum(grad_attended.astype(jnp.float32) * attn_float, -1), (1, 0))[
        :, :, None
    ]
    gathered_keys, gathered_values = (
        lax.all_gather(keys16, "ep", axis=0, tiled=True),
        lax.all_gather(values16, "ep", axis=0, tiled=True),
    )
    total_rows = gathered_keys.shape[0]
    blk_rows = math.gcd(total_rows, 1024)
    last_query_block = positions[-1] // BLOCK

    def query_step(grad_now, block_num):
        begin_row = block_num * blk_rows

        def query_compute(grad_cur):
            key_blk = lax.dynamic_slice_in_dim(gathered_keys, begin_row, blk_rows, 0).reshape(
                blk_rows, HEADS, HD
            )
            value_blk = lax.dynamic_slice_in_dim(gathered_values, begin_row, blk_rows, 0).reshape(
                blk_rows, HEADS, HD
            )
            key_pos = begin_row + jnp.arange(blk_rows, dtype=jnp.int32)
            prob_vals, grad_scores = score_grads(
                queries16, grad_attended, row_delta, log_sum, positions, key_blk, value_blk, key_pos
            )
            return (
                grad_cur
                + jnp.einsum(
                    "hqk,khd->qhd", grad_scores, key_blk, preferred_element_type=jnp.float32
                )
                * score_scale
            )

        def query_passing(grad_cur):
            return grad_cur

        return (
            lax.cond(
                begin_row // BLOCK <= last_query_block, query_compute, query_passing, grad_now
            ),
            None,
        )

    grad_queries, unused = lax.scan(
        query_step,
        jnp.zeros((TOK_DEV, HEADS, HD), jnp.float32),
        jnp.arange(total_rows // blk_rows, dtype=jnp.int32),
    )
    all_queries, all_grad_att = (
        lax.all_gather(queries16, "ep", axis=0, tiled=True),
        lax.all_gather(grad_attended, "ep", axis=0, tiled=True),
    )
    all_delta, all_log_sum = (
        lax.all_gather(row_delta, "ep", axis=1, tiled=True),
        lax.all_gather(log_sum, "ep", axis=1, tiled=True),
    )
    query_rows = all_queries.shape[0]
    query_blk_rows = math.gcd(query_rows, 1024)
    own_keys = keys16.reshape(TOK_DEV, HEADS, HD)
    own_values = values16.reshape(TOK_DEV, HEADS, HD)
    first_key_block = positions[0] // BLOCK

    def key_step(grads_now, block_num):
        begin_row = block_num * query_blk_rows

        def key_compute(grads_cur):
            query_blk = lax.dynamic_slice_in_dim(all_queries, begin_row, query_blk_rows, 0)
            grad_att_blk = lax.dynamic_slice_in_dim(all_grad_att, begin_row, query_blk_rows, 0)
            delta_blk = lax.dynamic_slice_in_dim(all_delta, begin_row, query_blk_rows, 1)
            log_blk = lax.dynamic_slice_in_dim(all_log_sum, begin_row, query_blk_rows, 1)
            query_pos = begin_row + jnp.arange(query_blk_rows, dtype=jnp.int32)
            prob_vals, grad_scores = score_grads(
                query_blk,
                grad_att_blk,
                delta_blk,
                log_blk,
                query_pos,
                own_keys,
                own_values,
                positions,
            )
            key_part = (
                jnp.einsum(
                    "hqk,qhd->khd", grad_scores, query_blk, preferred_element_type=jnp.float32
                )
                * score_scale
            )
            value_part = jnp.einsum(
                "hqk,qhd->khd",
                prob_vals.astype(jnp.bfloat16),
                grad_att_blk,
                preferred_element_type=jnp.float32,
            )
            return (grads_cur[0] + key_part, grads_cur[1] + value_part)

        def key_passing(grads_cur):
            return grads_cur

        return (
            lax.cond(
                (begin_row + query_blk_rows - 1) // BLOCK >= first_key_block,
                key_compute,
                key_passing,
                grads_now,
            ),
            None,
        )

    key_start = (
        jnp.zeros((TOK_DEV, HEADS, HD), jnp.float32),
        jnp.zeros((TOK_DEV, HEADS, HD), jnp.float32),
    )
    key_value_grads, unused = lax.scan(
        key_step, key_start, jnp.arange(query_rows // query_blk_rows, dtype=jnp.int32)
    )
    grad_keys16 = key_value_grads[0].astype(jnp.bfloat16)
    grad_values16 = key_value_grads[1].reshape(TOK_DEV, D).astype(jnp.bfloat16)
    grad_keys = lax.optimization_barrier(grad_keys16).astype(jnp.float32)
    grad_queries = lax.optimization_barrier(grad_queries.astype(jnp.bfloat16)).astype(jnp.float32)
    grad_query_rot = rotate_back(grad_queries, cosine, sine_tab).reshape(TOK_DEV, D)
    grad_query_raw, query_gain_grad = norm_back(grad_query_rot, query_raw, query_inv, query_scale)
    grad_query16 = grad_query_raw.astype(jnp.bfloat16)
    grad_key_rot = rotate_back(grad_keys, cosine, sine_tab).reshape(TOK_DEV, D)
    grad_key_raw, key_gain_grad = norm_back(grad_key_rot, key_raw, key_inv, key_scale)
    grad_key16 = grad_key_raw.astype(jnp.bfloat16)
    query_grad = jnp.einsum("td,tf->df", normed, grad_query16, preferred_element_type=jnp.float32)
    key_grad = jnp.einsum("td,tf->df", normed, grad_key16, preferred_element_type=jnp.float32)
    value_grad = jnp.einsum("td,tf->df", normed, grad_values16, preferred_element_type=jnp.float32)
    grad_normed = (
        jnp.einsum("tf,df->td", grad_query16, query_full, preferred_element_type=jnp.float32)
        + jnp.einsum("tf,df->td", grad_key16, key_full, preferred_element_type=jnp.float32)
        + jnp.einsum("tf,df->td", grad_values16, value_full, preferred_element_type=jnp.float32)
    )
    grad_tok_norm, attn_gain_grad = norm_back(grad_normed, inputs, attn_inv, attn_scale)
    tokens_grad = (grad_hidden + grad_tok_norm).astype(jnp.bfloat16)
    dense_sums = (
        lax.psum_scatter(query_grad, ("grp", "ep"), scatter_dimension=0, tiled=True),
        lax.psum_scatter(key_grad, ("grp", "ep"), scatter_dimension=0, tiled=True),
        lax.psum_scatter(value_grad, ("grp", "ep"), scatter_dimension=0, tiled=True),
        lax.psum_scatter(output_grad, ("grp", "ep"), scatter_dimension=0, tiled=True),
        lax.psum_scatter(router_grad, ("grp", "ep"), scatter_dimension=0, tiled=True),
        lax.psum_scatter(attn_gain_grad, ("grp", "ep"), scatter_dimension=0, tiled=True),
        lax.psum_scatter(query_gain_grad, ("grp", "ep"), scatter_dimension=0, tiled=True),
        lax.psum_scatter(key_gain_grad, ("grp", "ep"), scatter_dimension=0, tiled=True),
        lax.psum_scatter(moe_gain_grad, ("grp", "ep"), scatter_dimension=0, tiled=True),
    )
    expert_sums = (
        lax.psum_scatter(
            grad_gate_w.astype(jnp.bfloat16), "grp", scatter_dimension=1, tiled=True
        ).astype(jnp.float32),
        lax.psum_scatter(
            grad_up_w.astype(jnp.bfloat16), "grp", scatter_dimension=1, tiled=True
        ).astype(jnp.float32),
        lax.psum_scatter(
            grad_down.astype(jnp.bfloat16), "grp", scatter_dimension=1, tiled=True
        ).astype(jnp.float32),
    )
    return (
        output,
        tokens_grad,
        dense_sums[0],
        dense_sums[1],
        dense_sums[2],
        dense_sums[3],
        dense_sums[4],
        dense_sums[5],
        dense_sums[6],
        dense_sums[7],
        dense_sums[8],
        expert_sums[0],
        expert_sums[1],
        expert_sums[2],
        rms_stats,
    )


F32 = jnp.float32
BF16 = jnp.bfloat16
EP = ("z", "x", "core")
ALL = ("grp", "z", "x", "core")
PAIR = 2 * TOK_DEV
SLOTS = 2 * CAP
COST = 0.1
SIDES = {16: (4, 2, 2)}


def nt(left, right):
    return lax.dot_general(left, right, (((1,), (1,)), ((), ())), preferred_element_type=F32)


def nn(left, right):
    return lax.dot_general(left, right, (((1,), (0,)), ((), ())), preferred_element_type=F32)


def tn(left, right):
    return lax.dot_general(left, right, (((0,), (0,)), ((), ())), preferred_element_type=F32)


def as_row(column):
    return jnp.broadcast_to(column, (column.shape[0], 128)).T[0:1]


def as_column(row):
    return jnp.broadcast_to(row, (128, row.shape[1])).T


def inv_of(sum_row):
    return as_column(lax.rsqrt(sum_row / D + EPSILON))


def params(mebibytes):
    return pltpu.CompilerParams(vmem_limit_bytes=mebibytes * 1024 * 1024)


def cost(flops, moved):
    return pl.CostEstimate(flops=int(flops * COST), bytes_accessed=int(moved * COST), transcendentals=0)


def whole(*dims):
    return pl.BlockSpec(dims, lambda *_: (0,) * len(dims))


class Order:
    marks = []

    @classmethod
    def mark_of(cls, array):
        for known, mark in cls.marks:
            if known is array:
                return mark
        return array


MARK = (8, 128)


def ordered(kernel, after, specs, **settings):
    after = [Order.mark_of(array) for array in after]
    inputs = len(specs["in_specs"])
    prefetch = specs.pop("num_scalar_prefetch", 0)
    extra = len(after)
    single = not isinstance(specs["out_specs"], list)
    outputs = [specs["out_specs"]] if single else specs["out_specs"]
    shapes = settings.pop("out_shape")
    shapes = [shapes] if single else list(shapes)
    last = prefetch + inputs + extra + len(outputs)

    def body(*refs):
        refs[last][...] = jnp.zeros(MARK, F32)
        kernel(*refs[: prefetch + inputs], *refs[prefetch + inputs + extra : last], *refs[last + 1 :])

    specs["in_specs"] = list(specs["in_specs"]) + [pl.BlockSpec(memory_space=pl.ANY)] * extra
    specs["out_specs"] = outputs + [pl.BlockSpec(MARK, lambda *_: (0, 0))]
    call = pl.pallas_call(
        body,
        grid_spec=pltpu.PrefetchScalarGridSpec(num_scalar_prefetch=prefetch, **specs),
        out_shape=shapes + [jax.ShapeDtypeStruct(MARK, F32)],
        **settings,
    )

    def run(*args):
        *results, mark = call(*args, *after)
        Order.marks.extend((result, mark) for result in results)
        return results[0] if single else results

    return run


ANYWHERE = pl.BlockSpec(memory_space=pl.ANY)


def in_hbm(dims, kind):
    return pltpu.HBM(dims, kind)


BLOCK_SHAPE = (TOK_DEV, D)


def project_kernel(place_ref, own_ref, other_ref, w_ref, gain_ref, *refs):
    normed_ref, qkv_ref, stat_ref = refs[-3:]
    core = place_ref[1]
    for side, tok_ref in ((core, own_ref), (1 - core, other_ref)):
        here = pl.ds(pl.multiple_of(side * TOK_DEV, TOK_DEV), TOK_DEV)
        rows = tok_ref[...].astype(F32)
        inverse = lax.rsqrt(jnp.mean(rows * rows, -1, keepdims=True) + EPSILON)
        normed = (rows * inverse * gain_ref[...]).astype(BF16)
        normed_ref[here, :] = normed
        out = nn(normed, w_ref[...])
        qkv_ref[here, :] = out
        for part in range(2):
            piece = out[:, part * HD : (part + 1) * HD]
            stat_ref[part : part + 1, here] = as_row(jnp.sum(piece * piece, -1, keepdims=True))


def project(chip_core, own, other, w_head, gain_row, buffers, seq, after=()):
    kept = [] if buffers is None else list(buffers)
    return ordered(
        project_kernel,
        after,
        dict(
            num_scalar_prefetch=1,
            grid=(1,),
            in_specs=[whole(TOK_DEV, D), whole(TOK_DEV, D), whole(D, 3 * HD), whole(1, D)]
            + [ANYWHERE] * len(kept),
            out_specs=[
                pl.BlockSpec((PAIR, D), lambda i, s: (s[0], 0)),
                pl.BlockSpec((PAIR, 3 * HD), lambda i, s: (s[0], 0)),
                pl.BlockSpec((2, PAIR), lambda i, s: (0, s[0])),
            ],
        ),
        out_shape=[
            in_hbm((seq, D), BF16),
            in_hbm((seq, 3 * HD), F32),
            jax.ShapeDtypeStruct((2, seq), F32),
        ],
        input_output_aliases={5 + i: i for i in range(len(kept))},
        compiler_params=params(24),
        cost_estimate=cost(2 * PAIR * D * 3 * HD, 10 * PAIR * D),
        name="project",
    )(chip_core, own, other, w_head, gain_row, *kept)


def attend_kernel(
    qkv_ref, stat_ref, gq_ref, gk_ref, cos_ref, sin_ref,
    q_ref, k_ref, v_ref, of_ref, att_ref, lse_ref, vt_ref,
):
    blocks = q_ref.shape[0] // BLOCK
    for i in range(blocks):
        rows = slice(i * BLOCK, (i + 1) * BLOCK)
        cosine, sine = cos_ref[rows, :], sin_ref[rows, :]
        for part, gain_ref, out_ref in ((0, gq_ref, q_ref), (1, gk_ref, k_ref)):
            raw = qkv_ref[rows, part * HD : (part + 1) * HD]
            scaled = raw * inv_of(stat_ref[part : part + 1, rows]) * gain_ref[...]
            turned = scaled * cosine + pltpu.roll(scaled, HD // 2, 1) * sine
            out_ref[rows, :] = turned.astype(BF16)
        value = qkv_ref[rows, 2 * HD :]
        v_ref[rows, :] = value.astype(BF16)
        vt_ref[:, rows] = value.T.astype(BF16)
    for i in range(blocks):
        rows = slice(i * BLOCK, (i + 1) * BLOCK)
        reach = (i + 1) * BLOCK
        scores = nt(k_ref[0:reach, :], q_ref[rows, :]) * HD ** (-0.5)
        top = jnp.max(scores, 0, keepdims=True)
        weights = jnp.exp(scores - top)
        total = jnp.sum(weights, 0, keepdims=True)
        probs = (weights * (1.0 / total)).astype(BF16)
        out = nn(vt_ref[:, 0:reach], probs).T
        of_ref[rows, :] = out
        att_ref[rows, :] = out.astype(BF16)
        lse_ref[:, rows] = top + jnp.log(total)


def attend(qkv, stat, gain_q, gain_k, cosine, sine):
    rows = qkv.shape[0]
    shape = lambda kind: jax.ShapeDtypeStruct((rows, HD), kind)
    return ordered(
        attend_kernel,
        (),
        dict(
            grid=(1,),
            in_specs=[
                whole(rows, 3 * HD), whole(2, rows), whole(1, HD), whole(1, HD), whole(rows, HD), whole(rows, HD),
            ],
            out_specs=[whole(rows, HD)] * 5 + [whole(1, rows)],
            scratch_shapes=[pltpu.VMEM((HD, rows), BF16)],
        ),
        out_shape=[shape(BF16), shape(BF16), shape(BF16), shape(F32), shape(BF16),
                   jax.ShapeDtypeStruct((1, rows), F32)],
        compiler_params=params(48),
        cost_estimate=cost(8 * rows * rows * HD, 10 * rows * 384),
        name="attend",
    )(qkv, stat, gain_q, gain_k, cosine, sine)


def attend_back_kernel(
    q_ref, k_ref, v_ref, do_ref, of_ref, lse_ref, qkv_ref, stat_ref, gq_ref, gk_ref,
    cos_ref, sin_ref, dnq_ref, dnk_ref, dv_ref, means_ref, gains_ref, dk_acc, dv_acc,
):
    blocks = q_ref.shape[0] // BLOCK
    scale = HD ** (-0.5)
    dk_acc[...] = jnp.zeros_like(dk_acc)
    dv_acc[...] = jnp.zeros_like(dv_acc)

    def turn_back(grad, rows, part, gain_ref, out_ref):
        grad = grad.astype(BF16).astype(F32)
        grad = grad * cos_ref[rows, :] - pltpu.roll(grad, HD // 2, 1) * sin_ref[rows, :]
        raw = qkv_ref[rows, part * HD : (part + 1) * HD]
        out_ref[rows, :] = grad
        means_ref[part : part + 1, rows] = jnp.sum((grad * gain_ref[...] * raw).T, 0, keepdims=True)
        inverse = inv_of(stat_ref[part : part + 1, rows])
        return jnp.sum(grad * raw * inverse, 0, keepdims=True)

    gain_q = jnp.zeros((1, HD), F32)
    gain_k = jnp.zeros((1, HD), F32)
    for i in range(blocks):
        rows = slice(i * BLOCK, (i + 1) * BLOCK)
        reach = (i + 1) * BLOCK
        queries, grads = q_ref[rows, :], do_ref[rows, :]
        delta = jnp.sum((grads.astype(F32) * of_ref[rows, :]).T, 0, keepdims=True)
        scores = nt(k_ref[0:reach, :], queries) * scale
        probs = jnp.exp(scores - lse_ref[:, rows])
        slopes = nt(v_ref[0:reach, :], grads)
        grad_scores = (probs * (slopes - delta)).astype(BF16)
        dv_acc[0:reach, :] += nn(probs.astype(BF16), grads)
        dk_acc[0:reach, :] += nn(grad_scores, queries)
        gain_q += turn_back(tn(grad_scores, k_ref[0:reach, :]) * scale, rows, 0, gq_ref, dnq_ref)
    for i in range(blocks):
        rows = slice(i * BLOCK, (i + 1) * BLOCK)
        dv_ref[rows, :] = dv_acc[rows, :].astype(BF16)
        gain_k += turn_back(dk_acc[rows, :] * scale, rows, 1, gk_ref, dnk_ref)
    gains_ref[0:1, :] = gain_q
    gains_ref[1:2, :] = gain_k


def attend_back(q, k, v, grad, out, lse, qkv, stat, gain_q, gain_k, cosine, sine, after=()):
    rows = q.shape[0]
    shape = lambda kind: jax.ShapeDtypeStruct((rows, HD), kind)
    return ordered(
        attend_back_kernel,
        after,
        dict(
            grid=(1,),
            in_specs=[whole(rows, HD)] * 5
            + [whole(1, rows), whole(rows, 3 * HD), whole(2, rows), whole(1, HD), whole(1, HD)]
            + [whole(rows, HD)] * 2,
            out_specs=[whole(rows, HD)] * 3 + [whole(2, rows), whole(2, HD)],
            scratch_shapes=[pltpu.VMEM((rows, HD), F32), pltpu.VMEM((rows, HD), F32)],
        ),
        out_shape=[shape(F32), shape(F32), shape(BF16),
                   jax.ShapeDtypeStruct((2, rows), F32), jax.ShapeDtypeStruct((2, HD), F32)],
        compiler_params=params(48),
        cost_estimate=cost(20 * rows * rows * HD, 20 * rows * 384),
        name="attend_back",
    )(q, k, v, grad, out, lse, qkv, stat, gain_q, gain_k, cosine, sine)


def finish_kernel(
    dnq_ref, dnk_ref, dv_ref, qkv_ref, stat_ref, means_ref, gq_ref, gk_ref, out_ref
):
    for part, dn_ref, g_ref in ((0, dnq_ref, gq_ref), (1, dnk_ref, gk_ref)):
        raw = qkv_ref[:, part * HD : (part + 1) * HD]
        inverse = inv_of(stat_ref[part : part + 1, :])
        mean = as_column(means_ref[part : part + 1, :] / D)
        grad = inverse * (dn_ref[...] * g_ref[...] - raw * inverse * inverse * mean)
        out_ref[:, part * HD : (part + 1) * HD] = grad.astype(BF16)
    out_ref[:, 2 * HD :] = dv_ref[...]


def finish(dnq, dnk, dv, qkv, stat, means, gain_q, gain_k, after=()):
    rows = dnq.shape[0]
    head = pl.BlockSpec((PAIR, HD), lambda i: (i, 0))
    line = pl.BlockSpec((2, PAIR), lambda i: (0, i))
    full = pl.BlockSpec((PAIR, 3 * HD), lambda i: (i, 0))
    return ordered(
        finish_kernel,
        after,
        dict(
        grid=(rows // PAIR,),
        in_specs=[head, head, head, full, line, line, whole(1, HD), whole(1, HD)],
        out_specs=full,
        ),
        out_shape=jax.ShapeDtypeStruct((rows, 3 * HD), BF16),
        compiler_params=params(24),
        cost_estimate=cost(20 * rows * 3 * HD, 12 * rows * 3 * HD),
        name="finish",
    )(dnq, dnk, dv, qkv, stat, means, gain_q, gain_k)


def sort_cores(core, first, second, own_ref, other_ref, at):
    at = (0, at)

    @pl.when(core == 0)
    def _():
        own_ref[at] = first
        other_ref[at] = second

    @pl.when(core == 1)
    def _():
        own_ref[at] = second
        other_ref[at] = first


def normed_part_kernel(place_ref, a_ref, b_ref, w_ref, own_ref, other_ref):
    for at, g_ref in enumerate((a_ref, b_ref)):
        out = nt(g_ref[...], w_ref[...]).astype(BF16)
        sort_cores(place_ref[4], out[:TOK_DEV], out[TOK_DEV:], own_ref, other_ref, at)


def normed_part(place, grads, w_head, after=()):
    blocks = jax.ShapeDtypeStruct((2, 2, TOK_DEV, D), BF16)
    return ordered(
        normed_part_kernel,
        after,
        dict(
            num_scalar_prefetch=1,
            grid=(2,),
            in_specs=[
                pl.BlockSpec((PAIR, 3 * HD), lambda i, s: (s[2 * i], 0)),
                pl.BlockSpec((PAIR, 3 * HD), lambda i, s: (s[2 * i + 1], 0)),
                whole(D, 3 * HD),
            ],
            out_specs=[pl.BlockSpec((1, 2, TOK_DEV, D), lambda i, s: (i, 0, 0, 0))] * 2,
        ),
        out_shape=[blocks, blocks],
        compiler_params=params(24),
        cost_estimate=cost(8 * PAIR * D * 3 * HD, 16 * PAIR * D),
        name="normed_part",
    )(place, grads, grads, w_head)


def dw_kernel(normed_ref, grad_ref, out_ref):
    @pl.when(pl.program_id(0) == 0)
    def _():
        out_ref[...] = jnp.zeros_like(out_ref)

    out_ref[...] += tn(normed_ref[...], grad_ref[...])


def dw_product(normed, grads, after=()):
    rows = normed.shape[0]
    return ordered(
        dw_kernel,
        after,
        dict(
            grid=(rows // 512,),
            in_specs=[
                pl.BlockSpec((512, D), lambda i: (i, 0)),
                pl.BlockSpec((512, 3 * HD), lambda i: (i, 0)),
            ],
            out_specs=whole(D, 3 * HD),
        ),
        out_shape=jax.ShapeDtypeStruct((D, 3 * HD), F32),
        compiler_params=params(32),
        cost_estimate=cost(2 * rows * D * 3 * HD, 3 * rows * D),
        name="dw_product",
    )(normed, grads)


def picks(slots, dtype):
    shape = (SLOTS, slots.shape[1])
    numbers = lax.broadcasted_iota(jnp.int32, shape, 0)
    return [(numbers == slots[j : j + 1, :]).astype(dtype) for j in range(slots.shape[0])]


def pick_matrix(slots):
    return jnp.concatenate(picks(slots, F32), 0).astype(BF16)


def dispatch_kernel(place_ref, own_ref, other_ref, own_slot, other_slot, *refs):
    out_ref, column_ref, stack_ref = refs[-3:]
    stack_ref[0] = own_ref[...]
    core = place_ref[1]
    lanes = pl.ds(pl.multiple_of(place_ref[2] * HD, HD), HD)
    out = nn(pick_matrix(own_slot[0]), own_ref[...])
    out = (out + nn(pick_matrix(other_slot[0]), other_ref[...])).astype(BF16)
    for j in range(out_ref.shape[0]):
        out_ref[j] = out[j * SLOTS : (j + 1) * SLOTS]
    for side, row_ref in ((core, own_ref), (1 - core, other_ref)):
        column_ref[pl.ds(pl.multiple_of(side * TOK_DEV, TOK_DEV), TOK_DEV), :] = row_ref[:, lanes]


def dispatch(place, own, other, slots, buffers, after=()):
    blocks, local, _ = slots.shape
    kept = [] if buffers is None else list(buffers)
    return ordered(
        dispatch_kernel,
        after,
        dict(
            num_scalar_prefetch=1,
            grid=(1,),
            in_specs=[
                whole(*BLOCK_SHAPE),
                whole(*BLOCK_SHAPE),
                pl.BlockSpec((1, local, TOK_DEV), lambda i, s: (2 * s[0] + s[1], 0, 0)),
                pl.BlockSpec((1, local, TOK_DEV), lambda i, s: (2 * s[0] + 1 - s[1], 0, 0)),
            ]
            + [ANYWHERE] * len(kept),
            out_specs=[
                pl.BlockSpec((local, SLOTS, D), lambda i, s: (0, s[0], 0)),
                pl.BlockSpec((PAIR, HD), lambda i, s: (s[0], 0)),
                pl.BlockSpec((1, TOK_DEV, D), lambda i, s: (s[0], 0, 0)),
            ],
        ),
        out_shape=[
            in_hbm((local, blocks // 2 * SLOTS, D), BF16),
            in_hbm((blocks * TOK_DEV, HD), BF16),
            in_hbm((blocks // 2, TOK_DEV, D), BF16),
        ],
        input_output_aliases={5 + i: i for i in range(len(kept))},
        compiler_params=params(24),
        cost_estimate=cost(2 * PAIR * D * local * SLOTS, 4 * PAIR * D),
        name="dispatch",
    )(place, own, other, slots, slots, *kept)


def stack_kernel(place_ref, row_ref, out_ref):
    out_ref[0] = row_ref[0, 0]


def stack_of_core(core, rows, after=()):
    chips = rows.shape[0]
    return ordered(
        stack_kernel,
        after,
        dict(
            num_scalar_prefetch=1,
            grid=(chips,),
            in_specs=[pl.BlockSpec((1, 1, TOK_DEV, D), lambda i, s: (i, s[0], 0, 0))],
            out_specs=pl.BlockSpec((1, TOK_DEV, D), lambda i, s: (i, 0, 0)),
        ),
        out_shape=in_hbm((chips, TOK_DEV, D), BF16),
        compiler_params=params(16),
        cost_estimate=cost(0, 4 * chips * TOK_DEV * D),
        name="stack_of_core",
    )(core.reshape(1), rows)


def stack_dispatch_kernel(place_ref, own_ref, other_ref, own_slot, other_slot, out_ref):
    out = nn(pick_matrix(own_slot[0]), own_ref[0])
    out = (out + nn(pick_matrix(other_slot[0]), other_ref[0])).astype(BF16)
    for j in range(out_ref.shape[0]):
        out_ref[j] = out[j * SLOTS : (j + 1) * SLOTS]


def stack_dispatch(places, stacks, slots, after=()):
    chips = stacks.shape[1]
    blocks, local, _ = slots.shape
    row_shape = (None, 1, TOK_DEV, D)
    return ordered(
        stack_dispatch_kernel,
        after,
        dict(
            num_scalar_prefetch=1,
            grid=(chips,),
            in_specs=[
                pl.BlockSpec(row_shape, lambda i, s: (2 - 2 * s[chips + 1] + s[chips], i, 0, 0)),
                pl.BlockSpec(row_shape, lambda i, s: (3 - 2 * s[chips + 1] - s[chips], i, 0, 0)),
                pl.BlockSpec((1, local, TOK_DEV), lambda i, s: (2 * s[i] + s[chips], 0, 0)),
                pl.BlockSpec((1, local, TOK_DEV), lambda i, s: (2 * s[i] + 1 - s[chips], 0, 0)),
            ],
            out_specs=pl.BlockSpec((local, SLOTS, D), lambda i, s: (0, s[i], 0)),
        ),
        out_shape=in_hbm((local, blocks // 2 * SLOTS, D), BF16),
        compiler_params=params(24),
        cost_estimate=cost(2 * chips * PAIR * D * local * SLOTS, 4 * chips * PAIR * D),
        name="stack_dispatch",
    )(places, stacks, stacks, slots, slots)


def plain_dispatch_kernel(row_ref, slot_ref, out_ref):
    out = sum(nn(pick_matrix(slot_ref[i]), row_ref[i]) for i in range(2)).astype(BF16)
    for j in range(out_ref.shape[0]):
        out_ref[j] = out[j * SLOTS : (j + 1) * SLOTS]


def plain_dispatch(rows, slots, after=(), part=0, parts=1):
    blocks, local, _ = slots.shape
    rows = rows.reshape(blocks, parts, TOK_DEV, D)
    return ordered(
        plain_dispatch_kernel,
        after,
        dict(
            grid=(blocks // 2,),
            in_specs=[
                pl.BlockSpec((2, None, TOK_DEV, D), lambda i: (i, part, 0, 0)),
                pl.BlockSpec((2, local, TOK_DEV), lambda i: (i, 0, 0)),
            ],
            out_specs=pl.BlockSpec((local, SLOTS, D), lambda i: (0, i, 0)),
        ),
        out_shape=in_hbm((local, blocks // 2 * SLOTS, D), BF16),
        compiler_params=params(24),
        cost_estimate=cost(2 * blocks * TOK_DEV * D * local * SLOTS, 4 * blocks * TOK_DEV * D),
        name="plain_dispatch",
    )(rows, slots)


def combine_chip(row_ref, slot_ref):
    rows = jnp.concatenate([row_ref[j] for j in range(row_ref.shape[0])], 0)
    return [tn(pick_matrix(slot_ref[i]), rows).astype(BF16) for i in range(2)]


def combine_kernel(row_ref, slot_ref, out_ref):
    first, second = combine_chip(row_ref, slot_ref)
    out_ref[:TOK_DEV] = first
    out_ref[TOK_DEV:] = second


def combine(slot_rows, slots, after=()):
    blocks, local, _ = slots.shape
    rows = blocks * TOK_DEV
    return ordered(
        combine_kernel,
        after,
        dict(
            grid=(blocks // 2,),
            in_specs=[
                pl.BlockSpec((local, SLOTS, D), lambda i: (0, i, 0)),
                pl.BlockSpec((2, local, TOK_DEV), lambda i: (i, 0, 0)),
            ],
            out_specs=pl.BlockSpec((PAIR, D), lambda i: (i, 0)),
        ),
        out_shape=jax.ShapeDtypeStruct((rows, D), BF16),
        compiler_params=params(24),
        cost_estimate=cost(2 * rows * D * local * SLOTS, 4 * rows * D),
        name="combine",
    )(slot_rows, slots)


def combine_part_kernel(place_ref, a_ref, b_ref, a_slot, b_slot, own_ref, other_ref):
    for at, (row_ref, slot_ref) in enumerate(((a_ref, a_slot), (b_ref, b_slot))):
        first, second = combine_chip(row_ref, slot_ref)
        sort_cores(place_ref[4], first, second, own_ref, other_ref, at)


def chip_specs(slot_rows, slots):
    local, width = slots.shape[1], slot_rows.shape[2]
    rows = [
        pl.BlockSpec((local, SLOTS, width), lambda i, s, n=n: (0, s[2 * i + n], 0)) for n in (0, 1)
    ]
    spots = [
        pl.BlockSpec((2, local, TOK_DEV), lambda i, s, n=n: (s[2 * i + n], 0, 0)) for n in (0, 1)
    ]
    return rows + spots


def combine_part(place, slot_rows, slots, after=()):
    local, width = slots.shape[1], slot_rows.shape[2]
    shape = jax.ShapeDtypeStruct((2, 2, TOK_DEV, width), BF16)
    return ordered(
        combine_part_kernel,
        after,
        dict(
            num_scalar_prefetch=1,
            grid=(2,),
            in_specs=chip_specs(slot_rows, slots),
            out_specs=[pl.BlockSpec((1, 2, TOK_DEV, width), lambda i, s: (i, 0, 0, 0))] * 2,
        ),
        out_shape=[shape, shape],
        compiler_params=params(24),
        cost_estimate=cost(4 * PAIR * D * local * SLOTS, 8 * PAIR * D),
        name="combine_part",
    )(place, slot_rows, slot_rows, slots, slots)


def slope_kernel(g_ref, wd_ref, out_ref):
    out_ref[0] = nt(g_ref[0], wd_ref[0])


def slopes(grads, w_down, after=()):
    local, count, _ = grads.shape
    hidden = w_down.shape[1]
    chunk = hidden // 2
    return ordered(
        slope_kernel,
        after,
        dict(
            grid=(local, 2),
            in_specs=[
                pl.BlockSpec((1, count, D), lambda j, f: (j, 0, 0)),
                pl.BlockSpec((1, chunk, D), lambda j, f: (j, f, 0)),
            ],
            out_specs=pl.BlockSpec((1, count, chunk), lambda j, f: (j, 0, f)),
        ),
        out_shape=in_hbm((local, count, hidden), F32),
        compiler_params=params(24),
        cost_estimate=cost(2 * local * count * hidden * D, 2 * local * hidden * D),
        name="slopes",
    )(grads, w_down)


def expert_kernel(first_ref, x_ref, h_ref, wg_ref, wu_ref, wr_ref, *rest, full, offset):
    if full:
        (act_ref, dg_ref, du_ref, gate_ref, z_ref, z_s, dp_s) = rest
    else:
        (act_ref, dg_ref, du_ref, gate_ref) = rest
    step, steps = pl.program_id(1), pl.num_programs(1)
    rows = x_ref[0]

    @pl.when(step == 0)
    def _():
        logits = nn(rows, wr_ref[...])
        lane = lax.broadcasted_iota(jnp.int32, logits.shape, 1)
        logits = jnp.where(lane < EXPERTS, logits, NEG_FILL)
        powers = jnp.exp(logits - jnp.max(logits, -1, keepdims=True))
        mine = jnp.where(lane == first_ref[0] + offset + pl.program_id(0), powers, 0.0)
        gate = jnp.sum(mine, -1, keepdims=True) / jnp.sum(powers, -1, keepdims=True)
        gate_ref[0] = jnp.broadcast_to(gate, gate_ref.shape[1:])
        if full:
            z_s[...] = jnp.zeros_like(z_s)
            dp_s[...] = jnp.zeros_like(dp_s)

    gate = gate_ref[0, :, 0:1]
    gate_pre = nn(rows, wg_ref[0])
    up_pre = nn(rows, wu_ref[0])
    slope = h_ref[0]
    sig = jax.nn.sigmoid(gate_pre)
    silu = gate_pre * sig
    act = (silu * up_pre).astype(BF16)
    grad_act = slope * gate
    grad_gate = (grad_act * up_pre * sig * (1.0 + gate_pre * (1.0 - sig))).astype(BF16)
    grad_up = (grad_act * silu).astype(BF16)
    act_ref[0] = act
    dg_ref[0] = grad_gate
    du_ref[0] = grad_up
    if full:
        dp_s[...] += jnp.broadcast_to(
            jnp.sum(act.astype(F32) * slope, -1, keepdims=True), dp_s.shape
        )
        z_s[...] += nt(grad_gate, wg_ref[0]) + nt(grad_up, wu_ref[0])

        @pl.when(step == steps - 1)
        def _():
            z_ref[0, :, :D] = z_s[...].astype(BF16)
            lane = lax.broadcasted_iota(jnp.int32, dp_s.shape, 1)
            mine = first_ref[0] + offset + pl.program_id(0)
            high = dp_s[...].astype(BF16).astype(F32)
            parts = jnp.where(lane == mine, high, 0.0)
            parts = jnp.where(lane == mine + EXPERTS, dp_s[...] - high, parts)
            z_ref[0, :, D:] = parts.astype(BF16)


def experts(first, rows, slope, w_gate, w_up, router, full, only=None, after=()):
    local, count, _ = rows.shape
    offset, number = (0, local) if only is None else only
    hidden = w_gate.shape[2]
    chunk = hidden // 2
    row_spec = pl.BlockSpec((1, count, D), lambda j, f, s: (j, 0, 0))
    mid_spec = pl.BlockSpec((1, count, chunk), lambda j, f, s: (j, 0, f))
    lane_spec = pl.BlockSpec((1, count, HD), lambda j, f, s: (j, 0, 0))
    in_w = pl.BlockSpec((1, D, chunk), lambda j, f, s: (j + offset, 0, f))
    mid_shape = in_hbm((number, count, hidden), BF16)
    lane_shape = jax.ShapeDtypeStruct((number, count, HD), F32)
    out_specs = [mid_spec, mid_spec, mid_spec, lane_spec]
    out_shape = [mid_shape, mid_shape, mid_shape, lane_shape]
    scratch = []
    if full:
        out_specs += [pl.BlockSpec((1, count, D + HD), lambda j, f, s: (j, 0, 0))]
        out_shape += [in_hbm((number, count, D + HD), BF16)]
        scratch += [pltpu.VMEM((count, D), F32), pltpu.VMEM((count, HD), F32)]
    unit = 2 * number * count * hidden * D
    return ordered(
        functools.partial(expert_kernel, full=full, offset=offset),
        after,
        dict(
            num_scalar_prefetch=1,
            grid=(number, 2),
            in_specs=[
                pl.BlockSpec((1, count, D), lambda j, f, s: (j + offset, 0, 0)),
                pl.BlockSpec((1, count, chunk), lambda j, f, s: (j + offset, 0, f)),
                in_w,
                in_w,
                pl.BlockSpec((D, HD), lambda j, f, s: (0, 0)),
            ],
            out_specs=out_specs,
            scratch_shapes=scratch,
        ),
        out_shape=out_shape,
        compiler_params=params(56),
        cost_estimate=cost((4 if full else 2) * unit, 4 * number * hidden * D + 8 * number * count * D),
        name="experts_full" if full else "experts_half",
    )(first, rows, slope, w_gate, w_up, router)


def down_kernel(act_ref, gate_ref, wd_ref, out_ref):
    out_ref[0] = (nn(act_ref[0], wd_ref[0]) * gate_ref[0, :, 0:1]).astype(BF16)


def down(act, gate, w_down, after=()):
    local, count, hidden = act.shape
    chunk = D // 2
    return ordered(
        down_kernel,
        after,
        dict(
            grid=(local, 2),
            in_specs=[
                pl.BlockSpec((1, count, hidden), lambda j, f: (j, 0, 0)),
                pl.BlockSpec((1, count, HD), lambda j, f: (j, 0, 0)),
                pl.BlockSpec((1, hidden, chunk), lambda j, f: (j, 0, f)),
            ],
            out_specs=pl.BlockSpec((1, count, chunk), lambda j, f: (j, 0, f)),
        ),
        out_shape=jax.ShapeDtypeStruct((local, count, D), BF16),
        compiler_params=params(24),
        cost_estimate=cost(2 * local * count * hidden * D, 2 * local * hidden * D),
        name="down",
    )(act, gate, w_down)


def weights_kernel(
    half_ref, xa, xb, dga, dgb, dua, dub, aa, ab, ga, gb, gate_a, gate_b, *refs
):
    gate_ref, up_ref, down_ref = refs[-3:]
    rows = jnp.concatenate([xa[0], xb[0]], 0)
    gate_ref[0] = tn(rows, jnp.concatenate([dga[0], dgb[0]], 0))
    up_ref[0] = tn(rows, jnp.concatenate([dua[0], dub[0]], 0))
    grad_a = (ga[0].astype(F32) * gate_a[0, :, 0:1]).astype(BF16)
    grad_b = (gb[0].astype(F32) * gate_b[0, :, 0:1]).astype(BF16)
    down_ref[0] = tn(
        jnp.concatenate([aa[0], ab[0]], 0), jnp.concatenate([grad_a, grad_b], 0)
    )


def weight_grads(only, half, x_pair, dg_pair, du_pair, act_pair, g_pair, gate_pair, buffers, after=()):
    local, count, _ = x_pair[0].shape
    start, number = only
    hidden = dg_pair[0].shape[2]
    kept = [] if buffers is None else list(buffers)
    chunk = hidden // 2

    def spec(width, by_half, single):
        at = 0 if single else start
        if by_half is None:
            return pl.BlockSpec((1, count, width), lambda j, f, s: (j + at, 0, 0))
        if by_half:
            return pl.BlockSpec((1, count, width), lambda j, f, s: (j + at, 0, s[0]))
        return pl.BlockSpec((1, count, width), lambda j, f, s: (j + at, 0, f))

    in_specs = [
        spec(D // 2, True, False), spec(D // 2, True, False),
        spec(chunk, False, False), spec(chunk, False, True),
        spec(chunk, False, False), spec(chunk, False, True),
        spec(chunk, True, False), spec(chunk, True, True),
        spec(D // 2, False, False), spec(D // 2, False, False),
        spec(HD, None, False), spec(HD, None, True),
    ]
    unit = 2 * number * count * hidden * D
    return ordered(
        weights_kernel,
        after,
        dict(
            num_scalar_prefetch=1,
            grid=(number, 2),
            in_specs=in_specs + [ANYWHERE] * len(kept),
            out_specs=[
                pl.BlockSpec((1, D // 2, chunk), lambda j, f, s: (j + start, 0, f)),
                pl.BlockSpec((1, D // 2, chunk), lambda j, f, s: (j + start, 0, f)),
                pl.BlockSpec((1, chunk, D // 2), lambda j, f, s: (j + start, 0, f)),
            ],
        ),
        out_shape=[
            in_hbm((local, D // 2, hidden), F32),
            in_hbm((local, D // 2, hidden), F32),
            in_hbm((local, hidden // 2, D), F32),
        ],
        input_output_aliases={13 + i: i for i in range(len(kept))},
        compiler_params=params(56),
        cost_estimate=cost(3 * unit, 6 * number * hidden * D + 8 * number * count * D),
        name="weight_grads",
    )(half, *x_pair, *dg_pair, *du_pair, *act_pair, *g_pair, *gate_pair, *kept)


def softmax_of(mixed, router):
    logits = nn(mixed, router)
    lane = lax.broadcasted_iota(jnp.int32, logits.shape, 1)
    logits = jnp.where(lane < EXPERTS, logits, NEG_FILL)
    powers = jnp.exp(logits - jnp.max(logits, -1, keepdims=True))
    return powers / jnp.sum(powers, -1, keepdims=True)


def pair_kernel(group_ref, near_ref, far_ref, out_ref):
    out_ref[group_ref[0]] = near_ref[...]
    out_ref[1 - group_ref[0]] = far_ref[...]


def pair_up(group, near, far, after=()):
    return ordered(
        pair_kernel,
        after,
        dict(
            num_scalar_prefetch=1,
            grid=(1,),
            in_specs=[whole(*near.shape)] * 2,
            out_specs=whole(2, *near.shape),
        ),
        out_shape=jax.ShapeDtypeStruct((2,) + near.shape, near.dtype),
        compiler_params=params(16),
        name="pair_up",
    )(group.reshape(1).astype(jnp.int32), near, far)


def out_kernel(att_ref, w_ref, tok_ref, gain_ref, hidden_ref, mixed_ref, sums_ref, acc_ref):
    step, steps = pl.program_id(0), pl.num_programs(0)
    heads = jnp.concatenate([att_ref[i] for i in range(att_ref.shape[0])], 1)
    part = nn(heads, w_ref[...].reshape(heads.shape[1], D))

    @pl.when(step == 0)
    def _():
        acc_ref[...] = part

    @pl.when(step > 0)
    def _():
        acc_ref[...] += part

    @pl.when(step == steps - 1)
    def _():
        branch = acc_ref[...]
        hidden = tok_ref[...].astype(F32) + branch
        hidden_ref[...] = hidden
        mixed_ref[...] = (hidden * inv_rms(hidden) * gain_ref[...]).astype(BF16)
        total = jnp.sum(jnp.sum(branch * branch, -1, keepdims=True), 0, keepdims=True)
        sums_ref[...] = jnp.broadcast_to(total, sums_ref.shape)


def out_rows_spec(weights, heads):
    members, groups, rows, _ = weights.shape
    count = heads * HD // rows
    steps = members // count
    return pl.BlockSpec((count, None, rows, D), lambda i: (i % steps, i // steps, 0, 0))


def project_out(att, weights, tokens, gain_row, after=()):
    chunk = 4
    return ordered(
        out_kernel,
        after,
        dict(
        grid=(HEADS // chunk,),
        in_specs=[
            pl.BlockSpec((chunk, TOK_DEV, HD), lambda i, *_: (i, 0, 0)),
            out_rows_spec(weights, chunk),
            whole(*BLOCK_SHAPE),
            whole(1, D),
        ],
        out_specs=[whole(*BLOCK_SHAPE), whole(*BLOCK_SHAPE), whole(1, HD)],
        scratch_shapes=[pltpu.VMEM(BLOCK_SHAPE, F32)],
        ),
        out_shape=[
            jax.ShapeDtypeStruct(BLOCK_SHAPE, F32),
            jax.ShapeDtypeStruct(BLOCK_SHAPE, BF16),
            jax.ShapeDtypeStruct((1, HD), F32),
        ],
        compiler_params=params(24),
        cost_estimate=cost(2 * TOK_DEV * D * D, 2 * D * D),
        name="project_out",
    )(att, weights, tokens, gain_row)


def token_back_kernel(
    a, b, c, d, e, mixed_ref, hidden_ref, cot_ref, router_ref, gain_ref,
    grad_ref, wide_ref,
):
    probs = softmax_of(mixed_ref[...], router_ref[...])
    grad = sum(ref[...].astype(F32) for ref in (a, b, c, d, e))
    dp = grad[:, D : D + HD] + pltpu.roll(grad[:, D : D + HD], EXPERTS, 1)
    logits = (probs * (dp - jnp.sum(probs * dp, -1, keepdims=True))).astype(BF16)
    grad = grad[:, :D] + nt(logits, router_ref[...])
    hidden = hidden_ref[...]
    inverse = inv_rms(hidden)
    scaled = grad * gain_ref[...]
    mean = jnp.mean(scaled * hidden, -1, keepdims=True)
    result = cot_ref[...].astype(F32) + inverse * (scaled - hidden * inverse * inverse * mean)
    grad_ref[...] = result
    wide_ref[:, :D] = result.astype(BF16)
    wide_ref[:, D : D + HD] = logits
    wide_ref[:, D + HD :] = jnp.zeros((TOK_DEV, HD), BF16)
    part = jnp.sum(grad * hidden * inverse, 0, keepdims=True)
    high = part.astype(BF16).astype(F32)
    rows = lax.broadcasted_iota(jnp.int32, (2 * HEADS, HD), 0)
    spread = jnp.zeros((2 * HEADS, HD), F32)
    for i in range(HEADS):
        lanes = slice(i * HD, (i + 1) * HD)
        spread = jnp.where(rows == i, high[:, lanes], spread)
        spread = jnp.where(rows == HEADS + i, part[:, lanes] - high[:, lanes], spread)
    wide_ref[: 2 * HEADS, D + HD :] = spread.astype(BF16)


def term_specs(terms):
    specs, arrays = [], []
    for term in terms:
        if isinstance(term, tuple):
            arrays.append(term[0])
            shape = (None, None) + term[0].shape[2:]
            specs.append(pl.BlockSpec(shape, lambda i, n=term[1]: n + (0, 0)))
        else:
            arrays.append(term)
            specs.append(whole(*term.shape))
    return specs, arrays


def token_back(terms, mixed, hidden, cotangent, router, gain_row, after=()):
    specs, arrays = term_specs(terms)
    return ordered(
        token_back_kernel,
        after,
        dict(
            grid=(1,),
            in_specs=specs
            + [whole(*BLOCK_SHAPE)] * 3
            + [whole(D, HD), whole(1, D)],
            out_specs=[whole(*BLOCK_SHAPE), whole(TOK_DEV, D + 2 * HD)],
        ),
        out_shape=[
            jax.ShapeDtypeStruct(BLOCK_SHAPE, F32),
            jax.ShapeDtypeStruct((TOK_DEV, D + 2 * HD), BF16),
        ],
        compiler_params=params(40),
        cost_estimate=cost(30 * TOK_DEV * D, 20 * TOK_DEV * D),
        name="token_back",
    )(*arrays, mixed, hidden, cotangent, router, gain_row)


def out_back_kernel(grad_ref, w_ref, out_ref):
    out = nt(grad_ref[...], w_ref[...].reshape(-1, D)).astype(BF16)
    for i in range(out_ref.shape[0]):
        out_ref[i] = out[:, i * HD : (i + 1) * HD]


def out_back(wide, weights):
    chunk = 4
    return ordered(
        out_back_kernel,
        (),
        dict(
        grid=(HEADS // chunk,),
        in_specs=[
            pl.BlockSpec(BLOCK_SHAPE, lambda i: (0, 0)),
            out_rows_spec(weights, chunk),
        ],
        out_specs=pl.BlockSpec((chunk, TOK_DEV, HD), lambda i: (i, 0, 0)),
        ),
        out_shape=jax.ShapeDtypeStruct((HEADS, TOK_DEV, HD), BF16),
        compiler_params=params(24),
        cost_estimate=cost(2 * TOK_DEV * D * D, 2 * D * D),
        name="out_back",
    )(wide, weights)


def tokens_grad_kernel(
    a, b, c, d, e, tok_ref, gain_ref, grad_ref, out_ref
):
    grad = sum(ref[...].astype(F32) for ref in (a, b, c, d, e))
    inputs = tok_ref[...].astype(F32)
    inverse = inv_rms(inputs)
    scaled = grad * gain_ref[...]
    mean = jnp.mean(scaled * inputs, -1, keepdims=True)
    result = grad_ref[...] + inverse * (scaled - inputs * inverse * inverse * mean)
    out_ref[...] = result.astype(BF16)


def final_tokens(terms, tokens, gain_row, grad_hidden, after=()):
    specs, arrays = term_specs(terms)
    return ordered(
        tokens_grad_kernel,
        after,
        dict(
            grid=(1,),
            in_specs=specs
            + [whole(*BLOCK_SHAPE), whole(1, D), whole(*BLOCK_SHAPE)],
            out_specs=whole(*BLOCK_SHAPE),
        ),
        out_shape=jax.ShapeDtypeStruct(BLOCK_SHAPE, BF16),
        compiler_params=params(40),
        cost_estimate=cost(30 * TOK_DEV * D, 20 * TOK_DEV * D),
        name="final_tokens",
    )(*arrays, tokens, gain_row, grad_hidden)


def owner_rows_kernel(place_ref, att_ref, mixed_ref, wide_ref, out_ref, moe_ref):
    step, steps = pl.program_id(0), pl.num_programs(0)

    @pl.when(step == 0)
    def _():
        out_ref[...] = jnp.zeros_like(out_ref)
        moe_ref[...] = jnp.zeros_like(moe_ref)

    out_ref[:, :D] += tn(att_ref[...], wide_ref[:, :D])
    out_ref[:, D:] += tn(mixed_ref[...], wide_ref[:, D : D + HD])
    tail = wide_ref[:, D + HD :].astype(F32)
    rows = lax.broadcasted_iota(jnp.int32, tail.shape, 0) % TOK_DEV
    mine = (rows == place_ref[0]) | (rows == place_ref[0] + HEADS)
    moe_ref[...] += jnp.sum(jnp.where(mine, tail, 0.0), 0, keepdims=True)

    @pl.when(step == steps - 1)
    def _():
        lane = lax.broadcasted_iota(jnp.int32, (HD, HD), 1)
        out_ref[:, D:] = jnp.where(lane == EXPERTS, as_column(moe_ref[...]), out_ref[:, D:])


def owner_rows(place, att, mixed_columns, wide_all, after=()):
    rows, width = wide_all.shape
    chunk = rows // 4
    return ordered(
        owner_rows_kernel,
        after,
        dict(
            num_scalar_prefetch=1,
            grid=(4,),
            in_specs=[
                pl.BlockSpec((chunk, HD), lambda i, s: (i, 0)),
                pl.BlockSpec((chunk, HD), lambda i, s: (i, 0)),
                pl.BlockSpec((chunk, width), lambda i, s: (i, 0)),
            ],
            out_specs=whole(HD, D + HD),
            scratch_shapes=[pltpu.VMEM((1, HD), F32)],
        ),
        out_shape=jax.ShapeDtypeStruct((HD, D + HD), F32),
        compiler_params=params(24),
        cost_estimate=cost(2 * rows * D * HD, 2 * rows * D),
        name="owner_rows",
    )(place.reshape(1).astype(jnp.int32), att, mixed_columns, wide_all)


def unpack_kernel(in_ref, wq_ref, wk_ref, wv_ref, gain_ref, q_ref, k_ref, v_ref, sums_ref):
    heads = in_ref.shape[0]
    total = jnp.zeros((q_ref.shape[0], 1), F32)
    for part, (w_ref, out_ref) in enumerate(((wq_ref, q_ref), (wk_ref, k_ref), (wv_ref, v_ref))):
        for h in range(heads):
            piece = in_ref[h, : q_ref.shape[0], part * HD : (part + 1) * HD].astype(F32)
            lanes = slice(h * HD, (h + 1) * HD)
            out_ref[:, lanes] = piece
            total += jnp.sum(w_ref[:, lanes].astype(F32) * piece, -1, keepdims=True)
    sums_ref[...] = jnp.broadcast_to(total / gain_ref[...], sums_ref.shape)


def unpack(arrived, weights, gain, after=()):
    rows = weights[0].shape[0]
    shape = jax.ShapeDtypeStruct((rows, D), F32)
    return ordered(
        unpack_kernel,
        after,
        dict(
            grid=(1,),
            in_specs=[whole(*arrived.shape)] + [whole(rows, D)] * 3 + [whole(rows, 1)],
            out_specs=[whole(rows, D)] * 3 + [whole(rows, HD)],
        ),
        out_shape=[shape] * 3 + [jax.ShapeDtypeStruct((rows, HD), F32)],
        compiler_params=params(24),
        cost_estimate=cost(6 * rows * D, 20 * rows * D),
        name="unpack",
    )(arrived, *weights, gain.astype(F32).reshape(rows, 1))


def tie_kernel(in_ref, out_ref):
    out_ref[...] = in_ref[...]


def tie(array, after):
    return ordered(
        tie_kernel,
        after,
        dict(grid=(1,), in_specs=[whole(*array.shape)], out_specs=whole(*array.shape)),
        out_shape=jax.ShapeDtypeStruct(array.shape, array.dtype),
        compiler_params=params(16),
        name="tie",
    )(array)


def swap(value, axis):
    return lax.ppermute(value, axis, [(0, 1), (1, 0)])


def total_over_ep(value):
    value = value + swap(value, "core")
    value = value + swap(value, "x")
    value = value + lax.ppermute(value, "z", [(0, 1), (1, 0), (2, 3), (3, 2)])
    return value + lax.ppermute(value, "z", [(0, 2), (2, 0), (1, 3), (3, 1)])


def of_groups(value):
    return lax.all_gather(value, ("grp", "core"))


def gather_rows(value):
    return lax.all_gather(value, EP, axis=0, tiled=True)


def reduce_rows(value):
    return lax.psum_scatter(value, EP, scatter_dimension=0, tiled=True)


CHIP_ORDER = ((0, 1, 2, 3), (1, 0, 2, 3), (2, 1, 3, 0), (3, 2, 1, 0))


def chip_places():
    z, x = lax.axis_index("z"), lax.axis_index("x")
    order = jnp.asarray(CHIP_ORDER, jnp.int32)[z]
    return [[order[s] * 2 + (x if r == 0 else 1 - x) for r in range(2)] for s in range(4)]


def shift(value, pairs):
    return lax.ppermute(value, "z", pairs)


def choose_kernel(flag_ref, *refs):
    out_ref = refs[-1]
    for i in range(len(refs) - 1):

        @pl.when(flag_ref[i] == 1)
        def _(i=i):
            out_ref[...] = refs[i][...]


def choose(flags, options, after=()):
    return ordered(
        choose_kernel,
        after,
        dict(
            num_scalar_prefetch=1,
            grid=(1,),
            in_specs=[whole(*BLOCK_SHAPE)] * len(options),
            out_specs=whole(*BLOCK_SHAPE),
        ),
        out_shape=jax.ShapeDtypeStruct(BLOCK_SHAPE, BF16),
        compiler_params=params(16),
        cost_estimate=cost(TOK_DEV * D, 2 * (len(options) + 1) * TOK_DEV * D),
        name="choose",
    )(flags, *options)


def gather_steps(block, use, work):
    z = lax.axis_index("z")
    flags = lambda *tests: jnp.stack([jnp.asarray(test, jnp.int32) for test in tests])

    def use_now(arrived, last):
        for s, r, own, far in arrived:
            last = use(s, r, own, far, [last])
        return last

    below1 = shift(block, [(0, 1), (1, 2), (2, 3)])
    above1 = shift(block, [(3, 2), (2, 1), (1, 0)])
    across0 = swap(block, "x")
    far00 = swap(block, "core")
    last = work(0, block)
    column1 = last = choose(flags(z == 0, z != 0), [above1, below1], [last])
    below2 = shift(below1, [(1, 2), (2, 3)])
    above2 = shift(above1, [(2, 1), (1, 0)])
    across1 = swap(column1, "x")
    far01, far10 = swap(across0, "core"), swap(column1, "core")
    last = use_now([(0, 0, block, far00), (0, 1, across0, far01), (1, 0, column1, far10)], last)
    last = work(1, last)
    column2 = last = choose(
        flags(z == 0, z == 3, (z == 1) | (z == 2)), [above2, below2, above1], [last]
    )
    below3 = shift(below2, [(2, 3)])
    above3 = shift(above2, [(1, 0)])
    across2 = swap(column2, "x")
    far11, far20 = swap(across1, "core"), swap(column2, "core")
    last = use_now([(1, 1, across1, far11), (2, 0, column2, far20)], last)
    last = work(2, last)
    column3 = last = choose(
        flags(z == 0, z == 1, z == 2, z == 3), [above3, above2, below2, below3], [last]
    )
    across3 = swap(column3, "x")
    far21, far30 = swap(across2, "core"), swap(column3, "core")
    last = use_now([(2, 1, across2, far21), (3, 0, column3, far30)], last)
    last = work(3, last)
    far31 = swap(across3, "core")
    return use_now([(3, 1, across3, far31)], last)


def sum_kernel(*refs):
    out_ref = refs[-1]
    total = refs[0][...].astype(F32)
    for ref in refs[1:-1]:
        total = total + ref[...].astype(F32)
    out_ref[...] = total.astype(out_ref.dtype)


def sum_blocks(terms, after=(), dtype=BF16):
    specs, arrays = term_specs(terms)
    return ordered(
        sum_kernel,
        after,
        dict(grid=(1,), in_specs=specs, out_specs=whole(*arrays[0].shape[-2:])),
        out_shape=jax.ShapeDtypeStruct(arrays[0].shape[-2:], dtype),
        compiler_params=params(16),
        cost_estimate=cost(len(terms) * TOK_DEV * D, 2 * (len(terms) + 1) * TOK_DEV * D),
        name="sum_blocks",
    )(*arrays)


def pass_on(place, near_up, far_up, near_down, far_down, below, above, after=()):
    def kernel(place_ref, nu, fu, nd, fd, below_ref, above_ref, up_ref, down_ref):
        z = place_ref[0]

        def store(out_ref, source_ref, arrived_ref):
            total = source_ref[...].astype(F32) + arrived_ref[...].astype(F32)
            out_ref[...] = total.astype(BF16)

        for edge, near, far, arrived, out_ref in (
            (0, nu, fu, below_ref, up_ref),
            (3, nd, fd, above_ref, down_ref),
        ):
            pl.when(z == edge)(functools.partial(store, out_ref, near, arrived))
            pl.when(z != edge)(functools.partial(store, out_ref, far, arrived))

    shape = jax.ShapeDtypeStruct(below.shape, BF16)
    return ordered(
        kernel,
        after,
        dict(
            num_scalar_prefetch=1,
            grid=(1,),
            in_specs=[whole(*below.shape)] * 6,
            out_specs=[whole(*below.shape)] * 2,
        ),
        out_shape=[shape, shape],
        compiler_params=params(24),
        cost_estimate=cost(4 * TOK_DEV * D, 16 * TOK_DEV * D),
        name="pass_on",
    )(place, near_up, far_up, near_down, far_down, below, above)


def reduce_steps(parts, work):
    place = lax.axis_index("z").reshape(1).astype(jnp.int32)
    last, sources = [], {}
    for s in (3, 1):
        own, other = parts(s, last)
        near = swap(other, "core")
        last = [own]
        for i in range(2):
            sources[s - i] = lambda r, i=i, own=own, near=near: [(own, (i, r)), (near, (i, r))]
    crossed = {}
    last = last[0]
    for s in (3, 2, 1, 0):
        last = sum_blocks(sources[s](1), [last])
        crossed[s] = swap(last, "x")
    last = work(0, last)
    low = {}
    low[3] = last = sum_blocks(sources[3](0) + [crossed[3]], [last])
    up3 = shift(low[3], [(0, 1)])
    down3 = shift(low[3], [(3, 2)])
    last = work(1, last)
    low[2] = last = sum_blocks(sources[2](0) + [crossed[2]], [last])
    up2, down2 = pass_on(place, low[2], low[3], low[2], low[3], up3, down3)
    last = work(2, up2)
    up2 = shift(up2, [(0, 1), (1, 2)])
    down2 = shift(down2, [(3, 2), (2, 1)])
    low[1] = last = sum_blocks(sources[1](0) + [crossed[1]], [last])
    up1, down1 = pass_on(place, low[1], low[2], low[1], low[1], up2, down2)
    last = work(3, up1)
    up1 = shift(up1, [(0, 1), (1, 2), (2, 3)])
    down1 = shift(down1, [(3, 2), (2, 1), (1, 0)])
    return sources[0](0) + [crossed[0], up1, down1], last


def expert_slots(routes_all, first, local):
    rows = routes_all.shape[0]
    ids = first + jnp.arange(local, dtype=jnp.int32)
    named = jnp.any(routes_all[None, :, :] == ids[:, None, None], -1).reshape(
        local, rows // TOK_DEV, TOK_DEV
    )
    places = jnp.arange(TOK_DEV, dtype=jnp.int32)
    upto = (places[:, None] <= places[None, :]).astype(BF16)
    rank = jnp.einsum(
        "ebt,ts->ebs", named.astype(BF16), upto, preferred_element_type=F32
    ).astype(jnp.int32)
    base = (jnp.arange(rows // TOK_DEV, dtype=jnp.int32) % 2) * CAP
    slots = jnp.where(named, rank - 1 + base[None, :, None], -1)
    return jnp.transpose(slots, (1, 0, 2))


def fast_shards(
    tokens, w_query, w_key, w_value, w_output, w_router, attn_gain, query_gain, key_gain,
    moe_gain, w_gate, w_up, w_down, routes, cotangent,
):
    Order.marks.clear()
    group = lax.axis_index("grp")
    place = lax.axis_index(EP)
    members = lax.axis_size(EP)
    seq = TOK_DEV * members
    local = w_gate.shape[0]
    wide = w_query.shape[0]
    first = (place * local).reshape(1).astype(jnp.int32)

    core = lax.axis_index("core").astype(jnp.int32)
    chips = chip_places()
    small = jnp.concatenate(
        [
            w_router,
            routes.reshape(-1, EXPERTS).astype(BF16),
            jnp.stack([attn_gain, query_gain, key_gain, moe_gain]),
            jnp.zeros((12, EXPERTS), BF16),
        ],
        0,
    ).reshape(16, 3 * HD)
    columns = jnp.stack([w_query, w_key, w_value], 1).reshape(wide, 3, HEADS, HD)
    columns = jnp.transpose(columns, (2, 0, 1, 3)).reshape(HEADS, wide, 3 * HD)
    columns = jnp.concatenate([columns, jnp.broadcast_to(small, (HEADS,) + small.shape)], 1)
    mine = lax.all_to_all(columns, EP, 0, 0, tiled=True)
    other = swap(mine, "grp")
    both = jnp.where(group == 0, jnp.stack([mine, other]), jnp.stack([other, mine]))
    w_head = both[:, :, :wide].reshape(D, 3 * HD)
    small_all = both[:, :, wide:].reshape(2 * members, -1, EXPERTS)
    route_rows = TOK_DEV * TOPK // EXPERTS
    router_full = small_all[:, :wide].reshape(D, EXPERTS)
    routes_all = (
        small_all[:, wide : wide + route_rows].reshape(2, seq, TOPK).astype(jnp.int32)
    )
    gains = jnp.transpose(
        small_all[:, wide + route_rows : wide + route_rows + 4], (1, 0, 2)
    ).reshape(4, D).astype(F32)
    router_wide = jnp.concatenate([router_full, jnp.zeros((D, HD - EXPERTS), BF16)], 1)
    head_gains = lax.dynamic_slice(gains, (0, place * HD), (4, HD))
    gain_q, gain_k = head_gains[1:2], head_gains[2:3]
    attn_row, moe_row = gains[0:1], gains[3:4]

    far_out = swap(w_output, "grp")

    slots_own = expert_slots(lax.dynamic_index_in_dim(routes_all, group, 0, False), first, local)
    slots_other = expert_slots(
        lax.dynamic_index_in_dim(routes_all, 1 - group, 0, False), first, local
    )

    positions = jnp.arange(seq, dtype=jnp.int32)
    half_dim = HD // 2
    frequency = jnp.exp(-(2.0 * jnp.arange(half_dim, dtype=F32) / HD) * math.log(10000.0))
    angles = positions.astype(F32)[:, None] * frequency[None, :]
    cosine = jnp.concatenate([jnp.cos(angles)] * 2, 1)
    sine = jnp.concatenate([-jnp.sin(angles), jnp.sin(angles)], 1)

    kept = [None]

    def use_tokens(s, r, own, far, after):
        spot = jnp.stack([chips[s][r], core])
        kept[0] = project(spot, own, far, w_head, attn_row, kept[0], seq, after)
        return kept[0][2]

    def start_work(step, last):
        if step == 3:
            kept.append(pair_up(group, w_output, far_out, [last, mine]))
            return kept[1]
        return last

    gather_steps(tokens, use_tokens, start_work)
    output_full = gather_rows(kept[1][None])
    cot_own = gather_rows(cotangent)
    normed_all, qkv, stat = kept[0]
    stat = total_over_ep(stat)
    q16, k16, v16, attn_float, att_head, lse = attend(qkv, stat, gain_q, gain_k, cosine, sine)
    attended = lax.all_to_all(att_head.reshape(members, TOK_DEV, HD), EP, 0, 0, tiled=True)
    g_own = plain_dispatch(cot_own, slots_own, [att_head])
    cot_stack = stack_of_core(core, cot_own.reshape(members // 2, 2, TOK_DEV, D), [g_own])
    hidden, mixed, branch_sums = project_out(attended, output_full, tokens, moe_row, [cot_stack])
    early = {}

    def early_work(step, last):
        if step == 2:
            early["slope"] = slopes(g_own, w_down, [last])
            return early["slope"]
        return last

    rows = [None]

    def use_mixed(s, r, own, far, after):
        spot = jnp.stack([chips[s][r], core, place.astype(jnp.int32)])
        rows[0] = dispatch(spot, own, far, slots_own, rows[0], after)
        return rows[0][0]

    gather_steps(mixed, use_mixed, early_work)
    x_own, mixed_columns, mixed_stack = rows[0]
    slope_own = early["slope"]
    sides = jnp.stack([core, group.astype(jnp.int32)])
    cot_near = of_groups(cot_stack)
    mixed_near = of_groups(mixed_stack)
    every = jnp.concatenate([jnp.arange(members // 2, dtype=jnp.int32), sides])
    act_a, dg_a, du_a, gate_a, z_rows = experts(
        first, x_own, slope_own, w_gate, w_up, router_wide, True
    )

    def place_of(s):
        return jnp.stack([chips[s][0], chips[s][1], chips[s - 1][0], chips[s - 1][1], core])

    late = {}

    def late_work(step, last):
        if step == 1:
            late["y"] = down(act_a, gate_a, w_down, [last])
            return late["y"]
        if step == 2:
            late["branch"] = combine(late["y"], slots_own, [last])
            late["g"] = stack_dispatch(every, cot_near, slots_other, [late["branch"]])
            return late["g"]
        if step == 3:
            late["slope"] = slopes(late["g"], w_down, [last])
            return late["slope"]
        return last

    terms, last = reduce_steps(
        lambda s, after: combine_part(place_of(s), z_rows, slots_own, after), late_work
    )
    branch_moe = reduce_rows(late["branch"]).astype(F32)
    output = (hidden + branch_moe).astype(BF16)
    grad_hidden, wide_branch = token_back(
        terms, mixed, hidden, cotangent, router_wide, moe_row, [last]
    )
    grad_out = out_back(wide_branch, output_full)
    grad_att_head = lax.all_to_all(grad_out, EP, 0, 0, tiled=True).reshape(seq, HD)
    branch_all = gather_rows(wide_branch)

    def expert_other(only, last):
        late[only] = experts(
            first, late["x"], late["slope"], w_gate, w_up, router_wide, False, only, [last]
        )
        return late[only][3]

    groups = [(0, local // 2), (local // 2, local - local // 2)]
    late["x"] = stack_dispatch(every, mixed_near, slots_other, [grad_out])
    last = expert_other(groups[0], late["x"])

    dnq, dnk, dv16, means, gain_parts = attend_back(
        q16, k16, v16, grad_att_head, attn_float, lse, qkv, stat, gain_q, gain_k, cosine, sine, [last],
    )
    means = total_over_ep(means)
    qkv_grads = finish(dnq, dnk, dv16, qkv, stat, means, gain_q, gain_k)
    half = group.reshape(1).astype(jnp.int32)

    def expert_grads(only, last):
        act_b, dg_b, du_b, gate_b = late[only]
        late["grads"] = weight_grads(
            only, half, (x_own, late["x"]), (dg_a, dg_b), (du_a, du_b), (act_a, act_b),
            (g_own, late["g"]), (gate_a, gate_b), late.get("grads"), [last],
        )
        return late["grads"][0]

    def last_work(step, last):
        if step == 0:
            late["dw"] = dw_product(normed_all, qkv_grads, [last])
            return late["dw"]
        if step == 1:
            return expert_other(groups[1], last)
        if step == 2:
            return expert_grads(groups[0], last)
        return last

    terms, last = reduce_steps(
        lambda s, after: normed_part(place_of(s), qkv_grads, w_head, after),
        last_work,
    )
    tokens_grad = final_tokens(terms, tokens, attn_row, grad_hidden, [last])
    dw_head = late["dw"]
    last = tokens_grad
    out_part = owner_rows(place, att_head, mixed_columns, branch_all, [last])
    last = expert_grads(groups[1], out_part)
    gate_grad, up_grad, down_grad = late["grads"]
    inputs = tokens.astype(F32)
    sums = jnp.stack(
        [jnp.sum(inputs * inputs), branch_sums[0, 0], jnp.sum(branch_moe * branch_moe)]
    )
    sums = jnp.pad(sums[None, :], ((0, 0), (0, HD - 3)))
    rms_stats = jnp.sqrt(total_over_ep(sums)[:, :3] / (seq * D))

    dw_keep = lax.dynamic_slice_in_dim(dw_head, group * (D // 2), D // 2, 0)
    dw_send = lax.dynamic_slice_in_dim(dw_head, (1 - group) * (D // 2), D // 2, 0)
    dw_half = (dw_keep + swap(dw_send.astype(BF16), "grp").astype(F32)).astype(BF16)
    gain_parts = gain_parts + swap(gain_parts, "grp")
    extra = gain_parts.reshape(1, 2 * HD)
    high = extra.astype(BF16)
    low = (extra - high.astype(F32)).astype(BF16)
    extra = jnp.pad(jnp.concatenate([high, low], 0), ((0, 14), (0, HD)))
    payload = jnp.concatenate(
        [
            dw_half.reshape(members, wide, 3 * HD),
            jnp.broadcast_to(extra, (members,) + extra.shape),
        ],
        1,
    )
    arrived = lax.all_to_all(payload, EP, 0, 0, tiled=True)
    *dense, attn_sums = unpack(arrived, (w_query, w_key, w_value), attn_gain, [last])
    attn_gain_grad = attn_sums[:, 0]
    extras = arrived[:, wide].astype(F32) + arrived[:, wide + 1].astype(F32)
    flat = group * members + place
    head_row = lax.dynamic_slice(
        extras[:, : 2 * HD].reshape(HEADS, 2, HD // wide, wide),
        (flat // (HD // wide), 0, flat % (HD // wide), 0),
        (1, 2, 1, wide),
    ).reshape(2, wide)

    out_part = out_part.reshape(2, wide, D + HD)
    out_keep = lax.dynamic_index_in_dim(out_part, group, 0, False)
    out_send = lax.dynamic_index_in_dim(out_part, 1 - group, 0, False).astype(BF16)
    out_sum = (out_keep + swap(out_send, "grp").astype(F32)).astype(BF16)
    owners = [(g * members + e, 2 * e + g) for g in range(2) for e in range(members)]
    owned = lax.ppermute(out_sum, ALL, owners).astype(F32)
    output_grad = owned[:, :D]
    router_grad, moe_gain_grad = owned[:, D : D + EXPERTS], owned[:, D + EXPERTS]

    return (
        output, tokens_grad, dense[0], dense[1], dense[2], output_grad, router_grad,
        attn_gain_grad, head_row[0], head_row[1], moe_gain_grad, gate_grad, up_grad, down_grad,
        rms_stats,
    )


def fast_solution(mesh, sides):
    inner = jax.sharding.Mesh(mesh.devices.reshape((2,) + sides), ALL)
    rows = P(ALL, None)
    expert = P(EP, None, None)
    return jax.shard_map(
        fast_shards,
        mesh=inner,
        in_specs=(rows,) * 6 + (P(ALL),) * 4 + (expert,) * 3 + (rows,) * 2,
        out_specs=(rows,) * 7 + (P(ALL),) * 4 + (P(EP, "grp", None),) * 3 + (P("grp", None),),
        check_vma=False,
    )


def solution(mesh):
    sides = SIDES.get(mesh.shape["ep"])
    if sides is not None and mesh.shape["grp"] == 2:
        return fast_solution(mesh, sides)
    return jax.shard_map(
        shards,
        mesh=mesh,
        in_specs=(
            P(("grp", "ep"), None),
            P(("grp", "ep"), None),
            P(("grp", "ep"), None),
            P(("grp", "ep"), None),
            P(("grp", "ep"), None),
            P(("grp", "ep"), None),
            P(("grp", "ep")),
            P(("grp", "ep")),
            P(("grp", "ep")),
            P(("grp", "ep")),
            P("ep", None, None),
            P("ep", None, None),
            P("ep", None, None),
            P(("grp", "ep"), None),
            P(("grp", "ep"), None),
        ),
        out_specs=(
            P(("grp", "ep"), None),
            P(("grp", "ep"), None),
            P(("grp", "ep"), None),
            P(("grp", "ep"), None),
            P(("grp", "ep"), None),
            P(("grp", "ep"), None),
            P(("grp", "ep"), None),
            P(("grp", "ep")),
            P(("grp", "ep")),
            P(("grp", "ep")),
            P(("grp", "ep")),
            P("ep", "grp", None),
            P("ep", "grp", None),
            P("ep", "grp", None),
            P("grp", None),
        ),
        check_vma=False,
    )
```
